32 devices in a mesh: row: 8 (over y, x, core), col: 4 (over z).
Axes of the slice: x: 2, y: 2, z: 4, core: 2. Of those that a mesh axis runs over, the one named last changes fastest.
Arguments:
- tile_entries: float32 [8, 4, 64, 128, 128], P('row', 'col'), may hold values from 0 to 65520, as said below
- tile_rows: int32 [8, 4, 64], P('row', 'col'), may hold values from 0 to 7, as said below
- tile_cols: int32 [8, 4, 64], P('row', 'col'), may hold values from 0 to 15, as said below
- tile_count: int32 [8, 4], P('row', 'col'), may hold values from 8 to 64, as said below
- block_x: float32 [64, 8192], P(None, ('row', 'col')), may hold values from 0 to 65520, as said below
- block_y: float32 [64, 8192], P(None, ('row', 'col')), may hold values from 0 to 65520, as said below
Outputs:
- matrix_poly: float32 [3, 64, 64], replicated
- vector_last: float32 [64, 8192], P(None, ('row', 'col'))
The draws below stay inside these ranges and needn't reach their ends.
Inputs may be any that keep to these rules, and one draw needn't show every extreme that they name: `tile_entries`: whole numbers. `block_x`: whole numbers. `block_y`: whole numbers. The slots of one device name distinct block pairs (tile_rows, tile_cols), among them (0, 0) and (7, 15) in some slot. `tile_cols`: block column k of column group c is the global block column (k // 2) * 8 + c * 2 + k % 2. Slots 0 to tile_count - 1 of a device hold its tiles, the rest are unused; some device fills all 64 slots.
All inputs are finite; a program needn't handle non-finite values.
Results may differ from the reference program's by a relative error of at most 0.0003.
Values sent between devices are 32-bit elements; how exact they have to be, the bound alone decides.
No kernel may reach another device: no remote copies, remote signals or barrier semaphores. Data moves between devices by JAX's collectives and lax.ppermute only.
A program may use at most 64 MiB of HBM per device.

```python
import jax
import jax.numpy as jnp
from jax import lax

TILE_SIZE = 128
BLOCK_WIDTH = 64
PIECE_BLOCKS = 2
SLOTS = 64
STEP_COUNT = 3
ROW_BLOCKS = 8
COL_BLOCKS = 16
ALL_BLOCKS = 64
MATRIX_ORDER = 8192
N_ROW = 8
N_COL = 4


def slot_positions(key):
    base_key = jax.random.fold_in(key, 7)
    cell_count = ROW_BLOCKS * COL_BLOCKS
    device_total = N_ROW * N_COL

    def one_device(device_key):
        perm_key, shuffle_key = jax.random.split(device_key)
        middle = jax.random.permutation(perm_key, cell_count - 2)[:SLOTS - 2] + 1
        listed = jnp.concatenate([jnp.array([0, cell_count - 1], jnp.int32), middle.astype(jnp.int32)])
        shuffle = jax.random.permutation(shuffle_key, SLOTS)
        return listed[shuffle]
    device_keys = jax.random.split(base_key, device_total)
    return jax.vmap(one_device)(device_keys).reshape(N_ROW, N_COL, SLOTS)


def draw_tile_rows(key, part):
    return (slot_positions(key) // COL_BLOCKS).astype(jnp.int32)


def draw_tile_cols(key, part):
    return (slot_positions(key) % COL_BLOCKS).astype(jnp.int32)


def draw_tile_count(key, part):
    base_key = jax.random.fold_in(key, 11)
    key_first, key_second, key_busy, key_other = jax.random.split(base_key, 4)
    device_total = N_ROW * N_COL
    least_count = max(SLOTS // 8, 1)
    first_draw = jax.random.randint(key_first, (device_total,), 0, SLOTS)
    second_draw = jax.random.randint(key_second, (device_total,), 0, SLOTS)
    counts = jnp.clip(jnp.minimum(first_draw, second_draw) + 1, least_count, SLOTS)
    busiest = jax.random.randint(key_busy, (), 0, device_total)
    other_device = (busiest + 1 + jax.random.randint(key_other, (), 0, device_total - 1)) % device_total
    device_ids = jnp.arange(device_total)
    counts = jnp.where(device_ids == busiest, SLOTS, jnp.where(device_ids == other_device, least_count, counts))
    return counts.reshape(N_ROW, N_COL).astype(jnp.int32)


def draw_tile_entries(key, part):
    values = jax.random.randint(jax.random.fold_in(key, 3), (N_ROW, N_COL, SLOTS, TILE_SIZE, TILE_SIZE), 0, 65521)
    return values.astype(jnp.float32)


def draw_block_x(key, part):
    values = jax.random.randint(jax.random.fold_in(key, 5), (BLOCK_WIDTH, MATRIX_ORDER), 0, 65521)
    return values.astype(jnp.float32)


def draw_block_y(key, part):
    values = jax.random.randint(jax.random.fold_in(key, 9), (BLOCK_WIDTH, MATRIX_ORDER), 0, 65521)
    return values.astype(jnp.float32)


def setup_inputs(seed: int = 0) -> dict:
    arg_keys = jax.random.split(jax.random.key(seed), 7)
    return {
        "tile_entries": draw_tile_entries(jax.random.fold_in(arg_keys[6], 71), 0),
        "tile_rows": draw_tile_rows(jax.random.fold_in(arg_keys[6], 71), 0),
        "tile_cols": draw_tile_cols(jax.random.fold_in(arg_keys[6], 71), 0),
        "tile_count": draw_tile_count(jax.random.fold_in(arg_keys[6], 71), 0),
        "block_x": draw_block_x(jax.random.fold_in(arg_keys[6], 71), 0),
        "block_y": draw_block_y(jax.random.fold_in(arg_keys[6], 71), 0),
    }


MODULUS = 65521.0


def reduce_mod(values):
    quotient = jnp.floor(values / MODULUS)
    leftover = values - quotient * MODULUS
    leftover = jnp.where(leftover < 0, leftover + MODULUS, leftover)
    return jnp.where(leftover >= MODULUS, leftover - MODULUS, leftover)


def split_digits(values):
    high_digit = jnp.floor(values / 256.0)
    return high_digit, values - 256.0 * high_digit


def combine_parts(high_part, middle_part, low_part):
    return reduce_mod(15.0 * reduce_mod(high_part) + reduce_mod(256.0 * reduce_mod(middle_part)) + reduce_mod(low_part))


def poly_product(left_side, right_side):
    span_width = left_side.shape[-1]
    left_high, left_low = split_digits(left_side)
    right_high, right_low = split_digits(right_side)
    stacked_left = jnp.concatenate([left_high, left_low], 1).astype(jnp.float32)
    stacked_right = jnp.concatenate([right_high, right_low], 2).astype(jnp.float32)
    products = jnp.einsum('kmj,kjn->kmn', stacked_left, stacked_right, precision=lax.Precision.HIGHEST)
    return combine_parts(products[:, :span_width, :span_width],
                         products[:, :span_width, span_width:] + products[:, span_width:, :span_width],
                         products[:, span_width:, span_width:])


def sigma_update(projections):
    span_width = projections[0].shape[0]
    term_count = len(projections) + 1
    identity = jnp.eye(span_width, dtype=jnp.float32)[None]
    polynomial = jnp.concatenate([identity, jnp.zeros((term_count - 1, span_width, span_width), jnp.float32)], 0)
    for step_index in range(1, term_count):
        known_terms = jnp.stack([projections[step_index - 1 - shift] for shift in range(step_index)])
        discrepancy = reduce_mod(jnp.sum(poly_product(polynomial[:step_index], known_terms), 0))
        scaled = poly_product(jnp.broadcast_to(discrepancy, polynomial.shape), polynomial)
        shifted = jnp.concatenate([jnp.zeros((1, span_width, span_width), jnp.float32), polynomial[:-1]], 0)
        polynomial = reduce_mod(shifted - scaled)
    return polynomial


def reference(tile_entries, tile_rows, tile_cols, tile_count, block_x, block_y):
    span_width = block_y.shape[0]
    tile_len = TILE_SIZE
    col_ids = jnp.arange(N_COL, dtype=jnp.int32)[:, None]
    global_cols = ((tile_cols // PIECE_BLOCKS) * ROW_BLOCKS + col_ids * PIECE_BLOCKS + tile_cols % PIECE_BLOCKS).astype(jnp.int32)
    live_slots = (jnp.arange(SLOTS, dtype=jnp.int32)[None, None, :] < tile_count[:, :, None]).astype(jnp.float32)
    onehot = (tile_rows[:, :, None, :] == jnp.arange(ROW_BLOCKS, dtype=jnp.int32)[None, None, :, None]).astype(jnp.float32)
    onehot = onehot * live_slots[:, :, None, :]

    def multiply(vector):
        high_v, low_v = split_digits(vector)
        v_digits = jnp.concatenate([high_v, low_v], 0).reshape(2 * span_width, ALL_BLOCKS, tile_len)

        def one_group(group_data):
            entries_group, group_cols, onehot_group = group_data
            high_a, low_a = split_digits(entries_group)
            a_digits = jnp.stack([high_a, low_a], 2)
            picked = v_digits[:, group_cols]
            products = jnp.einsum('nctk,ctdik->ctdni', picked, a_digits, precision=lax.Precision.HIGHEST)
            residues = combine_parts(products[:, :, 0, :span_width],
                                     products[:, :, 0, span_width:] + products[:, :, 1, :span_width],
                                     products[:, :, 1, span_width:])
            summed = reduce_mod(jnp.einsum('cbt,ctwi->cwbi', onehot_group, residues, precision=lax.Precision.HIGHEST))
            return reduce_mod(jnp.sum(summed, 0)).reshape(span_width, ROW_BLOCKS * tile_len)

        groups = lax.map(one_group, (tile_entries, global_cols, onehot))
        return jnp.transpose(groups, (1, 0, 2)).reshape(span_width, MATRIX_ORDER)

    def project(vector):
        high_x, low_x = split_digits(block_x)
        high_v, low_v = split_digits(vector)
        x_digits = jnp.concatenate([high_x, low_x], 0).reshape(2 * span_width, ALL_BLOCKS, tile_len)
        v_digits = jnp.concatenate([high_v, low_v], 0).reshape(2 * span_width, ALL_BLOCKS, tile_len)
        products = jnp.einsum('mbk,nbk->bmn', x_digits, v_digits, precision=lax.Precision.HIGHEST)
        residues = combine_parts(products[:, :span_width, :span_width],
                                 products[:, :span_width, span_width:] + products[:, span_width:, :span_width],
                                 products[:, span_width:, span_width:])
        residues = residues.reshape(N_ROW, N_COL, PIECE_BLOCKS, span_width, span_width)
        residues = reduce_mod(jnp.sum(residues, 2))
        residues = reduce_mod(jnp.sum(residues, 1))
        return reduce_mod(jnp.sum(residues, 0))

    vector = block_y
    projections = []
    for step_index in range(STEP_COUNT):
        vector = multiply(vector)
        projections.append(project(vector))
    polynomial = sigma_update(projections)
    return polynomial[:STEP_COUNT] / MODULUS, vector / MODULUS
```

```python
import functools

import jax
import jax.numpy as jnp
from jax import lax
from jax.experimental import pallas as pl
from jax.experimental.pallas import tpu as pltpu
from jax.sharding import PartitionSpec as P

STEP_COUNT = 3

MODULUS = 65521.0
HALF_MODULUS = 32760.0
BASE = 256.0
EXACT_DEPTH = 1024
DENSE_CELLS = 4
VMEM_LIMIT = 48 * 1024 * 1024


def reduce_centered(values):
    return values - MODULUS * jnp.floor(values * (1.0 / MODULUS) + 0.5)


def canonical(values):
    reduced = reduce_centered(values)
    return jnp.where(reduced < 0, reduced + MODULUS, reduced)


def balanced_digits(values):
    high = jnp.floor(values * (1.0 / BASE) + 0.5)
    return high, values - BASE * high


def stacked_digits(values):
    high, low = balanced_digits(values)
    return jnp.concatenate([high, low], 0).astype(jnp.bfloat16)


def partner(index, shift, size):
    return index ^ shift if size & (size - 1) == 0 else (index + shift) % size


def shift_of(index, other, size):
    return index ^ other if size & (size - 1) == 0 else (other - index) % size


def gather_pieces(piece, axis):
    size = lax.axis_size(axis)
    return [piece] + [
        lax.ppermute(piece, axis, [(partner(i, shift, size), i) for i in range(size)])
        for shift in range(1, size)
    ]


def scatter_pieces(pieces, axis):
    size = lax.axis_size(axis)
    return [pieces[0]] + [
        lax.ppermute(pieces[shift], axis, [(i, partner(i, shift, size)) for i in range(size)])
        for shift in range(1, size)
    ]


def dot_pairs(left, right):
    return lax.dot_general(left, right, (((1,), (1,)), ((), ())), preferred_element_type=jnp.float32)


def projection_residues(products, span):
    middle = reduce_centered(products[:span, span:]) + reduce_centered(products[span:, :span])
    return reduce_centered(
        15.0 * reduce_centered(products[:span, :span])
        + 256.0 * reduce_centered(middle)
        + reduce_centered(products[span:, span:])
    )


def pack_square(square, width):
    span = square.shape[0]
    rows = span * span // width
    return jnp.concatenate([square[j * rows : (j + 1) * rows] for j in range(width // span)], 1)


def unpack_square(packed, span):
    count = packed.shape[1] // span
    return jnp.concatenate([packed[:, j * span : (j + 1) * span] for j in range(count)], 0)


def build_kernel(group, positions_ref, entries_ref, dense_ref):
    step = pl.program_id(0)
    tile_len = entries_ref.shape[1]

    @pl.when(step == 0)
    def _():
        def clear(block, carry):
            dense_ref[block] = jnp.zeros(dense_ref.shape[1:], dense_ref.dtype)
            return carry

        lax.fori_loop(0, dense_ref.shape[0], clear, 0)

    for index in range(group):
        slot = step * group + index

        @pl.when(slot < positions_ref[2, 0])
        def _():
            values = entries_ref[index]
            values = jnp.where(values > HALF_MODULUS, values - MODULUS, values)
            high, low = balanced_digits(values)
            start = pl.multiple_of(positions_ref[1, slot] * tile_len, tile_len)
            both = jnp.concatenate([high.T, low.T], 1).astype(jnp.bfloat16)
            dense_ref[positions_ref[0, slot], pl.ds(start, tile_len), :] = both


def build_dense(entries, positions, row_blocks, col_blocks):
    slot_count, tile_len, _ = entries.shape
    group = next(size for size in (8, 4, 2, 1) if slot_count % size == 0)
    shape = (row_blocks, col_blocks * tile_len, 2 * tile_len)
    return pl.pallas_call(
        functools.partial(build_kernel, group),
        grid_spec=pltpu.PrefetchScalarGridSpec(
            num_scalar_prefetch=1,
            grid=(slot_count // group,),
            in_specs=[pl.BlockSpec((group, tile_len, tile_len), lambda i, p: (i, 0, 0))],
            out_specs=pl.BlockSpec(shape, lambda i, p: (0, 0, 0)),
        ),
        out_shape=jax.ShapeDtypeStruct(shape, jnp.bfloat16),
        compiler_params=pltpu.CompilerParams(vmem_limit_bytes=VMEM_LIMIT),
        cost_estimate=pl.CostEstimate(
            flops=8 * entries.size, bytes_accessed=16 * entries.size, transcendentals=0
        ),
    )(positions, entries)


def step_kernel(n_row, n_col, span, first, *refs):
    pieces, refs = refs[:n_row], refs[n_row:]
    x_pieces, refs = refs[:n_col], refs[n_col:]
    dense_ref, refs = refs[0], refs[1:]
    outs, refs = refs[:n_col], refs[n_col:]
    if not first:
        total_ref, refs = refs[0], refs[1:]
    held, digits, sems = refs
    row_blocks, depth, width = dense_ref.shape
    tile_len = width // 2
    piece_len = x_pieces[0].shape[1]
    piece_blocks = piece_len // tile_len
    copies = [
        pltpu.make_async_copy(dense_ref.at[b], held.at[b], sems.at[b]) for b in range(row_blocks)
    ]
    for copy in copies:
        copy.start()
    for d, piece in enumerate(pieces):
        vector = reduce_centered(piece[:span, :])
        digits[:, d * piece_len : (d + 1) * piece_len] = stacked_digits(vector)
    if not first:
        packed = pieces[0][span:, :]
        for piece in pieces[1:]:
            packed = packed + piece[span:, :]
        total_ref[...] = unpack_square(reduce_centered(packed), span)
    projected = None
    for e in range(n_col):
        for sub in range(piece_blocks):
            block = e * piece_blocks + sub
            copies[block].wait()
            high = middle = low = 0.0
            for start in range(0, depth, EXACT_DEPTH):
                stop = min(start + EXACT_DEPTH, depth)
                products = jnp.dot(
                    digits[:, start:stop],
                    held[block, start:stop, :],
                    preferred_element_type=jnp.float32,
                )
                products = reduce_centered(products)
                high = high + products[:span, :tile_len]
                middle = middle + products[:span, tile_len:] + products[span:, :tile_len]
                low = low + products[span:, tile_len:]
            outs[e][:span, sub * tile_len : (sub + 1) * tile_len] = reduce_centered(
                15.0 * high + 256.0 * reduce_centered(middle) + low
            )
        x_values = x_pieces[e][...]
        x_values = jnp.where(x_values > HALF_MODULUS, x_values - MODULUS, x_values)
        products = dot_pairs(stacked_digits(x_values), stacked_digits(outs[e][:span, :]))
        if n_col * piece_len > EXACT_DEPTH:
            products = reduce_centered(products)
        projected = products if projected is None else projected + products
    packed = pack_square(projection_residues(projected, span), piece_len)
    for out in outs:
        out[span:, :] = packed


def dense_step(pieces, x_pieces, dense, first):
    n_row, n_col = len(pieces), len(x_pieces)
    span, piece_len = x_pieces[0].shape
    row_blocks, depth, width = dense.shape
    rows = span + span * span // piece_len
    outs = [jax.ShapeDtypeStruct((rows, piece_len), jnp.float32)] * n_col
    if not first:
        outs = outs + [jax.ShapeDtypeStruct((span, span), jnp.float32)]
    vmem = pl.BlockSpec(memory_space=pltpu.VMEM)
    results = pl.pallas_call(
        functools.partial(step_kernel, n_row, n_col, span, first),
        in_specs=[vmem] * (n_row + n_col) + [pl.BlockSpec(memory_space=pl.ANY)],
        out_specs=[vmem] * len(outs),
        out_shape=outs,
        scratch_shapes=[
            pltpu.VMEM(dense.shape, dense.dtype),
            pltpu.VMEM((2 * span, depth), jnp.bfloat16),
            pltpu.SemaphoreType.DMA((row_blocks,)),
        ],
        compiler_params=pltpu.CompilerParams(vmem_limit_bytes=VMEM_LIMIT),
        cost_estimate=pl.CostEstimate(
            flops=4 * span * dense.size, bytes_accessed=2 * dense.size, transcendentals=0
        ),
    )(*pieces, *x_pieces, dense)
    return list(results[:n_col]), (None if first else results[n_col])


def sparse_step(pieces, x_pieces, a_digits, positions, first):
    span, piece_len = x_pieces[0].shape
    slot_count, _, tile_len, _ = a_digits.shape
    n_col = len(x_pieces)
    row_blocks = piece_len // tile_len * n_col
    total = None
    if not first:
        packed = functools.reduce(jnp.add, [piece[span:] for piece in pieces])
        total = unpack_square(reduce_centered(packed), span)
    vector = reduce_centered(jnp.concatenate([piece[:span] for piece in pieces], 1))
    v_digits = stacked_digits(vector).reshape(2 * span, -1, tile_len)
    picked = jnp.take(v_digits, positions[1], axis=1)
    products = jnp.einsum("ntk,tdik->tdni", picked, a_digits, preferred_element_type=jnp.float32)
    products = reduce_centered(products)
    residues = reduce_centered(
        15.0 * products[:, 0, :span]
        + 256.0 * reduce_centered(products[:, 0, span:] + products[:, 1, :span])
        + products[:, 1, span:]
    )
    live = jnp.arange(slot_count, dtype=jnp.int32) < positions[2, 0]
    onehot = positions[0][None, :] == jnp.arange(row_blocks, dtype=jnp.int32)[:, None]
    onehot = (onehot & live[None, :]).astype(jnp.float32)
    summed = jnp.einsum("bt,twi->wbi", onehot, residues, precision=lax.Precision.HIGHEST)
    outs = reduce_centered(summed).reshape(span, n_col, piece_len)
    projected = 0.0
    for e in range(n_col):
        x_values = x_pieces[e]
        x_values = jnp.where(x_values > HALF_MODULUS, x_values - MODULUS, x_values)
        products = dot_pairs(stacked_digits(x_values), stacked_digits(outs[:, e]))
        projected = projected + reduce_centered(products)
    packed = pack_square(projection_residues(projected, span), piece_len)
    return [jnp.concatenate([outs[:, e], packed], 0) for e in range(n_col)], total


def multiply_mod(left, right):
    span = left.shape[0]
    left = stacked_digits(left)
    high, low = (part.astype(jnp.bfloat16) for part in balanced_digits(right))
    by_high = jnp.dot(left, high, preferred_element_type=jnp.float32)
    by_low = jnp.dot(left, low, preferred_element_type=jnp.float32)
    return reduce_centered(
        reduce_centered(15.0 * by_high[:span])
        + 256.0 * reduce_centered(by_low[:span] + by_high[span:])
        + by_low[span:]
    )


def sigma_kernel(count, first_ref, second_ref, *refs):
    thirds, out_ref = refs[:count], refs[count]
    c_1, c_2 = first_ref[...], second_ref[...]
    c_3 = thirds[0][...]
    for piece in thirds[1:]:
        c_3 = c_3 + piece[...]
    c_3 = reduce_centered(c_3)
    e_2 = reduce_centered(c_1 - multiply_mod(c_1, c_2))
    both = reduce_centered(c_1 + e_2)
    start = multiply_mod(e_2, c_1)
    rest = c_1 - multiply_mod(both, c_2)
    e_3 = reduce_centered(multiply_mod(start, c_3) + rest)
    out_ref[0] = canonical(-multiply_mod(e_3, start)) * (1.0 / MODULUS)
    out_ref[1] = canonical(start + multiply_mod(e_3, both)) * (1.0 / MODULUS)
    out_ref[2] = canonical(-both - e_3) * (1.0 / MODULUS)


def sigma_update(c_1, c_2, c_3_pieces):
    span = c_1.shape[0]
    return pl.pallas_call(
        functools.partial(sigma_kernel, len(c_3_pieces)),
        out_shape=jax.ShapeDtypeStruct((STEP_COUNT, span, span), jnp.float32),
    )(c_1, c_2, *c_3_pieces)


def local(tile_entries, tile_rows, tile_cols, tile_count, block_x, block_y):
    entries = tile_entries[0, 0]
    slot_count, tile_len, _ = entries.shape
    span, piece_len = block_y.shape
    piece_blocks = piece_len // tile_len
    n_row, n_col = lax.axis_size("row"), lax.axis_size("col")
    row_blocks, col_blocks = n_col * piece_blocks, n_row * piece_blocks
    rows_here, cols_here = tile_rows[0, 0], tile_cols[0, 0]
    row_shift = shift_of(lax.axis_index("col"), rows_here // piece_blocks, n_col)
    col_shift = shift_of(lax.axis_index("row"), cols_here // piece_blocks, n_row)
    positions = jnp.stack(
        [
            row_shift * piece_blocks + rows_here % piece_blocks,
            col_shift * piece_blocks + cols_here % piece_blocks,
            jnp.full((slot_count,), tile_count[0, 0], jnp.int32),
        ]
    )
    pieces = gather_pieces(block_y, "row")
    x_pieces = gather_pieces(block_x, "col")
    if row_blocks * col_blocks <= DENSE_CELLS * slot_count:
        dense = build_dense(entries, positions, row_blocks, col_blocks)
        multiply = functools.partial(dense_step, dense=dense)
    else:
        centred = jnp.where(entries > HALF_MODULUS, entries - MODULUS, entries)
        a_digits = jnp.stack(balanced_digits(centred), 1).astype(jnp.bfloat16)
        multiply = functools.partial(sparse_step, a_digits=a_digits, positions=positions)
    totals = []
    for step_index in range(STEP_COUNT):
        outs, total = multiply(pieces, x_pieces, first=step_index == 0)
        totals.append(total)
        summed = functools.reduce(jnp.add, scatter_pieces(outs, "col"))
        if step_index < STEP_COUNT - 1:
            pieces = gather_pieces(summed, "row")
    thirds = gather_pieces(unpack_square(summed[span:], span), "row")
    polynomial = sigma_update(totals[1], totals[2], thirds)
    return polynomial, canonical(summed[:span]) * (1.0 / MODULUS)


def solution(mesh):
    placed = (
        P("row", "col", None, None, None),
        P("row", "col", None),
        P("row", "col", None),
        P("row", "col"),
        P(None, ("row", "col")),
        P(None, ("row", "col")),
    )
    return jax.shard_map(
        local, mesh=mesh, in_specs=placed, out_specs=(P(), P(None, ("row", "col"))), check_vma=False
    )
```

```python
import functools

import jax
import jax.numpy as jnp
from jax import lax
from jax.experimental import pallas as pl
from jax.experimental.pallas import tpu as pltpu
from jax.sharding import PartitionSpec as P

STEP_COUNT = 3

MODULUS = 65521.0
HALF_MODULUS = 32760.0
BASE = 256.0
EXACT_DEPTH = 1024
DENSE_CELLS = 4
VMEM_LIMIT = 48 * 1024 * 1024


def reduce_centered(values):
    return values - MODULUS * jnp.floor(values * (1.0 / MODULUS) + 0.5)


def canonical(values):
    reduced = reduce_centered(values)
    return jnp.where(reduced < 0, reduced + MODULUS, reduced)


def balanced_digits(values):
    high = jnp.floor(values * (1.0 / BASE) + 0.5)
    return high, values - BASE * high


def stacked_digits(values):
    high, low = balanced_digits(values)
    return jnp.concatenate([high, low], 0).astype(jnp.bfloat16)


def partner(index, shift, size):
    return index ^ shift if size & (size - 1) == 0 else (index + shift) % size


def shift_of(index, other, size):
    return index ^ other if size & (size - 1) == 0 else (other - index) % size


def fetch(piece, axis, shift):
    size = lax.axis_size(axis)
    return lax.ppermute(piece, axis, [(partner(i, shift, size), i) for i in range(size)])


def gather_pieces(piece, axis):
    return [piece] + [fetch(piece, axis, shift) for shift in range(1, lax.axis_size(axis))]


def gather_in_pairs(piece, axis):
    size = lax.axis_size(axis)
    if size & (size - 1) or size == 1:
        pieces = gather_pieces(piece, axis)
        return [jnp.stack(pieces[:1])] if size == 1 else [jnp.stack(pieces[k::2]) for k in (0, 1)]
    evens = jnp.stack([piece] + [fetch(piece, axis, shift) for shift in range(2, size, 2)])
    return [evens, fetch(evens, axis, 1)]


def piece_at(pairs, shift):
    return pairs[shift % len(pairs)][shift // len(pairs)]


def dot_pairs(left, right):
    return lax.dot_general(left, right, (((1,), (1,)), ((), ())), preferred_element_type=jnp.float32)


def projection_residues(products, span):
    middle = reduce_centered(products[:span, span:]) + reduce_centered(products[span:, :span])
    return reduce_centered(
        15.0 * reduce_centered(products[:span, :span])
        + 256.0 * reduce_centered(middle)
        + reduce_centered(products[span:, span:])
    )


def pack_square(square, width):
    span = square.shape[0]
    rows = span * span // width
    return jnp.concatenate([square[j * rows : (j + 1) * rows] for j in range(width // span)], 1)


def unpack_square(packed, span):
    count = packed.shape[1] // span
    return jnp.concatenate([packed[:, j * span : (j + 1) * span] for j in range(count)], 0)


def build_kernel(group, positions_ref, entries_ref, dense_ref):
    step = pl.program_id(0)
    tile_len = entries_ref.shape[1]

    @pl.when(step == 0)
    def _():
        def clear(block, carry):
            dense_ref[block] = jnp.zeros(dense_ref.shape[1:], dense_ref.dtype)
            return carry

        lax.fori_loop(0, dense_ref.shape[0], clear, 0)

    for index in range(group):
        slot = step * group + index

        @pl.when(slot < positions_ref[2, 0])
        def _():
            values = entries_ref[index]
            values = jnp.where(values > HALF_MODULUS, values - MODULUS, values)
            high, low = balanced_digits(values)
            start = pl.multiple_of(positions_ref[1, slot] * tile_len, tile_len)
            both = jnp.concatenate([high.T, low.T], 1).astype(jnp.bfloat16)
            dense_ref[positions_ref[0, slot], pl.ds(start, tile_len), :] = both


def build_dense(entries, positions, row_blocks, col_blocks):
    slot_count, tile_len, _ = entries.shape
    group = next(size for size in (8, 4, 2, 1) if slot_count % size == 0)
    shape = (row_blocks, col_blocks * tile_len, 2 * tile_len)
    return pl.pallas_call(
        functools.partial(build_kernel, group),
        grid_spec=pltpu.PrefetchScalarGridSpec(
            num_scalar_prefetch=1,
            grid=(slot_count // group,),
            in_specs=[pl.BlockSpec((group, tile_len, tile_len), lambda i, p: (i, 0, 0))],
            out_specs=pl.BlockSpec(shape, lambda i, p: (0, 0, 0)),
        ),
        out_shape=jax.ShapeDtypeStruct(shape, jnp.bfloat16),
        compiler_params=pltpu.CompilerParams(vmem_limit_bytes=VMEM_LIMIT),
        cost_estimate=pl.CostEstimate(
            flops=8 * entries.size, bytes_accessed=16 * entries.size, transcendentals=0
        ),
    )(positions, entries)


def step_kernel(n_pairs, n_row, n_col, span, first, positions_ref, *refs):
    pairs, refs = refs[:n_pairs], refs[n_pairs:]
    x_pieces, refs = refs[:n_col], refs[n_col:]
    dense_ref, out_ref, refs = refs[0], refs[1], refs[2:]
    if not first:
        total_ref, refs = refs[0], refs[1:]
    held, digits, sems = refs
    row_blocks, depth, width = dense_ref.shape
    tile_len = width // 2
    piece_len = x_pieces[0].shape[1]
    piece_blocks = piece_len // tile_len
    copies = [
        pltpu.make_async_copy(dense_ref.at[b], held.at[b], sems.at[b]) for b in range(row_blocks)
    ]
    for copy in copies:
        copy.start()
    for d in range(n_row):
        vector = reduce_centered(piece_at(pairs, d)[:span])
        digits[:, d * piece_len : (d + 1) * piece_len] = stacked_digits(vector)
    if not first:
        packed = sum(jnp.sum(pair[:, span:, :], 0) for pair in pairs)
        total_ref[...] = unpack_square(reduce_centered(packed), span)
    projected = None
    for e in range(n_col):
        target = positions_ref[3, e]
        parts = []
        for sub in range(piece_blocks):
            block = e * piece_blocks + sub
            copies[block].wait()
            high = middle = low = 0.0
            for start in range(0, depth, EXACT_DEPTH):
                stop = min(start + EXACT_DEPTH, depth)
                products = jnp.dot(
                    digits[:, start:stop],
                    held[block, start:stop, :],
                    preferred_element_type=jnp.float32,
                )
                products = reduce_centered(products)
                high = high + products[:span, :tile_len]
                middle = middle + products[:span, tile_len:] + products[span:, :tile_len]
                low = low + products[span:, tile_len:]
            parts.append(reduce_centered(15.0 * high + 256.0 * reduce_centered(middle) + low))
        piece = jnp.concatenate(parts, 1)
        out_ref[target, :span, :] = piece
        x_values = x_pieces[e][...]
        x_values = jnp.where(x_values > HALF_MODULUS, x_values - MODULUS, x_values)
        products = dot_pairs(stacked_digits(x_values), stacked_digits(piece))
        if n_col * piece_len > EXACT_DEPTH:
            products = reduce_centered(products)
        projected = products if projected is None else projected + products
    packed = pack_square(projection_residues(projected, span), piece_len)
    for e in range(n_col):
        out_ref[e, span:, :] = packed


def dense_step(pairs, x_pieces, positions, dense, first):
    n_row, n_col = len(pairs) * pairs[0].shape[0], len(x_pieces)
    span, piece_len = x_pieces[0].shape
    row_blocks, depth, width = dense.shape
    rows = span + span * span // piece_len
    outs = [jax.ShapeDtypeStruct((n_col, rows, piece_len), jnp.float32)]
    if not first:
        outs = outs + [jax.ShapeDtypeStruct((span, span), jnp.float32)]
    vmem = pl.BlockSpec(memory_space=pltpu.VMEM)
    results = pl.pallas_call(
        functools.partial(step_kernel, len(pairs), n_row, n_col, span, first),
        in_specs=[pl.BlockSpec(memory_space=pltpu.SMEM)]
        + [vmem] * (len(pairs) + n_col)
        + [pl.BlockSpec(memory_space=pl.ANY)],
        out_specs=[vmem] * len(outs),
        out_shape=outs,
        scratch_shapes=[
            pltpu.VMEM(dense.shape, dense.dtype),
            pltpu.VMEM((2 * span, depth), jnp.bfloat16),
            pltpu.SemaphoreType.DMA((row_blocks,)),
        ],
        compiler_params=pltpu.CompilerParams(vmem_limit_bytes=VMEM_LIMIT),
        cost_estimate=pl.CostEstimate(
            flops=4 * span * dense.size, bytes_accessed=2 * dense.size, transcendentals=0
        ),
    )(positions, *pairs, *x_pieces, dense)
    return results[0], (None if first else results[1])


def sparse_step(pairs, x_pieces, positions, a_digits, first):
    span, piece_len = x_pieces[0].shape
    pieces = [piece_at(pairs, d) for d in range(len(pairs) * pairs[0].shape[0])]
    slot_count, _, tile_len, _ = a_digits.shape
    n_col = len(x_pieces)
    row_blocks = piece_len // tile_len * n_col
    total = None
    if not first:
        packed = functools.reduce(jnp.add, [piece[span:] for piece in pieces])
        total = unpack_square(reduce_centered(packed), span)
    vector = reduce_centered(jnp.concatenate([piece[:span] for piece in pieces], 1))
    v_digits = stacked_digits(vector).reshape(2 * span, -1, tile_len)
    picked = jnp.take(v_digits, positions[1], axis=1)
    products = jnp.einsum("ntk,tdik->tdni", picked, a_digits, preferred_element_type=jnp.float32)
    products = reduce_centered(products)
    residues = reduce_centered(
        15.0 * products[:, 0, :span]
        + 256.0 * reduce_centered(products[:, 0, span:] + products[:, 1, :span])
        + products[:, 1, span:]
    )
    live = jnp.arange(slot_count, dtype=jnp.int32) < positions[2, 0]
    onehot = positions[0][None, :] == jnp.arange(row_blocks, dtype=jnp.int32)[:, None]
    onehot = (onehot & live[None, :]).astype(jnp.float32)
    summed = jnp.einsum("bt,twi->wbi", onehot, residues, precision=lax.Precision.HIGHEST)
    outs = reduce_centered(summed).reshape(span, n_col, piece_len)
    projected = 0.0
    for e in range(n_col):
        x_values = x_pieces[e]
        x_values = jnp.where(x_values > HALF_MODULUS, x_values - MODULUS, x_values)
        products = dot_pairs(stacked_digits(x_values), stacked_digits(outs[:, e]))
        projected = projected + reduce_centered(products)
    packed = pack_square(projection_residues(projected, span), piece_len)
    outs = jnp.stack([jnp.concatenate([outs[:, e], packed], 0) for e in range(n_col)])
    return jnp.zeros_like(outs).at[positions[3, :n_col]].set(outs), total


def multiply_mod(left, right):
    span = left.shape[0]
    left = stacked_digits(left)
    high, low = (part.astype(jnp.bfloat16) for part in balanced_digits(right))
    by_high = jnp.dot(left, high, preferred_element_type=jnp.float32)
    by_low = jnp.dot(left, low, preferred_element_type=jnp.float32)
    return reduce_centered(
        reduce_centered(15.0 * by_high[:span])
        + 256.0 * reduce_centered(by_low[:span] + by_high[span:])
        + by_low[span:]
    )


def sigma_kernel(count, first_ref, second_ref, *refs):
    thirds, out_ref = refs[:count], refs[count]
    c_1, c_2 = first_ref[...], second_ref[...]
    packed = sum(jnp.sum(pair[...], 0) for pair in thirds)
    c_3 = unpack_square(reduce_centered(packed), c_1.shape[0])
    e_2 = reduce_centered(c_1 - multiply_mod(c_1, c_2))
    both = reduce_centered(c_1 + e_2)
    start = multiply_mod(e_2, c_1)
    rest = c_1 - multiply_mod(both, c_2)
    e_3 = reduce_centered(multiply_mod(start, c_3) + rest)
    out_ref[0] = canonical(-multiply_mod(e_3, start)) * (1.0 / MODULUS)
    out_ref[1] = canonical(start + multiply_mod(e_3, both)) * (1.0 / MODULUS)
    out_ref[2] = canonical(-both - e_3) * (1.0 / MODULUS)


def sigma_update(c_1, c_2, c_3_pairs):
    span = c_1.shape[0]
    return pl.pallas_call(
        functools.partial(sigma_kernel, len(c_3_pairs)),
        out_shape=jax.ShapeDtypeStruct((STEP_COUNT, span, span), jnp.float32),
    )(c_1, c_2, *c_3_pairs)


def local(tile_entries, tile_rows, tile_cols, tile_count, block_x, block_y):
    entries = tile_entries[0, 0]
    slot_count, tile_len, _ = entries.shape
    span, piece_len = block_y.shape
    piece_blocks = piece_len // tile_len
    n_row, n_col = lax.axis_size("row"), lax.axis_size("col")
    row_blocks, col_blocks = n_col * piece_blocks, n_row * piece_blocks
    rows_here, cols_here = tile_rows[0, 0], tile_cols[0, 0]
    row_shift = shift_of(lax.axis_index("col"), rows_here // piece_blocks, n_col)
    col_shift = shift_of(lax.axis_index("row"), cols_here // piece_blocks, n_row)
    positions = jnp.stack(
        [
            row_shift * piece_blocks + rows_here % piece_blocks,
            col_shift * piece_blocks + cols_here % piece_blocks,
            jnp.full((slot_count,), tile_count[0, 0], jnp.int32),
            partner(lax.axis_index("col"), jnp.arange(slot_count, dtype=jnp.int32) % n_col, n_col),
        ]
    )
    pairs = gather_in_pairs(block_y, "row")
    x_pieces = gather_pieces(block_x, "col")
    if row_blocks * col_blocks <= DENSE_CELLS * slot_count:
        dense = build_dense(entries, positions, row_blocks, col_blocks)
        multiply = functools.partial(dense_step, positions=positions, dense=dense)
    else:
        centred = jnp.where(entries > HALF_MODULUS, entries - MODULUS, entries)
        a_digits = jnp.stack(balanced_digits(centred), 1).astype(jnp.bfloat16)
        multiply = functools.partial(sparse_step, positions=positions, a_digits=a_digits)
    totals = []
    for step_index in range(STEP_COUNT):
        outs, total = multiply(pairs, x_pieces, first=step_index == 0)
        totals.append(total)
        summed = jnp.sum(lax.all_to_all(outs, "col", 0, 0), 0)
        if step_index < STEP_COUNT - 1:
            pairs = gather_in_pairs(summed, "row")
    thirds = gather_in_pairs(summed[span:], "row")
    polynomial = sigma_update(totals[1], totals[2], thirds)
    return polynomial, canonical(summed[:span]) * (1.0 / MODULUS)


def solution(mesh):
    placed = (
        P("row", "col", None, None, None),
        P("row", "col", None),
        P("row", "col", None),
        P("row", "col"),
        P(None, ("row", "col")),
        P(None, ("row", "col")),
    )
    return jax.shard_map(
        local, mesh=mesh, in_specs=placed, out_specs=(P(), P(None, ("row", "col"))), check_vma=False
    )
```

```python
import functools

import jax
import jax.numpy as jnp
from jax import lax
from jax.experimental import pallas as pl
from jax.experimental.pallas import tpu as pltpu
from jax.sharding import PartitionSpec as P

STEP_COUNT = 3

MODULUS = 65521.0
HALF_MODULUS = 32760.0
BASE = 256.0
EXACT_DEPTH = 1024
DENSE_CELLS = 4
VMEM_LIMIT = 20 * 1024 * 1024


def reduce_centered(values):
    return values - MODULUS * jnp.floor(values * (1.0 / MODULUS) + 0.5)


def canonical(values):
    reduced = reduce_centered(values)
    return jnp.where(reduced < 0, reduced + MODULUS, reduced)


def balanced_digits(values):
    high = jnp.floor(values * (1.0 / BASE) + 0.5)
    return high, values - BASE * high


def stacked_digits(values):
    high, low = balanced_digits(values)
    return jnp.concatenate([high, low], 0).astype(jnp.bfloat16)


def partner(index, shift, size):
    return index ^ shift if size & (size - 1) == 0 else (index + shift) % size


def shift_of(index, other, size):
    return index ^ other if size & (size - 1) == 0 else (other - index) % size


def fetch(piece, axis, shift):
    size = lax.axis_size(axis)
    return lax.ppermute(piece, axis, [(partner(i, shift, size), i) for i in range(size)])


def gather_pieces(piece, axis):
    return [piece] + [fetch(piece, axis, shift) for shift in range(1, lax.axis_size(axis))]


def scatter_pieces(pieces, axis):
    size = lax.axis_size(axis)
    came = [
        lax.ppermute(pieces[shift], axis, [(i, partner(i, shift, size)) for i in range(size)])
        for shift in reversed(range(1, size))
    ]
    return [pieces[0]] + came


def gather_in_pairs(piece, axis):
    size = lax.axis_size(axis)
    if size & (size - 1) or size == 1:
        pieces = gather_pieces(piece, axis)
        return [jnp.stack(pieces[:1])] if size == 1 else [jnp.stack(pieces[k::2]) for k in (0, 1)]
    evens = jnp.stack([piece] + [fetch(piece, axis, shift) for shift in range(2, size, 2)])
    return [evens, fetch(evens, axis, 1)]


def piece_at(pairs, shift):
    return pairs[shift % len(pairs)][shift // len(pairs)]


def dot_pairs(left, right):
    return lax.dot_general(left, right, (((1,), (1,)), ((), ())), preferred_element_type=jnp.float32)


def projection_residues(products, span):
    middle = reduce_centered(products[:span, span:]) + reduce_centered(products[span:, :span])
    return reduce_centered(
        15.0 * reduce_centered(products[:span, :span])
        + 256.0 * reduce_centered(middle)
        + reduce_centered(products[span:, span:])
    )


def pack_square(square, width):
    span = square.shape[0]
    rows = span * span // width
    return jnp.concatenate([square[j * rows : (j + 1) * rows] for j in range(width // span)], 1)


def unpack_square(packed, span):
    count = packed.shape[1] // span
    return jnp.concatenate([packed[:, j * span : (j + 1) * span] for j in range(count)], 0)


def build_kernel(sizes, rows_ref, cols_ref, count_ref, entries_ref, dense_ref, held, sems):
    n_row, n_col, piece_blocks, group = sizes
    _, _, slot_count, tile_len, _ = entries_ref.shape
    me_row, me_col = lax.axis_index("row"), lax.axis_index("col")

    def chunk(index):
        source = entries_ref.at[0, 0, pl.ds(index * group, group)]
        return pltpu.make_async_copy(source, held.at[pl.ds(index * group, group)], sems.at[index])

    chunk_count = slot_count // group
    for index in range(chunk_count):
        chunk(index).start()

    def clear(block, carry):
        dense_ref[block] = jnp.zeros(dense_ref.shape[1:], dense_ref.dtype)
        return carry

    lax.fori_loop(0, dense_ref.shape[0], clear, 0)

    def place(slot):
        row, col = rows_ref[0, 0, slot], cols_ref[0, 0, slot]
        row_shift = shift_of(me_col, row // piece_blocks, n_col)
        col_shift = shift_of(me_row, col // piece_blocks, n_row)
        block = row_shift * piece_blocks + row % piece_blocks
        start = (col_shift * piece_blocks + col % piece_blocks) * tile_len
        values = jnp.where(slot < count_ref[0, 0], held[slot], 0.0)
        values = jnp.where(values > HALF_MODULUS, values - MODULUS, values)
        high, low = balanced_digits(values)
        both = jnp.concatenate([high.T, low.T], 1).astype(jnp.bfloat16)
        dense_ref[block, pl.ds(pl.multiple_of(start, tile_len), tile_len), :] = both

    def step(index, carry):
        chunk(index).wait()
        for offset in range(group):
            place(index * group + offset)
        return carry

    lax.fori_loop(0, chunk_count, step, 0)


def build_dense(tile_entries, tile_rows, tile_cols, tile_count, sizes):
    n_row, n_col, piece_blocks = sizes
    _, _, slot_count, tile_len, _ = tile_entries.shape
    group = next(size for size in (8, 4, 2, 1) if slot_count % size == 0)
    shape = (n_col * piece_blocks, n_row * piece_blocks * tile_len, 2 * tile_len)
    smem = pl.BlockSpec(memory_space=pltpu.SMEM)
    return pl.pallas_call(
        functools.partial(build_kernel, (*sizes, group)),
        in_specs=[smem, smem, smem, pl.BlockSpec(memory_space=pltpu.HBM)],
        out_specs=pl.BlockSpec(memory_space=pltpu.VMEM),
        out_shape=pltpu.VMEM(shape, jnp.bfloat16),
        scratch_shapes=[
            pltpu.VMEM((slot_count, tile_len, tile_len), jnp.float32),
            pltpu.SemaphoreType.DMA((slot_count // group,)),
        ],
        compiler_params=pltpu.CompilerParams(vmem_limit_bytes=VMEM_LIMIT),
        cost_estimate=pl.CostEstimate(
            flops=8 * tile_entries.size, bytes_accessed=8 * tile_entries.size, transcendentals=0
        ),
    )(tile_rows, tile_cols, tile_count, tile_entries)


def step_kernel(n_pairs, n_row, n_col, span, first, *refs):
    pairs, refs = refs[:n_pairs], refs[n_pairs:]
    x_pieces, refs = refs[:n_col], refs[n_col:]
    dense_ref, refs = refs[0], refs[1:]
    outs, refs = refs[:n_col], refs[n_col:]
    if not first:
        total_ref, refs = refs[0], refs[1:]
    digits = refs[0]
    row_blocks, depth, width = dense_ref.shape
    tile_len = width // 2
    piece_len = x_pieces[0].shape[1]
    piece_blocks = piece_len // tile_len
    for d in range(n_row):
        vector = reduce_centered(piece_at(pairs, d)[:span])
        digits[:, d * piece_len : (d + 1) * piece_len] = stacked_digits(vector)
    if not first:
        packed = sum(jnp.sum(pair[:, span:, :], 0) for pair in pairs)
        total_ref[...] = unpack_square(reduce_centered(packed), span)
    projected = None
    for e in range(n_col):
        parts = []
        for sub in range(piece_blocks):
            block = e * piece_blocks + sub
            high = middle = low = 0.0
            for start in range(0, depth, EXACT_DEPTH):
                stop = min(start + EXACT_DEPTH, depth)
                products = jnp.dot(
                    digits[:, start:stop],
                    dense_ref[block, start:stop, :],
                    preferred_element_type=jnp.float32,
                )
                products = reduce_centered(products)
                high = high + products[:span, :tile_len]
                middle = middle + products[:span, tile_len:] + products[span:, :tile_len]
                low = low + products[span:, tile_len:]
            parts.append(reduce_centered(15.0 * high + 256.0 * reduce_centered(middle) + low))
        piece = jnp.concatenate(parts, 1)
        outs[e][:span, :] = piece
        x_values = x_pieces[e][...]
        x_values = jnp.where(x_values > HALF_MODULUS, x_values - MODULUS, x_values)
        products = dot_pairs(stacked_digits(x_values), stacked_digits(piece))
        if n_col * piece_len > EXACT_DEPTH:
            products = reduce_centered(products)
        projected = products if projected is None else projected + products
    packed = pack_square(projection_residues(projected, span), piece_len)
    for out in outs:
        out[span:, :] = packed


def dense_step(pairs, x_pieces, dense, first):
    n_row, n_col = len(pairs) * pairs[0].shape[0], len(x_pieces)
    span, piece_len = x_pieces[0].shape
    row_blocks, depth, width = dense.shape
    rows = span + span * span // piece_len
    outs = [pltpu.VMEM((rows, piece_len), jnp.float32)] * n_col
    if not first:
        outs = outs + [jax.ShapeDtypeStruct((span, span), jnp.float32)]
    vmem = pl.BlockSpec(memory_space=pltpu.VMEM)
    results = pl.pallas_call(
        functools.partial(step_kernel, len(pairs), n_row, n_col, span, first),
        in_specs=[vmem] * (len(pairs) + n_col + 1),
        out_specs=[vmem] * len(outs),
        out_shape=outs,
        scratch_shapes=[pltpu.VMEM((2 * span, depth), jnp.bfloat16)],
        compiler_params=pltpu.CompilerParams(vmem_limit_bytes=VMEM_LIMIT),
        cost_estimate=pl.CostEstimate(
            flops=4 * span * dense.size, bytes_accessed=2 * dense.size, transcendentals=0
        ),
    )(*(pltpu.with_memory_space_constraint(part, pltpu.VMEM) for part in (*pairs, *x_pieces, dense)))
    return list(results[:n_col]), (None if first else results[n_col])


def sparse_step(pairs, x_pieces, positions, a_digits, first):
    span, piece_len = x_pieces[0].shape
    pieces = [piece_at(pairs, d) for d in range(len(pairs) * pairs[0].shape[0])]
    slot_count, _, tile_len, _ = a_digits.shape
    n_col = len(x_pieces)
    row_blocks = piece_len // tile_len * n_col
    total = None
    if not first:
        packed = functools.reduce(jnp.add, [piece[span:] for piece in pieces])
        total = unpack_square(reduce_centered(packed), span)
    vector = reduce_centered(jnp.concatenate([piece[:span] for piece in pieces], 1))
    v_digits = stacked_digits(vector).reshape(2 * span, -1, tile_len)
    picked = jnp.take(v_digits, positions[1], axis=1)
    products = jnp.einsum("ntk,tdik->tdni", picked, a_digits, preferred_element_type=jnp.float32)
    products = reduce_centered(products)
    residues = reduce_centered(
        15.0 * products[:, 0, :span]
        + 256.0 * reduce_centered(products[:, 0, span:] + products[:, 1, :span])
        + products[:, 1, span:]
    )
    live = jnp.arange(slot_count, dtype=jnp.int32) < positions[2]
    onehot = positions[0][None, :] == jnp.arange(row_blocks, dtype=jnp.int32)[:, None]
    onehot = (onehot & live[None, :]).astype(jnp.float32)
    summed = jnp.einsum("bt,twi->wbi", onehot, residues, precision=lax.Precision.HIGHEST)
    outs = reduce_centered(summed).reshape(span, n_col, piece_len)
    projected = 0.0
    for e in range(n_col):
        x_values = x_pieces[e]
        x_values = jnp.where(x_values > HALF_MODULUS, x_values - MODULUS, x_values)
        products = dot_pairs(stacked_digits(x_values), stacked_digits(outs[:, e]))
        projected = projected + reduce_centered(products)
    packed = pack_square(projection_residues(projected, span), piece_len)
    return [jnp.concatenate([outs[:, e], packed], 0) for e in range(n_col)], total


def multiply_mod(left, right):
    span = left.shape[0]
    left = stacked_digits(left)
    high, low = (part.astype(jnp.bfloat16) for part in balanced_digits(right))
    by_high = jnp.dot(left, high, preferred_element_type=jnp.float32)
    by_low = jnp.dot(left, low, preferred_element_type=jnp.float32)
    return reduce_centered(
        reduce_centered(15.0 * by_high[:span])
        + 256.0 * reduce_centered(by_low[:span] + by_high[span:])
        + by_low[span:]
    )


def sigma_kernel(count, first_ref, second_ref, *refs):
    thirds, out_ref = refs[:count], refs[count]
    c_1, c_2 = first_ref[...], second_ref[...]
    packed = sum(jnp.sum(pair[...], 0) for pair in thirds)
    c_3 = unpack_square(reduce_centered(packed), c_1.shape[0])
    e_2 = reduce_centered(c_1 - multiply_mod(c_1, c_2))
    both = reduce_centered(c_1 + e_2)
    start = multiply_mod(e_2, c_1)
    rest = c_1 - multiply_mod(both, c_2)
    e_3 = reduce_centered(multiply_mod(start, c_3) + rest)
    out_ref[0] = canonical(-multiply_mod(e_3, start)) * (1.0 / MODULUS)
    out_ref[1] = canonical(start + multiply_mod(e_3, both)) * (1.0 / MODULUS)
    out_ref[2] = canonical(-both - e_3) * (1.0 / MODULUS)


def sigma_update(c_1, c_2, c_3_pairs):
    span = c_1.shape[0]
    return pl.pallas_call(
        functools.partial(sigma_kernel, len(c_3_pairs)),
        out_shape=jax.ShapeDtypeStruct((STEP_COUNT, span, span), jnp.float32),
    )(c_1, c_2, *c_3_pairs)


def sparse_tiles(tile_entries, tile_rows, tile_cols, tile_count, sizes):
    n_row, n_col, piece_blocks = sizes
    entries, rows, cols = tile_entries[0, 0], tile_rows[0, 0], tile_cols[0, 0]
    row_shift = shift_of(lax.axis_index("col"), rows // piece_blocks, n_col)
    col_shift = shift_of(lax.axis_index("row"), cols // piece_blocks, n_row)
    positions = [
        row_shift * piece_blocks + rows % piece_blocks,
        col_shift * piece_blocks + cols % piece_blocks,
        tile_count[0, 0],
    ]
    entries = jnp.where(entries > HALF_MODULUS, entries - MODULUS, entries)
    return jnp.stack(balanced_digits(entries), 1).astype(jnp.bfloat16), positions


def local(tile_entries, tile_rows, tile_cols, tile_count, block_x, block_y):
    _, _, slot_count, tile_len, _ = tile_entries.shape
    span, piece_len = block_y.shape
    piece_blocks = piece_len // tile_len
    n_row, n_col = lax.axis_size("row"), lax.axis_size("col")
    tiles = (tile_entries, tile_rows, tile_cols, tile_count)
    sizes = (n_row, n_col, piece_blocks)
    pairs = gather_in_pairs(block_y, "row")
    x_pieces = gather_pieces(block_x, "col")
    if n_col * piece_blocks * n_row * piece_blocks <= DENSE_CELLS * slot_count:
        multiply = functools.partial(dense_step, dense=build_dense(*tiles, sizes))
    else:
        a_digits, positions = sparse_tiles(*tiles, sizes)
        multiply = functools.partial(sparse_step, positions=positions, a_digits=a_digits)
    totals = []
    for step_index in range(STEP_COUNT):
        outs, total = multiply(pairs, x_pieces, first=step_index == 0)
        totals.append(total)
        summed = functools.reduce(jnp.add, scatter_pieces(outs, "col"))
        if step_index < STEP_COUNT - 1:
            pairs = gather_in_pairs(summed, "row")
    thirds = gather_in_pairs(summed[span:], "row")
    polynomial = sigma_update(totals[1], totals[2], thirds)
    return polynomial, canonical(summed[:span]) * (1.0 / MODULUS)


def solution(mesh):
    placed = (
        P("row", "col", None, None, None),
        P("row", "col", None),
        P("row", "col", None),
        P("row", "col"),
        P(None, ("row", "col")),
        P(None, ("row", "col")),
    )
    return jax.shard_map(
        local, mesh=mesh, in_specs=placed, out_specs=(P(), P(None, ("row", "col"))), check_vma=False
    )
```

```python
import functools

import jax
import jax.numpy as jnp
from jax import lax
from jax.experimental import pallas as pl
from jax.experimental.pallas import tpu as pltpu
from jax.sharding import PartitionSpec as P

STEP_COUNT = 3

MODULUS = 65521.0
HALF_MODULUS = 32760.0
BASE = 256.0
EXACT_DEPTH = 1024
DENSE_CELLS = 4
VMEM_LIMIT = 20 * 1024 * 1024


def reduce_centered(values):
    return values - MODULUS * jnp.floor(values * (1.0 / MODULUS) + 0.5)


def canonical(values):
    reduced = reduce_centered(values)
    return jnp.where(reduced < 0, reduced + MODULUS, reduced)


def balanced_digits(values):
    high = jnp.floor(values * (1.0 / BASE) + 0.5)
    return high, values - BASE * high


def stacked_digits(values):
    high, low = balanced_digits(values)
    return jnp.concatenate([high, low], 0).astype(jnp.bfloat16)


def centred_digits(residues):
    return stacked_digits(jnp.where(residues > HALF_MODULUS, residues - MODULUS, residues))


def partner(index, shift, size):
    return index ^ shift if size & (size - 1) == 0 else (index + shift) % size


def shift_of(index, other, size):
    return index ^ other if size & (size - 1) == 0 else (other - index) % size


def fetch(piece, axis, shift):
    size = lax.axis_size(axis)
    return lax.ppermute(piece, axis, [(partner(i, shift, size), i) for i in range(size)])


def gather_pieces(piece, axis):
    return [piece] + [fetch(piece, axis, shift) for shift in range(1, lax.axis_size(axis))]


def scatter_pieces(pieces, axis):
    size = lax.axis_size(axis)
    came = [
        lax.ppermute(pieces[shift], axis, [(i, partner(i, shift, size)) for i in range(size)])
        for shift in reversed(range(1, size))
    ]
    return [pieces[0]] + came


def zero_after(*arrays):
    return sum(array[(0,) * array.ndim] for array in arrays) * 0.0


def gather_in_pairs(piece, axis, *before):
    size = lax.axis_size(axis)
    if size & (size - 1) or size == 1:
        pieces = gather_pieces(piece, axis)
        return [jnp.stack(pieces[:1])] if size == 1 else [jnp.stack(pieces[k::2]) for k in (0, 1)]
    evens = jnp.stack([piece] + [fetch(piece, axis, shift) for shift in range(2, size, 2)])
    if before:
        evens = evens + zero_after(*before)
    return [evens, fetch(evens, axis, 1)]


def piece_at(pairs, shift):
    return pairs[shift % len(pairs)][shift // len(pairs)]


def dot_pairs(left, right):
    return lax.dot_general(left, right, (((1,), (1,)), ((), ())), preferred_element_type=jnp.float32)


def projection_residues(products, span):
    middle = reduce_centered(products[:span, span:]) + reduce_centered(products[span:, :span])
    return reduce_centered(
        15.0 * reduce_centered(products[:span, :span])
        + 256.0 * reduce_centered(middle)
        + reduce_centered(products[span:, span:])
    )


def pack_square(square, width):
    span = square.shape[0]
    rows = span * span // width
    return jnp.concatenate([square[j * rows : (j + 1) * rows] for j in range(width // span)], 1)


def unpack_square(packed, span):
    count = packed.shape[1] // span
    return jnp.concatenate([packed[:, j * span : (j + 1) * span] for j in range(count)], 0)


def build_kernel(sizes, *refs):
    count_ref, entries_ref, dense_ref, token_ref = refs[2:6]
    rows_ref, cols_ref, held, sems = refs[6:]
    n_row, n_col, piece_blocks, group = sizes
    _, _, slot_count, tile_len, _ = entries_ref.shape
    me_row, me_col = lax.axis_index("row"), lax.axis_index("col")

    def chunk(index):
        source = entries_ref.at[0, 0, pl.ds(index * group, group)]
        return pltpu.make_async_copy(source, held.at[pl.ds(index * group, group)], sems.at[index])

    chunk_count = slot_count // group
    positions = [
        pltpu.make_async_copy(refs[index], refs[6 + index], sems.at[chunk_count + index])
        for index in range(2)
    ]
    for copy in positions:
        copy.start()
    for index in range(chunk_count):
        chunk(index).start()

    def clear(block, carry):
        dense_ref[block] = jnp.zeros(dense_ref.shape[1:], dense_ref.dtype)
        return carry

    lax.fori_loop(0, dense_ref.shape[0], clear, 0)
    for copy in positions:
        copy.wait()

    def place(slot):
        row, col = rows_ref[0, 0, slot], cols_ref[0, 0, slot]
        row_shift = shift_of(me_col, row // piece_blocks, n_col)
        col_shift = shift_of(me_row, col // piece_blocks, n_row)
        block = row_shift * piece_blocks + row % piece_blocks
        start = (col_shift * piece_blocks + col % piece_blocks) * tile_len
        values = jnp.where(slot < count_ref[0, 0], held[slot], 0.0)
        values = jnp.where(values > HALF_MODULUS, values - MODULUS, values)
        high, low = balanced_digits(values)
        both = jnp.concatenate([high.T, low.T], 1).astype(jnp.bfloat16)
        dense_ref[block, pl.ds(pl.multiple_of(start, tile_len), tile_len), :] = both

    def step(index, carry):
        chunk(index).wait()
        for offset in range(group):
            place(index * group + offset)
        return carry

    lax.fori_loop(0, chunk_count, step, 0)
    token_ref[...] = jnp.zeros_like(token_ref)


def build_dense(tile_entries, tile_rows, tile_cols, tile_count, sizes):
    n_row, n_col, piece_blocks = sizes
    _, _, slot_count, tile_len, _ = tile_entries.shape
    group = next(size for size in (8, 4, 2, 1) if slot_count % size == 0)
    shape = (n_col * piece_blocks, n_row * piece_blocks * tile_len, 2 * tile_len)
    hbm = pl.BlockSpec(memory_space=pltpu.HBM)
    rows, cols, entries = (
        pltpu.with_memory_space_constraint(part, pltpu.HBM)
        for part in (tile_rows, tile_cols, tile_entries)
    )
    return pl.pallas_call(
        functools.partial(build_kernel, (*sizes, group)),
        in_specs=[hbm, hbm, pl.BlockSpec(memory_space=pltpu.SMEM), hbm],
        out_specs=[pl.BlockSpec(memory_space=pltpu.VMEM)] * 2,
        out_shape=[pltpu.VMEM(shape, jnp.bfloat16), pltpu.VMEM((8, 128), jnp.float32)],
        scratch_shapes=[
            *(pltpu.SMEM(part.shape, part.dtype) for part in (tile_rows, tile_cols)),
            pltpu.VMEM((slot_count, tile_len, tile_len), jnp.float32),
            pltpu.SemaphoreType.DMA((slot_count // group + 2,)),
        ],
        compiler_params=pltpu.CompilerParams(vmem_limit_bytes=VMEM_LIMIT),
        cost_estimate=pl.CostEstimate(
            flops=8 * tile_entries.size, bytes_accessed=8 * tile_entries.size, transcendentals=0
        ),
    )(rows, cols, tile_count, entries)


def step_kernel(n_pairs, n_row, n_col, span, first, last, *refs):
    pairs, refs = refs[:n_pairs], refs[n_pairs:]
    if not last:
        x_pieces, refs = refs[:n_col], refs[n_col:]
    dense_ref, refs = refs[0], refs[1:]
    outs, refs = refs[:n_col], refs[n_col:]
    if not first:
        total_ref, refs = refs[0], refs[1:]
    digits = refs[0]
    row_blocks, depth, width = dense_ref.shape
    tile_len = width // 2
    piece_len = outs[0].shape[1]
    piece_blocks = piece_len // tile_len
    packed_rows = span * span // piece_len
    for d in range(n_row):
        vector = reduce_centered(piece_at(pairs, d)[:span])
        digits[:, d * piece_len : (d + 1) * piece_len] = stacked_digits(vector)
    if not first:
        packed = sum(jnp.sum(pair[:, span : span + packed_rows, :], 0) for pair in pairs)
        total_ref[...] = unpack_square(reduce_centered(packed), span)
    projected = None
    for e in reversed(range(n_col)):
        parts = []
        for sub in range(piece_blocks):
            block = e * piece_blocks + sub
            high = middle = low = 0.0
            for start in range(0, depth, EXACT_DEPTH):
                stop = min(start + EXACT_DEPTH, depth)
                products = jnp.dot(
                    digits[:, start:stop],
                    dense_ref[block, start:stop, :],
                    preferred_element_type=jnp.float32,
                )
                products = reduce_centered(products)
                high = high + products[:span, :tile_len]
                middle = middle + products[:span, tile_len:] + products[span:, :tile_len]
                low = low + products[span:, tile_len:]
            parts.append(reduce_centered(15.0 * high + 256.0 * reduce_centered(middle) + low))
        piece = jnp.concatenate(parts, 1)
        outs[e][:span, :] = piece
        if not last:
            products = dot_pairs(centred_digits(x_pieces[e][...]), stacked_digits(piece))
            if n_col * piece_len > EXACT_DEPTH:
                products = reduce_centered(products)
            projected = products if projected is None else projected + products
    if last:
        packed = sum(jnp.sum(pair[:, span + packed_rows :, :], 0) for pair in pairs)
    else:
        packed = pack_square(projection_residues(projected, span), piece_len)
    for out in outs:
        out[span:, :] = packed


def in_vmem(*arrays):
    return [pltpu.with_memory_space_constraint(array, pltpu.VMEM) for array in arrays]


def dense_step(pairs, x_pieces, dense, first, last):
    n_row, n_col = len(pairs) * pairs[0].shape[0], len(x_pieces)
    span, piece_len = x_pieces[0].shape
    _, depth, _ = dense.shape
    rows = span + span * span // piece_len
    outs = [pltpu.VMEM((rows, piece_len), jnp.float32)] * n_col
    if not first:
        outs = outs + [jax.ShapeDtypeStruct((span, span), jnp.float32)]
    operands = in_vmem(*pairs, *([] if last else x_pieces), dense)
    results = pl.pallas_call(
        functools.partial(step_kernel, len(pairs), n_row, n_col, span, first, last),
        in_specs=[pl.BlockSpec(memory_space=pltpu.VMEM)] * len(operands),
        out_specs=[pl.BlockSpec(memory_space=pltpu.VMEM)] * len(outs),
        out_shape=outs,
        scratch_shapes=[pltpu.VMEM((2 * span, depth), jnp.bfloat16)],
        compiler_params=pltpu.CompilerParams(vmem_limit_bytes=VMEM_LIMIT),
        cost_estimate=pl.CostEstimate(
            flops=4 * span * dense.size, bytes_accessed=2 * dense.size, transcendentals=0
        ),
    )(*operands)
    return list(results[:n_col]), (None if first else results[n_col])


def left_kernel(n_col, n_row, *refs):
    x_pieces, (dense_ref, _, out_ref) = refs[:n_col], refs[n_col:]
    me_row = lax.axis_index("row")
    row_blocks, _, width = dense_ref.shape
    tile_len = width // 2
    span, piece_len = x_pieces[0].shape
    piece_blocks = piece_len // tile_len
    x_digits = [centred_digits(piece[...]) for piece in x_pieces]
    for d in range(n_row):
        by_high = by_low = 0.0
        for block in range(row_blocks):
            sub = block % piece_blocks
            left = x_digits[block // piece_blocks][:, sub * tile_len : (sub + 1) * tile_len]
            right = dense_ref[block, d * piece_len : (d + 1) * piece_len, :]
            by_high = by_high + dot_pairs(left, right[:, :tile_len])
            by_low = by_low + dot_pairs(left, right[:, tile_len:])
            if (block + 1) * tile_len % EXACT_DEPTH == 0:
                by_high, by_low = reduce_centered(by_high), reduce_centered(by_low)
        by_high, by_low = reduce_centered(by_high), reduce_centered(by_low)
        piece = reduce_centered(
            15.0 * by_high[:span]
            + 256.0 * reduce_centered(by_low[:span] + by_high[span:])
            + by_low[span:]
        )
        out_ref[partner(me_row, d, n_row)] = piece


def dense_left(x_pieces, dense, after, n_row):
    n_col = len(x_pieces)
    span, piece_len = x_pieces[0].shape
    operands = in_vmem(*x_pieces, dense, after)
    return pl.pallas_call(
        functools.partial(left_kernel, n_col, n_row),
        in_specs=[pl.BlockSpec(memory_space=pltpu.VMEM)] * (n_col + 1)
        + [pl.BlockSpec(memory_space=pl.ANY)],
        out_specs=pl.BlockSpec(memory_space=pltpu.VMEM),
        out_shape=jax.ShapeDtypeStruct((n_row, span, piece_len), jnp.float32),
        compiler_params=pltpu.CompilerParams(vmem_limit_bytes=VMEM_LIMIT),
        cost_estimate=pl.CostEstimate(
            flops=4 * span * dense.size, bytes_accessed=2 * dense.size, transcendentals=0
        ),
    )(*operands)


def append_kernel(w_ref, *refs):
    pieces, out_ref = refs[:-1], refs[-1]
    span = w_ref.shape[0]
    summed = pieces[0][...]
    for piece in pieces[1:]:
        summed = summed + piece[...]
    rows = summed.shape[0]
    out_ref[:rows, :] = summed
    products = dot_pairs(
        stacked_digits(reduce_centered(w_ref[...])),
        stacked_digits(reduce_centered(summed[:span])),
    )
    out_ref[rows:, :] = pack_square(projection_residues(products, span), summed.shape[1])


def append_projection(w_piece, pieces):
    span, piece_len = w_piece.shape
    rows = pieces[0].shape[0] + span * span // piece_len
    return pl.pallas_call(
        append_kernel,
        out_shape=jax.ShapeDtypeStruct((rows, piece_len), jnp.float32),
    )(w_piece, *pieces)


def sparse_step(pairs, x_pieces, positions, a_digits, first, last):
    span, piece_len = x_pieces[0].shape
    pieces = [piece_at(pairs, d) for d in range(len(pairs) * pairs[0].shape[0])]
    tile_len = a_digits.shape[-1]
    n_col = len(x_pieces)
    packed_rows = span * span // piece_len
    total = None
    if not first:
        packed = functools.reduce(jnp.add, [piece[span : span + packed_rows] for piece in pieces])
        total = unpack_square(reduce_centered(packed), span)
    vector = reduce_centered(jnp.concatenate([piece[:span] for piece in pieces], 1))
    residues = sparse_residues(vector, positions[1], a_digits, "ntk,tdik->tdni")
    summed = sparse_sum(residues, positions[0], positions[2], piece_len // tile_len * n_col)
    outs = reduce_centered(summed).reshape(span, n_col, piece_len)
    if last:
        packed = functools.reduce(jnp.add, [piece[span + packed_rows :] for piece in pieces])
    else:
        projected = 0.0
        for e in range(n_col):
            products = dot_pairs(centred_digits(x_pieces[e]), stacked_digits(outs[:, e]))
            projected = projected + reduce_centered(products)
        packed = pack_square(projection_residues(projected, span), piece_len)
    return [jnp.concatenate([outs[:, e], packed], 0) for e in range(n_col)], total


def sparse_residues(vector, places, a_digits, spec):
    span, tile_len = vector.shape[0], a_digits.shape[-1]
    v_digits = stacked_digits(vector).reshape(2 * span, -1, tile_len)
    picked = jnp.take(v_digits, places, axis=1)
    products = jnp.einsum(spec, picked, a_digits, preferred_element_type=jnp.float32)
    products = reduce_centered(products)
    return reduce_centered(
        15.0 * products[:, 0, :span]
        + 256.0 * reduce_centered(products[:, 0, span:] + products[:, 1, :span])
        + products[:, 1, span:]
    )


def sparse_sum(residues, places, count, blocks):
    live = jnp.arange(places.shape[0], dtype=jnp.int32) < count
    onehot = places[None, :] == jnp.arange(blocks, dtype=jnp.int32)[:, None]
    onehot = (onehot & live[None, :]).astype(jnp.float32)
    return jnp.einsum("bt,twi->wbi", onehot, residues, precision=lax.Precision.HIGHEST)


def sparse_left(x_pieces, after, positions, a_digits, n_row):
    del after
    span, piece_len = x_pieces[0].shape
    tile_len = a_digits.shape[-1]
    values = jnp.concatenate(x_pieces, 1)
    values = jnp.where(values > HALF_MODULUS, values - MODULUS, values)
    residues = sparse_residues(values, positions[0], a_digits, "nti,tdik->tdnk")
    summed = sparse_sum(residues, positions[1], positions[2], piece_len // tile_len * n_row)
    pieces = reduce_centered(summed).reshape(span, n_row, piece_len)
    order = partner(lax.axis_index("row"), jnp.arange(n_row, dtype=jnp.int32), n_row)
    return jnp.zeros((n_row, span, piece_len)).at[order].set(jnp.moveaxis(pieces, 1, 0))


def multiply_mod(left, right):
    span = left.shape[0]
    left = stacked_digits(left)
    high, low = (part.astype(jnp.bfloat16) for part in balanced_digits(right))
    by_high = jnp.dot(left, high, preferred_element_type=jnp.float32)
    by_low = jnp.dot(left, low, preferred_element_type=jnp.float32)
    return reduce_centered(
        reduce_centered(15.0 * by_high[:span])
        + 256.0 * reduce_centered(by_low[:span] + by_high[span:])
        + by_low[span:]
    )


def sigma_start_kernel(first_ref, second_ref, start_ref, both_ref, rest_ref):
    c_1, c_2 = first_ref[...], second_ref[...]
    e_2 = reduce_centered(c_1 - multiply_mod(c_1, c_2))
    both = reduce_centered(c_1 + e_2)
    start_ref[...] = multiply_mod(e_2, c_1)
    both_ref[...] = both
    rest_ref[...] = c_1 - multiply_mod(both, c_2)


def sigma_end_kernel(start_ref, both_ref, rest_ref, packed_ref, out_ref):
    start, both = start_ref[...], both_ref[...]
    c_3 = unpack_square(reduce_centered(packed_ref[...]), start.shape[0])
    e_3 = reduce_centered(multiply_mod(start, c_3) + rest_ref[...])
    out_ref[0] = canonical(-multiply_mod(e_3, start)) * (1.0 / MODULUS)
    out_ref[1] = canonical(start + multiply_mod(e_3, both)) * (1.0 / MODULUS)
    out_ref[2] = canonical(-both - e_3) * (1.0 / MODULUS)


def sigma_update(c_1, c_2, packed_3):
    square = jax.ShapeDtypeStruct(c_1.shape, jnp.float32)
    known = pl.pallas_call(sigma_start_kernel, out_shape=[square] * 3)(c_1, c_2)
    shape = jax.ShapeDtypeStruct((STEP_COUNT, *c_1.shape), jnp.float32)
    return pl.pallas_call(sigma_end_kernel, out_shape=shape)(*known, packed_3)


def sparse_tiles(tile_entries, tile_rows, tile_cols, tile_count, sizes):
    n_row, n_col, piece_blocks = sizes
    entries, rows, cols = tile_entries[0, 0], tile_rows[0, 0], tile_cols[0, 0]
    row_shift = shift_of(lax.axis_index("col"), rows // piece_blocks, n_col)
    col_shift = shift_of(lax.axis_index("row"), cols // piece_blocks, n_row)
    positions = [
        row_shift * piece_blocks + rows % piece_blocks,
        col_shift * piece_blocks + cols % piece_blocks,
        tile_count[0, 0],
    ]
    entries = jnp.where(entries > HALF_MODULUS, entries - MODULUS, entries)
    return jnp.stack(balanced_digits(entries), 1).astype(jnp.bfloat16), positions


def local(tile_entries, tile_rows, tile_cols, tile_count, block_x, block_y):
    _, _, slot_count, tile_len, _ = tile_entries.shape
    span, piece_len = block_y.shape
    piece_blocks = piece_len // tile_len
    n_row, n_col = lax.axis_size("row"), lax.axis_size("col")
    tiles = (tile_entries, tile_rows, tile_cols, tile_count)
    sizes = (n_row, n_col, piece_blocks)
    x_pieces = gather_pieces(block_x, "col")
    before = list(x_pieces[1:])
    if n_col * piece_blocks * n_row * piece_blocks <= DENSE_CELLS * slot_count:
        dense, token = build_dense(*tiles, sizes)
        before.append(token)
        multiply = functools.partial(dense_step, dense=dense)
        multiply_left = functools.partial(dense_left, dense=dense)
    else:
        a_digits, positions = sparse_tiles(*tiles, sizes)
        multiply = functools.partial(sparse_step, positions=positions, a_digits=a_digits)
        multiply_left = functools.partial(sparse_left, positions=positions, a_digits=a_digits)
    pairs = gather_in_pairs(block_y, "row", *before)
    totals = []
    for step_index in range(STEP_COUNT):
        first, last = step_index == 0, step_index == STEP_COUNT - 1
        outs, total = multiply(pairs, x_pieces, first=first, last=last)
        totals.append(total)
        pieces = scatter_pieces(outs, "col")
        if step_index == STEP_COUNT - 2:
            pairs = gather_in_pairs(append_projection(w_piece, pieces), "row")
            continue
        summed = functools.reduce(jnp.add, pieces)
        if first:
            left = multiply_left(x_pieces, after=outs[0], n_row=n_row)
            w_piece = lax.psum_scatter(left, "row")
            summed = summed + zero_after(left)
        if not last:
            pairs = gather_in_pairs(summed, "row")
    polynomial = sigma_update(totals[1], totals[2], summed[span:])
    return polynomial, canonical(summed[:span]) * (1.0 / MODULUS)


def solution(mesh):
    placed = (
        P("row", "col", None, None, None),
        P("row", "col", None),
        P("row", "col", None),
        P("row", "col"),
        P(None, ("row", "col")),
        P(None, ("row", "col")),
    )
    return jax.shard_map(
        local, mesh=mesh, in_specs=placed, out_specs=(P(), P(None, ("row", "col"))), check_vma=False
    )
```

```python
import functools

import jax
import jax.numpy as jnp
from jax import lax
from jax.experimental import pallas as pl
from jax.experimental.pallas import tpu as pltpu
from jax.sharding import PartitionSpec as P

STEP_COUNT = 3

MODULUS = 65521.0
HALF_MODULUS = 32760.0
BASE = 256.0
EXACT_DEPTH = 1024
DENSE_CELLS = 4
VMEM_LIMIT = 16 * 1024 * 1024
SMALL_LIMIT = 4 * 1024 * 1024


def reduce_centered(values):
    return values - MODULUS * jnp.floor(values * (1.0 / MODULUS) + 0.5)


def canonical(values):
    reduced = reduce_centered(values)
    return jnp.where(reduced < 0, reduced + MODULUS, reduced)


def balanced_digits(values):
    high = jnp.floor(values * (1.0 / BASE) + 0.5)
    return high, values - BASE * high


def stacked_digits(values):
    high, low = balanced_digits(values)
    return jnp.concatenate([high, low], 0).astype(jnp.bfloat16)


def centred_digits(residues):
    return stacked_digits(jnp.where(residues > HALF_MODULUS, residues - MODULUS, residues))


def partner(index, shift, size):
    return index ^ shift if size & (size - 1) == 0 else (index + shift) % size


def shift_of(index, other, size):
    return index ^ other if size & (size - 1) == 0 else (other - index) % size


def fetch(piece, axis, shift):
    size = lax.axis_size(axis)
    return lax.ppermute(piece, axis, [(partner(i, shift, size), i) for i in range(size)])


def gather_pieces(piece, axis):
    return [piece] + [fetch(piece, axis, shift) for shift in range(1, lax.axis_size(axis))]


def scatter_pieces(pieces, axis):
    size = lax.axis_size(axis)
    came = [
        lax.ppermute(pieces[shift], axis, [(i, partner(i, shift, size)) for i in range(size)])
        for shift in reversed(range(1, size))
    ]
    return [pieces[0]] + came


def stack_kernel(count, *refs):
    out_ref = refs[-1]
    for index in range(count):
        out_ref[index] = refs[index][...]


def stack_after(pieces, before):
    return pl.pallas_call(
        functools.partial(stack_kernel, len(pieces)),
        in_specs=[pl.BlockSpec(memory_space=pltpu.VMEM)] * len(pieces)
        + [pl.BlockSpec(memory_space=pl.ANY)] * len(before),
        out_specs=pl.BlockSpec(memory_space=pltpu.VMEM),
        out_shape=pltpu.VMEM((len(pieces), *pieces[0].shape), pieces[0].dtype),
        compiler_params=pltpu.CompilerParams(vmem_limit_bytes=SMALL_LIMIT),
    )(*in_vmem(*pieces), *before)


def gather_in_pairs(piece, axis, before=()):
    size = lax.axis_size(axis)
    if size & (size - 1) or size == 1:
        pieces = gather_pieces(piece, axis)
        return [jnp.stack(pieces[:1])] if size == 1 else [jnp.stack(pieces[k::2]) for k in (0, 1)]
    evens = [piece] + [fetch(piece, axis, shift) for shift in range(2, size, 2)]
    evens = stack_after(evens, before) if before else jnp.stack(evens)
    return [evens, fetch(evens, axis, 1)]


def reduce_pieces(evens, odds, axis):
    came = None
    if odds is not None:
        came = fetch(odds, axis, 1)
        evens = [even + came[index] for index, even in enumerate(evens)]
    parts = [evens[0]]
    for index in reversed(range(1, len(evens))):
        parts.append(fetch(evens[index], axis, 2 * index))
    return parts, came


def piece_at(pairs, shift):
    return pairs[shift % len(pairs)][shift // len(pairs)]


def dot_pairs(left, right):
    return lax.dot_general(left, right, (((1,), (1,)), ((), ())), preferred_element_type=jnp.float32)


def projection_residues(products, span):
    middle = reduce_centered(products[:span, span:]) + reduce_centered(products[span:, :span])
    return reduce_centered(
        15.0 * reduce_centered(products[:span, :span])
        + 256.0 * reduce_centered(middle)
        + reduce_centered(products[span:, span:])
    )


def pack_square(square, width):
    span = square.shape[0]
    rows = span * span // width
    return jnp.concatenate([square[j * rows : (j + 1) * rows] for j in range(width // span)], 1)


def unpack_square(packed, span):
    count = packed.shape[1] // span
    return jnp.concatenate([packed[:, j * span : (j + 1) * span] for j in range(count)], 0)


def build_kernel(sizes, *refs):
    count_ref, entries_ref, dense_ref, token_ref = refs[2:6]
    rows_ref, cols_ref, held, sems = refs[6:]
    n_row, n_col, piece_blocks, group = sizes
    _, _, slot_count, tile_len, _ = entries_ref.shape
    me_row, me_col = lax.axis_index("row"), lax.axis_index("col")

    def chunk(index):
        source = entries_ref.at[0, 0, pl.ds(index * group, group)]
        return pltpu.make_async_copy(source, held.at[pl.ds(index * group, group)], sems.at[index])

    chunk_count = slot_count // group
    positions = [
        pltpu.make_async_copy(refs[index], refs[6 + index], sems.at[chunk_count + index])
        for index in range(2)
    ]
    for copy in positions:
        copy.start()
    for index in range(chunk_count):
        chunk(index).start()

    def clear(block, carry):
        dense_ref[block] = jnp.zeros(dense_ref.shape[1:], dense_ref.dtype)
        return carry

    lax.fori_loop(0, dense_ref.shape[0], clear, 0)
    for copy in positions:
        copy.wait()

    def place(slot):
        row, col = rows_ref[0, 0, slot], cols_ref[0, 0, slot]
        row_shift = shift_of(me_col, row // piece_blocks, n_col)
        col_shift = shift_of(me_row, col // piece_blocks, n_row)
        block = row_shift * piece_blocks + row % piece_blocks
        start = (col_shift * piece_blocks + col % piece_blocks) * tile_len
        values = jnp.where(slot < count_ref[0, 0], held[slot], 0.0)
        values = jnp.where(values > HALF_MODULUS, values - MODULUS, values)
        high, low = balanced_digits(values)
        both = jnp.concatenate([high.T, low.T], 1).astype(jnp.bfloat16)
        dense_ref[block, pl.ds(pl.multiple_of(start, tile_len), tile_len), :] = both

    def step(index, carry):
        chunk(index).wait()
        for offset in range(group):
            place(index * group + offset)
        return carry

    lax.fori_loop(0, chunk_count, step, 0)
    token_ref[...] = jnp.zeros_like(token_ref)


def build_dense(tile_entries, tile_rows, tile_cols, tile_count, sizes):
    n_row, n_col, piece_blocks = sizes
    _, _, slot_count, tile_len, _ = tile_entries.shape
    group = next(size for size in (8, 4, 2, 1) if slot_count % size == 0)
    shape = (n_col * piece_blocks, n_row * piece_blocks * tile_len, 2 * tile_len)
    hbm = pl.BlockSpec(memory_space=pltpu.HBM)
    rows, cols, entries = (
        pltpu.with_memory_space_constraint(part, pltpu.HBM)
        for part in (tile_rows, tile_cols, tile_entries)
    )
    return pl.pallas_call(
        functools.partial(build_kernel, (*sizes, group)),
        in_specs=[hbm, hbm, pl.BlockSpec(memory_space=pltpu.SMEM), hbm],
        out_specs=[pl.BlockSpec(memory_space=pltpu.VMEM)] * 2,
        out_shape=[pltpu.VMEM(shape, jnp.bfloat16), pltpu.VMEM((8, 128), jnp.float32)],
        scratch_shapes=[
            *(pltpu.SMEM(part.shape, part.dtype) for part in (tile_rows, tile_cols)),
            pltpu.VMEM((slot_count, tile_len, tile_len), jnp.float32),
            pltpu.SemaphoreType.DMA((slot_count // group + 2,)),
        ],
        compiler_params=pltpu.CompilerParams(vmem_limit_bytes=VMEM_LIMIT),
        cost_estimate=pl.CostEstimate(
            flops=8 * tile_entries.size, bytes_accessed=8 * tile_entries.size, transcendentals=0
        ),
    )(rows, cols, tile_count, entries)


def step_kernel(n_pairs, n_row, n_col, span, first, last, n_before, *refs):
    pairs, refs = refs[:n_pairs], refs[n_pairs:]
    if not last:
        x_pieces, refs = refs[:n_col], refs[n_col:]
    dense_ref, refs = refs[0], refs[1 + n_before :]
    outs, refs = refs[:n_col], refs[n_col:]
    if not first:
        total_ref, refs = refs[0], refs[1:]
    digits = refs[0]
    row_blocks, depth, width = dense_ref.shape
    tile_len = width // 2
    piece_len = outs[0].shape[1]
    piece_blocks = piece_len // tile_len
    packed_rows = span * span // piece_len
    for d in range(n_row):
        vector = reduce_centered(piece_at(pairs, d)[:span])
        digits[:, d * piece_len : (d + 1) * piece_len] = stacked_digits(vector)
    if not first:
        packed = sum(jnp.sum(pair[:, span : span + packed_rows, :], 0) for pair in pairs)
        total_ref[...] = unpack_square(reduce_centered(packed), span)
    projected = None
    for e in reversed(range(n_col)):
        parts = []
        for sub in range(piece_blocks):
            block = e * piece_blocks + sub
            high = middle = low = 0.0
            for start in range(0, depth, EXACT_DEPTH):
                stop = min(start + EXACT_DEPTH, depth)
                products = jnp.dot(
                    digits[:, start:stop],
                    dense_ref[block, start:stop, :],
                    preferred_element_type=jnp.float32,
                )
                products = reduce_centered(products)
                high = high + products[:span, :tile_len]
                middle = middle + products[:span, tile_len:] + products[span:, :tile_len]
                low = low + products[span:, tile_len:]
            parts.append(reduce_centered(15.0 * high + 256.0 * reduce_centered(middle) + low))
        piece = jnp.concatenate(parts, 1)
        outs[e][:span, :] = piece
        if not last:
            products = dot_pairs(centred_digits(x_pieces[e][...]), stacked_digits(piece))
            if n_col * piece_len > EXACT_DEPTH:
                products = reduce_centered(products)
            projected = products if projected is None else projected + products
    if last:
        packed = sum(jnp.sum(pair[:, span + packed_rows :, :], 0) for pair in pairs)
    else:
        packed = pack_square(projection_residues(projected, span), piece_len)
    for out in outs:
        out[span:, :] = packed


def in_vmem(*arrays):
    return [pltpu.with_memory_space_constraint(array, pltpu.VMEM) for array in arrays]


def dense_step(pairs, x_pieces, dense, first, last, before=()):
    n_row, n_col = len(pairs) * pairs[0].shape[0], len(x_pieces)
    span, piece_len = x_pieces[0].shape
    _, depth, _ = dense.shape
    rows = span + span * span // piece_len
    outs = [pltpu.VMEM((rows, piece_len), jnp.float32)] * n_col
    if not first:
        outs = outs + [jax.ShapeDtypeStruct((span, span), jnp.float32)]
    operands = in_vmem(*pairs, *([] if last else x_pieces), dense)
    results = pl.pallas_call(
        functools.partial(step_kernel, len(pairs), n_row, n_col, span, first, last, len(before)),
        in_specs=[pl.BlockSpec(memory_space=pltpu.VMEM)] * len(operands)
        + [pl.BlockSpec(memory_space=pl.ANY)] * len(before),
        out_specs=[pl.BlockSpec(memory_space=pltpu.VMEM)] * len(outs),
        out_shape=outs,
        scratch_shapes=[pltpu.VMEM((2 * span, depth), jnp.bfloat16)],
        compiler_params=pltpu.CompilerParams(vmem_limit_bytes=VMEM_LIMIT),
        cost_estimate=pl.CostEstimate(
            flops=4 * span * dense.size, bytes_accessed=2 * dense.size, transcendentals=0
        ),
    )(*operands, *before)
    return list(results[:n_col]), (None if first else results[n_col])


def left_kernel(n_col, n_row, *refs):
    x_pieces, dense_ref, refs = refs[:n_col], refs[n_col], refs[n_col + 2 :]
    n_evens = (n_row + 1) // 2
    evens, odds = refs[:n_evens], refs[n_evens:]
    row_blocks, _, width = dense_ref.shape
    tile_len = width // 2
    span, piece_len = x_pieces[0].shape
    piece_blocks = piece_len // tile_len
    x_digits = [centred_digits(piece[...]) for piece in x_pieces]
    for d in range(n_row):
        by_high = by_low = 0.0
        for block in range(row_blocks):
            sub = block % piece_blocks
            left = x_digits[block // piece_blocks][:, sub * tile_len : (sub + 1) * tile_len]
            right = dense_ref[block, d * piece_len : (d + 1) * piece_len, :]
            by_high = by_high + dot_pairs(left, right[:, :tile_len])
            by_low = by_low + dot_pairs(left, right[:, tile_len:])
            if (block + 1) * tile_len % EXACT_DEPTH == 0:
                by_high, by_low = reduce_centered(by_high), reduce_centered(by_low)
        by_high, by_low = reduce_centered(by_high), reduce_centered(by_low)
        piece = reduce_centered(
            15.0 * by_high[:span]
            + 256.0 * reduce_centered(by_low[:span] + by_high[span:])
            + by_low[span:]
        )
        if d % 2 == 0:
            evens[d // 2][...] = piece
        else:
            odds[0][d // 2] = piece


def dense_left(x_pieces, dense, after, n_row):
    n_col = len(x_pieces)
    span, piece_len = x_pieces[0].shape
    n_evens = (n_row + 1) // 2
    outs = [pltpu.VMEM((span, piece_len), jnp.float32)] * n_evens
    if n_row > 1:
        outs = outs + [pltpu.VMEM((n_row // 2, span, piece_len), jnp.float32)]
    results = pl.pallas_call(
        functools.partial(left_kernel, n_col, n_row),
        in_specs=[pl.BlockSpec(memory_space=pltpu.VMEM)] * (n_col + 1)
        + [pl.BlockSpec(memory_space=pl.ANY)],
        out_specs=[pl.BlockSpec(memory_space=pltpu.VMEM)] * len(outs),
        out_shape=outs,
        compiler_params=pltpu.CompilerParams(vmem_limit_bytes=VMEM_LIMIT),
        cost_estimate=pl.CostEstimate(
            flops=4 * span * dense.size, bytes_accessed=2 * dense.size, transcendentals=0
        ),
    )(*in_vmem(*x_pieces, dense), after)
    return list(results[:n_evens]), (results[n_evens] if n_row > 1 else None)


def append_kernel(n_parts, *refs):
    w_parts, pieces, out_ref = refs[:n_parts], refs[n_parts:-1], refs[-1]
    span = w_parts[0].shape[0]
    w_piece = functools.reduce(jnp.add, [part[...] for part in w_parts])
    summed = functools.reduce(jnp.add, [piece[...] for piece in pieces])
    rows = summed.shape[0]
    out_ref[:rows, :] = summed
    products = dot_pairs(
        stacked_digits(reduce_centered(w_piece)), stacked_digits(reduce_centered(summed[:span]))
    )
    out_ref[rows:, :] = pack_square(projection_residues(products, span), summed.shape[1])


def append_projection(w_parts, pieces):
    span, piece_len = w_parts[0].shape
    rows = pieces[0].shape[0] + span * span // piece_len
    operands = in_vmem(*w_parts, *pieces)
    return pl.pallas_call(
        functools.partial(append_kernel, len(w_parts)),
        in_specs=[pl.BlockSpec(memory_space=pltpu.VMEM)] * len(operands),
        out_specs=pl.BlockSpec(memory_space=pltpu.VMEM),
        out_shape=pltpu.VMEM((rows, piece_len), jnp.float32),
        compiler_params=pltpu.CompilerParams(vmem_limit_bytes=SMALL_LIMIT),
    )(*operands)


def sparse_step(pairs, x_pieces, positions, a_digits, first, last, before=()):
    del before
    span, piece_len = x_pieces[0].shape
    pieces = [piece_at(pairs, d) for d in range(len(pairs) * pairs[0].shape[0])]
    tile_len = a_digits.shape[-1]
    n_col = len(x_pieces)
    packed_rows = span * span // piece_len
    total = None
    if not first:
        packed = functools.reduce(jnp.add, [piece[span : span + packed_rows] for piece in pieces])
        total = unpack_square(reduce_centered(packed), span)
    vector = reduce_centered(jnp.concatenate([piece[:span] for piece in pieces], 1))
    residues = sparse_residues(vector, positions[1], a_digits, "ntk,tdik->tdni")
    summed = sparse_sum(residues, positions[0], positions[2], piece_len // tile_len * n_col)
    outs = reduce_centered(summed).reshape(span, n_col, piece_len)
    if last:
        packed = functools.reduce(jnp.add, [piece[span + packed_rows :] for piece in pieces])
    else:
        projected = 0.0
        for e in range(n_col):
            products = dot_pairs(centred_digits(x_pieces[e]), stacked_digits(outs[:, e]))
            projected = projected + reduce_centered(products)
        packed = pack_square(projection_residues(projected, span), piece_len)
    return [jnp.concatenate([outs[:, e], packed], 0) for e in range(n_col)], total


def sparse_residues(vector, places, a_digits, spec):
    span, tile_len = vector.shape[0], a_digits.shape[-1]
    v_digits = stacked_digits(vector).reshape(2 * span, -1, tile_len)
    picked = jnp.take(v_digits, places, axis=1)
    products = jnp.einsum(spec, picked, a_digits, preferred_element_type=jnp.float32)
    products = reduce_centered(products)
    return reduce_centered(
        15.0 * products[:, 0, :span]
        + 256.0 * reduce_centered(products[:, 0, span:] + products[:, 1, :span])
        + products[:, 1, span:]
    )


def sparse_sum(residues, places, count, blocks):
    live = jnp.arange(places.shape[0], dtype=jnp.int32) < count
    onehot = places[None, :] == jnp.arange(blocks, dtype=jnp.int32)[:, None]
    onehot = (onehot & live[None, :]).astype(jnp.float32)
    return jnp.einsum("bt,twi->wbi", onehot, residues, precision=lax.Precision.HIGHEST)


def sparse_left(x_pieces, after, positions, a_digits, n_row):
    del after
    span, piece_len = x_pieces[0].shape
    tile_len = a_digits.shape[-1]
    values = jnp.concatenate(x_pieces, 1)
    values = jnp.where(values > HALF_MODULUS, values - MODULUS, values)
    residues = sparse_residues(values, positions[0], a_digits, "nti,tdik->tdnk")
    summed = sparse_sum(residues, positions[1], positions[2], piece_len // tile_len * n_row)
    pieces = reduce_centered(summed).reshape(span, n_row, piece_len)
    odds = jnp.moveaxis(pieces[:, 1::2], 1, 0) if n_row > 1 else None
    return [pieces[:, d] for d in range(0, n_row, 2)], odds


def multiply_mod(left, right):
    span = left.shape[0]
    left = stacked_digits(left)
    high, low = (part.astype(jnp.bfloat16) for part in balanced_digits(right))
    by_high = jnp.dot(left, high, preferred_element_type=jnp.float32)
    by_low = jnp.dot(left, low, preferred_element_type=jnp.float32)
    return reduce_centered(
        reduce_centered(15.0 * by_high[:span])
        + 256.0 * reduce_centered(by_low[:span] + by_high[span:])
        + by_low[span:]
    )


def sigma_start_kernel(first_ref, second_ref, start_ref, both_ref, rest_ref):
    c_1, c_2 = first_ref[...], second_ref[...]
    e_2 = reduce_centered(c_1 - multiply_mod(c_1, c_2))
    both = reduce_centered(c_1 + e_2)
    start_ref[...] = multiply_mod(e_2, c_1)
    both_ref[...] = both
    rest_ref[...] = c_1 - multiply_mod(both, c_2)


def sigma_end_kernel(start_ref, both_ref, rest_ref, packed_ref, out_ref):
    start, both = start_ref[...], both_ref[...]
    c_3 = unpack_square(reduce_centered(packed_ref[...]), start.shape[0])
    e_3 = reduce_centered(multiply_mod(start, c_3) + rest_ref[...])
    out_ref[0] = canonical(-multiply_mod(e_3, start)) * (1.0 / MODULUS)
    out_ref[1] = canonical(start + multiply_mod(e_3, both)) * (1.0 / MODULUS)
    out_ref[2] = canonical(-both - e_3) * (1.0 / MODULUS)


def sigma_update(c_1, c_2, packed_3):
    square = jax.ShapeDtypeStruct(c_1.shape, jnp.float32)
    params = pltpu.CompilerParams(vmem_limit_bytes=SMALL_LIMIT)
    known = pl.pallas_call(sigma_start_kernel, out_shape=[square] * 3, compiler_params=params)(c_1, c_2)
    shape = jax.ShapeDtypeStruct((STEP_COUNT, *c_1.shape), jnp.float32)
    return pl.pallas_call(sigma_end_kernel, out_shape=shape, compiler_params=params)(*known, packed_3)


def sparse_tiles(tile_entries, tile_rows, tile_cols, tile_count, sizes):
    n_row, n_col, piece_blocks = sizes
    entries, rows, cols = tile_entries[0, 0], tile_rows[0, 0], tile_cols[0, 0]
    row_shift = shift_of(lax.axis_index("col"), rows // piece_blocks, n_col)
    col_shift = shift_of(lax.axis_index("row"), cols // piece_blocks, n_row)
    positions = [
        row_shift * piece_blocks + rows % piece_blocks,
        col_shift * piece_blocks + cols % piece_blocks,
        tile_count[0, 0],
    ]
    entries = jnp.where(entries > HALF_MODULUS, entries - MODULUS, entries)
    return jnp.stack(balanced_digits(entries), 1).astype(jnp.bfloat16), positions


def local(tile_entries, tile_rows, tile_cols, tile_count, block_x, block_y):
    _, _, slot_count, tile_len, _ = tile_entries.shape
    span, piece_len = block_y.shape
    piece_blocks = piece_len // tile_len
    n_row, n_col = lax.axis_size("row"), lax.axis_size("col")
    tiles = (tile_entries, tile_rows, tile_cols, tile_count)
    sizes = (n_row, n_col, piece_blocks)
    x_pieces = gather_pieces(block_x, "col")
    before = list(x_pieces[1:])
    if n_col * piece_blocks * n_row * piece_blocks <= DENSE_CELLS * slot_count:
        dense, token = build_dense(*tiles, sizes)
        before.append(token)
        multiply = functools.partial(dense_step, dense=dense)
        multiply_left = functools.partial(dense_left, dense=dense)
    else:
        a_digits, positions = sparse_tiles(*tiles, sizes)
        multiply = functools.partial(sparse_step, positions=positions, a_digits=a_digits)
        multiply_left = functools.partial(sparse_left, positions=positions, a_digits=a_digits)
    pairs = gather_in_pairs(block_y, "row", before)
    totals, before = [], []
    for step_index in range(STEP_COUNT):
        first, last = step_index == 0, step_index == STEP_COUNT - 1
        outs, total = multiply(pairs, x_pieces, first=first, last=last, before=before)
        totals.append(total)
        pieces = scatter_pieces(outs, "col")
        if step_index == STEP_COUNT - 2:
            pairs = gather_in_pairs(append_projection(w_parts, pieces), "row")
            continue
        summed = functools.reduce(jnp.add, pieces)
        before = []
        if first:
            evens, odds = multiply_left(x_pieces, after=outs[0], n_row=n_row)
            w_parts, came = reduce_pieces(evens, odds, "row")
            before = [came if odds is not None else evens[0]]
        if not last:
            pairs = gather_in_pairs(summed, "row")
    polynomial = sigma_update(totals[1], totals[2], summed[span:])
    return polynomial, canonical(summed[:span]) * (1.0 / MODULUS)


def solution(mesh):
    placed = (
        P("row", "col", None, None, None),
        P("row", "col", None),
        P("row", "col", None),
        P("row", "col"),
        P(None, ("row", "col")),
        P(None, ("row", "col")),
    )
    return jax.shard_map(
        local, mesh=mesh, in_specs=placed, out_specs=(P(), P(None, ("row", "col"))), check_vma=False
    )
```

```python
import functools

import jax
import jax.numpy as jnp
from jax import lax
from jax.experimental import pallas as pl
from jax.experimental.pallas import tpu as pltpu
from jax.sharding import PartitionSpec as P

STEP_COUNT = 3

MODULUS = 65521.0
HALF_MODULUS = 32760.0
BASE = 256.0
EXACT_DEPTH = 1024
DENSE_CELLS = 4
VMEM_LIMIT = 16 * 1024 * 1024
SMALL_LIMIT = 4 * 1024 * 1024


def reduce_centered(values):
    return values - MODULUS * jnp.floor(values * (1.0 / MODULUS) + 0.5)


def canonical(values):
    reduced = reduce_centered(values)
    return jnp.where(reduced < 0, reduced + MODULUS, reduced)


def balanced_digits(values):
    high = jnp.floor(values * (1.0 / BASE) + 0.5)
    return high, values - BASE * high


def stacked_digits(values):
    high, low = balanced_digits(values)
    return jnp.concatenate([high, low], 0).astype(jnp.bfloat16)


def centred_digits(residues):
    return stacked_digits(jnp.where(residues > HALF_MODULUS, residues - MODULUS, residues))


def partner(index, shift, size):
    return index ^ shift if size & (size - 1) == 0 else (index + shift) % size


def shift_of(index, other, size):
    return index ^ other if size & (size - 1) == 0 else (other - index) % size


def fetch(piece, axis, shift):
    size = lax.axis_size(axis)
    return lax.ppermute(piece, axis, [(partner(i, shift, size), i) for i in range(size)])


def scatter_pieces(pieces, axis):
    size = lax.axis_size(axis)
    came = [
        lax.ppermute(pieces[shift], axis, [(i, partner(i, shift, size)) for i in range(size)])
        for shift in reversed(range(1, size))
    ]
    return [pieces[0]] + came


def call(kernel, operands, outs, before=(), scratch=(), limit=SMALL_LIMIT, flops=0):
    def body(*refs):
        kernel(*refs[: len(operands)], *refs[len(operands) + len(before) :])

    vmem = pl.BlockSpec(memory_space=pltpu.VMEM)
    return pl.pallas_call(
        body,
        in_specs=[vmem] * len(operands) + [pl.BlockSpec(memory_space=pl.ANY)] * len(before),
        out_specs=[vmem] * len(outs),
        out_shape=outs,
        scratch_shapes=list(scratch),
        compiler_params=pltpu.CompilerParams(vmem_limit_bytes=limit),
        cost_estimate=pl.CostEstimate(flops=flops, bytes_accessed=0, transcendentals=0),
    )(*(pltpu.with_memory_space_constraint(part, pltpu.VMEM) for part in operands), *before)


def held(*shape):
    return pltpu.VMEM(shape, jnp.float32)


def stack_after(pieces, before=()):
    def kernel(*refs):
        for index, ref in enumerate(refs[:-1]):
            refs[-1][index] = ref[...]

    return call(kernel, pieces, [held(len(pieces), *pieces[0].shape)], before)[0]


def sum_after(pieces, before=()):
    def kernel(*refs):
        refs[-1][...] = functools.reduce(jnp.add, [ref[...] for ref in refs[:-1]])

    return call(kernel, pieces, [held(*pieces[0].shape)], before)[0]


def fetch_evens(piece, axis):
    return [fetch(piece, axis, shift) for shift in range(2, lax.axis_size(axis), 2)]


def gather_evens(piece, axis):
    return stack_after([piece] + fetch_evens(piece, axis))


def gather_odds(evens, axis):
    size = lax.axis_size(axis)
    assert size > 1 and size & (size - 1) == 0
    return fetch(evens, axis, 1)


def dot_pairs(left, right):
    return lax.dot_general(left, right, (((1,), (1,)), ((), ())), preferred_element_type=jnp.float32)


def combine(high, middle, low):
    return reduce_centered(15.0 * high + 256.0 * reduce_centered(middle) + low)


def pack_square(square, width):
    span = square.shape[0]
    rows = span * span // width
    return jnp.concatenate([square[j * rows : (j + 1) * rows] for j in range(width // span)], 1)


def unpack_square(packed, span):
    count = packed.shape[1] // span
    return jnp.concatenate([packed[:, j * span : (j + 1) * span] for j in range(count)], 0)


def build_kernel(sizes, *refs):
    count_ref, entries_ref, x_ref, y_ref, dense_ref, x_out, y_out, token_ref = refs[2:10]
    rows_ref, cols_ref, tiles, sems = refs[10:]
    n_row, n_col, piece_blocks, group = sizes
    _, _, slot_count, tile_len, _ = entries_ref.shape
    me_row, me_col = lax.axis_index("row"), lax.axis_index("col")
    chunk_count = slot_count // group

    def chunk(index):
        source = entries_ref.at[0, 0, pl.ds(index * group, group)]
        return pltpu.make_async_copy(source, tiles.at[pl.ds(index * group, group)], sems.at[index])

    small = [(refs[0], rows_ref), (refs[1], cols_ref), (y_ref, y_out), (x_ref, x_out)]
    small = [
        pltpu.make_async_copy(source, target, sems.at[chunk_count + index])
        for index, (source, target) in enumerate(small)
    ]
    for copy in small[:2]:
        copy.start()
    for index in range(chunk_count):
        chunk(index).start()
    for copy in small[2:]:
        copy.start()

    def clear(block, carry):
        dense_ref[block] = jnp.zeros(dense_ref.shape[1:], dense_ref.dtype)
        return carry

    lax.fori_loop(0, dense_ref.shape[0], clear, 0)
    for copy in small[:2]:
        copy.wait()

    def place(slot):
        row, col = rows_ref[0, 0, slot], cols_ref[0, 0, slot]
        row_shift = shift_of(me_col, row // piece_blocks, n_col)
        col_shift = shift_of(me_row, col // piece_blocks, n_row)
        col_place = col_shift % 2 * (n_row // 2) + col_shift // 2
        block = row_shift * piece_blocks + row % piece_blocks
        start = (col_place * piece_blocks + col % piece_blocks) * tile_len
        values = jnp.where(slot < count_ref[0, 0], tiles[slot], 0.0)
        values = jnp.where(values > HALF_MODULUS, values - MODULUS, values).T
        both = jnp.concatenate(balanced_digits(values), 1).astype(jnp.bfloat16)
        dense_ref[block, pl.ds(pl.multiple_of(start, tile_len), tile_len), :] = both

    def step(index, carry):
        chunk(index).wait()
        for offset in range(group):
            place(index * group + offset)
        return carry

    lax.fori_loop(0, chunk_count, step, 0)
    for copy in small[2:]:
        copy.wait()
    token_ref[...] = jnp.zeros_like(token_ref)


def build_dense(tiles, block_x, block_y, sizes):
    tile_rows, tile_cols, tile_count, tile_entries = tiles
    n_row, n_col, piece_blocks = sizes
    _, _, slot_count, tile_len, _ = tile_entries.shape
    group = next(size for size in (8, 4, 2, 1) if slot_count % size == 0)
    shape = (n_col * piece_blocks, n_row * piece_blocks * tile_len, 2 * tile_len)
    hbm = pl.BlockSpec(memory_space=pltpu.HBM)
    rows, cols, entries, x_piece, y_piece = (
        pltpu.with_memory_space_constraint(part, pltpu.HBM)
        for part in (tile_rows, tile_cols, tile_entries, block_x, block_y)
    )
    return pl.pallas_call(
        functools.partial(build_kernel, (*sizes, group)),
        in_specs=[hbm, hbm, pl.BlockSpec(memory_space=pltpu.SMEM), hbm, hbm, hbm],
        out_specs=[pl.BlockSpec(memory_space=pltpu.VMEM)] * 4,
        out_shape=[
            pltpu.VMEM(shape, jnp.bfloat16),
            held(*block_x.shape),
            held(*block_y.shape),
            held(8, 128),
        ],
        scratch_shapes=[
            *(pltpu.SMEM(part.shape, part.dtype) for part in (tile_rows, tile_cols)),
            pltpu.VMEM((slot_count, tile_len, tile_len), jnp.float32),
            pltpu.SemaphoreType.DMA((slot_count // group + 4,)),
        ],
        compiler_params=pltpu.CompilerParams(vmem_limit_bytes=VMEM_LIMIT),
        cost_estimate=pl.CostEstimate(
            flops=8 * tile_entries.size, bytes_accessed=8 * tile_entries.size, transcendentals=0
        ),
    )(rows, cols, tile_count, entries, x_piece, y_piece)


def half_products(half, span, pieces_ref, dense_ref, digits, block):
    _, depth, width = dense_ref.shape
    tile_len, half_depth = width // 2, depth // 2
    high = middle = low = 0.0
    for start in range(0, half_depth, EXACT_DEPTH):
        stop = min(start + EXACT_DEPTH, half_depth)
        products = jnp.dot(
            digits[:, start:stop],
            dense_ref[block, half * half_depth + start : half * half_depth + stop, :],
            preferred_element_type=jnp.float32,
        )
        products = reduce_centered(products)
        high = high + products[:span, :tile_len]
        middle = middle + products[:span, tile_len:] + products[span:, :tile_len]
        low = low + products[span:, tile_len:]
    return high, middle, low


def fill_digits(span, pieces_ref, digits):
    piece_len = pieces_ref.shape[2]
    for d in range(pieces_ref.shape[0]):
        vector = reduce_centered(pieces_ref[d, :span, :])
        digits[:, d * piece_len : (d + 1) * piece_len] = stacked_digits(vector)


def first_half_kernel(span, pieces_ref, dense_ref, sums_ref, digits):
    fill_digits(span, pieces_ref, digits)
    tile_len = dense_ref.shape[2] // 2
    for block in range(dense_ref.shape[0]):
        parts = half_products(0, span, pieces_ref, dense_ref, digits, block)
        for index, part in enumerate(parts):
            sums_ref[index, :, block * tile_len : (block + 1) * tile_len] = part


def second_half_kernel(span, n_col, pieces_ref, evens_ref, sums_ref, dense_ref, *refs):
    outs, refs = refs[:n_col], refs[n_col:]
    digits = refs[-1]
    fill_digits(span, pieces_ref, digits)
    row_blocks, _, width = dense_ref.shape
    tile_len = width // 2
    piece_blocks = row_blocks // n_col
    for e in reversed(range(n_col)):
        for sub in range(piece_blocks):
            block = e * piece_blocks + sub
            parts = half_products(1, span, pieces_ref, dense_ref, digits, block)
            parts = (
                part + sums_ref[index, :, block * tile_len : (block + 1) * tile_len]
                for index, part in enumerate(parts)
            )
            outs[e][:span, sub * tile_len : (sub + 1) * tile_len] = combine(*parts)
    if len(refs) > 1:
        packed = jnp.sum(pieces_ref[:, span:, :], 0) + jnp.sum(evens_ref[:, span:, :], 0)
        tail = outs[0].shape[0] - span
        for out in outs:
            out[span:, :] = packed[:tail]
        refs[0][...] = packed[tail:]


def dense_first(evens, span, dense):
    row_blocks, depth, width = dense.shape
    return call(
        functools.partial(first_half_kernel, span),
        [evens, dense],
        [held(3, span, row_blocks * width // 2)],
        scratch=[pltpu.VMEM((2 * span, depth // 2), jnp.bfloat16)],
        limit=VMEM_LIMIT,
        flops=2 * span * dense.size,
    )[0]


def dense_second(odds, evens, sums, span, n_col, tail, dense, before):
    _, depth, _ = dense.shape
    piece_len = odds.shape[2]
    outs = [held(span + tail, piece_len)] * n_col
    if tail:
        outs = outs + [held(odds.shape[1] - span - tail, piece_len)]
    results = call(
        functools.partial(second_half_kernel, span, n_col),
        [odds, evens, sums, dense],
        outs,
        before,
        scratch=[pltpu.VMEM((2 * span, depth // 2), jnp.bfloat16)],
        limit=VMEM_LIMIT,
        flops=2 * span * dense.size,
    )
    return list(results[:n_col]), (results[n_col] if tail else None)


def left_kernel(n_row, x_evens, x_odds, dense_ref, *refs):
    evens, odds_ref = refs[:-1], refs[-1]
    row_blocks, _, width = dense_ref.shape
    tile_len = width // 2
    _, span, piece_len = x_evens.shape
    piece_blocks = piece_len // tile_len
    x_digits = [
        centred_digits((x_odds if e % 2 else x_evens)[e // 2])
        for e in range(row_blocks // piece_blocks)
    ]
    for place in range(n_row):
        by_high = by_low = high_part = low_part = 0.0
        for block in range(row_blocks):
            sub = block % piece_blocks
            left = x_digits[block // piece_blocks][:, sub * tile_len : (sub + 1) * tile_len]
            right = dense_ref[block, place * piece_len : (place + 1) * piece_len, :]
            high_part = high_part + dot_pairs(left, right[:, :tile_len])
            low_part = low_part + dot_pairs(left, right[:, tile_len:])
            if (block + 1) * tile_len % EXACT_DEPTH == 0 or block == row_blocks - 1:
                by_high = by_high + reduce_centered(high_part)
                by_low = by_low + reduce_centered(low_part)
                high_part = low_part = 0.0
        piece = combine(by_high[:span], by_low[:span] + by_high[span:], by_low[span:])
        if place < n_row // 2:
            evens[place][...] = piece
        else:
            odds_ref[place - n_row // 2] = piece


def dense_left(x_pairs, n_row, dense, before):
    _, span, piece_len = x_pairs[0].shape
    results = call(
        functools.partial(left_kernel, n_row),
        [*x_pairs, dense],
        [held(span, piece_len)] * (n_row // 2) + [held(n_row // 2, span, piece_len)],
        before,
        limit=VMEM_LIMIT,
        flops=4 * span * dense.size,
    )
    return list(results[:-1]), results[-1]


def sparse_tiles(tiles, sizes):
    tile_rows, tile_cols, tile_count, tile_entries = tiles
    n_row, n_col, piece_blocks = sizes
    entries, rows, cols = tile_entries[0, 0], tile_rows[0, 0], tile_cols[0, 0]
    row_shift = shift_of(lax.axis_index("col"), rows // piece_blocks, n_col)
    col_shift = shift_of(lax.axis_index("row"), cols // piece_blocks, n_row)
    col_place = col_shift % 2 * (n_row // 2) + col_shift // 2
    positions = (
        row_shift * piece_blocks + rows % piece_blocks,
        col_place * piece_blocks + cols % piece_blocks,
        tile_count[0, 0],
    )
    entries = jnp.where(entries > HALF_MODULUS, entries - MODULUS, entries)
    return positions, jnp.stack(balanced_digits(entries), 1).astype(jnp.bfloat16)


def sparse_product(vector, spec, places, targets, count, blocks, a_digits):
    span, tile_len = vector.shape[0], a_digits.shape[-1]
    v_digits = stacked_digits(vector).reshape(2 * span, -1, tile_len)
    picked = jnp.take(v_digits, places, axis=1)
    products = jnp.einsum(spec, picked, a_digits, preferred_element_type=jnp.float32)
    products = reduce_centered(products)
    residues = combine(
        products[:, 0, :span],
        products[:, 0, span:] + products[:, 1, :span],
        products[:, 1, span:],
    )
    live = jnp.arange(targets.shape[0], dtype=jnp.int32) < count
    onehot = targets[None, :] == jnp.arange(blocks, dtype=jnp.int32)[:, None]
    onehot = (onehot & live[None, :]).astype(jnp.float32)
    summed = jnp.einsum("bt,twi->wbi", onehot, residues, precision=lax.Precision.HIGHEST)
    return reduce_centered(summed).reshape(span, blocks * tile_len)


def sparse_second(odds, evens, span, n_col, tail, positions, a_digits):
    rows, cols, count = positions
    pieces = [*evens, *odds]
    piece_len = pieces[0].shape[1]
    blocks = n_col * piece_len // a_digits.shape[-1]
    vector = reduce_centered(jnp.concatenate([piece[:span] for piece in pieces], 1))
    product = sparse_product(vector, "ntk,tdik->tdni", cols, rows, count, blocks, a_digits)
    outs = [product[:, e * piece_len : (e + 1) * piece_len] for e in range(n_col)]
    if not tail:
        return outs, None
    packed = functools.reduce(jnp.add, [piece[span:] for piece in pieces])
    return [jnp.concatenate([out, packed[:tail]], 0) for out in outs], packed[tail:]


def sparse_left(x_pairs, n_row, positions, a_digits):
    rows, cols, count = positions
    n_col = 2 * x_pairs[0].shape[0]
    x_pieces = [x_pairs[e % 2][e // 2] for e in range(n_col)]
    piece_len = x_pieces[0].shape[1]
    values = jnp.concatenate(x_pieces, 1)
    values = jnp.where(values > HALF_MODULUS, values - MODULUS, values)
    blocks = n_row * piece_len // a_digits.shape[-1]
    product = sparse_product(values, "nti,tdik->tdnk", rows, cols, count, blocks, a_digits)
    pieces = [product[:, d * piece_len : (d + 1) * piece_len] for d in range(n_row)]
    return pieces[: n_row // 2], jnp.stack(pieces[n_row // 2 :])


def add_came(evens, odds_came, before):
    def kernel(*refs):
        for index in range(len(evens)):
            refs[len(evens) + 1 + index][...] = refs[index][...] + refs[len(evens)][index]

    return list(call(kernel, [*evens, odds_came], [held(*evens[0].shape)] * len(evens), before))


def append_projections(w_parts, pieces, earlier):
    span, piece_len = pieces[0].shape
    rows = span * span // piece_len
    count = len(earlier) + 1

    def kernel(*refs):
        w_refs, refs = refs[: len(w_parts)], refs[len(w_parts) :]
        piece_refs, refs = refs[: len(pieces)], refs[len(pieces) :]
        out_ref = refs[-1]
        summed = functools.reduce(jnp.add, [ref[...] for ref in piece_refs])
        out_ref[:span, :] = summed
        w_piece = functools.reduce(jnp.add, [ref[...] for ref in w_refs])
        w_digits = stacked_digits(reduce_centered(w_piece))
        for index, vector in enumerate([summed] + [ref[...] for ref in refs[:-1]]):
            products = dot_pairs(w_digits, stacked_digits(reduce_centered(vector)))
            square = combine(
                reduce_centered(products[:span, :span]),
                reduce_centered(products[:span, span:]) + reduce_centered(products[span:, :span]),
                reduce_centered(products[span:, span:]),
            )
            start = span + index * rows
            out_ref[start : start + rows, :] = pack_square(square, piece_len)

    outs = [held(span + count * rows, piece_len)]
    return call(kernel, [*w_parts, *pieces, *earlier], outs)[0]


def multiply_mod(left, right):
    span = left.shape[0]
    left = stacked_digits(left)
    high, low = (part.astype(jnp.bfloat16) for part in balanced_digits(right))
    by_high = jnp.dot(left, high, preferred_element_type=jnp.float32)
    by_low = jnp.dot(left, low, preferred_element_type=jnp.float32)
    return combine(
        reduce_centered(by_high[:span]), by_low[:span] + by_high[span:], by_low[span:]
    )


def sigma_start(packed, span):
    def kernel(packed_ref, start_ref, both_ref, rest_ref):
        rows = packed_ref.shape[0] // 2
        c_1 = unpack_square(reduce_centered(packed_ref[:rows, :]), span)
        c_2 = unpack_square(reduce_centered(packed_ref[rows:, :]), span)
        e_2 = reduce_centered(c_1 - multiply_mod(c_1, c_2))
        both = reduce_centered(c_1 + e_2)
        start_ref[...] = multiply_mod(e_2, c_1)
        both_ref[...] = both
        rest_ref[...] = c_1 - multiply_mod(both, c_2)

    return call(kernel, [packed], [held(span, span)] * 3)


def finish(pieces, known, span):
    def kernel(*refs):
        piece_refs, (start_ref, both_ref, rest_ref, poly_ref, vector_ref) = refs[:-5], refs[-5:]
        summed = functools.reduce(jnp.add, [ref[...] for ref in piece_refs])
        vector_ref[...] = canonical(summed[:span]) * (1.0 / MODULUS)
        start, both = start_ref[...], both_ref[...]
        c_3 = unpack_square(reduce_centered(summed[span:]), span)
        e_3 = reduce_centered(multiply_mod(start, c_3) + rest_ref[...])
        poly_ref[0] = canonical(-multiply_mod(e_3, start)) * (1.0 / MODULUS)
        poly_ref[1] = canonical(start + multiply_mod(e_3, both)) * (1.0 / MODULUS)
        poly_ref[2] = canonical(-both - e_3) * (1.0 / MODULUS)

    outs = [
        jax.ShapeDtypeStruct((STEP_COUNT, span, span), jnp.float32),
        jax.ShapeDtypeStruct((span, pieces[0].shape[1]), jnp.float32),
    ]
    return tuple(call(kernel, [*pieces, *known], outs))


def local(tile_entries, tile_rows, tile_cols, tile_count, block_x, block_y):
    _, _, slot_count, tile_len, _ = tile_entries.shape
    span, piece_len = block_y.shape
    piece_blocks = piece_len // tile_len
    n_row, n_col = lax.axis_size("row"), lax.axis_size("col")
    packed_rows = span * span // piece_len
    tiles = (tile_rows, tile_cols, tile_count, tile_entries)
    sizes = (n_row, n_col, piece_blocks)
    is_dense = n_col * piece_blocks * n_row * piece_blocks <= DENSE_CELLS * slot_count
    if is_dense:
        dense, x_own, y_own, token = build_dense(tiles, block_x, block_y, sizes)
        before = [token]
    else:
        positions, a_digits = sparse_tiles(tiles, sizes)
        x_own, y_own, before = block_x, block_y, []

    def multiply(evens, tail=0, before=()):
        odds = gather_odds(evens, "row")
        if is_dense:
            sums = dense_first(evens, span, dense)
            return dense_second(odds, evens, sums, span, n_col, tail, dense, before)
        return sparse_second(odds, evens, span, n_col, tail, positions, a_digits)

    x_came = fetch_evens(block_x, "col")
    evens = stack_after([y_own] + fetch_evens(block_y, "row"), [*before, *x_came])
    x_evens = stack_after([x_own] + x_came)
    outs, _ = multiply(evens, before=[x_evens])
    x_pairs = [x_evens, gather_odds(x_evens, "col")]
    if is_dense:
        w_evens, w_odds = dense_left(x_pairs, n_row, dense, [outs[0]])
    else:
        w_evens, w_odds = sparse_left(x_pairs, n_row, positions, a_digits)
    vector_1 = sum_after(scatter_pieces(outs, "col"), [w_odds])
    w_came = fetch(w_odds, "row", 1)
    evens = gather_evens(vector_1, "row")
    outs, _ = multiply(evens, before=[w_came])
    pieces = scatter_pieces(outs, "col")
    w_evens = add_came(w_evens, w_came, [outs[0]])
    w_parts = [w_evens[0]] + [
        fetch(w_evens[index], "row", 2 * index) for index in reversed(range(1, n_row // 2))
    ]
    vector_2 = append_projections(w_parts, pieces, [y_own, vector_1])
    evens = gather_evens(vector_2, "row")
    outs, packed = multiply(evens, packed_rows)
    pieces = scatter_pieces(outs, "col")
    shift = 1
    while shift < n_col:
        packed = packed + fetch(packed, "col", shift)
        shift *= 2
    return finish(pieces, sigma_start(packed, span), span)


def solution(mesh):
    placed = (
        P("row", "col", None, None, None),
        P("row", "col", None),
        P("row", "col", None),
        P("row", "col"),
        P(None, ("row", "col")),
        P(None, ("row", "col")),
    )
    return jax.shard_map(
        local, mesh=mesh, in_specs=placed, out_specs=(P(), P(None, ("row", "col"))), check_vma=False
    )
```

```python
import functools

import jax
import jax.numpy as jnp
from jax import lax
from jax.experimental import pallas as pl
from jax.experimental.pallas import tpu as pltpu
from jax.sharding import PartitionSpec as P

STEP_COUNT = 3

MODULUS = 65521.0
HALF_MODULUS = 32760.0
BASE = 256.0
EXACT_DEPTH = 1024
DENSE_CELLS = 4
VMEM_LIMIT = 16 * 1024 * 1024
SMALL_LIMIT = 4 * 1024 * 1024


def reduce_centered(values):
    return values - MODULUS * jnp.floor(values * (1.0 / MODULUS) + 0.5)


def canonical(values):
    reduced = reduce_centered(values)
    return jnp.where(reduced < 0, reduced + MODULUS, reduced)


def balanced_digits(values):
    high = jnp.floor(values * (1.0 / BASE) + 0.5)
    return high, values - BASE * high


def stacked_digits(values):
    high, low = balanced_digits(values)
    return jnp.concatenate([high, low], 0).astype(jnp.bfloat16)


def centred_digits(residues):
    return stacked_digits(jnp.where(residues > HALF_MODULUS, residues - MODULUS, residues))


def partner(index, shift, size):
    return index ^ shift if size & (size - 1) == 0 else (index + shift) % size


def shift_of(index, other, size):
    return index ^ other if size & (size - 1) == 0 else (other - index) % size


def fetch(piece, axis, shift):
    size = lax.axis_size(axis)
    return lax.ppermute(piece, axis, [(partner(i, shift, size), i) for i in range(size)])


def scatter_pieces(pieces, axis):
    size = lax.axis_size(axis)
    came = [
        lax.ppermute(pieces[shift], axis, [(i, partner(i, shift, size)) for i in range(size)])
        for shift in reversed(range(1, size))
    ]
    return [pieces[0]] + came


def call(kernel, operands, outs, before=(), scratch=(), limit=SMALL_LIMIT, flops=0):
    def body(*refs):
        kernel(*refs[: len(operands)], *refs[len(operands) + len(before) :])

    vmem = pl.BlockSpec(memory_space=pltpu.VMEM)
    return pl.pallas_call(
        body,
        in_specs=[vmem] * len(operands) + [pl.BlockSpec(memory_space=pl.ANY)] * len(before),
        out_specs=[vmem] * len(outs),
        out_shape=outs,
        scratch_shapes=list(scratch),
        compiler_params=pltpu.CompilerParams(vmem_limit_bytes=limit),
        cost_estimate=pl.CostEstimate(flops=flops, bytes_accessed=0, transcendentals=0),
    )(*(pltpu.with_memory_space_constraint(part, pltpu.VMEM) for part in operands), *before)


def held(*shape):
    return pltpu.VMEM(shape, jnp.float32)


def stack_after(pieces, before=()):
    def kernel(*refs):
        for index, ref in enumerate(refs[:-1]):
            refs[-1][index] = ref[...]

    return call(kernel, pieces, [held(len(pieces), *pieces[0].shape)], before)[0]


def sum_after(pieces, before=()):
    def kernel(*refs):
        refs[-1][...] = functools.reduce(jnp.add, [ref[...] for ref in refs[:-1]])

    return call(kernel, pieces, [held(*pieces[0].shape)], before)[0]


def fetch_evens(piece, axis):
    return [fetch(piece, axis, shift) for shift in range(2, lax.axis_size(axis), 2)]


def gather_evens(piece, axis, before=()):
    return stack_after([piece] + fetch_evens(piece, axis), before)


def gather_odds(evens, axis):
    size = lax.axis_size(axis)
    assert size > 1 and size & (size - 1) == 0
    return fetch(evens, axis, 1)


def dot_pairs(left, right):
    return lax.dot_general(left, right, (((1,), (1,)), ((), ())), preferred_element_type=jnp.float32)


def combine(high, middle, low):
    return reduce_centered(15.0 * high + 256.0 * reduce_centered(middle) + low)


def pack_square(square, width):
    span = square.shape[0]
    rows = span * span // width
    return jnp.concatenate([square[j * rows : (j + 1) * rows] for j in range(width // span)], 1)


def unpack_square(packed, span):
    count = packed.shape[1] // span
    return jnp.concatenate([packed[:, j * span : (j + 1) * span] for j in range(count)], 0)


def build_kernel(sizes, *refs):
    entries_ref, x_ref, y_ref, dense_ref, x_out, y_out, token_ref = refs[3:10]
    rows_ref, cols_ref, count_ref, tiles, sems = refs[10:]
    n_row, n_col, piece_blocks, group = sizes
    _, _, slot_count, tile_len, _ = entries_ref.shape
    me_row, me_col = lax.axis_index("row"), lax.axis_index("col")
    chunk_count = slot_count // group

    def chunk(index):
        source = entries_ref.at[0, 0, pl.ds(index * group, group)]
        return pltpu.make_async_copy(source, tiles.at[pl.ds(index * group, group)], sems.at[index])

    small = [*zip(refs[:3], refs[10:13]), (y_ref, y_out), (x_ref, x_out)]
    small = [
        pltpu.make_async_copy(source, target, sems.at[chunk_count + index])
        for index, (source, target) in enumerate(small)
    ]
    for copy in small[:3]:
        copy.start()
    for index in range(chunk_count):
        chunk(index).start()
    for copy in small[3:]:
        copy.start()

    def clear(block, carry):
        dense_ref[block] = jnp.zeros(dense_ref.shape[1:], dense_ref.dtype)
        return carry

    lax.fori_loop(0, dense_ref.shape[0], clear, 0)
    for copy in small[:3]:
        copy.wait()

    def place(slot):
        row, col = rows_ref[0, 0, slot], cols_ref[0, 0, slot]
        row_shift = shift_of(me_col, row // piece_blocks, n_col)
        col_shift = shift_of(me_row, col // piece_blocks, n_row)
        col_place = col_shift % 2 * (n_row // 2) + col_shift // 2
        block = row_shift * piece_blocks + row % piece_blocks
        start = (col_place * piece_blocks + col % piece_blocks) * tile_len
        values = jnp.where(slot < count_ref[0, 0], tiles[slot], 0.0)
        values = jnp.where(values > HALF_MODULUS, values - MODULUS, values).T
        both = jnp.concatenate(balanced_digits(values), 1).astype(jnp.bfloat16)
        dense_ref[block, pl.ds(pl.multiple_of(start, tile_len), tile_len), :] = both

    def step(index, carry):
        chunk(index).wait()
        for offset in range(group):
            place(index * group + offset)
        return carry

    lax.fori_loop(0, chunk_count, step, 0)
    for copy in small[3:]:
        copy.wait()
    token_ref[...] = jnp.zeros_like(token_ref)


def build_dense(tiles, block_x, block_y, sizes):
    tile_rows, tile_cols, tile_count, tile_entries = tiles
    n_row, n_col, piece_blocks = sizes
    _, _, slot_count, tile_len, _ = tile_entries.shape
    group = next(size for size in (8, 4, 2, 1) if slot_count % size == 0)
    shape = (n_col * piece_blocks, n_row * piece_blocks * tile_len, 2 * tile_len)
    hbm = pl.BlockSpec(memory_space=pltpu.HBM)
    rows, cols, entries, x_piece, y_piece = (
        pltpu.with_memory_space_constraint(part, pltpu.HBM)
        for part in (tile_rows, tile_cols, tile_entries, block_x, block_y)
    )
    return pl.pallas_call(
        functools.partial(build_kernel, (*sizes, group)),
        in_specs=[hbm, hbm, pl.BlockSpec(memory_space=pl.ANY), hbm, hbm, hbm],
        out_specs=[pl.BlockSpec(memory_space=pltpu.VMEM)] * 4,
        out_shape=[
            pltpu.VMEM(shape, jnp.bfloat16),
            held(*block_x.shape),
            held(*block_y.shape),
            held(8, 128),
        ],
        scratch_shapes=[
            *(pltpu.SMEM(part.shape, part.dtype) for part in (tile_rows, tile_cols, tile_count)),
            pltpu.VMEM((slot_count, tile_len, tile_len), jnp.float32),
            pltpu.SemaphoreType.DMA((slot_count // group + 5,)),
        ],
        compiler_params=pltpu.CompilerParams(vmem_limit_bytes=VMEM_LIMIT),
        cost_estimate=pl.CostEstimate(
            flops=8 * tile_entries.size, bytes_accessed=8 * tile_entries.size, transcendentals=0
        ),
    )(rows, cols, tile_count, entries, x_piece, y_piece)


def half_products(half, span, pieces_ref, dense_ref, digits, block):
    _, depth, width = dense_ref.shape
    tile_len, half_depth = width // 2, depth // 2
    high = middle = low = 0.0
    for start in range(0, half_depth, EXACT_DEPTH):
        stop = min(start + EXACT_DEPTH, half_depth)
        products = jnp.dot(
            digits[:, start:stop],
            dense_ref[block, half * half_depth + start : half * half_depth + stop, :],
            preferred_element_type=jnp.float32,
        )
        products = reduce_centered(products)
        high = high + products[:span, :tile_len]
        middle = middle + products[:span, tile_len:] + products[span:, :tile_len]
        low = low + products[span:, tile_len:]
    return high, middle, low


def fill_digits(span, pieces_ref, digits):
    piece_len = pieces_ref.shape[2]
    for d in range(pieces_ref.shape[0]):
        vector = reduce_centered(pieces_ref[d, :span, :])
        digits[:, d * piece_len : (d + 1) * piece_len] = stacked_digits(vector)


def first_half_kernel(span, pieces_ref, dense_ref, sums_ref, digits):
    fill_digits(span, pieces_ref, digits)
    tile_len = dense_ref.shape[2] // 2
    for block in range(dense_ref.shape[0]):
        parts = half_products(0, span, pieces_ref, dense_ref, digits, block)
        for index, part in enumerate(parts):
            sums_ref[index, :, block * tile_len : (block + 1) * tile_len] = part


def second_half_kernel(span, pieces_ref, evens_ref, sums_ref, dense_ref, *refs):
    outs, digits = refs[:-1], refs[-1]
    n_col = len(outs)
    fill_digits(span, pieces_ref, digits)
    row_blocks, _, width = dense_ref.shape
    tile_len = width // 2
    piece_blocks = row_blocks // n_col
    for e in reversed(range(n_col)):
        for sub in range(piece_blocks):
            block = e * piece_blocks + sub
            parts = half_products(1, span, pieces_ref, dense_ref, digits, block)
            parts = (
                part + sums_ref[index, :, block * tile_len : (block + 1) * tile_len]
                for index, part in enumerate(parts)
            )
            outs[e][:span, sub * tile_len : (sub + 1) * tile_len] = combine(*parts)
    if outs[0].shape[0] > span:
        packed = jnp.sum(pieces_ref[:, span:, :], 0) + jnp.sum(evens_ref[:, span:, :], 0)
        for out in outs:
            out[span:, :] = packed


def dense_first(evens, span, dense):
    row_blocks, depth, width = dense.shape
    return call(
        functools.partial(first_half_kernel, span),
        [evens, dense],
        [held(3, span, row_blocks * width // 2)],
        scratch=[pltpu.VMEM((2 * span, depth // 2), jnp.bfloat16)],
        limit=VMEM_LIMIT,
        flops=2 * span * dense.size,
    )[0]


def dense_second(odds, evens, sums, span, n_col, dense, before):
    _, depth, _ = dense.shape
    _, rows, piece_len = odds.shape
    return list(
        call(
            functools.partial(second_half_kernel, span),
            [odds, evens, sums, dense],
            [held(rows, piece_len)] * n_col,
            before,
            scratch=[pltpu.VMEM((2 * span, depth // 2), jnp.bfloat16)],
            limit=VMEM_LIMIT,
            flops=2 * span * dense.size,
        )
    )


def left_kernel(n_row, x_evens, x_odds, dense_ref, *refs):
    evens, odds_ref = refs[:-1], refs[-1]
    row_blocks, _, width = dense_ref.shape
    tile_len = width // 2
    _, span, piece_len = x_evens.shape
    piece_blocks = piece_len // tile_len
    x_digits = [
        centred_digits((x_odds if e % 2 else x_evens)[e // 2])
        for e in range(row_blocks // piece_blocks)
    ]
    for place in range(n_row):
        by_high = by_low = high_part = low_part = 0.0
        for block in range(row_blocks):
            sub = block % piece_blocks
            left = x_digits[block // piece_blocks][:, sub * tile_len : (sub + 1) * tile_len]
            right = dense_ref[block, place * piece_len : (place + 1) * piece_len, :]
            high_part = high_part + dot_pairs(left, right[:, :tile_len])
            low_part = low_part + dot_pairs(left, right[:, tile_len:])
            if (block + 1) * tile_len % EXACT_DEPTH == 0 or block == row_blocks - 1:
                by_high = by_high + reduce_centered(high_part)
                by_low = by_low + reduce_centered(low_part)
                high_part = low_part = 0.0
        piece = combine(by_high[:span], by_low[:span] + by_high[span:], by_low[span:])
        if place < n_row // 2:
            evens[place][...] = piece
        else:
            odds_ref[place - n_row // 2] = piece


def dense_left(x_pairs, n_row, dense, before):
    _, span, piece_len = x_pairs[0].shape
    results = call(
        functools.partial(left_kernel, n_row),
        [*x_pairs, dense],
        [held(span, piece_len)] * (n_row // 2) + [held(n_row // 2, span, piece_len)],
        before,
        limit=VMEM_LIMIT,
        flops=4 * span * dense.size,
    )
    return list(results[:-1]), results[-1]


def sparse_tiles(tiles, sizes):
    tile_rows, tile_cols, tile_count, tile_entries = tiles
    n_row, n_col, piece_blocks = sizes
    entries, rows, cols = tile_entries[0, 0], tile_rows[0, 0], tile_cols[0, 0]
    row_shift = shift_of(lax.axis_index("col"), rows // piece_blocks, n_col)
    col_shift = shift_of(lax.axis_index("row"), cols // piece_blocks, n_row)
    col_place = col_shift % 2 * (n_row // 2) + col_shift // 2
    positions = (
        row_shift * piece_blocks + rows % piece_blocks,
        col_place * piece_blocks + cols % piece_blocks,
        tile_count[0, 0],
    )
    entries = jnp.where(entries > HALF_MODULUS, entries - MODULUS, entries)
    return positions, jnp.stack(balanced_digits(entries), 1).astype(jnp.bfloat16)


def sparse_product(vector, spec, places, targets, count, blocks, a_digits):
    span, tile_len = vector.shape[0], a_digits.shape[-1]
    v_digits = stacked_digits(vector).reshape(2 * span, -1, tile_len)
    picked = jnp.take(v_digits, places, axis=1)
    products = jnp.einsum(spec, picked, a_digits, preferred_element_type=jnp.float32)
    products = reduce_centered(products)
    residues = combine(
        products[:, 0, :span],
        products[:, 0, span:] + products[:, 1, :span],
        products[:, 1, span:],
    )
    live = jnp.arange(targets.shape[0], dtype=jnp.int32) < count
    onehot = targets[None, :] == jnp.arange(blocks, dtype=jnp.int32)[:, None]
    onehot = (onehot & live[None, :]).astype(jnp.float32)
    summed = jnp.einsum("bt,twi->wbi", onehot, residues, precision=lax.Precision.HIGHEST)
    return reduce_centered(summed).reshape(span, blocks * tile_len)


def sparse_second(odds, evens, span, n_col, positions, a_digits):
    rows, cols, count = positions
    pieces = [*evens, *odds]
    piece_len = pieces[0].shape[1]
    blocks = n_col * piece_len // a_digits.shape[-1]
    vector = reduce_centered(jnp.concatenate([piece[:span] for piece in pieces], 1))
    product = sparse_product(vector, "ntk,tdik->tdni", cols, rows, count, blocks, a_digits)
    packed = functools.reduce(jnp.add, [piece[span:] for piece in pieces])
    outs = [product[:, e * piece_len : (e + 1) * piece_len] for e in range(n_col)]
    return [jnp.concatenate([out, packed], 0) for out in outs]


def sparse_left(x_pairs, n_row, positions, a_digits):
    rows, cols, count = positions
    n_col = 2 * x_pairs[0].shape[0]
    x_pieces = [x_pairs[e % 2][e // 2] for e in range(n_col)]
    piece_len = x_pieces[0].shape[1]
    values = jnp.concatenate(x_pieces, 1)
    values = jnp.where(values > HALF_MODULUS, values - MODULUS, values)
    blocks = n_row * piece_len // a_digits.shape[-1]
    product = sparse_product(values, "nti,tdik->tdnk", rows, cols, count, blocks, a_digits)
    pieces = [product[:, d * piece_len : (d + 1) * piece_len] for d in range(n_row)]
    return pieces[: n_row // 2], jnp.stack(pieces[n_row // 2 :])


def add_came(evens, odds_came, index, before=()):
    def kernel(even_ref, came_ref, out_ref):
        out_ref[...] = even_ref[...] + came_ref[index]

    return call(kernel, [evens[index], odds_came], [held(*evens[index].shape)], before)[0]


def sum_over(packed, axis, shift=1):
    while shift < lax.axis_size(axis):
        packed = packed + fetch(packed, axis, shift)
        shift *= 2
    return packed


def append_projections(w_parts, pieces, earlier):
    span, piece_len = pieces[0].shape
    rows = span * span // piece_len

    def kernel(*refs):
        w_refs, refs = refs[: len(w_parts)], refs[len(w_parts) :]
        piece_refs, refs = refs[: len(pieces)], refs[len(pieces) :]
        earlier_refs, (out_ref, terms_ref) = refs[:-2], refs[-2:]
        summed = functools.reduce(jnp.add, [ref[...] for ref in piece_refs])
        out_ref[:span, :] = summed
        w_piece = functools.reduce(jnp.add, [ref[...] for ref in w_refs])
        w_digits = stacked_digits(reduce_centered(w_piece))
        for index, vector in enumerate([summed] + [ref[...] for ref in earlier_refs]):
            products = dot_pairs(w_digits, stacked_digits(reduce_centered(vector)))
            square = combine(
                reduce_centered(products[:span, :span]),
                reduce_centered(products[:span, span:]) + reduce_centered(products[span:, :span]),
                reduce_centered(products[span:, span:]),
            )
            square = pack_square(square, piece_len)
            if index == 0:
                out_ref[span:, :] = square
            else:
                terms_ref[(index - 1) * rows : index * rows, :] = square

    outs = [held(span + rows, piece_len), held(len(earlier) * rows, piece_len)]
    return call(kernel, [*w_parts, *pieces, *earlier], outs)


def multiply_mod(left, right):
    span = left.shape[0]
    left = stacked_digits(left)
    high, low = (part.astype(jnp.bfloat16) for part in balanced_digits(right))
    by_high = jnp.dot(left, high, preferred_element_type=jnp.float32)
    by_low = jnp.dot(left, low, preferred_element_type=jnp.float32)
    return combine(
        reduce_centered(by_high[:span]), by_low[:span] + by_high[span:], by_low[span:]
    )


def sigma_start(packed, span):
    def kernel(packed_ref, start_ref, both_ref, rest_ref):
        rows = packed_ref.shape[0] // 2
        c_1 = unpack_square(reduce_centered(packed_ref[:rows, :]), span)
        c_2 = unpack_square(reduce_centered(packed_ref[rows:, :]), span)
        e_2 = reduce_centered(c_1 - multiply_mod(c_1, c_2))
        both = reduce_centered(c_1 + e_2)
        start_ref[...] = multiply_mod(e_2, c_1)
        both_ref[...] = both
        rest_ref[...] = c_1 - multiply_mod(both, c_2)

    return call(kernel, [packed], [held(span, span)] * 3)


def finish(pieces, known, span):
    def kernel(*refs):
        piece_refs, (start_ref, both_ref, rest_ref, poly_ref, vector_ref) = refs[:-5], refs[-5:]
        summed = functools.reduce(jnp.add, [ref[...] for ref in piece_refs])
        vector_ref[...] = canonical(summed[:span]) * (1.0 / MODULUS)
        start, both = start_ref[...], both_ref[...]
        c_3 = unpack_square(reduce_centered(summed[span:]), span)
        e_3 = reduce_centered(multiply_mod(start, c_3) + rest_ref[...])
        poly_ref[0] = canonical(-multiply_mod(e_3, start)) * (1.0 / MODULUS)
        poly_ref[1] = canonical(start + multiply_mod(e_3, both)) * (1.0 / MODULUS)
        poly_ref[2] = canonical(-both - e_3) * (1.0 / MODULUS)

    outs = [
        jax.ShapeDtypeStruct((STEP_COUNT, span, span), jnp.float32),
        jax.ShapeDtypeStruct((span, pieces[0].shape[1]), jnp.float32),
    ]
    return tuple(call(kernel, [*pieces, *known], outs))


def local(tile_entries, tile_rows, tile_cols, tile_count, block_x, block_y):
    _, _, slot_count, tile_len, _ = tile_entries.shape
    span, piece_len = block_y.shape
    piece_blocks = piece_len // tile_len
    n_row, n_col = lax.axis_size("row"), lax.axis_size("col")
    packed_rows = span * span // piece_len
    tiles = (tile_rows, tile_cols, tile_count, tile_entries)
    sizes = (n_row, n_col, piece_blocks)
    is_dense = n_col * piece_blocks * n_row * piece_blocks <= DENSE_CELLS * slot_count
    if is_dense:
        dense, x_own, y_own, token = build_dense(tiles, block_x, block_y, sizes)
        before = [token]
    else:
        positions, a_digits = sparse_tiles(tiles, sizes)
        x_own, y_own, before = block_x, block_y, []

    def multiply_evens(evens):
        return dense_first(evens, span, dense) if is_dense else evens

    def multiply_odds(odds, evens, sums, before):
        if is_dense:
            return dense_second(odds, evens, sums, span, n_col, dense, before)
        return sparse_second(odds, evens, span, n_col, positions, a_digits)

    def multiply(evens, before):
        return multiply_odds(gather_odds(evens, "row"), evens, multiply_evens(evens), before)

    x_came = fetch_evens(block_x, "col")
    evens = stack_after([y_own] + fetch_evens(block_y, "row"), [*before, *x_came])
    x_evens = stack_after([x_own] + x_came)
    outs = multiply(evens, [x_evens])
    x_pairs = [x_evens, gather_odds(x_evens, "col")]
    if is_dense:
        w_evens, w_odds = dense_left(x_pairs, n_row, dense, [outs[0]])
    else:
        w_evens, w_odds = sparse_left(x_pairs, n_row, positions, a_digits)
    vector_1 = sum_after(scatter_pieces(outs, "col"), [w_odds])
    w_came = fetch(w_odds, "row", 1)
    outs = multiply(gather_evens(vector_1, "row"), [w_came])
    pieces = scatter_pieces(outs, "col")
    w_last = n_row // 2 - 1
    w_parts = [
        add_came(w_evens, w_came, index, [] if index == w_last else [outs[0]])
        for index in range(n_row // 2)
    ]
    w_parts = w_parts[:1] + [
        fetch(w_parts[index], "row", 2 * index) for index in reversed(range(1, n_row // 2))
    ]
    vector_2, terms = append_projections(w_parts, pieces, [y_own, vector_1])
    terms = terms + fetch(terms, "col", 1)
    evens = gather_evens(vector_2, "row", [terms])
    odds, sums = gather_odds(evens, "row"), multiply_evens(evens)
    if n_col > 2:
        terms = sum_after([terms, fetch(terms, "col", 2)], [sums])
    terms = sum_over(terms, "col", 4)
    outs = multiply_odds(odds, evens, sums, [terms])
    terms = sum_over(sum_after([terms], [outs[0]]), "row")
    return finish(scatter_pieces(outs, "col"), sigma_start(terms, span), span)


def solution(mesh):
    placed = (
        P("row", "col", None, None, None),
        P("row", "col", None),
        P("row", "col", None),
        P("row", "col"),
        P(None, ("row", "col")),
        P(None, ("row", "col")),
    )
    return jax.shard_map(
        local, mesh=mesh, in_specs=placed, out_specs=(P(), P(None, ("row", "col"))), check_vma=False
    )
```

```python
import functools

import jax
import jax.numpy as jnp
from jax import lax
from jax.experimental import pallas as pl
from jax.experimental.pallas import tpu as pltpu
from jax.sharding import PartitionSpec as P

STEP_COUNT = 3

MODULUS = 65521.0
HALF_MODULUS = 32760.0
BASE = 256.0
EXACT_DEPTH = 1024
DENSE_CELLS = 4
VMEM_LIMIT = 16 * 1024 * 1024
SMALL_LIMIT = 4 * 1024 * 1024


def reduce_centered(values):
    return values - MODULUS * jnp.floor(values * (1.0 / MODULUS) + 0.5)


def canonical(values):
    reduced = reduce_centered(values)
    return jnp.where(reduced < 0, reduced + MODULUS, reduced)


def balanced_digits(values):
    high = jnp.floor(values * (1.0 / BASE) + 0.5)
    return high, values - BASE * high


def stacked_digits(values):
    high, low = balanced_digits(values)
    return jnp.concatenate([high, low], 0).astype(jnp.bfloat16)


def centred_digits(residues):
    return stacked_digits(jnp.where(residues > HALF_MODULUS, residues - MODULUS, residues))


def partner(index, shift, size):
    return index ^ shift if size & (size - 1) == 0 else (index + shift) % size


def shift_of(index, other, size):
    return index ^ other if size & (size - 1) == 0 else (other - index) % size


def fetch(piece, axis, shift):
    size = lax.axis_size(axis)
    return lax.ppermute(piece, axis, [(partner(i, shift, size), i) for i in range(size)])


def scatter_pieces(pieces, axis):
    size = lax.axis_size(axis)
    came = [
        lax.ppermute(pieces[shift], axis, [(i, partner(i, shift, size)) for i in range(size)])
        for shift in reversed(range(1, size))
    ]
    return [pieces[0]] + came


def call(kernel, operands, outs, before=(), scratch=(), limit=SMALL_LIMIT, flops=0):
    def body(*refs):
        kernel(*refs[: len(operands)], *refs[len(operands) + len(before) :])

    vmem = pl.BlockSpec(memory_space=pltpu.VMEM)
    return pl.pallas_call(
        body,
        in_specs=[vmem] * len(operands) + [pl.BlockSpec(memory_space=pl.ANY)] * len(before),
        out_specs=[vmem] * len(outs),
        out_shape=outs,
        scratch_shapes=list(scratch),
        compiler_params=pltpu.CompilerParams(vmem_limit_bytes=limit),
        cost_estimate=pl.CostEstimate(flops=flops, bytes_accessed=0, transcendentals=0),
    )(*(pltpu.with_memory_space_constraint(part, pltpu.VMEM) for part in operands), *before)


def held(*shape):
    return pltpu.VMEM(shape, jnp.float32)


def stack_after(pieces, before=()):
    def kernel(*refs):
        for index, ref in enumerate(refs[:-1]):
            refs[-1][index] = ref[...]

    return call(kernel, pieces, [held(len(pieces), *pieces[0].shape)], before)[0]


def sum_after(pieces, before=()):
    def kernel(*refs):
        refs[-1][...] = functools.reduce(jnp.add, [ref[...] for ref in refs[:-1]])

    return call(kernel, pieces, [held(*pieces[0].shape)], before)[0]


def fetch_evens(piece, axis):
    return [fetch(piece, axis, shift) for shift in range(2, lax.axis_size(axis), 2)]


def gather_evens(piece, axis, before=()):
    return stack_after([piece] + fetch_evens(piece, axis), before)


def gather_odds(evens, axis):
    size = lax.axis_size(axis)
    assert size > 1 and size & (size - 1) == 0
    return fetch(evens, axis, 1)


def dot_pairs(left, right):
    return lax.dot_general(left, right, (((1,), (1,)), ((), ())), preferred_element_type=jnp.float32)


def combine(high, middle, low):
    return reduce_centered(15.0 * high + 256.0 * reduce_centered(middle) + low)


def pack_square(square, width):
    span = square.shape[0]
    rows = span * span // width
    return jnp.concatenate([square[j * rows : (j + 1) * rows] for j in range(width // span)], 1)


def unpack_square(packed, span):
    count = packed.shape[1] // span
    return jnp.concatenate([packed[:, j * span : (j + 1) * span] for j in range(count)], 0)


def build_kernel(sizes, *refs):
    entries_ref, x_ref, y_ref, dense_ref, x_out, y_out, token_ref = refs[3:10]
    rows_ref, cols_ref, count_ref, tiles, sems = refs[10:]
    n_row, n_col, piece_blocks, group = sizes
    _, _, slot_count, tile_len, _ = entries_ref.shape
    me_row, me_col = lax.axis_index("row"), lax.axis_index("col")
    chunk_count = slot_count // group

    def chunk(index):
        source = entries_ref.at[0, 0, pl.ds(index * group, group)]
        return pltpu.make_async_copy(source, tiles.at[pl.ds(index * group, group)], sems.at[index])

    small = [*zip(refs[:3], refs[10:13]), (y_ref, y_out), (x_ref, x_out)]
    small = [
        pltpu.make_async_copy(source, target, sems.at[chunk_count + index])
        for index, (source, target) in enumerate(small)
    ]
    for copy in small[:3]:
        copy.start()
    for index in range(chunk_count):
        chunk(index).start()
    for copy in small[3:]:
        copy.start()

    def clear(block, carry):
        dense_ref[block] = jnp.zeros(dense_ref.shape[1:], dense_ref.dtype)
        return carry

    lax.fori_loop(0, dense_ref.shape[0], clear, 0)
    for copy in small[:3]:
        copy.wait()

    def place(slot):
        row, col = rows_ref[0, 0, slot], cols_ref[0, 0, slot]
        row_shift = shift_of(me_col, row // piece_blocks, n_col)
        col_shift = shift_of(me_row, col // piece_blocks, n_row)
        col_place = col_shift % 2 * (n_row // 2) + col_shift // 2
        block = row_shift * piece_blocks + row % piece_blocks
        start = (col_place * piece_blocks + col % piece_blocks) * tile_len
        values = jnp.where(slot < count_ref[0, 0], tiles[slot], 0.0)
        values = jnp.where(values > HALF_MODULUS, values - MODULUS, values).T
        both = jnp.concatenate(balanced_digits(values), 1).astype(jnp.bfloat16)
        dense_ref[block, pl.ds(pl.multiple_of(start, tile_len), tile_len), :] = both

    def step(index, carry):
        chunk(index).wait()
        for offset in range(group):
            place(index * group + offset)
        return carry

    lax.fori_loop(0, chunk_count, step, 0)
    for copy in small[3:]:
        copy.wait()
    token_ref[...] = jnp.zeros_like(token_ref)


def build_dense(tiles, block_x, block_y, sizes):
    tile_rows, tile_cols, tile_count, tile_entries = tiles
    n_row, n_col, piece_blocks = sizes
    _, _, slot_count, tile_len, _ = tile_entries.shape
    group = next(size for size in (8, 4, 2, 1) if slot_count % size == 0)
    shape = (n_col * piece_blocks, n_row * piece_blocks * tile_len, 2 * tile_len)
    hbm = pl.BlockSpec(memory_space=pltpu.HBM)
    rows, cols, entries, x_piece, y_piece = (
        pltpu.with_memory_space_constraint(part, pltpu.HBM)
        for part in (tile_rows, tile_cols, tile_entries, block_x, block_y)
    )
    return pl.pallas_call(
        functools.partial(build_kernel, (*sizes, group)),
        in_specs=[hbm, hbm, pl.BlockSpec(memory_space=pl.ANY), hbm, hbm, hbm],
        out_specs=[pl.BlockSpec(memory_space=pltpu.VMEM)] * 4,
        out_shape=[
            pltpu.VMEM(shape, jnp.bfloat16),
            held(*block_x.shape),
            held(*block_y.shape),
            held(8, 128),
        ],
        scratch_shapes=[
            *(pltpu.SMEM(part.shape, part.dtype) for part in (tile_rows, tile_cols, tile_count)),
            pltpu.VMEM((slot_count, tile_len, tile_len), jnp.float32),
            pltpu.SemaphoreType.DMA((slot_count // group + 5,)),
        ],
        compiler_params=pltpu.CompilerParams(vmem_limit_bytes=VMEM_LIMIT),
        cost_estimate=pl.CostEstimate(
            flops=8 * tile_entries.size, bytes_accessed=8 * tile_entries.size, transcendentals=0
        ),
    )(rows, cols, tile_count, entries, x_piece, y_piece)


def half_products(half, span, pieces_ref, dense_ref, digits, block):
    _, depth, width = dense_ref.shape
    tile_len, half_depth = width // 2, depth // 2
    high = middle = low = 0.0
    for start in range(0, half_depth, EXACT_DEPTH):
        stop = min(start + EXACT_DEPTH, half_depth)
        products = jnp.dot(
            digits[:, start:stop],
            dense_ref[block, half * half_depth + start : half * half_depth + stop, :],
            preferred_element_type=jnp.float32,
        )
        products = reduce_centered(products)
        high = high + products[:span, :tile_len]
        middle = middle + products[:span, tile_len:] + products[span:, :tile_len]
        low = low + products[span:, tile_len:]
    return high, middle, low


def fill_digits(span, pieces_ref, digits):
    piece_len = pieces_ref.shape[2]
    for d in range(pieces_ref.shape[0]):
        vector = reduce_centered(pieces_ref[d, :span, :])
        digits[:, d * piece_len : (d + 1) * piece_len] = stacked_digits(vector)


def first_half_kernel(span, pieces_ref, dense_ref, sums_ref, digits):
    fill_digits(span, pieces_ref, digits)
    tile_len = dense_ref.shape[2] // 2
    for block in range(dense_ref.shape[0]):
        parts = half_products(0, span, pieces_ref, dense_ref, digits, block)
        for index, part in enumerate(parts):
            sums_ref[index, :, block * tile_len : (block + 1) * tile_len] = part


def half_of_core(packed):
    rows = packed.shape[0] // 2
    return jnp.where(lax.axis_index("row") % 2 == 0, packed[:rows], packed[rows:])


def second_half_kernel(span, pieces_ref, evens_ref, sums_ref, dense_ref, *refs):
    outs, digits = refs[:-1], refs[-1]
    n_col = len(outs)
    fill_digits(span, pieces_ref, digits)
    row_blocks, _, width = dense_ref.shape
    tile_len = width // 2
    piece_blocks = row_blocks // n_col
    for e in reversed(range(n_col)):
        for sub in range(piece_blocks):
            block = e * piece_blocks + sub
            parts = half_products(1, span, pieces_ref, dense_ref, digits, block)
            parts = (
                part + sums_ref[index, :, block * tile_len : (block + 1) * tile_len]
                for index, part in enumerate(parts)
            )
            outs[e][:span, sub * tile_len : (sub + 1) * tile_len] = combine(*parts)
    if outs[0].shape[0] > span:
        packed = jnp.sum(pieces_ref[:, span:, :], 0) + jnp.sum(evens_ref[:, span:, :], 0)
        packed = half_of_core(packed)
        for out in outs:
            out[span:, :] = packed


def dense_first(evens, span, dense):
    row_blocks, depth, width = dense.shape
    return call(
        functools.partial(first_half_kernel, span),
        [evens, dense],
        [held(3, span, row_blocks * width // 2)],
        scratch=[pltpu.VMEM((2 * span, depth // 2), jnp.bfloat16)],
        limit=VMEM_LIMIT,
        flops=2 * span * dense.size,
    )[0]


def dense_second(odds, evens, sums, span, n_col, dense, before):
    _, depth, _ = dense.shape
    _, rows, piece_len = odds.shape
    return list(
        call(
            functools.partial(second_half_kernel, span),
            [odds, evens, sums, dense],
            [held(span + (rows - span) // 2, piece_len)] * n_col,
            before,
            scratch=[pltpu.VMEM((2 * span, depth // 2), jnp.bfloat16)],
            limit=VMEM_LIMIT,
            flops=2 * span * dense.size,
        )
    )


def left_kernel(n_row, x_evens, x_odds, dense_ref, *refs):
    evens, odds_ref = refs[:-1], refs[-1]
    row_blocks, _, width = dense_ref.shape
    tile_len = width // 2
    _, span, piece_len = x_evens.shape
    piece_blocks = piece_len // tile_len
    x_digits = [
        centred_digits((x_odds if e % 2 else x_evens)[e // 2])
        for e in range(row_blocks // piece_blocks)
    ]
    for place in range(n_row):
        by_high = by_low = high_part = low_part = 0.0
        for block in range(row_blocks):
            sub = block % piece_blocks
            left = x_digits[block // piece_blocks][:, sub * tile_len : (sub + 1) * tile_len]
            right = dense_ref[block, place * piece_len : (place + 1) * piece_len, :]
            high_part = high_part + dot_pairs(left, right[:, :tile_len])
            low_part = low_part + dot_pairs(left, right[:, tile_len:])
            if (block + 1) * tile_len % EXACT_DEPTH == 0 or block == row_blocks - 1:
                by_high = by_high + reduce_centered(high_part)
                by_low = by_low + reduce_centered(low_part)
                high_part = low_part = 0.0
        piece = combine(by_high[:span], by_low[:span] + by_high[span:], by_low[span:])
        if place < n_row // 2:
            evens[place][...] = piece
        else:
            odds_ref[place - n_row // 2] = piece


def dense_left(x_pairs, n_row, dense, before):
    _, span, piece_len = x_pairs[0].shape
    results = call(
        functools.partial(left_kernel, n_row),
        [*x_pairs, dense],
        [held(span, piece_len)] * (n_row // 2) + [held(n_row // 2, span, piece_len)],
        before,
        limit=VMEM_LIMIT,
        flops=4 * span * dense.size,
    )
    return list(results[:-1]), results[-1]


def sparse_tiles(tiles, sizes):
    tile_rows, tile_cols, tile_count, tile_entries = tiles
    n_row, n_col, piece_blocks = sizes
    entries, rows, cols = tile_entries[0, 0], tile_rows[0, 0], tile_cols[0, 0]
    row_shift = shift_of(lax.axis_index("col"), rows // piece_blocks, n_col)
    col_shift = shift_of(lax.axis_index("row"), cols // piece_blocks, n_row)
    col_place = col_shift % 2 * (n_row // 2) + col_shift // 2
    positions = (
        row_shift * piece_blocks + rows % piece_blocks,
        col_place * piece_blocks + cols % piece_blocks,
        tile_count[0, 0],
    )
    entries = jnp.where(entries > HALF_MODULUS, entries - MODULUS, entries)
    return positions, jnp.stack(balanced_digits(entries), 1).astype(jnp.bfloat16)


def sparse_product(vector, spec, places, targets, count, blocks, a_digits):
    span, tile_len = vector.shape[0], a_digits.shape[-1]
    v_digits = stacked_digits(vector).reshape(2 * span, -1, tile_len)
    picked = jnp.take(v_digits, places, axis=1)
    products = jnp.einsum(spec, picked, a_digits, preferred_element_type=jnp.float32)
    products = reduce_centered(products)
    residues = combine(
        products[:, 0, :span],
        products[:, 0, span:] + products[:, 1, :span],
        products[:, 1, span:],
    )
    live = jnp.arange(targets.shape[0], dtype=jnp.int32) < count
    onehot = targets[None, :] == jnp.arange(blocks, dtype=jnp.int32)[:, None]
    onehot = (onehot & live[None, :]).astype(jnp.float32)
    summed = jnp.einsum("bt,twi->wbi", onehot, residues, precision=lax.Precision.HIGHEST)
    return reduce_centered(summed).reshape(span, blocks * tile_len)


def sparse_second(odds, evens, span, n_col, positions, a_digits):
    rows, cols, count = positions
    pieces = [*evens, *odds]
    piece_len = pieces[0].shape[1]
    blocks = n_col * piece_len // a_digits.shape[-1]
    vector = reduce_centered(jnp.concatenate([piece[:span] for piece in pieces], 1))
    product = sparse_product(vector, "ntk,tdik->tdni", cols, rows, count, blocks, a_digits)
    packed = half_of_core(functools.reduce(jnp.add, [piece[span:] for piece in pieces]))
    outs = [product[:, e * piece_len : (e + 1) * piece_len] for e in range(n_col)]
    return [jnp.concatenate([out, packed], 0) for out in outs]


def sparse_left(x_pairs, n_row, positions, a_digits):
    rows, cols, count = positions
    n_col = 2 * x_pairs[0].shape[0]
    x_pieces = [x_pairs[e % 2][e // 2] for e in range(n_col)]
    piece_len = x_pieces[0].shape[1]
    values = jnp.concatenate(x_pieces, 1)
    values = jnp.where(values > HALF_MODULUS, values - MODULUS, values)
    blocks = n_row * piece_len // a_digits.shape[-1]
    product = sparse_product(values, "nti,tdik->tdnk", rows, cols, count, blocks, a_digits)
    pieces = [product[:, d * piece_len : (d + 1) * piece_len] for d in range(n_row)]
    return pieces[: n_row // 2], jnp.stack(pieces[n_row // 2 :])


def add_came(evens, odds_came, index, before=()):
    def kernel(even_ref, came_ref, out_ref):
        out_ref[...] = even_ref[...] + came_ref[index]

    return call(kernel, [evens[index], odds_came], [held(*evens[index].shape)], before)[0]


def append_projections(w_parts, pieces, earlier):
    span, piece_len = pieces[0].shape
    rows = span * span // piece_len

    def kernel(*refs):
        w_refs, refs = refs[: len(w_parts)], refs[len(w_parts) :]
        piece_refs, refs = refs[: len(pieces)], refs[len(pieces) :]
        earlier_refs, out_ref = refs[:-1], refs[-1]
        summed = functools.reduce(jnp.add, [ref[...] for ref in piece_refs])
        out_ref[:span, :] = summed
        w_piece = functools.reduce(jnp.add, [ref[...] for ref in w_refs])
        w_digits = stacked_digits(reduce_centered(w_piece))
        for index, vector in enumerate([summed] + [ref[...] for ref in earlier_refs]):
            products = dot_pairs(w_digits, stacked_digits(reduce_centered(vector)))
            square = combine(
                reduce_centered(products[:span, :span]),
                reduce_centered(products[:span, span:]) + reduce_centered(products[span:, :span]),
                reduce_centered(products[span:, span:]),
            )
            start = span + index * rows
            out_ref[start : start + rows, :] = pack_square(square, piece_len)

    outs = [held(span + (len(earlier) + 1) * rows, piece_len)]
    return call(kernel, [*w_parts, *pieces, *earlier], outs)[0]


def multiply_mod(left, right):
    span = left.shape[0]
    left = stacked_digits(left)
    high, low = (part.astype(jnp.bfloat16) for part in balanced_digits(right))
    by_high = jnp.dot(left, high, preferred_element_type=jnp.float32)
    by_low = jnp.dot(left, low, preferred_element_type=jnp.float32)
    return combine(
        reduce_centered(by_high[:span]), by_low[:span] + by_high[span:], by_low[span:]
    )


def sigma_update(mine, other, span):
    rows = span * span // mine.shape[1]

    def kernel(mine_ref, other_ref, out_ref):
        first = lax.axis_index("row") % 2 == 0
        mine, other = reduce_centered(mine_ref[...]), reduce_centered(other_ref[...])
        packed = jnp.concatenate([jnp.where(first, mine, other), jnp.where(first, other, mine)], 0)
        c_3, c_1, c_2 = (
            unpack_square(packed[index * rows : (index + 1) * rows], span) for index in range(3)
        )
        e_2 = reduce_centered(c_1 - multiply_mod(c_1, c_2))
        both = reduce_centered(c_1 + e_2)
        start = multiply_mod(e_2, c_1)
        rest = c_1 - multiply_mod(both, c_2)
        e_3 = reduce_centered(multiply_mod(start, c_3) + rest)
        out_ref[0] = canonical(-multiply_mod(e_3, start)) * (1.0 / MODULUS)
        out_ref[1] = canonical(start + multiply_mod(e_3, both)) * (1.0 / MODULUS)
        out_ref[2] = canonical(-both - e_3) * (1.0 / MODULUS)

    outs = [jax.ShapeDtypeStruct((STEP_COUNT, span, span), jnp.float32)]
    return call(kernel, [mine, other], outs)[0]


def local(tile_entries, tile_rows, tile_cols, tile_count, block_x, block_y):
    _, _, slot_count, tile_len, _ = tile_entries.shape
    span, piece_len = block_y.shape
    piece_blocks = piece_len // tile_len
    n_row, n_col = lax.axis_size("row"), lax.axis_size("col")
    packed_rows = span * span // piece_len
    tiles = (tile_rows, tile_cols, tile_count, tile_entries)
    sizes = (n_row, n_col, piece_blocks)
    is_dense = n_col * piece_blocks * n_row * piece_blocks <= DENSE_CELLS * slot_count
    if is_dense:
        dense, x_own, y_own, token = build_dense(tiles, block_x, block_y, sizes)
        before = [token]
    else:
        positions, a_digits = sparse_tiles(tiles, sizes)
        x_own, y_own, before = block_x, block_y, []

    def multiply_evens(evens):
        return dense_first(evens, span, dense) if is_dense else evens

    def multiply_odds(odds, evens, sums, before):
        if is_dense:
            return dense_second(odds, evens, sums, span, n_col, dense, before)
        return sparse_second(odds, evens, span, n_col, positions, a_digits)

    def multiply(evens, before):
        return multiply_odds(gather_odds(evens, "row"), evens, multiply_evens(evens), before)

    x_came = fetch_evens(block_x, "col")
    evens = stack_after([y_own] + fetch_evens(block_y, "row"), [*before, *x_came])
    x_evens = stack_after([x_own] + x_came)
    outs = multiply(evens, [x_evens])
    x_pairs = [x_evens, gather_odds(x_evens, "col")]
    if is_dense:
        w_evens, w_odds = dense_left(x_pairs, n_row, dense, [outs[0]])
    else:
        w_evens, w_odds = sparse_left(x_pairs, n_row, positions, a_digits)
    vector_1 = sum_after(scatter_pieces(outs, "col"), [w_odds])
    w_came = fetch(w_odds, "row", 1)
    outs = multiply(gather_evens(vector_1, "row"), [w_came])
    pieces = scatter_pieces(outs, "col")
    w_last = n_row // 2 - 1
    w_parts = [
        add_came(w_evens, w_came, index, [] if index == w_last else [outs[0]])
        for index in range(n_row // 2)
    ]
    w_parts = w_parts[:1] + [
        fetch(w_parts[index], "row", 2 * index) for index in reversed(range(1, n_row // 2))
    ]
    vector_2 = append_projections(w_parts, pieces, [y_own, vector_1])
    outs = multiply(gather_evens(vector_2, "row"), [])
    pieces = scatter_pieces(outs, "col")
    terms = functools.reduce(jnp.add, [piece[span:] for piece in pieces])
    vector_3 = functools.reduce(jnp.add, [piece[:span] for piece in pieces])
    return sigma_update(terms, fetch(terms, "row", 1), span), canonical(vector_3) * (1.0 / MODULUS)


def solution(mesh):
    placed = (
        P("row", "col", None, None, None),
        P("row", "col", None),
        P("row", "col", None),
        P("row", "col"),
        P(None, ("row", "col")),
        P(None, ("row", "col")),
    )
    return jax.shard_map(
        local, mesh=mesh, in_specs=placed, out_specs=(P(), P(None, ("row", "col"))), check_vma=False
    )
```

```python
import functools

import jax
import jax.numpy as jnp
from jax import lax
from jax.experimental import pallas as pl
from jax.experimental.pallas import tpu as pltpu
from jax.sharding import PartitionSpec as P

STEP_COUNT = 3

MODULUS = 65521.0
HALF_MODULUS = 32760.0
BASE = 256.0
EXACT_DEPTH = 1024
DENSE_CELLS = 4
VMEM_LIMIT = 16 * 1024 * 1024
SMALL_LIMIT = 4 * 1024 * 1024


def reduce_centered(values):
    return values - MODULUS * jnp.floor(values * (1.0 / MODULUS) + 0.5)


def canonical(values):
    reduced = reduce_centered(values)
    return jnp.where(reduced < 0, reduced + MODULUS, reduced)


def balanced_digits(values):
    high = jnp.floor(values * (1.0 / BASE) + 0.5)
    return high, values - BASE * high


def stacked_digits(values):
    high, low = balanced_digits(values)
    return jnp.concatenate([high, low], 0).astype(jnp.bfloat16)


def centred_digits(residues):
    return stacked_digits(jnp.where(residues > HALF_MODULUS, residues - MODULUS, residues))


def partner(index, shift, size):
    return index ^ shift if size & (size - 1) == 0 else (index + shift) % size


def shift_of(index, other, size):
    return index ^ other if size & (size - 1) == 0 else (other - index) % size


def fetch(piece, axis, shift):
    size = lax.axis_size(axis)
    return lax.ppermute(piece, axis, [(partner(i, shift, size), i) for i in range(size)])


def scatter_pieces(pieces, axis):
    size = lax.axis_size(axis)
    came = [
        lax.ppermute(pieces[shift], axis, [(i, partner(i, shift, size)) for i in range(size)])
        for shift in reversed(range(1, size))
    ]
    return [pieces[0]] + came


def call(kernel, operands, outs, before=(), scratch=(), limit=SMALL_LIMIT, flops=0):
    def body(*refs):
        kernel(*refs[: len(operands)], *refs[len(operands) + len(before) :])

    vmem = pl.BlockSpec(memory_space=pltpu.VMEM)
    return pl.pallas_call(
        body,
        in_specs=[vmem] * len(operands) + [pl.BlockSpec(memory_space=pl.ANY)] * len(before),
        out_specs=[vmem] * len(outs),
        out_shape=outs,
        scratch_shapes=list(scratch),
        compiler_params=pltpu.CompilerParams(vmem_limit_bytes=limit),
        cost_estimate=pl.CostEstimate(flops=flops, bytes_accessed=0, transcendentals=0),
    )(*(pltpu.with_memory_space_constraint(part, pltpu.VMEM) for part in operands), *before)


def held(*shape):
    return pltpu.VMEM(shape, jnp.float32)


def stack_after(pieces, before=()):
    def kernel(*refs):
        for index, ref in enumerate(refs[:-1]):
            refs[-1][index] = ref[...]

    return call(kernel, pieces, [held(len(pieces), *pieces[0].shape)], before)[0]


def sum_after(pieces, before=()):
    def kernel(*refs):
        refs[-1][...] = functools.reduce(jnp.add, [ref[...] for ref in refs[:-1]])

    return call(kernel, pieces, [held(*pieces[0].shape)], before)[0]


def fetch_evens(piece, axis):
    return [fetch(piece, axis, shift) for shift in range(2, lax.axis_size(axis), 2)]


def gather_evens(piece, axis, before=()):
    return stack_after([piece] + fetch_evens(piece, axis), before)


def gather_odds(evens, axis):
    size = lax.axis_size(axis)
    assert size > 1 and size & (size - 1) == 0
    return fetch(evens, axis, 1)


def dot_pairs(left, right):
    return lax.dot_general(left, right, (((1,), (1,)), ((), ())), preferred_element_type=jnp.float32)


def combine(high, middle, low):
    return reduce_centered(15.0 * high + 256.0 * reduce_centered(middle) + low)


def pack_square(square, width):
    span = square.shape[0]
    rows = span * span // width
    return jnp.concatenate([square[j * rows : (j + 1) * rows] for j in range(width // span)], 1)


def unpack_square(packed, span):
    count = packed.shape[1] // span
    return jnp.concatenate([packed[:, j * span : (j + 1) * span] for j in range(count)], 0)


def build_kernel(sizes, *refs):
    entries_ref, x_ref, y_ref, dense_ref, x_out, y_out, token_ref = refs[3:10]
    rows_ref, cols_ref, count_ref, tiles, sems = refs[10:]
    n_row, n_col, piece_blocks, group = sizes
    _, _, slot_count, tile_len, _ = entries_ref.shape
    me_row, me_col = lax.axis_index("row"), lax.axis_index("col")
    chunk_count = slot_count // group

    def chunk(index):
        source = entries_ref.at[0, 0, pl.ds(index * group, group)]
        return pltpu.make_async_copy(source, tiles.at[pl.ds(index * group, group)], sems.at[index])

    small = [*zip(refs[:3], refs[10:13]), (y_ref, y_out), (x_ref, x_out)]
    small = [
        pltpu.make_async_copy(source, target, sems.at[chunk_count + index])
        for index, (source, target) in enumerate(small)
    ]
    for copy in small[:3]:
        copy.start()
    for index in range(chunk_count):
        chunk(index).start()
    for copy in small[3:]:
        copy.start()

    def clear(block, carry):
        dense_ref[block] = jnp.zeros(dense_ref.shape[1:], dense_ref.dtype)
        return carry

    lax.fori_loop(0, dense_ref.shape[0], clear, 0)
    for copy in small[:3]:
        copy.wait()

    def place(slot):
        row, col = rows_ref[0, 0, slot], cols_ref[0, 0, slot]
        row_shift = shift_of(me_col, row // piece_blocks, n_col)
        col_shift = shift_of(me_row, col // piece_blocks, n_row)
        col_place = col_shift % 2 * (n_row // 2) + col_shift // 2
        block = row_shift * piece_blocks + row % piece_blocks
        start = (col_place * piece_blocks + col % piece_blocks) * tile_len
        values = jnp.where(slot < count_ref[0, 0], tiles[slot], 0.0)
        values = jnp.where(values > HALF_MODULUS, values - MODULUS, values).T
        both = jnp.concatenate(balanced_digits(values), 1).astype(jnp.bfloat16)
        dense_ref[block, pl.ds(pl.multiple_of(start, tile_len), tile_len), :] = both

    def step(index, carry):
        chunk(index).wait()
        for offset in range(group):
            place(index * group + offset)
        return carry

    lax.fori_loop(0, chunk_count, step, 0)
    for copy in small[3:]:
        copy.wait()
    token_ref[...] = jnp.zeros_like(token_ref)


def build_dense(tiles, block_x, block_y, sizes):
    tile_rows, tile_cols, tile_count, tile_entries = tiles
    n_row, n_col, piece_blocks = sizes
    _, _, slot_count, tile_len, _ = tile_entries.shape
    group = next(size for size in (8, 4, 2, 1) if slot_count % size == 0)
    shape = (n_col * piece_blocks, n_row * piece_blocks * tile_len, 2 * tile_len)
    hbm = pl.BlockSpec(memory_space=pltpu.HBM)
    rows, cols, entries, x_piece, y_piece = (
        pltpu.with_memory_space_constraint(part, pltpu.HBM)
        for part in (tile_rows, tile_cols, tile_entries, block_x, block_y)
    )
    return pl.pallas_call(
        functools.partial(build_kernel, (*sizes, group)),
        in_specs=[hbm, hbm, pl.BlockSpec(memory_space=pl.ANY), hbm, hbm, hbm],
        out_specs=[pl.BlockSpec(memory_space=pltpu.VMEM)] * 4,
        out_shape=[
            pltpu.VMEM(shape, jnp.bfloat16),
            held(*block_x.shape),
            held(*block_y.shape),
            held(8, 128),
        ],
        scratch_shapes=[
            *(pltpu.SMEM(part.shape, part.dtype) for part in (tile_rows, tile_cols, tile_count)),
            pltpu.VMEM((slot_count, tile_len, tile_len), jnp.float32),
            pltpu.SemaphoreType.DMA((slot_count // group + 5,)),
        ],
        compiler_params=pltpu.CompilerParams(vmem_limit_bytes=VMEM_LIMIT),
        cost_estimate=pl.CostEstimate(
            flops=8 * tile_entries.size, bytes_accessed=8 * tile_entries.size, transcendentals=0
        ),
    )(rows, cols, tile_count, entries, x_piece, y_piece)


def half_products(half, span, pieces_ref, dense_ref, digits, block):
    _, depth, width = dense_ref.shape
    tile_len, half_depth = width // 2, depth // 2
    high = middle = low = 0.0
    for start in range(0, half_depth, EXACT_DEPTH):
        stop = min(start + EXACT_DEPTH, half_depth)
        products = jnp.dot(
            digits[:, start:stop],
            dense_ref[block, half * half_depth + start : half * half_depth + stop, :],
            preferred_element_type=jnp.float32,
        )
        products = reduce_centered(products)
        high = high + products[:span, :tile_len]
        middle = middle + products[:span, tile_len:] + products[span:, :tile_len]
        low = low + products[span:, tile_len:]
    return high, middle, low


def fill_digits(span, pieces_ref, digits):
    piece_len = pieces_ref.shape[2]
    for d in range(pieces_ref.shape[0]):
        vector = reduce_centered(pieces_ref[d, :span, :])
        digits[:, d * piece_len : (d + 1) * piece_len] = stacked_digits(vector)


def first_half_kernel(span, pieces_ref, dense_ref, sums_ref, digits):
    fill_digits(span, pieces_ref, digits)
    tile_len = dense_ref.shape[2] // 2
    for block in range(dense_ref.shape[0]):
        parts = half_products(0, span, pieces_ref, dense_ref, digits, block)
        for index, part in enumerate(parts):
            sums_ref[index, :, block * tile_len : (block + 1) * tile_len] = part


def half_of_core(packed):
    rows = packed.shape[0] // 2
    return jnp.where(lax.axis_index("row") % 2 == 0, packed[:rows], packed[rows:])


def second_half_kernel(span, pieces_ref, evens_ref, sums_ref, dense_ref, *refs):
    outs, digits = refs[:-1], refs[-1]
    n_col = len(outs)
    fill_digits(span, pieces_ref, digits)
    row_blocks, _, width = dense_ref.shape
    tile_len = width // 2
    piece_blocks = row_blocks // n_col
    for e in reversed(range(n_col)):
        for sub in range(piece_blocks):
            block = e * piece_blocks + sub
            parts = half_products(1, span, pieces_ref, dense_ref, digits, block)
            parts = (
                part + sums_ref[index, :, block * tile_len : (block + 1) * tile_len]
                for index, part in enumerate(parts)
            )
            outs[e][:span, sub * tile_len : (sub + 1) * tile_len] = combine(*parts)
    if outs[0].shape[0] > span:
        packed = jnp.sum(pieces_ref[:, span:, :], 0) + jnp.sum(evens_ref[:, span:, :], 0)
        packed = half_of_core(packed)
        for out in outs:
            out[span:, :] = packed


def dense_first(evens, span, dense):
    row_blocks, depth, width = dense.shape
    return call(
        functools.partial(first_half_kernel, span),
        [evens, dense],
        [held(3, span, row_blocks * width // 2)],
        scratch=[pltpu.VMEM((2 * span, depth // 2), jnp.bfloat16)],
        limit=VMEM_LIMIT,
        flops=2 * span * dense.size,
    )[0]


def dense_second(odds, evens, sums, span, n_col, dense, before):
    _, depth, _ = dense.shape
    _, rows, piece_len = odds.shape
    return list(
        call(
            functools.partial(second_half_kernel, span),
            [odds, evens, sums, dense],
            [held(span + (rows - span) // 2, piece_len)] * n_col,
            before,
            scratch=[pltpu.VMEM((2 * span, depth // 2), jnp.bfloat16)],
            limit=VMEM_LIMIT,
            flops=2 * span * dense.size,
        )
    )


def left_kernel(n_row, x_evens, x_odds, dense_ref, evens_ref, odds_ref):
    row_blocks, _, width = dense_ref.shape
    tile_len = width // 2
    _, span, piece_len = x_evens.shape
    piece_blocks = piece_len // tile_len
    x_digits = [
        centred_digits((x_odds if e % 2 else x_evens)[e // 2])
        for e in range(row_blocks // piece_blocks)
    ]
    for place in range(n_row):
        by_high = by_low = high_part = low_part = 0.0
        for block in range(row_blocks):
            sub = block % piece_blocks
            left = x_digits[block // piece_blocks][:, sub * tile_len : (sub + 1) * tile_len]
            right = dense_ref[block, place * piece_len : (place + 1) * piece_len, :]
            high_part = high_part + dot_pairs(left, right[:, :tile_len])
            low_part = low_part + dot_pairs(left, right[:, tile_len:])
            if (block + 1) * tile_len % EXACT_DEPTH == 0 or block == row_blocks - 1:
                by_high = by_high + reduce_centered(high_part)
                by_low = by_low + reduce_centered(low_part)
                high_part = low_part = 0.0
        piece = combine(by_high[:span], by_low[:span] + by_high[span:], by_low[span:])
        if place < n_row // 2:
            evens_ref[place] = piece
        else:
            odds_ref[place - n_row // 2] = piece


def dense_left(x_pairs, n_row, dense, before):
    _, span, piece_len = x_pairs[0].shape
    return call(
        functools.partial(left_kernel, n_row),
        [*x_pairs, dense],
        [held(n_row // 2, span, piece_len)] * 2,
        before,
        limit=VMEM_LIMIT,
        flops=4 * span * dense.size,
    )


def sparse_tiles(tiles, sizes):
    tile_rows, tile_cols, tile_count, tile_entries = tiles
    n_row, n_col, piece_blocks = sizes
    entries, rows, cols = tile_entries[0, 0], tile_rows[0, 0], tile_cols[0, 0]
    row_shift = shift_of(lax.axis_index("col"), rows // piece_blocks, n_col)
    col_shift = shift_of(lax.axis_index("row"), cols // piece_blocks, n_row)
    col_place = col_shift % 2 * (n_row // 2) + col_shift // 2
    positions = (
        row_shift * piece_blocks + rows % piece_blocks,
        col_place * piece_blocks + cols % piece_blocks,
        tile_count[0, 0],
    )
    entries = jnp.where(entries > HALF_MODULUS, entries - MODULUS, entries)
    return positions, jnp.stack(balanced_digits(entries), 1).astype(jnp.bfloat16)


def sparse_product(vector, spec, places, targets, count, blocks, a_digits):
    span, tile_len = vector.shape[0], a_digits.shape[-1]
    v_digits = stacked_digits(vector).reshape(2 * span, -1, tile_len)
    picked = jnp.take(v_digits, places, axis=1)
    products = jnp.einsum(spec, picked, a_digits, preferred_element_type=jnp.float32)
    products = reduce_centered(products)
    residues = combine(
        products[:, 0, :span],
        products[:, 0, span:] + products[:, 1, :span],
        products[:, 1, span:],
    )
    live = jnp.arange(targets.shape[0], dtype=jnp.int32) < count
    onehot = targets[None, :] == jnp.arange(blocks, dtype=jnp.int32)[:, None]
    onehot = (onehot & live[None, :]).astype(jnp.float32)
    summed = jnp.einsum("bt,twi->wbi", onehot, residues, precision=lax.Precision.HIGHEST)
    return reduce_centered(summed).reshape(span, blocks * tile_len)


def sparse_second(odds, evens, span, n_col, positions, a_digits):
    rows, cols, count = positions
    pieces = [*evens, *odds]
    piece_len = pieces[0].shape[1]
    blocks = n_col * piece_len // a_digits.shape[-1]
    vector = reduce_centered(jnp.concatenate([piece[:span] for piece in pieces], 1))
    product = sparse_product(vector, "ntk,tdik->tdni", cols, rows, count, blocks, a_digits)
    packed = half_of_core(functools.reduce(jnp.add, [piece[span:] for piece in pieces]))
    outs = [product[:, e * piece_len : (e + 1) * piece_len] for e in range(n_col)]
    return [jnp.concatenate([out, packed], 0) for out in outs]


def sparse_left(x_pairs, n_row, positions, a_digits):
    rows, cols, count = positions
    n_col = 2 * x_pairs[0].shape[0]
    x_pieces = [x_pairs[e % 2][e // 2] for e in range(n_col)]
    piece_len = x_pieces[0].shape[1]
    values = jnp.concatenate(x_pieces, 1)
    values = jnp.where(values > HALF_MODULUS, values - MODULUS, values)
    blocks = n_row * piece_len // a_digits.shape[-1]
    product = sparse_product(values, "nti,tdik->tdnk", rows, cols, count, blocks, a_digits)
    pieces = [product[:, d * piece_len : (d + 1) * piece_len] for d in range(n_row)]
    return jnp.stack(pieces[: n_row // 2]), jnp.stack(pieces[n_row // 2 :])


def add_and_part(kept, came, before=()):
    def kernel(kept_ref, came_ref, evens_ref, odds_ref):
        for index in range(kept.shape[0]):
            (odds_ref if index % 2 else evens_ref)[index // 2] = kept_ref[index] + came_ref[index]

    return call(kernel, [kept, came], [held(kept.shape[0] // 2, *kept.shape[1:])] * 2, before)


def append_projections(w_parts, pieces, earlier):
    span, piece_len = pieces[0].shape
    rows = span * span // piece_len

    def kernel(*refs):
        piece_refs, refs = refs[: len(pieces)], refs[len(pieces) :]
        earlier_refs, refs = refs[: len(earlier)], refs[len(earlier) :]
        w_refs, out_ref = refs[:-1], refs[-1]
        summed = functools.reduce(jnp.add, [ref[...] for ref in piece_refs])
        out_ref[:span, :] = summed
        w_piece = functools.reduce(jnp.add, [ref[...] for ref in w_refs])
        w_digits = stacked_digits(reduce_centered(w_piece))
        for index, vector in enumerate([summed] + [ref[...] for ref in earlier_refs]):
            products = dot_pairs(w_digits, stacked_digits(reduce_centered(vector)))
            square = combine(
                reduce_centered(products[:span, :span]),
                reduce_centered(products[:span, span:]) + reduce_centered(products[span:, :span]),
                reduce_centered(products[span:, span:]),
            )
            start = span + index * rows
            out_ref[start : start + rows, :] = pack_square(square, piece_len)

    outs = [held(span + (len(earlier) + 1) * rows, piece_len)]
    return call(kernel, [*pieces, *earlier, *w_parts], outs)[0]


def multiply_mod(left, right):
    span = left.shape[0]
    left = stacked_digits(left)
    high, low = (part.astype(jnp.bfloat16) for part in balanced_digits(right))
    by_high = jnp.dot(left, high, preferred_element_type=jnp.float32)
    by_low = jnp.dot(left, low, preferred_element_type=jnp.float32)
    return combine(
        reduce_centered(by_high[:span]), by_low[:span] + by_high[span:], by_low[span:]
    )


def sigma_update(mine, other, span):
    rows = span * span // mine.shape[1]

    def kernel(mine_ref, other_ref, out_ref):
        first = lax.axis_index("row") % 2 == 0
        mine, other = reduce_centered(mine_ref[...]), reduce_centered(other_ref[...])
        packed = jnp.concatenate([jnp.where(first, mine, other), jnp.where(first, other, mine)], 0)
        c_3, c_1, c_2 = (
            unpack_square(packed[index * rows : (index + 1) * rows], span) for index in range(3)
        )
        e_2 = reduce_centered(c_1 - multiply_mod(c_1, c_2))
        both = reduce_centered(c_1 + e_2)
        start = multiply_mod(e_2, c_1)
        rest = c_1 - multiply_mod(both, c_2)
        e_3 = reduce_centered(multiply_mod(start, c_3) + rest)
        out_ref[0] = canonical(-multiply_mod(e_3, start)) * (1.0 / MODULUS)
        out_ref[1] = canonical(start + multiply_mod(e_3, both)) * (1.0 / MODULUS)
        out_ref[2] = canonical(-both - e_3) * (1.0 / MODULUS)

    outs = [jax.ShapeDtypeStruct((STEP_COUNT, span, span), jnp.float32)]
    return call(kernel, [mine, other], outs)[0]


def local(tile_entries, tile_rows, tile_cols, tile_count, block_x, block_y):
    _, _, slot_count, tile_len, _ = tile_entries.shape
    span, piece_len = block_y.shape
    piece_blocks = piece_len // tile_len
    n_row, n_col = lax.axis_size("row"), lax.axis_size("col")
    packed_rows = span * span // piece_len
    tiles = (tile_rows, tile_cols, tile_count, tile_entries)
    sizes = (n_row, n_col, piece_blocks)
    is_dense = n_col * piece_blocks * n_row * piece_blocks <= DENSE_CELLS * slot_count
    if is_dense:
        dense, x_own, y_own, token = build_dense(tiles, block_x, block_y, sizes)
        before = [token]
    else:
        positions, a_digits = sparse_tiles(tiles, sizes)
        x_own, y_own, before = block_x, block_y, []

    def multiply_evens(evens):
        return dense_first(evens, span, dense) if is_dense else evens

    def multiply_odds(odds, evens, sums, before):
        if is_dense:
            return dense_second(odds, evens, sums, span, n_col, dense, before)
        return sparse_second(odds, evens, span, n_col, positions, a_digits)

    def multiply(evens, before):
        return multiply_odds(gather_odds(evens, "row"), evens, multiply_evens(evens), before)

    y_came = fetch_evens(block_y, "row")
    x_came = fetch_evens(block_x, "col")
    evens = stack_after([y_own] + y_came, [*before, *x_came])
    x_evens = stack_after([x_own] + x_came)
    outs = multiply(evens, [x_evens])
    x_pairs = [x_evens, gather_odds(x_evens, "col")]
    if is_dense:
        w_evens, w_odds = dense_left(x_pairs, n_row, dense, [outs[0]])
    else:
        w_evens, w_odds = sparse_left(x_pairs, n_row, positions, a_digits)
    vector_1 = sum_after(scatter_pieces(outs, "col"), [w_odds])
    w_came = fetch(w_odds, "row", 1)
    outs = multiply(gather_evens(vector_1, "row"), [w_came])
    pieces = scatter_pieces(outs, "col")
    w_kept, shift, before = w_evens, 2, []
    while shift < n_row:
        w_kept, w_sent = add_and_part(w_kept, w_came, before)
        w_came = fetch(w_sent, "row", shift)
        shift, before = 2 * shift, [outs[0]]
    vector_2 = append_projections([w_kept[0], w_came[0]], pieces, [y_own, vector_1])
    outs = multiply(gather_evens(vector_2, "row"), [])
    pieces = scatter_pieces(outs, "col")
    terms = functools.reduce(jnp.add, [piece[span:] for piece in pieces])
    vector_3 = functools.reduce(jnp.add, [piece[:span] for piece in pieces])
    return sigma_update(terms, fetch(terms, "row", 1), span), canonical(vector_3) * (1.0 / MODULUS)


def solution(mesh):
    placed = (
        P("row", "col", None, None, None),
        P("row", "col", None),
        P("row", "col", None),
        P("row", "col"),
        P(None, ("row", "col")),
        P(None, ("row", "col")),
    )
    return jax.shard_map(
        local, mesh=mesh, in_specs=placed, out_specs=(P(), P(None, ("row", "col"))), check_vma=False
    )
```

```python
import functools

import jax
import jax.numpy as jnp
from jax import lax
from jax.experimental import pallas as pl
from jax.experimental.pallas import tpu as pltpu
from jax.sharding import PartitionSpec as P

STEP_COUNT = 3

MODULUS = 65521.0
HALF_MODULUS = 32760.0
BASE = 256.0
EXACT_DEPTH = 1024
DENSE_CELLS = 4
VMEM_LIMIT = 16 * 1024 * 1024
SMALL_LIMIT = 4 * 1024 * 1024


def reduce_centered(values):
    return values - MODULUS * jnp.floor(values * (1.0 / MODULUS) + 0.5)


def canonical(values):
    reduced = reduce_centered(values)
    return jnp.where(reduced < 0, reduced + MODULUS, reduced)


def balanced_digits(values):
    high = jnp.floor(values * (1.0 / BASE) + 0.5)
    return high, values - BASE * high


def stacked_digits(values):
    high, low = balanced_digits(values)
    return jnp.concatenate([high, low], 0).astype(jnp.bfloat16)


def centred_digits(residues):
    return stacked_digits(jnp.where(residues > HALF_MODULUS, residues - MODULUS, residues))


def partner(index, shift, size):
    return index ^ shift if size & (size - 1) == 0 else (index + shift) % size


def shift_of(index, other, size):
    return index ^ other if size & (size - 1) == 0 else (other - index) % size


def fetch(piece, axis, shift):
    size = lax.axis_size(axis)
    return lax.ppermute(piece, axis, [(partner(i, shift, size), i) for i in range(size)])


def scatter_pieces(pieces, axis):
    size = lax.axis_size(axis)
    came = [
        lax.ppermute(pieces[shift], axis, [(i, partner(i, shift, size)) for i in range(size)])
        for shift in reversed(range(1, size))
    ]
    return [pieces[0]] + came


def call(kernel, operands, outs, before=(), scratch=(), limit=SMALL_LIMIT, flops=0):
    def body(*refs):
        kernel(*refs[: len(operands)], *refs[len(operands) + len(before) :])

    vmem = pl.BlockSpec(memory_space=pltpu.VMEM)
    return pl.pallas_call(
        body,
        in_specs=[vmem] * len(operands) + [pl.BlockSpec(memory_space=pl.ANY)] * len(before),
        out_specs=[vmem] * len(outs),
        out_shape=outs,
        scratch_shapes=list(scratch),
        compiler_params=pltpu.CompilerParams(vmem_limit_bytes=limit),
        cost_estimate=pl.CostEstimate(flops=flops, bytes_accessed=0, transcendentals=0),
    )(*(pltpu.with_memory_space_constraint(part, pltpu.VMEM) for part in operands), *before)


def held(*shape):
    return pltpu.VMEM(shape, jnp.float32)


def stack_after(pieces, before=()):
    def kernel(*refs):
        for index, ref in enumerate(refs[:-1]):
            refs[-1][index] = ref[...]

    return call(kernel, pieces, [held(len(pieces), *pieces[0].shape)], before)[0]


def sum_after(pieces, before=()):
    def kernel(*refs):
        refs[-1][...] = functools.reduce(jnp.add, [ref[...] for ref in refs[:-1]])

    return call(kernel, pieces, [held(*pieces[0].shape)], before)[0]


def fetch_evens(piece, axis):
    return [fetch(piece, axis, shift) for shift in range(2, lax.axis_size(axis), 2)]


def gather_evens(piece, axis, before=()):
    return stack_after([piece] + fetch_evens(piece, axis), before)


def gather_odds(evens, axis):
    size = lax.axis_size(axis)
    assert size > 1 and size & (size - 1) == 0
    return fetch(evens, axis, 1)


def dot_pairs(left, right):
    return lax.dot_general(left, right, (((1,), (1,)), ((), ())), preferred_element_type=jnp.float32)


def combine(high, middle, low):
    return reduce_centered(15.0 * high + 256.0 * reduce_centered(middle) + low)


def pack_square(square, width):
    span = square.shape[0]
    rows = span * span // width
    return jnp.concatenate([square[j * rows : (j + 1) * rows] for j in range(width // span)], 1)


def unpack_square(packed, span):
    count = packed.shape[1] // span
    return jnp.concatenate([packed[:, j * span : (j + 1) * span] for j in range(count)], 0)


def build_kernel(sizes, *refs):
    entries_ref, x_ref, y_ref, dense_ref, x_out, y_out, token_ref = refs[3:10]
    rows_ref, cols_ref, count_ref, tiles, sems = refs[10:]
    n_row, n_col, piece_blocks, group = sizes
    _, _, slot_count, tile_len, _ = entries_ref.shape
    me_row, me_col = lax.axis_index("row"), lax.axis_index("col")
    chunk_count = slot_count // group

    def chunk(index):
        source = entries_ref.at[0, 0, pl.ds(index * group, group)]
        return pltpu.make_async_copy(source, tiles.at[pl.ds(index * group, group)], sems.at[index])

    small = [*zip(refs[:3], refs[10:13]), (y_ref, y_out), (x_ref, x_out)]
    small = [
        pltpu.make_async_copy(source, target, sems.at[chunk_count + index])
        for index, (source, target) in enumerate(small)
    ]
    for copy in small[:3]:
        copy.start()
    for index in range(chunk_count):
        chunk(index).start()
    for copy in small[3:]:
        copy.start()

    def clear(block, carry):
        dense_ref[block] = jnp.zeros(dense_ref.shape[1:], dense_ref.dtype)
        return carry

    lax.fori_loop(0, dense_ref.shape[0], clear, 0)
    for copy in small[:3]:
        copy.wait()

    def place(slot):
        row, col = rows_ref[0, 0, slot], cols_ref[0, 0, slot]
        row_shift = shift_of(me_col, row // piece_blocks, n_col)
        col_shift = shift_of(me_row, col // piece_blocks, n_row)
        col_place = col_shift % 2 * (n_row // 2) + col_shift // 2
        block = row_shift * piece_blocks + row % piece_blocks
        start = (col_place * piece_blocks + col % piece_blocks) * tile_len
        values = jnp.where(slot < count_ref[0, 0], tiles[slot], 0.0)
        values = jnp.where(values > HALF_MODULUS, values - MODULUS, values).T
        both = jnp.concatenate(balanced_digits(values), 1).astype(jnp.bfloat16)
        dense_ref[block, pl.ds(pl.multiple_of(start, tile_len), tile_len), :] = both

    def step(index, carry):
        chunk(index).wait()
        for offset in range(group):
            place(index * group + offset)
        return carry

    lax.fori_loop(0, chunk_count, step, 0)
    for copy in small[3:]:
        copy.wait()
    token_ref[...] = jnp.zeros_like(token_ref)


def build_dense(tiles, block_x, block_y, sizes):
    tile_rows, tile_cols, tile_count, tile_entries = tiles
    n_row, n_col, piece_blocks = sizes
    _, _, slot_count, tile_len, _ = tile_entries.shape
    group = next(size for size in (8, 4, 2, 1) if slot_count % size == 0)
    shape = (n_col * piece_blocks, n_row * piece_blocks * tile_len, 2 * tile_len)
    hbm = pl.BlockSpec(memory_space=pltpu.HBM)
    rows, cols, entries, x_piece, y_piece = (
        pltpu.with_memory_space_constraint(part, pltpu.HBM)
        for part in (tile_rows, tile_cols, tile_entries, block_x, block_y)
    )
    return pl.pallas_call(
        functools.partial(build_kernel, (*sizes, group)),
        in_specs=[hbm, hbm, pl.BlockSpec(memory_space=pl.ANY), hbm, hbm, hbm],
        out_specs=[pl.BlockSpec(memory_space=pltpu.VMEM)] * 4,
        out_shape=[
            pltpu.VMEM(shape, jnp.bfloat16),
            held(*block_x.shape),
            held(*block_y.shape),
            held(8, 128),
        ],
        scratch_shapes=[
            *(pltpu.SMEM(part.shape, part.dtype) for part in (tile_rows, tile_cols, tile_count)),
            pltpu.VMEM((slot_count, tile_len, tile_len), jnp.float32),
            pltpu.SemaphoreType.DMA((slot_count // group + 5,)),
        ],
        compiler_params=pltpu.CompilerParams(vmem_limit_bytes=VMEM_LIMIT),
        cost_estimate=pl.CostEstimate(
            flops=8 * tile_entries.size, bytes_accessed=8 * tile_entries.size, transcendentals=0
        ),
    )(rows, cols, tile_count, entries, x_piece, y_piece)


def half_products(half, span, pieces_ref, dense_ref, digits, block):
    _, depth, width = dense_ref.shape
    tile_len, half_depth = width // 2, depth // 2
    high = middle = low = 0.0
    for start in range(0, half_depth, EXACT_DEPTH):
        stop = min(start + EXACT_DEPTH, half_depth)
        products = jnp.dot(
            digits[:, start:stop],
            dense_ref[block, half * half_depth + start : half * half_depth + stop, :],
            preferred_element_type=jnp.float32,
        )
        products = reduce_centered(products)
        high = high + products[:span, :tile_len]
        middle = middle + products[:span, tile_len:] + products[span:, :tile_len]
        low = low + products[span:, tile_len:]
    return high, middle, low


def fill_digits(span, pieces_ref, digits):
    piece_len = pieces_ref.shape[2]
    for d in range(pieces_ref.shape[0]):
        vector = reduce_centered(pieces_ref[d, :span, :])
        digits[:, d * piece_len : (d + 1) * piece_len] = stacked_digits(vector)


def first_half_kernel(span, pieces_ref, dense_ref, sums_ref, digits):
    fill_digits(span, pieces_ref, digits)
    tile_len = dense_ref.shape[2] // 2
    for block in range(dense_ref.shape[0]):
        parts = half_products(0, span, pieces_ref, dense_ref, digits, block)
        for index, part in enumerate(parts):
            sums_ref[index, :, block * tile_len : (block + 1) * tile_len] = part


def half_of_core(packed):
    rows = packed.shape[0] // 2
    return jnp.where(lax.axis_index("row") % 2 == 0, packed[:rows], packed[rows:])


def second_half_kernel(span, shifts, pieces_ref, evens_ref, sums_ref, dense_ref, *refs):
    outs, digits = dict(zip(shifts, refs[:-1])), refs[-1]
    fill_digits(span, pieces_ref, digits)
    tile_len = dense_ref.shape[2] // 2
    piece_blocks = pieces_ref.shape[2] // tile_len
    for e in shifts:
        for sub in range(piece_blocks):
            block = e * piece_blocks + sub
            parts = half_products(1, span, pieces_ref, dense_ref, digits, block)
            parts = (
                part + sums_ref[index, :, block * tile_len : (block + 1) * tile_len]
                for index, part in enumerate(parts)
            )
            outs[e][:span, sub * tile_len : (sub + 1) * tile_len] = combine(*parts)
    if pieces_ref.shape[1] > span:
        packed = jnp.sum(pieces_ref[:, span:, :], 0) + jnp.sum(evens_ref[:, span:, :], 0)
        packed = half_of_core(packed)
        for out in outs.values():
            out[span:, :] = packed


def dense_first(evens, span, dense):
    row_blocks, depth, width = dense.shape
    return call(
        functools.partial(first_half_kernel, span),
        [evens, dense],
        [held(3, span, row_blocks * width // 2)],
        scratch=[pltpu.VMEM((2 * span, depth // 2), jnp.bfloat16)],
        limit=VMEM_LIMIT,
        flops=2 * span * dense.size,
    )[0]


def dense_second(odds, evens, sums, span, n_col, dense, before):
    _, depth, _ = dense.shape
    _, rows, piece_len = odds.shape
    outs = {}
    for shifts in (range(n_col // 2, n_col), range(n_col // 2)):
        shifts = [*reversed(shifts)]
        parts = call(
            functools.partial(second_half_kernel, span, shifts),
            [odds, evens, sums, dense],
            [held(span + (rows - span) // 2, piece_len)] * len(shifts),
            before,
            scratch=[pltpu.VMEM((2 * span, depth // 2), jnp.bfloat16)],
            limit=VMEM_LIMIT,
            flops=span * dense.size,
        )
        outs.update(zip(shifts, parts))
    return [outs[e] for e in range(n_col)]


def left_kernel(n_row, x_evens, x_odds, dense_ref, evens_ref, odds_ref):
    row_blocks, _, width = dense_ref.shape
    tile_len = width // 2
    _, span, piece_len = x_evens.shape
    piece_blocks = piece_len // tile_len
    x_digits = [
        centred_digits((x_odds if e % 2 else x_evens)[e // 2])
        for e in range(row_blocks // piece_blocks)
    ]
    for place in range(n_row):
        by_high = by_low = high_part = low_part = 0.0
        for block in range(row_blocks):
            sub = block % piece_blocks
            left = x_digits[block // piece_blocks][:, sub * tile_len : (sub + 1) * tile_len]
            right = dense_ref[block, place * piece_len : (place + 1) * piece_len, :]
            high_part = high_part + dot_pairs(left, right[:, :tile_len])
            low_part = low_part + dot_pairs(left, right[:, tile_len:])
            if (block + 1) * tile_len % EXACT_DEPTH == 0 or block == row_blocks - 1:
                by_high = by_high + reduce_centered(high_part)
                by_low = by_low + reduce_centered(low_part)
                high_part = low_part = 0.0
        piece = combine(by_high[:span], by_low[:span] + by_high[span:], by_low[span:])
        if place < n_row // 2:
            evens_ref[place] = piece
        else:
            odds_ref[place - n_row // 2] = piece


def dense_left(x_pairs, n_row, dense, before):
    _, span, piece_len = x_pairs[0].shape
    return call(
        functools.partial(left_kernel, n_row),
        [*x_pairs, dense],
        [held(n_row // 2, span, piece_len)] * 2,
        before,
        limit=VMEM_LIMIT,
        flops=4 * span * dense.size,
    )


def sparse_tiles(tiles, sizes):
    tile_rows, tile_cols, tile_count, tile_entries = tiles
    n_row, n_col, piece_blocks = sizes
    entries, rows, cols = tile_entries[0, 0], tile_rows[0, 0], tile_cols[0, 0]
    row_shift = shift_of(lax.axis_index("col"), rows // piece_blocks, n_col)
    col_shift = shift_of(lax.axis_index("row"), cols // piece_blocks, n_row)
    col_place = col_shift % 2 * (n_row // 2) + col_shift // 2
    positions = (
        row_shift * piece_blocks + rows % piece_blocks,
        col_place * piece_blocks + cols % piece_blocks,
        tile_count[0, 0],
    )
    entries = jnp.where(entries > HALF_MODULUS, entries - MODULUS, entries)
    return positions, jnp.stack(balanced_digits(entries), 1).astype(jnp.bfloat16)


def sparse_product(vector, spec, places, targets, count, blocks, a_digits):
    span, tile_len = vector.shape[0], a_digits.shape[-1]
    v_digits = stacked_digits(vector).reshape(2 * span, -1, tile_len)
    picked = jnp.take(v_digits, places, axis=1)
    products = jnp.einsum(spec, picked, a_digits, preferred_element_type=jnp.float32)
    products = reduce_centered(products)
    residues = combine(
        products[:, 0, :span],
        products[:, 0, span:] + products[:, 1, :span],
        products[:, 1, span:],
    )
    live = jnp.arange(targets.shape[0], dtype=jnp.int32) < count
    onehot = targets[None, :] == jnp.arange(blocks, dtype=jnp.int32)[:, None]
    onehot = (onehot & live[None, :]).astype(jnp.float32)
    summed = jnp.einsum("bt,twi->wbi", onehot, residues, precision=lax.Precision.HIGHEST)
    return reduce_centered(summed).reshape(span, blocks * tile_len)


def sparse_second(odds, evens, span, n_col, positions, a_digits):
    rows, cols, count = positions
    pieces = [*evens, *odds]
    piece_len = pieces[0].shape[1]
    blocks = n_col * piece_len // a_digits.shape[-1]
    vector = reduce_centered(jnp.concatenate([piece[:span] for piece in pieces], 1))
    product = sparse_product(vector, "ntk,tdik->tdni", cols, rows, count, blocks, a_digits)
    packed = half_of_core(functools.reduce(jnp.add, [piece[span:] for piece in pieces]))
    outs = [product[:, e * piece_len : (e + 1) * piece_len] for e in range(n_col)]
    return [jnp.concatenate([out, packed], 0) for out in outs]


def sparse_left(x_pairs, n_row, positions, a_digits):
    rows, cols, count = positions
    n_col = 2 * x_pairs[0].shape[0]
    x_pieces = [x_pairs[e % 2][e // 2] for e in range(n_col)]
    piece_len = x_pieces[0].shape[1]
    values = jnp.concatenate(x_pieces, 1)
    values = jnp.where(values > HALF_MODULUS, values - MODULUS, values)
    blocks = n_row * piece_len // a_digits.shape[-1]
    product = sparse_product(values, "nti,tdik->tdnk", rows, cols, count, blocks, a_digits)
    pieces = [product[:, d * piece_len : (d + 1) * piece_len] for d in range(n_row)]
    return jnp.stack(pieces[: n_row // 2]), jnp.stack(pieces[n_row // 2 :])


def add_and_part(kept, came, before=()):
    def kernel(kept_ref, came_ref, evens_ref, odds_ref):
        for index in range(kept.shape[0]):
            (odds_ref if index % 2 else evens_ref)[index // 2] = kept_ref[index] + came_ref[index]

    return call(kernel, [kept, came], [held(kept.shape[0] // 2, *kept.shape[1:])] * 2, before)


def append_projections(w_parts, pieces, earlier):
    span, piece_len = pieces[0].shape
    rows = span * span // piece_len

    def kernel(*refs):
        piece_refs, refs = refs[: len(pieces)], refs[len(pieces) :]
        earlier_refs, refs = refs[: len(earlier)], refs[len(earlier) :]
        w_refs, out_ref = refs[:-1], refs[-1]
        summed = functools.reduce(jnp.add, [ref[...] for ref in piece_refs])
        out_ref[:span, :] = summed
        w_piece = functools.reduce(jnp.add, [ref[...] for ref in w_refs])
        w_digits = stacked_digits(reduce_centered(w_piece))
        for index, vector in enumerate([summed] + [ref[...] for ref in earlier_refs]):
            products = dot_pairs(w_digits, stacked_digits(reduce_centered(vector)))
            square = combine(
                reduce_centered(products[:span, :span]),
                reduce_centered(products[:span, span:]) + reduce_centered(products[span:, :span]),
                reduce_centered(products[span:, span:]),
            )
            start = span + index * rows
            out_ref[start : start + rows, :] = pack_square(square, piece_len)

    outs = [held(span + (len(earlier) + 1) * rows, piece_len)]
    return call(kernel, [*pieces, *earlier, *w_parts], outs)[0]


def multiply_mod(left, right):
    span = left.shape[0]
    left = stacked_digits(left)
    high, low = (part.astype(jnp.bfloat16) for part in balanced_digits(right))
    by_high = jnp.dot(left, high, preferred_element_type=jnp.float32)
    by_low = jnp.dot(left, low, preferred_element_type=jnp.float32)
    return combine(
        reduce_centered(by_high[:span]), by_low[:span] + by_high[span:], by_low[span:]
    )


def sigma_update(mine, other, span):
    rows = span * span // mine.shape[1]

    def kernel(mine_ref, other_ref, out_ref):
        first = lax.axis_index("row") % 2 == 0
        mine, other = reduce_centered(mine_ref[...]), reduce_centered(other_ref[...])
        packed = jnp.concatenate([jnp.where(first, mine, other), jnp.where(first, other, mine)], 0)
        c_3, c_1, c_2 = (
            unpack_square(packed[index * rows : (index + 1) * rows], span) for index in range(3)
        )
        e_2 = reduce_centered(c_1 - multiply_mod(c_1, c_2))
        both = reduce_centered(c_1 + e_2)
        start = multiply_mod(e_2, c_1)
        rest = c_1 - multiply_mod(both, c_2)
        e_3 = reduce_centered(multiply_mod(start, c_3) + rest)
        out_ref[0] = canonical(-multiply_mod(e_3, start)) * (1.0 / MODULUS)
        out_ref[1] = canonical(start + multiply_mod(e_3, both)) * (1.0 / MODULUS)
        out_ref[2] = canonical(-both - e_3) * (1.0 / MODULUS)

    outs = [jax.ShapeDtypeStruct((STEP_COUNT, span, span), jnp.float32)]
    return call(kernel, [mine, other], outs)[0]


def local(tile_entries, tile_rows, tile_cols, tile_count, block_x, block_y):
    _, _, slot_count, tile_len, _ = tile_entries.shape
    span, piece_len = block_y.shape
    piece_blocks = piece_len // tile_len
    n_row, n_col = lax.axis_size("row"), lax.axis_size("col")
    packed_rows = span * span // piece_len
    tiles = (tile_rows, tile_cols, tile_count, tile_entries)
    sizes = (n_row, n_col, piece_blocks)
    is_dense = n_col * piece_blocks * n_row * piece_blocks <= DENSE_CELLS * slot_count
    if is_dense:
        dense, x_own, y_own, token = build_dense(tiles, block_x, block_y, sizes)
        before = [token]
    else:
        positions, a_digits = sparse_tiles(tiles, sizes)
        x_own, y_own, before = block_x, block_y, []

    def multiply_evens(evens):
        return dense_first(evens, span, dense) if is_dense else evens

    def multiply_odds(odds, evens, sums, before):
        if is_dense:
            return dense_second(odds, evens, sums, span, n_col, dense, before)
        return sparse_second(odds, evens, span, n_col, positions, a_digits)

    def multiply(evens, before):
        return multiply_odds(gather_odds(evens, "row"), evens, multiply_evens(evens), before)

    y_came = fetch_evens(block_y, "row")
    x_came = fetch_evens(block_x, "col")
    evens = stack_after([y_own] + y_came, [*before, *x_came])
    x_evens = stack_after([x_own] + x_came)
    outs = multiply(evens, [x_evens])
    x_pairs = [x_evens, gather_odds(x_evens, "col")]
    if is_dense:
        w_evens, w_odds = dense_left(x_pairs, n_row, dense, [outs[0]])
    else:
        w_evens, w_odds = sparse_left(x_pairs, n_row, positions, a_digits)
    vector_1 = sum_after(scatter_pieces(outs, "col"), [w_odds])
    w_came = fetch(w_odds, "row", 1)
    outs = multiply(gather_evens(vector_1, "row"), [w_came])
    pieces = scatter_pieces(outs, "col")
    w_kept, shift, before = w_evens, 2, []
    while shift < n_row:
        w_kept, w_sent = add_and_part(w_kept, w_came, before)
        w_came = fetch(w_sent, "row", shift)
        shift, before = 2 * shift, [outs[0]]
    vector_2 = append_projections([w_kept[0], w_came[0]], pieces, [y_own, vector_1])
    outs = multiply(gather_evens(vector_2, "row"), [])
    pieces = scatter_pieces(outs, "col")
    terms = functools.reduce(jnp.add, [piece[span:] for piece in pieces])
    vector_3 = functools.reduce(jnp.add, [piece[:span] for piece in pieces])
    return sigma_update(terms, fetch(terms, "row", 1), span), canonical(vector_3) * (1.0 / MODULUS)


def solution(mesh):
    placed = (
        P("row", "col", None, None, None),
        P("row", "col", None),
        P("row", "col", None),
        P("row", "col"),
        P(None, ("row", "col")),
        P(None, ("row", "col")),
    )
    return jax.shard_map(
        local, mesh=mesh, in_specs=placed, out_specs=(P(), P(None, ("row", "col"))), check_vma=False
    )
```

```python
import functools

import jax
import jax.numpy as jnp
from jax import lax
from jax.experimental import pallas as pl
from jax.experimental.pallas import tpu as pltpu
from jax.sharding import PartitionSpec as P

STEP_COUNT = 3

MODULUS = 65521.0
HALF_MODULUS = 32760.0
BASE = 256.0
EXACT_DEPTH = 1024
DENSE_CELLS = 4
VMEM_LIMIT = 16 * 1024 * 1024
SMALL_LIMIT = 4 * 1024 * 1024


def reduce_centered(values):
    return values - MODULUS * jnp.floor(values * (1.0 / MODULUS) + 0.5)


def canonical(values):
    reduced = reduce_centered(values)
    return jnp.where(reduced < 0, reduced + MODULUS, reduced)


def balanced_digits(values):
    high = jnp.floor(values * (1.0 / BASE) + 0.5)
    return high, values - BASE * high


def stacked_digits(values):
    high, low = balanced_digits(values)
    return jnp.concatenate([high, low], 0).astype(jnp.bfloat16)


def centred_digits(residues):
    return stacked_digits(jnp.where(residues > HALF_MODULUS, residues - MODULUS, residues))


def partner(index, shift, size):
    return index ^ shift if size & (size - 1) == 0 else (index + shift) % size


def shift_of(index, other, size):
    return index ^ other if size & (size - 1) == 0 else (other - index) % size


def fetch(piece, axis, shift):
    size = lax.axis_size(axis)
    return lax.ppermute(piece, axis, [(partner(i, shift, size), i) for i in range(size)])


def scatter_pieces(pieces, axis):
    size = lax.axis_size(axis)
    order = sorted(range(1, size), key=lambda shift: (shift < size // 2, shift))
    came = [
        lax.ppermute(pieces[shift], axis, [(i, partner(i, shift, size)) for i in range(size)])
        for shift in order
    ]
    return [pieces[0]] + came


def call(kernel, operands, outs, before=(), scratch=(), limit=SMALL_LIMIT, flops=0):
    def body(*refs):
        kernel(*refs[: len(operands)], *refs[len(operands) + len(before) :])

    vmem = pl.BlockSpec(memory_space=pltpu.VMEM)
    return pl.pallas_call(
        body,
        in_specs=[vmem] * len(operands) + [pl.BlockSpec(memory_space=pl.ANY)] * len(before),
        out_specs=[vmem] * len(outs),
        out_shape=outs,
        scratch_shapes=list(scratch),
        compiler_params=pltpu.CompilerParams(vmem_limit_bytes=limit),
        cost_estimate=pl.CostEstimate(flops=flops, bytes_accessed=0, transcendentals=0),
    )(*(pltpu.with_memory_space_constraint(part, pltpu.VMEM) for part in operands), *before)


def held(*shape):
    return pltpu.VMEM(shape, jnp.float32)


def stack_after(pieces, before=()):
    def kernel(*refs):
        for index, ref in enumerate(refs[:-1]):
            refs[-1][index] = ref[...]

    return call(kernel, pieces, [held(len(pieces), *pieces[0].shape)], before)[0]


def sum_after(pieces, before=()):
    def kernel(*refs):
        refs[-1][...] = functools.reduce(jnp.add, [ref[...] for ref in refs[:-1]])

    return call(kernel, pieces, [held(*pieces[0].shape)], before)[0]


def fetch_evens(piece, axis):
    return [fetch(piece, axis, shift) for shift in range(2, lax.axis_size(axis), 2)]


def gather_evens(piece, axis, before=()):
    return stack_after([piece] + fetch_evens(piece, axis), before)


def gather_odds(evens, axis):
    size = lax.axis_size(axis)
    assert size > 1 and size & (size - 1) == 0
    return fetch(evens, axis, 1)


def dot_pairs(left, right):
    return lax.dot_general(left, right, (((1,), (1,)), ((), ())), preferred_element_type=jnp.float32)


def combine(high, middle, low):
    return reduce_centered(15.0 * high + 256.0 * reduce_centered(middle) + low)


def pack_square(square, width):
    span = square.shape[0]
    rows = span * span // width
    return jnp.concatenate([square[j * rows : (j + 1) * rows] for j in range(width // span)], 1)


def unpack_square(packed, span):
    count = packed.shape[1] // span
    return jnp.concatenate([packed[:, j * span : (j + 1) * span] for j in range(count)], 0)


def build_kernel(sizes, *refs):
    entries_ref, x_ref, y_ref, dense_ref, x_out, y_out, token_ref = refs[3:10]
    rows_ref, cols_ref, count_ref, tiles, sems = refs[10:]
    n_row, n_col, piece_blocks, group = sizes
    _, _, slot_count, tile_len, _ = entries_ref.shape
    me_row, me_col = lax.axis_index("row"), lax.axis_index("col")
    chunk_count = slot_count // group

    def chunk(index):
        source = entries_ref.at[0, 0, pl.ds(index * group, group)]
        return pltpu.make_async_copy(source, tiles.at[pl.ds(index * group, group)], sems.at[index])

    small = [*zip(refs[:3], refs[10:13]), (y_ref, y_out), (x_ref, x_out)]
    small = [
        pltpu.make_async_copy(source, target, sems.at[chunk_count + index])
        for index, (source, target) in enumerate(small)
    ]
    for copy in small[:3]:
        copy.start()
    for index in range(chunk_count):
        chunk(index).start()
    for copy in small[3:]:
        copy.start()

    def clear(block, carry):
        dense_ref[block] = jnp.zeros(dense_ref.shape[1:], dense_ref.dtype)
        return carry

    lax.fori_loop(0, dense_ref.shape[0], clear, 0)
    for copy in small[:3]:
        copy.wait()

    def place(slot):
        row, col = rows_ref[0, 0, slot], cols_ref[0, 0, slot]
        row_shift = shift_of(me_col, row // piece_blocks, n_col)
        col_shift = shift_of(me_row, col // piece_blocks, n_row)
        col_place = col_shift % 2 * (n_row // 2) + col_shift // 2
        block = row_shift * piece_blocks + row % piece_blocks
        start = (col_place * piece_blocks + col % piece_blocks) * tile_len
        values = jnp.where(slot < count_ref[0, 0], tiles[slot], 0.0)
        values = jnp.where(values > HALF_MODULUS, values - MODULUS, values).T
        both = jnp.concatenate(balanced_digits(values), 1).astype(jnp.bfloat16)
        dense_ref[block, pl.ds(pl.multiple_of(start, tile_len), tile_len), :] = both

    def step(index, carry):
        chunk(index).wait()
        for offset in range(group):
            place(index * group + offset)
        return carry

    lax.fori_loop(0, chunk_count, step, 0)
    for copy in small[3:]:
        copy.wait()
    token_ref[...] = jnp.zeros_like(token_ref)


def build_dense(tiles, block_x, block_y, sizes):
    tile_rows, tile_cols, tile_count, tile_entries = tiles
    n_row, n_col, piece_blocks = sizes
    _, _, slot_count, tile_len, _ = tile_entries.shape
    group = next(size for size in (8, 4, 2, 1) if slot_count % size == 0)
    shape = (n_col * piece_blocks, n_row * piece_blocks * tile_len, 2 * tile_len)
    hbm = pl.BlockSpec(memory_space=pltpu.HBM)
    rows, cols, entries, x_piece, y_piece = (
        pltpu.with_memory_space_constraint(part, pltpu.HBM)
        for part in (tile_rows, tile_cols, tile_entries, block_x, block_y)
    )
    return pl.pallas_call(
        functools.partial(build_kernel, (*sizes, group)),
        in_specs=[hbm, hbm, pl.BlockSpec(memory_space=pl.ANY), hbm, hbm, hbm],
        out_specs=[pl.BlockSpec(memory_space=pltpu.VMEM)] * 4,
        out_shape=[
            pltpu.VMEM(shape, jnp.bfloat16),
            held(*block_x.shape),
            held(*block_y.shape),
            held(8, 128),
        ],
        scratch_shapes=[
            *(pltpu.SMEM(part.shape, part.dtype) for part in (tile_rows, tile_cols, tile_count)),
            pltpu.VMEM((slot_count, tile_len, tile_len), jnp.float32),
            pltpu.SemaphoreType.DMA((slot_count // group + 5,)),
        ],
        compiler_params=pltpu.CompilerParams(vmem_limit_bytes=VMEM_LIMIT),
        cost_estimate=pl.CostEstimate(
            flops=8 * tile_entries.size, bytes_accessed=8 * tile_entries.size, transcendentals=0
        ),
    )(rows, cols, tile_count, entries, x_piece, y_piece)


def half_products(half, span, pieces_ref, dense_ref, digits, block):
    _, depth, width = dense_ref.shape
    tile_len, half_depth = width // 2, depth // 2
    high = middle = low = 0.0
    for start in range(0, half_depth, EXACT_DEPTH):
        stop = min(start + EXACT_DEPTH, half_depth)
        products = jnp.dot(
            digits[:, start:stop],
            dense_ref[block, half * half_depth + start : half * half_depth + stop, :],
            preferred_element_type=jnp.float32,
        )
        products = reduce_centered(products)
        high = high + products[:span, :tile_len]
        middle = middle + products[:span, tile_len:] + products[span:, :tile_len]
        low = low + products[span:, tile_len:]
    return high, middle, low


def fill_digits(span, pieces_ref, digits):
    piece_len = pieces_ref.shape[2]
    for d in range(pieces_ref.shape[0]):
        vector = reduce_centered(pieces_ref[d, :span, :])
        digits[:, d * piece_len : (d + 1) * piece_len] = stacked_digits(vector)


def first_half_kernel(span, pieces_ref, dense_ref, sums_ref, digits):
    fill_digits(span, pieces_ref, digits)
    tile_len = dense_ref.shape[2] // 2
    for block in range(dense_ref.shape[0]):
        parts = half_products(0, span, pieces_ref, dense_ref, digits, block)
        for index, part in enumerate(parts):
            sums_ref[index, :, block * tile_len : (block + 1) * tile_len] = part


def half_of_core(packed):
    rows = packed.shape[0] // 2
    return jnp.where(lax.axis_index("row") % 2 == 0, packed[:rows], packed[rows:])


def second_half_kernel(span, pieces_ref, evens_ref, sums_ref, dense_ref, *refs):
    outs, digits = refs[:-1], refs[-1]
    n_col = len(outs)
    fill_digits(span, pieces_ref, digits)
    row_blocks, _, width = dense_ref.shape
    tile_len = width // 2
    piece_blocks = row_blocks // n_col
    for e in reversed(range(n_col)):
        for sub in range(piece_blocks):
            block = e * piece_blocks + sub
            parts = half_products(1, span, pieces_ref, dense_ref, digits, block)
            parts = (
                part + sums_ref[index, :, block * tile_len : (block + 1) * tile_len]
                for index, part in enumerate(parts)
            )
            outs[e][:span, sub * tile_len : (sub + 1) * tile_len] = combine(*parts)
    if outs[0].shape[0] > span:
        packed = jnp.sum(pieces_ref[:, span:, :], 0) + jnp.sum(evens_ref[:, span:, :], 0)
        packed = half_of_core(packed)
        for out in outs:
            out[span:, :] = packed


def dense_first(evens, span, dense):
    row_blocks, depth, width = dense.shape
    return call(
        functools.partial(first_half_kernel, span),
        [evens, dense],
        [held(3, span, row_blocks * width // 2)],
        scratch=[pltpu.VMEM((2 * span, depth // 2), jnp.bfloat16)],
        limit=VMEM_LIMIT,
        flops=2 * span * dense.size,
    )[0]


def dense_second(odds, evens, sums, span, n_col, dense, before):
    _, depth, _ = dense.shape
    _, rows, piece_len = odds.shape
    return list(
        call(
            functools.partial(second_half_kernel, span),
            [odds, evens, sums, dense],
            [held(span + (rows - span) // 2, piece_len)] * n_col,
            before,
            scratch=[pltpu.VMEM((2 * span, depth // 2), jnp.bfloat16)],
            limit=VMEM_LIMIT,
            flops=2 * span * dense.size,
        )
    )


def left_kernel(n_row, x_evens, x_odds, dense_ref, evens_ref, odds_ref):
    row_blocks, _, width = dense_ref.shape
    tile_len = width // 2
    _, span, piece_len = x_evens.shape
    piece_blocks = piece_len // tile_len
    x_digits = [
        centred_digits((x_odds if e % 2 else x_evens)[e // 2])
        for e in range(row_blocks // piece_blocks)
    ]
    for place in range(n_row):
        by_high = by_low = high_part = low_part = 0.0
        for block in range(row_blocks):
            sub = block % piece_blocks
            left = x_digits[block // piece_blocks][:, sub * tile_len : (sub + 1) * tile_len]
            right = dense_ref[block, place * piece_len : (place + 1) * piece_len, :]
            high_part = high_part + dot_pairs(left, right[:, :tile_len])
            low_part = low_part + dot_pairs(left, right[:, tile_len:])
            if (block + 1) * tile_len % EXACT_DEPTH == 0 or block == row_blocks - 1:
                by_high = by_high + reduce_centered(high_part)
                by_low = by_low + reduce_centered(low_part)
                high_part = low_part = 0.0
        piece = combine(by_high[:span], by_low[:span] + by_high[span:], by_low[span:])
        if place < n_row // 2:
            evens_ref[place] = piece
        else:
            odds_ref[place - n_row // 2] = piece


def dense_left(x_pairs, n_row, dense, before):
    _, span, piece_len = x_pairs[0].shape
    return call(
        functools.partial(left_kernel, n_row),
        [*x_pairs, dense],
        [held(n_row // 2, span, piece_len)] * 2,
        before,
        limit=VMEM_LIMIT,
        flops=4 * span * dense.size,
    )


def sparse_tiles(tiles, sizes):
    tile_rows, tile_cols, tile_count, tile_entries = tiles
    n_row, n_col, piece_blocks = sizes
    entries, rows, cols = tile_entries[0, 0], tile_rows[0, 0], tile_cols[0, 0]
    row_shift = shift_of(lax.axis_index("col"), rows // piece_blocks, n_col)
    col_shift = shift_of(lax.axis_index("row"), cols // piece_blocks, n_row)
    col_place = col_shift % 2 * (n_row // 2) + col_shift // 2
    positions = (
        row_shift * piece_blocks + rows % piece_blocks,
        col_place * piece_blocks + cols % piece_blocks,
        tile_count[0, 0],
    )
    entries = jnp.where(entries > HALF_MODULUS, entries - MODULUS, entries)
    return positions, jnp.stack(balanced_digits(entries), 1).astype(jnp.bfloat16)


def sparse_product(vector, spec, places, targets, count, blocks, a_digits):
    span, tile_len = vector.shape[0], a_digits.shape[-1]
    v_digits = stacked_digits(vector).reshape(2 * span, -1, tile_len)
    picked = jnp.take(v_digits, places, axis=1)
    products = jnp.einsum(spec, picked, a_digits, preferred_element_type=jnp.float32)
    products = reduce_centered(products)
    residues = combine(
        products[:, 0, :span],
        products[:, 0, span:] + products[:, 1, :span],
        products[:, 1, span:],
    )
    live = jnp.arange(targets.shape[0], dtype=jnp.int32) < count
    onehot = targets[None, :] == jnp.arange(blocks, dtype=jnp.int32)[:, None]
    onehot = (onehot & live[None, :]).astype(jnp.float32)
    summed = jnp.einsum("bt,twi->wbi", onehot, residues, precision=lax.Precision.HIGHEST)
    return reduce_centered(summed).reshape(span, blocks * tile_len)


def sparse_second(odds, evens, span, n_col, positions, a_digits):
    rows, cols, count = positions
    pieces = [*evens, *odds]
    piece_len = pieces[0].shape[1]
    blocks = n_col * piece_len // a_digits.shape[-1]
    vector = reduce_centered(jnp.concatenate([piece[:span] for piece in pieces], 1))
    product = sparse_product(vector, "ntk,tdik->tdni", cols, rows, count, blocks, a_digits)
    packed = half_of_core(functools.reduce(jnp.add, [piece[span:] for piece in pieces]))
    outs = [product[:, e * piece_len : (e + 1) * piece_len] for e in range(n_col)]
    return [jnp.concatenate([out, packed], 0) for out in outs]


def sparse_left(x_pairs, n_row, positions, a_digits):
    rows, cols, count = positions
    n_col = 2 * x_pairs[0].shape[0]
    x_pieces = [x_pairs[e % 2][e // 2] for e in range(n_col)]
    piece_len = x_pieces[0].shape[1]
    values = jnp.concatenate(x_pieces, 1)
    values = jnp.where(values > HALF_MODULUS, values - MODULUS, values)
    blocks = n_row * piece_len // a_digits.shape[-1]
    product = sparse_product(values, "nti,tdik->tdnk", rows, cols, count, blocks, a_digits)
    pieces = [product[:, d * piece_len : (d + 1) * piece_len] for d in range(n_row)]
    return jnp.stack(pieces[: n_row // 2]), jnp.stack(pieces[n_row // 2 :])


def add_and_part(kept, came, before=()):
    def kernel(kept_ref, came_ref, evens_ref, odds_ref):
        for index in range(kept.shape[0]):
            (odds_ref if index % 2 else evens_ref)[index // 2] = kept_ref[index] + came_ref[index]

    return call(kernel, [kept, came], [held(kept.shape[0] // 2, *kept.shape[1:])] * 2, before)


def append_projections(w_parts, pieces, earlier):
    span, piece_len = pieces[0].shape
    rows = span * span // piece_len

    def kernel(*refs):
        piece_refs, refs = refs[: len(pieces)], refs[len(pieces) :]
        earlier_refs, refs = refs[: len(earlier)], refs[len(earlier) :]
        w_refs, out_ref = refs[:-1], refs[-1]
        summed = functools.reduce(jnp.add, [ref[...] for ref in piece_refs])
        out_ref[:span, :] = summed
        w_piece = functools.reduce(jnp.add, [ref[...] for ref in w_refs])
        w_digits = stacked_digits(reduce_centered(w_piece))
        for index, vector in enumerate([summed] + [ref[...] for ref in earlier_refs]):
            products = dot_pairs(w_digits, stacked_digits(reduce_centered(vector)))
            square = combine(
                reduce_centered(products[:span, :span]),
                reduce_centered(products[:span, span:]) + reduce_centered(products[span:, :span]),
                reduce_centered(products[span:, span:]),
            )
            start = span + index * rows
            out_ref[start : start + rows, :] = pack_square(square, piece_len)

    outs = [held(span + (len(earlier) + 1) * rows, piece_len)]
    return call(kernel, [*pieces, *earlier, *w_parts], outs)[0]


def multiply_mod(left, right):
    span = left.shape[0]
    left = stacked_digits(left)
    high, low = (part.astype(jnp.bfloat16) for part in balanced_digits(right))
    by_high = jnp.dot(left, high, preferred_element_type=jnp.float32)
    by_low = jnp.dot(left, low, preferred_element_type=jnp.float32)
    return combine(
        reduce_centered(by_high[:span]), by_low[:span] + by_high[span:], by_low[span:]
    )


def sigma_update(mine, other, span):
    rows = span * span // mine.shape[1]

    def kernel(mine_ref, other_ref, out_ref):
        first = lax.axis_index("row") % 2 == 0
        mine, other = reduce_centered(mine_ref[...]), reduce_centered(other_ref[...])
        packed = jnp.concatenate([jnp.where(first, mine, other), jnp.where(first, other, mine)], 0)
        c_3, c_1, c_2 = (
            unpack_square(packed[index * rows : (index + 1) * rows], span) for index in range(3)
        )
        e_2 = reduce_centered(c_1 - multiply_mod(c_1, c_2))
        both = reduce_centered(c_1 + e_2)
        start = multiply_mod(e_2, c_1)
        rest = c_1 - multiply_mod(both, c_2)
        e_3 = reduce_centered(multiply_mod(start, c_3) + rest)
        out_ref[0] = canonical(-multiply_mod(e_3, start)) * (1.0 / MODULUS)
        out_ref[1] = canonical(start + multiply_mod(e_3, both)) * (1.0 / MODULUS)
        out_ref[2] = canonical(-both - e_3) * (1.0 / MODULUS)

    outs = [jax.ShapeDtypeStruct((STEP_COUNT, span, span), jnp.float32)]
    return call(kernel, [mine, other], outs)[0]


def local(tile_entries, tile_rows, tile_cols, tile_count, block_x, block_y):
    _, _, slot_count, tile_len, _ = tile_entries.shape
    span, piece_len = block_y.shape
    piece_blocks = piece_len // tile_len
    n_row, n_col = lax.axis_size("row"), lax.axis_size("col")
    packed_rows = span * span // piece_len
    tiles = (tile_rows, tile_cols, tile_count, tile_entries)
    sizes = (n_row, n_col, piece_blocks)
    is_dense = n_col * piece_blocks * n_row * piece_blocks <= DENSE_CELLS * slot_count
    if is_dense:
        dense, x_own, y_own, token = build_dense(tiles, block_x, block_y, sizes)
        before = [token]
    else:
        positions, a_digits = sparse_tiles(tiles, sizes)
        x_own, y_own, before = block_x, block_y, []

    def multiply_evens(evens):
        return dense_first(evens, span, dense) if is_dense else evens

    def multiply_odds(odds, evens, sums, before):
        if is_dense:
            return dense_second(odds, evens, sums, span, n_col, dense, before)
        return sparse_second(odds, evens, span, n_col, positions, a_digits)

    def multiply(evens, before):
        return multiply_odds(gather_odds(evens, "row"), evens, multiply_evens(evens), before)

    y_came = fetch_evens(block_y, "row")
    x_came = fetch_evens(block_x, "col")
    evens = stack_after([y_own] + y_came, [*before, *x_came])
    x_evens = stack_after([x_own] + x_came)
    outs = multiply(evens, [x_evens])
    x_pairs = [x_evens, gather_odds(x_evens, "col")]
    if is_dense:
        w_evens, w_odds = dense_left(x_pairs, n_row, dense, [outs[0]])
    else:
        w_evens, w_odds = sparse_left(x_pairs, n_row, positions, a_digits)
    vector_1 = sum_after(scatter_pieces(outs, "col"), [w_odds])
    w_came = fetch(w_odds, "row", 1)
    outs = multiply(gather_evens(vector_1, "row"), [w_came])
    pieces = scatter_pieces(outs, "col")
    w_kept, shift, before = w_evens, 2, []
    while shift < n_row:
        w_kept, w_sent = add_and_part(w_kept, w_came, before)
        w_came = fetch(w_sent, "row", shift)
        shift, before = 2 * shift, [outs[0]]
    vector_2 = append_projections([w_kept[0], w_came[0]], pieces, [y_own, vector_1])
    outs = multiply(gather_evens(vector_2, "row"), [])
    pieces = scatter_pieces(outs, "col")
    terms = functools.reduce(jnp.add, [piece[span:] for piece in pieces])
    vector_3 = functools.reduce(jnp.add, [piece[:span] for piece in pieces])
    return sigma_update(terms, fetch(terms, "row", 1), span), canonical(vector_3) * (1.0 / MODULUS)


def solution(mesh):
    placed = (
        P("row", "col", None, None, None),
        P("row", "col", None),
        P("row", "col", None),
        P("row", "col"),
        P(None, ("row", "col")),
        P(None, ("row", "col")),
    )
    return jax.shard_map(
        local, mesh=mesh, in_specs=placed, out_specs=(P(), P(None, ("row", "col"))), check_vma=False
    )
```

```python
import functools

import jax
import jax.numpy as jnp
from jax import lax
from jax.experimental import pallas as pl
from jax.experimental.pallas import tpu as pltpu
from jax.sharding import PartitionSpec as P

STEP_COUNT = 3

MODULUS = 65521.0
HALF_MODULUS = 32760.0
BASE = 256.0
EXACT_DEPTH = 1024
DENSE_CELLS = 4
VMEM_LIMIT = 16 * 1024 * 1024
SMALL_LIMIT = 4 * 1024 * 1024


def reduce_centered(values):
    return values - MODULUS * jnp.floor(values * (1.0 / MODULUS) + 0.5)


def canonical(values):
    reduced = reduce_centered(values)
    return jnp.where(reduced < 0, reduced + MODULUS, reduced)


def balanced_digits(values):
    high = jnp.floor(values * (1.0 / BASE) + 0.5)
    return high, values - BASE * high


def stacked_digits(values):
    high, low = balanced_digits(values)
    return jnp.concatenate([high, low], 0).astype(jnp.bfloat16)


def centred_digits(residues):
    return stacked_digits(jnp.where(residues > HALF_MODULUS, residues - MODULUS, residues))


def partner(index, shift, size):
    return index ^ shift if size & (size - 1) == 0 else (index + shift) % size


def shift_of(index, other, size):
    return index ^ other if size & (size - 1) == 0 else (other - index) % size


def fetch(piece, axis, shift):
    size = lax.axis_size(axis)
    return lax.ppermute(piece, axis, [(partner(i, shift, size), i) for i in range(size)])


def scatter_pieces(pieces, axis):
    size = lax.axis_size(axis)
    came = [
        lax.ppermute(pieces[shift], axis, [(i, partner(i, shift, size)) for i in range(size)])
        for shift in reversed(range(1, size))
    ]
    return [pieces[0]] + came


def call(kernel, operands, outs, before=(), scratch=(), limit=SMALL_LIMIT, flops=0):
    def body(*refs):
        kernel(*refs[: len(operands)], *refs[len(operands) + len(before) :])

    vmem = pl.BlockSpec(memory_space=pltpu.VMEM)
    return pl.pallas_call(
        body,
        in_specs=[vmem] * len(operands) + [pl.BlockSpec(memory_space=pl.ANY)] * len(before),
        out_specs=[vmem] * len(outs),
        out_shape=outs,
        scratch_shapes=list(scratch),
        compiler_params=pltpu.CompilerParams(vmem_limit_bytes=limit),
        cost_estimate=pl.CostEstimate(flops=flops, bytes_accessed=0, transcendentals=0),
    )(*(pltpu.with_memory_space_constraint(part, pltpu.VMEM) for part in operands), *before)


def held(*shape):
    return pltpu.VMEM(shape, jnp.float32)


def stack_after(pieces, before=()):
    def kernel(*refs):
        for index, ref in enumerate(refs[:-1]):
            refs[-1][index] = ref[...]

    return call(kernel, pieces, [held(len(pieces), *pieces[0].shape)], before)[0]


def sum_after(pieces, before=()):
    def kernel(*refs):
        refs[-1][...] = functools.reduce(jnp.add, [ref[...] for ref in refs[:-1]])

    return call(kernel, pieces, [held(*pieces[0].shape)], before)[0]


def fetch_evens(piece, axis):
    return [fetch(piece, axis, shift) for shift in range(2, lax.axis_size(axis), 2)]


def gather_evens(piece, axis, before=()):
    return stack_after([piece] + fetch_evens(piece, axis), before)


def gather_odds(evens, axis):
    size = lax.axis_size(axis)
    assert size > 1 and size & (size - 1) == 0
    return fetch(evens, axis, 1)


def dot_pairs(left, right):
    return lax.dot_general(left, right, (((1,), (1,)), ((), ())), preferred_element_type=jnp.float32)


def combine(high, middle, low):
    return reduce_centered(15.0 * high + 256.0 * reduce_centered(middle) + low)


def pack_square(square, width):
    span = square.shape[0]
    rows = span * span // width
    return jnp.concatenate([square[j * rows : (j + 1) * rows] for j in range(width // span)], 1)


def unpack_square(packed, span):
    count = packed.shape[1] // span
    return jnp.concatenate([packed[:, j * span : (j + 1) * span] for j in range(count)], 0)


def build_kernel(sizes, *refs):
    entries_ref, x_ref, y_ref, dense_ref, x_out, y_out, token_ref = refs[3:10]
    rows_ref, cols_ref, count_ref, tiles, sems = refs[10:]
    n_row, n_col, piece_blocks, group = sizes
    _, _, slot_count, tile_len, _ = entries_ref.shape
    me_row, me_col = lax.axis_index("row"), lax.axis_index("col")
    chunk_count = slot_count // group

    def chunk(index):
        source = entries_ref.at[0, 0, pl.ds(index * group, group)]
        return pltpu.make_async_copy(source, tiles.at[pl.ds(index * group, group)], sems.at[index])

    small = [*zip(refs[:3], refs[10:13]), (y_ref, y_out), (x_ref, x_out)]
    small = [
        pltpu.make_async_copy(source, target, sems.at[chunk_count + index])
        for index, (source, target) in enumerate(small)
    ]
    for copy in small[:3]:
        copy.start()
    for copy in small[:3]:
        copy.wait()
    used_count = (count_ref[0, 0] + group - 1) // group
    for index in range(chunk_count):

        @pl.when(index < used_count)
        def _():
            chunk(index).start(priority=index % 2)

    for copy in small[3:]:
        copy.start()

    def clear(block, carry):
        dense_ref[block] = jnp.zeros(dense_ref.shape[1:], dense_ref.dtype)
        return carry

    lax.fori_loop(0, dense_ref.shape[0], clear, 0)

    def place(slot):
        row, col = rows_ref[0, 0, slot], cols_ref[0, 0, slot]
        row_shift = shift_of(me_col, row // piece_blocks, n_col)
        col_shift = shift_of(me_row, col // piece_blocks, n_row)
        col_place = col_shift % 2 * (n_row // 2) + col_shift // 2
        block = row_shift * piece_blocks + row % piece_blocks
        start = (col_place * piece_blocks + col % piece_blocks) * tile_len
        values = jnp.where(slot < count_ref[0, 0], tiles[slot], 0.0)
        values = jnp.where(values > HALF_MODULUS, values - MODULUS, values).T
        both = jnp.concatenate(balanced_digits(values), 1).astype(jnp.bfloat16)
        dense_ref[block, pl.ds(pl.multiple_of(start, tile_len), tile_len), :] = both

    def step(index, carry):
        chunk(index).wait()
        for offset in range(group):
            place(index * group + offset)
        return carry

    lax.fori_loop(0, used_count, step, 0)
    for copy in small[3:]:
        copy.wait()
    token_ref[...] = jnp.zeros_like(token_ref)


def build_dense(tiles, block_x, block_y, sizes):
    tile_rows, tile_cols, tile_count, tile_entries = tiles
    n_row, n_col, piece_blocks = sizes
    _, _, slot_count, tile_len, _ = tile_entries.shape
    group = next(size for size in (4, 2, 1) if slot_count % size == 0)
    shape = (n_col * piece_blocks, n_row * piece_blocks * tile_len, 2 * tile_len)
    hbm = pl.BlockSpec(memory_space=pltpu.HBM)
    rows, cols, entries, x_piece, y_piece = (
        pltpu.with_memory_space_constraint(part, pltpu.HBM)
        for part in (tile_rows, tile_cols, tile_entries, block_x, block_y)
    )
    return pl.pallas_call(
        functools.partial(build_kernel, (*sizes, group)),
        in_specs=[hbm, hbm, pl.BlockSpec(memory_space=pl.ANY), hbm, hbm, hbm],
        out_specs=[pl.BlockSpec(memory_space=pltpu.VMEM)] * 4,
        out_shape=[
            pltpu.VMEM(shape, jnp.bfloat16),
            held(*block_x.shape),
            held(*block_y.shape),
            held(8, 128),
        ],
        scratch_shapes=[
            *(pltpu.SMEM(part.shape, part.dtype) for part in (tile_rows, tile_cols, tile_count)),
            pltpu.VMEM((slot_count, tile_len, tile_len), jnp.float32),
            pltpu.SemaphoreType.DMA((slot_count // group + 5,)),
        ],
        compiler_params=pltpu.CompilerParams(vmem_limit_bytes=VMEM_LIMIT),
        cost_estimate=pl.CostEstimate(
            flops=8 * tile_entries.size, bytes_accessed=8 * tile_entries.size, transcendentals=0
        ),
    )(rows, cols, tile_count, entries, x_piece, y_piece)


def half_products(half, span, pieces_ref, dense_ref, digits, block):
    _, depth, width = dense_ref.shape
    tile_len, half_depth = width // 2, depth // 2
    high = middle = low = 0.0
    for start in range(0, half_depth, EXACT_DEPTH):
        stop = min(start + EXACT_DEPTH, half_depth)
        products = jnp.dot(
            digits[:, start:stop],
            dense_ref[block, half * half_depth + start : half * half_depth + stop, :],
            preferred_element_type=jnp.float32,
        )
        products = reduce_centered(products)
        high = high + products[:span, :tile_len]
        middle = middle + products[:span, tile_len:] + products[span:, :tile_len]
        low = low + products[span:, tile_len:]
    return high, middle, low


def fill_digits(span, pieces_ref, digits):
    piece_len = pieces_ref.shape[2]
    for d in range(pieces_ref.shape[0]):
        vector = reduce_centered(pieces_ref[d, :span, :])
        digits[:, d * piece_len : (d + 1) * piece_len] = stacked_digits(vector)


def first_half_kernel(span, pieces_ref, dense_ref, sums_ref, digits):
    fill_digits(span, pieces_ref, digits)
    tile_len = dense_ref.shape[2] // 2
    for block in range(dense_ref.shape[0]):
        parts = half_products(0, span, pieces_ref, dense_ref, digits, block)
        for index, part in enumerate(parts):
            sums_ref[index, :, block * tile_len : (block + 1) * tile_len] = part


def half_of_core(packed):
    rows = packed.shape[0] // 2
    return jnp.where(lax.axis_index("row") % 2 == 0, packed[:rows], packed[rows:])


def second_half_kernel(span, pieces_ref, evens_ref, sums_ref, dense_ref, *refs):
    outs, digits = refs[:-1], refs[-1]
    n_col = len(outs)
    fill_digits(span, pieces_ref, digits)
    row_blocks, _, width = dense_ref.shape
    tile_len = width // 2
    piece_blocks = row_blocks // n_col
    for e in reversed(range(n_col)):
        for sub in range(piece_blocks):
            block = e * piece_blocks + sub
            parts = half_products(1, span, pieces_ref, dense_ref, digits, block)
            parts = (
                part + sums_ref[index, :, block * tile_len : (block + 1) * tile_len]
                for index, part in enumerate(parts)
            )
            outs[e][:span, sub * tile_len : (sub + 1) * tile_len] = combine(*parts)
    if outs[0].shape[0] > span:
        packed = jnp.sum(pieces_ref[:, span:, :], 0) + jnp.sum(evens_ref[:, span:, :], 0)
        packed = half_of_core(packed)
        for out in outs:
            out[span:, :] = packed


def dense_first(evens, span, dense):
    row_blocks, depth, width = dense.shape
    return call(
        functools.partial(first_half_kernel, span),
        [evens, dense],
        [held(3, span, row_blocks * width // 2)],
        scratch=[pltpu.VMEM((2 * span, depth // 2), jnp.bfloat16)],
        limit=VMEM_LIMIT,
        flops=2 * span * dense.size,
    )[0]


def dense_second(odds, evens, sums, span, n_col, dense, before):
    _, depth, _ = dense.shape
    _, rows, piece_len = odds.shape
    return list(
        call(
            functools.partial(second_half_kernel, span),
            [odds, evens, sums, dense],
            [held(span + (rows - span) // 2, piece_len)] * n_col,
            before,
            scratch=[pltpu.VMEM((2 * span, depth // 2), jnp.bfloat16)],
            limit=VMEM_LIMIT,
            flops=2 * span * dense.size,
        )
    )


def left_kernel(n_row, x_evens, x_odds, dense_ref, evens_ref, odds_ref):
    row_blocks, _, width = dense_ref.shape
    tile_len = width // 2
    _, span, piece_len = x_evens.shape
    piece_blocks = piece_len // tile_len
    x_digits = [
        centred_digits((x_odds if e % 2 else x_evens)[e // 2])
        for e in range(row_blocks // piece_blocks)
    ]
    for place in range(n_row):
        by_high = by_low = high_part = low_part = 0.0
        for block in range(row_blocks):
            sub = block % piece_blocks
            left = x_digits[block // piece_blocks][:, sub * tile_len : (sub + 1) * tile_len]
            right = dense_ref[block, place * piece_len : (place + 1) * piece_len, :]
            high_part = high_part + dot_pairs(left, right[:, :tile_len])
            low_part = low_part + dot_pairs(left, right[:, tile_len:])
            if (block + 1) * tile_len % EXACT_DEPTH == 0 or block == row_blocks - 1:
                by_high = by_high + reduce_centered(high_part)
                by_low = by_low + reduce_centered(low_part)
                high_part = low_part = 0.0
        piece = combine(by_high[:span], by_low[:span] + by_high[span:], by_low[span:])
        if place < n_row // 2:
            evens_ref[place] = piece
        else:
            odds_ref[place - n_row // 2] = piece


def dense_left(x_pairs, n_row, dense, before):
    _, span, piece_len = x_pairs[0].shape
    return call(
        functools.partial(left_kernel, n_row),
        [*x_pairs, dense],
        [held(n_row // 2, span, piece_len)] * 2,
        before,
        limit=VMEM_LIMIT,
        flops=4 * span * dense.size,
    )


def sparse_tiles(tiles, sizes):
    tile_rows, tile_cols, tile_count, tile_entries = tiles
    n_row, n_col, piece_blocks = sizes
    entries, rows, cols = tile_entries[0, 0], tile_rows[0, 0], tile_cols[0, 0]
    row_shift = shift_of(lax.axis_index("col"), rows // piece_blocks, n_col)
    col_shift = shift_of(lax.axis_index("row"), cols // piece_blocks, n_row)
    col_place = col_shift % 2 * (n_row // 2) + col_shift // 2
    positions = (
        row_shift * piece_blocks + rows % piece_blocks,
        col_place * piece_blocks + cols % piece_blocks,
        tile_count[0, 0],
    )
    entries = jnp.where(entries > HALF_MODULUS, entries - MODULUS, entries)
    return positions, jnp.stack(balanced_digits(entries), 1).astype(jnp.bfloat16)


def sparse_product(vector, spec, places, targets, count, blocks, a_digits):
    span, tile_len = vector.shape[0], a_digits.shape[-1]
    v_digits = stacked_digits(vector).reshape(2 * span, -1, tile_len)
    picked = jnp.take(v_digits, places, axis=1)
    products = jnp.einsum(spec, picked, a_digits, preferred_element_type=jnp.float32)
    products = reduce_centered(products)
    residues = combine(
        products[:, 0, :span],
        products[:, 0, span:] + products[:, 1, :span],
        products[:, 1, span:],
    )
    live = jnp.arange(targets.shape[0], dtype=jnp.int32) < count
    onehot = targets[None, :] == jnp.arange(blocks, dtype=jnp.int32)[:, None]
    onehot = (onehot & live[None, :]).astype(jnp.float32)
    summed = jnp.einsum("bt,twi->wbi", onehot, residues, precision=lax.Precision.HIGHEST)
    return reduce_centered(summed).reshape(span, blocks * tile_len)


def sparse_second(odds, evens, span, n_col, positions, a_digits):
    rows, cols, count = positions
    pieces = [*evens, *odds]
    piece_len = pieces[0].shape[1]
    blocks = n_col * piece_len // a_digits.shape[-1]
    vector = reduce_centered(jnp.concatenate([piece[:span] for piece in pieces], 1))
    product = sparse_product(vector, "ntk,tdik->tdni", cols, rows, count, blocks, a_digits)
    packed = half_of_core(functools.reduce(jnp.add, [piece[span:] for piece in pieces]))
    outs = [product[:, e * piece_len : (e + 1) * piece_len] for e in range(n_col)]
    return [jnp.concatenate([out, packed], 0) for out in outs]


def sparse_left(x_pairs, n_row, positions, a_digits):
    rows, cols, count = positions
    n_col = 2 * x_pairs[0].shape[0]
    x_pieces = [x_pairs[e % 2][e // 2] for e in range(n_col)]
    piece_len = x_pieces[0].shape[1]
    values = jnp.concatenate(x_pieces, 1)
    values = jnp.where(values > HALF_MODULUS, values - MODULUS, values)
    blocks = n_row * piece_len // a_digits.shape[-1]
    product = sparse_product(values, "nti,tdik->tdnk", rows, cols, count, blocks, a_digits)
    pieces = [product[:, d * piece_len : (d + 1) * piece_len] for d in range(n_row)]
    return jnp.stack(pieces[: n_row // 2]), jnp.stack(pieces[n_row // 2 :])


def add_and_part(kept, came, before=()):
    def kernel(kept_ref, came_ref, evens_ref, odds_ref):
        for index in range(kept.shape[0]):
            (odds_ref if index % 2 else evens_ref)[index // 2] = kept_ref[index] + came_ref[index]

    return call(kernel, [kept, came], [held(kept.shape[0] // 2, *kept.shape[1:])] * 2, before)


def append_projections(w_parts, pieces, earlier):
    span, piece_len = pieces[0].shape
    rows = span * span // piece_len

    def kernel(*refs):
        piece_refs, refs = refs[: len(pieces)], refs[len(pieces) :]
        earlier_refs, refs = refs[: len(earlier)], refs[len(earlier) :]
        w_refs, out_ref = refs[:-1], refs[-1]
        summed = functools.reduce(jnp.add, [ref[...] for ref in piece_refs])
        out_ref[:span, :] = summed
        w_piece = functools.reduce(jnp.add, [ref[...] for ref in w_refs])
        w_digits = stacked_digits(reduce_centered(w_piece))
        for index, vector in enumerate([summed] + [ref[...] for ref in earlier_refs]):
            products = dot_pairs(w_digits, stacked_digits(reduce_centered(vector)))
            square = combine(
                reduce_centered(products[:span, :span]),
                reduce_centered(products[:span, span:]) + reduce_centered(products[span:, :span]),
                reduce_centered(products[span:, span:]),
            )
            start = span + index * rows
            out_ref[start : start + rows, :] = pack_square(square, piece_len)

    outs = [held(span + (len(earlier) + 1) * rows, piece_len)]
    return call(kernel, [*pieces, *earlier, *w_parts], outs)[0]


def multiply_mod(left, right):
    span = left.shape[0]
    left = stacked_digits(left)
    high, low = (part.astype(jnp.bfloat16) for part in balanced_digits(right))
    by_high = jnp.dot(left, high, preferred_element_type=jnp.float32)
    by_low = jnp.dot(left, low, preferred_element_type=jnp.float32)
    return combine(
        reduce_centered(by_high[:span]), by_low[:span] + by_high[span:], by_low[span:]
    )


def sigma_update(mine, other, span):
    rows = span * span // mine.shape[1]

    def kernel(mine_ref, other_ref, out_ref):
        first = lax.axis_index("row") % 2 == 0
        mine, other = reduce_centered(mine_ref[...]), reduce_centered(other_ref[...])
        packed = jnp.concatenate([jnp.where(first, mine, other), jnp.where(first, other, mine)], 0)
        c_3, c_1, c_2 = (
            unpack_square(packed[index * rows : (index + 1) * rows], span) for index in range(3)
        )
        e_2 = reduce_centered(c_1 - multiply_mod(c_1, c_2))
        both = reduce_centered(c_1 + e_2)
        start = multiply_mod(e_2, c_1)
        rest = c_1 - multiply_mod(both, c_2)
        e_3 = reduce_centered(multiply_mod(start, c_3) + rest)
        out_ref[0] = canonical(-multiply_mod(e_3, start)) * (1.0 / MODULUS)
        out_ref[1] = canonical(start + multiply_mod(e_3, both)) * (1.0 / MODULUS)
        out_ref[2] = canonical(-both - e_3) * (1.0 / MODULUS)

    outs = [jax.ShapeDtypeStruct((STEP_COUNT, span, span), jnp.float32)]
    return call(kernel, [mine, other], outs)[0]


def local(tile_entries, tile_rows, tile_cols, tile_count, block_x, block_y):
    _, _, slot_count, tile_len, _ = tile_entries.shape
    span, piece_len = block_y.shape
    piece_blocks = piece_len // tile_len
    n_row, n_col = lax.axis_size("row"), lax.axis_size("col")
    packed_rows = span * span // piece_len
    tiles = (tile_rows, tile_cols, tile_count, tile_entries)
    sizes = (n_row, n_col, piece_blocks)
    is_dense = n_col * piece_blocks * n_row * piece_blocks <= DENSE_CELLS * slot_count
    if is_dense:
        dense, x_own, y_own, token = build_dense(tiles, block_x, block_y, sizes)
        before = [token]
    else:
        positions, a_digits = sparse_tiles(tiles, sizes)
        x_own, y_own, before = block_x, block_y, []

    def multiply_evens(evens):
        return dense_first(evens, span, dense) if is_dense else evens

    def multiply_odds(odds, evens, sums, before):
        if is_dense:
            return dense_second(odds, evens, sums, span, n_col, dense, before)
        return sparse_second(odds, evens, span, n_col, positions, a_digits)

    def multiply(evens, before):
        return multiply_odds(gather_odds(evens, "row"), evens, multiply_evens(evens), before)

    y_came = fetch_evens(block_y, "row")
    x_came = fetch_evens(block_x, "col")
    evens = stack_after([y_own] + y_came, [*before, *x_came])
    x_evens = stack_after([x_own] + x_came)
    outs = multiply(evens, [x_evens])
    x_pairs = [x_evens, gather_odds(x_evens, "col")]
    if is_dense:
        w_evens, w_odds = dense_left(x_pairs, n_row, dense, [outs[0]])
    else:
        w_evens, w_odds = sparse_left(x_pairs, n_row, positions, a_digits)
    vector_1 = sum_after(scatter_pieces(outs, "col"), [w_odds])
    w_came = fetch(w_odds, "row", 1)
    outs = multiply(gather_evens(vector_1, "row"), [w_came])
    pieces = scatter_pieces(outs, "col")
    w_kept, shift, before = w_evens, 2, []
    while shift < n_row:
        w_kept, w_sent = add_and_part(w_kept, w_came, before)
        w_came = fetch(w_sent, "row", shift)
        shift, before = 2 * shift, [outs[0]]
    vector_2 = append_projections([w_kept[0], w_came[0]], pieces, [y_own, vector_1])
    outs = multiply(gather_evens(vector_2, "row"), [])
    pieces = scatter_pieces(outs, "col")
    terms = functools.reduce(jnp.add, [piece[span:] for piece in pieces])
    vector_3 = functools.reduce(jnp.add, [piece[:span] for piece in pieces])
    return sigma_update(terms, fetch(terms, "row", 1), span), canonical(vector_3) * (1.0 / MODULUS)


def solution(mesh):
    placed = (
        P("row", "col", None, None, None),
        P("row", "col", None),
        P("row", "col", None),
        P("row", "col"),
        P(None, ("row", "col")),
        P(None, ("row", "col")),
    )
    return jax.shard_map(
        local, mesh=mesh, in_specs=placed, out_specs=(P(), P(None, ("row", "col"))), check_vma=False
    )
```

```python
import functools

import jax
import jax.numpy as jnp
from jax import lax
from jax.experimental import pallas as pl
from jax.experimental.pallas import tpu as pltpu
from jax.sharding import PartitionSpec as P

STEP_COUNT = 3

MODULUS = 65521.0
HALF_MODULUS = 32760.0
BASE = 256.0
EXACT_DEPTH = 1024
DENSE_CELLS = 4
VMEM_LIMIT = 16 * 1024 * 1024
SMALL_LIMIT = 4 * 1024 * 1024


def reduce_centered(values):
    return values - MODULUS * jnp.floor(values * (1.0 / MODULUS) + 0.5)


def canonical(values):
    reduced = reduce_centered(values)
    return jnp.where(reduced < 0, reduced + MODULUS, reduced)


def balanced_digits(values):
    high = jnp.floor(values * (1.0 / BASE) + 0.5)
    return high, values - BASE * high


def stacked_digits(values):
    high, low = balanced_digits(values)
    return jnp.concatenate([high, low], 0).astype(jnp.bfloat16)


def centred_digits(residues):
    return stacked_digits(jnp.where(residues > HALF_MODULUS, residues - MODULUS, residues))


def partner(index, shift, size):
    return index ^ shift if size & (size - 1) == 0 else (index + shift) % size


def shift_of(index, other, size):
    return index ^ other if size & (size - 1) == 0 else (other - index) % size


def fetch(piece, axis, shift):
    size = lax.axis_size(axis)
    return lax.ppermute(piece, axis, [(partner(i, shift, size), i) for i in range(size)])


def scatter_pieces(pieces, axis):
    size = lax.axis_size(axis)
    came = [
        lax.ppermute(pieces[shift], axis, [(i, partner(i, shift, size)) for i in range(size)])
        for shift in reversed(range(1, size))
    ]
    return [pieces[0]] + came


def call(kernel, operands, outs, before=(), scratch=(), limit=SMALL_LIMIT, flops=0):
    def body(*refs):
        kernel(*refs[: len(operands)], *refs[len(operands) + len(before) :])

    vmem = pl.BlockSpec(memory_space=pltpu.VMEM)
    return pl.pallas_call(
        body,
        in_specs=[vmem] * len(operands) + [pl.BlockSpec(memory_space=pl.ANY)] * len(before),
        out_specs=[vmem] * len(outs),
        out_shape=outs,
        scratch_shapes=list(scratch),
        compiler_params=pltpu.CompilerParams(vmem_limit_bytes=limit),
        cost_estimate=pl.CostEstimate(flops=flops, bytes_accessed=0, transcendentals=0),
    )(*(pltpu.with_memory_space_constraint(part, pltpu.VMEM) for part in operands), *before)


def held(*shape):
    return pltpu.VMEM(shape, jnp.float32)


def stack_after(pieces, before=()):
    def kernel(*refs):
        for index, ref in enumerate(refs[:-1]):
            refs[-1][index] = ref[...]

    return call(kernel, pieces, [held(len(pieces), *pieces[0].shape)], before)[0]


def sum_after(pieces, before=()):
    def kernel(*refs):
        refs[-1][...] = functools.reduce(jnp.add, [ref[...] for ref in refs[:-1]])

    return call(kernel, pieces, [held(*pieces[0].shape)], before)[0]


def fetch_evens(piece, axis):
    return [fetch(piece, axis, shift) for shift in range(2, lax.axis_size(axis), 2)]


def gather_evens(piece, axis, before=()):
    return stack_after([piece] + fetch_evens(piece, axis), before)


def gather_odds(evens, axis):
    size = lax.axis_size(axis)
    assert size > 1 and size & (size - 1) == 0
    return fetch(evens, axis, 1)


def dot_pairs(left, right):
    return lax.dot_general(left, right, (((1,), (1,)), ((), ())), preferred_element_type=jnp.float32)


def combine(high, middle, low):
    return reduce_centered(15.0 * high + 256.0 * reduce_centered(middle) + low)


def pack_square(square, width):
    span = square.shape[0]
    rows = span * span // width
    return jnp.concatenate([square[j * rows : (j + 1) * rows] for j in range(width // span)], 1)


def unpack_square(packed, span):
    count = packed.shape[1] // span
    return jnp.concatenate([packed[:, j * span : (j + 1) * span] for j in range(count)], 0)


def build_kernel(sizes, *refs):
    entries_ref, x_ref, y_ref, dense_ref, x_out, y_out, token_ref = refs[3:10]
    rows_ref, cols_ref, count_ref, tiles, sems = refs[10:]
    n_row, n_col, piece_blocks, group = sizes
    _, _, slot_count, tile_len, _ = entries_ref.shape
    me_row, me_col = lax.axis_index("row"), lax.axis_index("col")
    chunk_count = slot_count // group

    def chunk(index):
        source = entries_ref.at[0, 0, pl.ds(index * group, group)]
        return pltpu.make_async_copy(source, tiles.at[pl.ds(index * group, group)], sems.at[index])

    small = [*zip(refs[:3], refs[10:13]), (y_ref, y_out), (x_ref, x_out)]
    small = [
        pltpu.make_async_copy(source, target, sems.at[chunk_count + index])
        for index, (source, target) in enumerate(small)
    ]
    for copy in small[:3]:
        copy.start()
    for copy in small[:3]:
        copy.wait()
    used_count = (count_ref[0, 0] + group - 1) // group
    for index in range(chunk_count):

        @pl.when(index < used_count)
        def _():
            chunk(index).start(priority=index % 2)

    for copy in small[3:]:
        copy.start()

    def clear(block, carry):
        dense_ref[block] = jnp.zeros(dense_ref.shape[1:], dense_ref.dtype)
        return carry

    lax.fori_loop(0, dense_ref.shape[0], clear, 0)

    def place(slot):
        row, col = rows_ref[0, 0, slot], cols_ref[0, 0, slot]
        row_shift = shift_of(me_col, row // piece_blocks, n_col)
        col_shift = shift_of(me_row, col // piece_blocks, n_row)
        col_place = col_shift % 2 * (n_row // 2) + col_shift // 2
        block = row_shift * piece_blocks + row % piece_blocks
        start = (col_place * piece_blocks + col % piece_blocks) * tile_len
        values = jnp.where(slot < count_ref[0, 0], tiles[slot], 0.0)
        values = jnp.where(values > HALF_MODULUS, values - MODULUS, values).T
        both = jnp.concatenate(balanced_digits(values), 1).astype(jnp.bfloat16)
        dense_ref[block, pl.ds(pl.multiple_of(start, tile_len), tile_len), :] = both

    def step(index, carry):
        chunk(index).wait()
        for offset in range(group):
            place(index * group + offset)
        return carry

    lax.fori_loop(0, used_count, step, 0)
    for copy in small[3:]:
        copy.wait()
    token_ref[...] = jnp.zeros_like(token_ref)


def build_dense(tiles, block_x, block_y, sizes):
    tile_rows, tile_cols, tile_count, tile_entries = tiles
    n_row, n_col, piece_blocks = sizes
    _, _, slot_count, tile_len, _ = tile_entries.shape
    group = next(size for size in (16, 8, 4, 2, 1) if slot_count % size == 0)
    shape = (n_col * piece_blocks, n_row * piece_blocks * tile_len, 2 * tile_len)
    hbm = pl.BlockSpec(memory_space=pltpu.HBM)
    rows, cols, entries, x_piece, y_piece = (
        pltpu.with_memory_space_constraint(part, pltpu.HBM)
        for part in (tile_rows, tile_cols, tile_entries, block_x, block_y)
    )
    return pl.pallas_call(
        functools.partial(build_kernel, (*sizes, group)),
        in_specs=[hbm, hbm, pl.BlockSpec(memory_space=pl.ANY), hbm, hbm, hbm],
        out_specs=[pl.BlockSpec(memory_space=pltpu.VMEM)] * 4,
        out_shape=[
            pltpu.VMEM(shape, jnp.bfloat16),
            held(*block_x.shape),
            held(*block_y.shape),
            held(8, 128),
        ],
        scratch_shapes=[
            *(pltpu.SMEM(part.shape, part.dtype) for part in (tile_rows, tile_cols, tile_count)),
            pltpu.VMEM((slot_count, tile_len, tile_len), jnp.float32),
            pltpu.SemaphoreType.DMA((slot_count // group + 5,)),
        ],
        compiler_params=pltpu.CompilerParams(vmem_limit_bytes=VMEM_LIMIT),
        cost_estimate=pl.CostEstimate(
            flops=8 * tile_entries.size, bytes_accessed=8 * tile_entries.size, transcendentals=0
        ),
    )(rows, cols, tile_count, entries, x_piece, y_piece)


def half_products(half, span, pieces_ref, dense_ref, digits, block):
    _, depth, width = dense_ref.shape
    tile_len, half_depth = width // 2, depth // 2
    high = middle = low = 0.0
    for start in range(0, half_depth, EXACT_DEPTH):
        stop = min(start + EXACT_DEPTH, half_depth)
        products = jnp.dot(
            digits[:, start:stop],
            dense_ref[block, half * half_depth + start : half * half_depth + stop, :],
            preferred_element_type=jnp.float32,
        )
        products = reduce_centered(products)
        high = high + products[:span, :tile_len]
        middle = middle + products[:span, tile_len:] + products[span:, :tile_len]
        low = low + products[span:, tile_len:]
    return high, middle, low


def fill_digits(span, pieces_ref, digits):
    piece_len = pieces_ref.shape[2]
    for d in range(pieces_ref.shape[0]):
        vector = reduce_centered(pieces_ref[d, :span, :])
        digits[:, d * piece_len : (d + 1) * piece_len] = stacked_digits(vector)


def first_half_kernel(span, pieces_ref, dense_ref, sums_ref, digits):
    fill_digits(span, pieces_ref, digits)
    tile_len = dense_ref.shape[2] // 2
    for block in range(dense_ref.shape[0]):
        parts = half_products(0, span, pieces_ref, dense_ref, digits, block)
        for index, part in enumerate(parts):
            sums_ref[index, :, block * tile_len : (block + 1) * tile_len] = part


def half_of_core(packed):
    rows = packed.shape[0] // 2
    return jnp.where(lax.axis_index("row") % 2 == 0, packed[:rows], packed[rows:])


def second_half_kernel(span, pieces_ref, evens_ref, sums_ref, dense_ref, *refs):
    outs, digits = refs[:-1], refs[-1]
    n_col = len(outs)
    fill_digits(span, pieces_ref, digits)
    row_blocks, _, width = dense_ref.shape
    tile_len = width // 2
    piece_blocks = row_blocks // n_col
    for e in reversed(range(n_col)):
        for sub in range(piece_blocks):
            block = e * piece_blocks + sub
            parts = half_products(1, span, pieces_ref, dense_ref, digits, block)
            parts = (
                part + sums_ref[index, :, block * tile_len : (block + 1) * tile_len]
                for index, part in enumerate(parts)
            )
            outs[e][:span, sub * tile_len : (sub + 1) * tile_len] = combine(*parts)
    if outs[0].shape[0] > span:
        packed = jnp.sum(pieces_ref[:, span:, :], 0) + jnp.sum(evens_ref[:, span:, :], 0)
        packed = half_of_core(packed)
        for out in outs:
            out[span:, :] = packed


def dense_first(evens, span, dense):
    row_blocks, depth, width = dense.shape
    return call(
        functools.partial(first_half_kernel, span),
        [evens, dense],
        [held(3, span, row_blocks * width // 2)],
        scratch=[pltpu.VMEM((2 * span, depth // 2), jnp.bfloat16)],
        limit=VMEM_LIMIT,
        flops=2 * span * dense.size,
    )[0]


def dense_second(odds, evens, sums, span, n_col, dense, before):
    _, depth, _ = dense.shape
    _, rows, piece_len = odds.shape
    return list(
        call(
            functools.partial(second_half_kernel, span),
            [odds, evens, sums, dense],
            [held(span + (rows - span) // 2, piece_len)] * n_col,
            before,
            scratch=[pltpu.VMEM((2 * span, depth // 2), jnp.bfloat16)],
            limit=VMEM_LIMIT,
            flops=2 * span * dense.size,
        )
    )


def left_kernel(n_row, x_evens, x_odds, dense_ref, evens_ref, odds_ref):
    row_blocks, _, width = dense_ref.shape
    tile_len = width // 2
    _, span, piece_len = x_evens.shape
    piece_blocks = piece_len // tile_len
    x_digits = [
        centred_digits((x_odds if e % 2 else x_evens)[e // 2])
        for e in range(row_blocks // piece_blocks)
    ]
    for place in range(n_row):
        by_high = by_low = high_part = low_part = 0.0
        for block in range(row_blocks):
            sub = block % piece_blocks
            left = x_digits[block // piece_blocks][:, sub * tile_len : (sub + 1) * tile_len]
            right = dense_ref[block, place * piece_len : (place + 1) * piece_len, :]
            high_part = high_part + dot_pairs(left, right[:, :tile_len])
            low_part = low_part + dot_pairs(left, right[:, tile_len:])
            if (block + 1) * tile_len % EXACT_DEPTH == 0 or block == row_blocks - 1:
                by_high = by_high + reduce_centered(high_part)
                by_low = by_low + reduce_centered(low_part)
                high_part = low_part = 0.0
        piece = combine(by_high[:span], by_low[:span] + by_high[span:], by_low[span:])
        if place < n_row // 2:
            evens_ref[place] = piece
        else:
            odds_ref[place - n_row // 2] = piece


def dense_left(x_pairs, n_row, dense, before):
    _, span, piece_len = x_pairs[0].shape
    return call(
        functools.partial(left_kernel, n_row),
        [*x_pairs, dense],
        [held(n_row // 2, span, piece_len)] * 2,
        before,
        limit=VMEM_LIMIT,
        flops=4 * span * dense.size,
    )


def sparse_tiles(tiles, sizes):
    tile_rows, tile_cols, tile_count, tile_entries = tiles
    n_row, n_col, piece_blocks = sizes
    entries, rows, cols = tile_entries[0, 0], tile_rows[0, 0], tile_cols[0, 0]
    row_shift = shift_of(lax.axis_index("col"), rows // piece_blocks, n_col)
    col_shift = shift_of(lax.axis_index("row"), cols // piece_blocks, n_row)
    col_place = col_shift % 2 * (n_row // 2) + col_shift // 2
    positions = (
        row_shift * piece_blocks + rows % piece_blocks,
        col_place * piece_blocks + cols % piece_blocks,
        tile_count[0, 0],
    )
    entries = jnp.where(entries > HALF_MODULUS, entries - MODULUS, entries)
    return positions, jnp.stack(balanced_digits(entries), 1).astype(jnp.bfloat16)


def sparse_product(vector, spec, places, targets, count, blocks, a_digits):
    span, tile_len = vector.shape[0], a_digits.shape[-1]
    v_digits = stacked_digits(vector).reshape(2 * span, -1, tile_len)
    picked = jnp.take(v_digits, places, axis=1)
    products = jnp.einsum(spec, picked, a_digits, preferred_element_type=jnp.float32)
    products = reduce_centered(products)
    residues = combine(
        products[:, 0, :span],
        products[:, 0, span:] + products[:, 1, :span],
        products[:, 1, span:],
    )
    live = jnp.arange(targets.shape[0], dtype=jnp.int32) < count
    onehot = targets[None, :] == jnp.arange(blocks, dtype=jnp.int32)[:, None]
    onehot = (onehot & live[None, :]).astype(jnp.float32)
    summed = jnp.einsum("bt,twi->wbi", onehot, residues, precision=lax.Precision.HIGHEST)
    return reduce_centered(summed).reshape(span, blocks * tile_len)


def sparse_second(odds, evens, span, n_col, positions, a_digits):
    rows, cols, count = positions
    pieces = [*evens, *odds]
    piece_len = pieces[0].shape[1]
    blocks = n_col * piece_len // a_digits.shape[-1]
    vector = reduce_centered(jnp.concatenate([piece[:span] for piece in pieces], 1))
    product = sparse_product(vector, "ntk,tdik->tdni", cols, rows, count, blocks, a_digits)
    packed = half_of_core(functools.reduce(jnp.add, [piece[span:] for piece in pieces]))
    outs = [product[:, e * piece_len : (e + 1) * piece_len] for e in range(n_col)]
    return [jnp.concatenate([out, packed], 0) for out in outs]


def sparse_left(x_pairs, n_row, positions, a_digits):
    rows, cols, count = positions
    n_col = 2 * x_pairs[0].shape[0]
    x_pieces = [x_pairs[e % 2][e // 2] for e in range(n_col)]
    piece_len = x_pieces[0].shape[1]
    values = jnp.concatenate(x_pieces, 1)
    values = jnp.where(values > HALF_MODULUS, values - MODULUS, values)
    blocks = n_row * piece_len // a_digits.shape[-1]
    product = sparse_product(values, "nti,tdik->tdnk", rows, cols, count, blocks, a_digits)
    pieces = [product[:, d * piece_len : (d + 1) * piece_len] for d in range(n_row)]
    return jnp.stack(pieces[: n_row // 2]), jnp.stack(pieces[n_row // 2 :])


def add_and_part(kept, came, before=()):
    def kernel(kept_ref, came_ref, evens_ref, odds_ref):
        for index in range(kept.shape[0]):
            (odds_ref if index % 2 else evens_ref)[index // 2] = kept_ref[index] + came_ref[index]

    return call(kernel, [kept, came], [held(kept.shape[0] // 2, *kept.shape[1:])] * 2, before)


def append_projections(w_parts, pieces, earlier):
    span, piece_len = pieces[0].shape
    rows = span * span // piece_len

    def kernel(*refs):
        piece_refs, refs = refs[: len(pieces)], refs[len(pieces) :]
        earlier_refs, refs = refs[: len(earlier)], refs[len(earlier) :]
        w_refs, out_ref = refs[:-1], refs[-1]
        summed = functools.reduce(jnp.add, [ref[...] for ref in piece_refs])
        out_ref[:span, :] = summed
        w_piece = functools.reduce(jnp.add, [ref[...] for ref in w_refs])
        w_digits = stacked_digits(reduce_centered(w_piece))
        for index, vector in enumerate([summed] + [ref[...] for ref in earlier_refs]):
            products = dot_pairs(w_digits, stacked_digits(reduce_centered(vector)))
            square = combine(
                reduce_centered(products[:span, :span]),
                reduce_centered(products[:span, span:]) + reduce_centered(products[span:, :span]),
                reduce_centered(products[span:, span:]),
            )
            start = span + index * rows
            out_ref[start : start + rows, :] = pack_square(square, piece_len)

    outs = [held(span + (len(earlier) + 1) * rows, piece_len)]
    return call(kernel, [*pieces, *earlier, *w_parts], outs)[0]


def multiply_mod(left, right):
    span = left.shape[0]
    left = stacked_digits(left)
    high, low = (part.astype(jnp.bfloat16) for part in balanced_digits(right))
    by_high = jnp.dot(left, high, preferred_element_type=jnp.float32)
    by_low = jnp.dot(left, low, preferred_element_type=jnp.float32)
    return combine(
        reduce_centered(by_high[:span]), by_low[:span] + by_high[span:], by_low[span:]
    )


def sigma_update(mine, other, span):
    rows = span * span // mine.shape[1]

    def kernel(mine_ref, other_ref, out_ref):
        first = lax.axis_index("row") % 2 == 0
        mine, other = reduce_centered(mine_ref[...]), reduce_centered(other_ref[...])
        packed = jnp.concatenate([jnp.where(first, mine, other), jnp.where(first, other, mine)], 0)
        c_3, c_1, c_2 = (
            unpack_square(packed[index * rows : (index + 1) * rows], span) for index in range(3)
        )
        e_2 = reduce_centered(c_1 - multiply_mod(c_1, c_2))
        both = reduce_centered(c_1 + e_2)
        start = multiply_mod(e_2, c_1)
        rest = c_1 - multiply_mod(both, c_2)
        e_3 = reduce_centered(multiply_mod(start, c_3) + rest)
        out_ref[0] = canonical(-multiply_mod(e_3, start)) * (1.0 / MODULUS)
        out_ref[1] = canonical(start + multiply_mod(e_3, both)) * (1.0 / MODULUS)
        out_ref[2] = canonical(-both - e_3) * (1.0 / MODULUS)

    outs = [jax.ShapeDtypeStruct((STEP_COUNT, span, span), jnp.float32)]
    return call(kernel, [mine, other], outs)[0]


def local(tile_entries, tile_rows, tile_cols, tile_count, block_x, block_y):
    _, _, slot_count, tile_len, _ = tile_entries.shape
    span, piece_len = block_y.shape
    piece_blocks = piece_len // tile_len
    n_row, n_col = lax.axis_size("row"), lax.axis_size("col")
    packed_rows = span * span // piece_len
    tiles = (tile_rows, tile_cols, tile_count, tile_entries)
    sizes = (n_row, n_col, piece_blocks)
    is_dense = n_col * piece_blocks * n_row * piece_blocks <= DENSE_CELLS * slot_count
    if is_dense:
        dense, x_own, y_own, token = build_dense(tiles, block_x, block_y, sizes)
        before = [token]
    else:
        positions, a_digits = sparse_tiles(tiles, sizes)
        x_own, y_own, before = block_x, block_y, []

    def multiply_evens(evens):
        return dense_first(evens, span, dense) if is_dense else evens

    def multiply_odds(odds, evens, sums, before):
        if is_dense:
            return dense_second(odds, evens, sums, span, n_col, dense, before)
        return sparse_second(odds, evens, span, n_col, positions, a_digits)

    def multiply(evens, before):
        return multiply_odds(gather_odds(evens, "row"), evens, multiply_evens(evens), before)

    y_came = fetch_evens(block_y, "row")
    x_came = fetch_evens(block_x, "col")
    evens = stack_after([y_own] + y_came, [*before, *x_came])
    x_evens = stack_after([x_own] + x_came)
    outs = multiply(evens, [x_evens])
    x_pairs = [x_evens, gather_odds(x_evens, "col")]
    if is_dense:
        w_evens, w_odds = dense_left(x_pairs, n_row, dense, [outs[0]])
    else:
        w_evens, w_odds = sparse_left(x_pairs, n_row, positions, a_digits)
    vector_1 = sum_after(scatter_pieces(outs, "col"), [w_odds])
    w_came = fetch(w_odds, "row", 1)
    outs = multiply(gather_evens(vector_1, "row"), [w_came])
    pieces = scatter_pieces(outs, "col")
    w_kept, shift, before = w_evens, 2, []
    while shift < n_row:
        w_kept, w_sent = add_and_part(w_kept, w_came, before)
        w_came = fetch(w_sent, "row", shift)
        shift, before = 2 * shift, [outs[0]]
    vector_2 = append_projections([w_kept[0], w_came[0]], pieces, [y_own, vector_1])
    outs = multiply(gather_evens(vector_2, "row"), [])
    pieces = scatter_pieces(outs, "col")
    terms = functools.reduce(jnp.add, [piece[span:] for piece in pieces])
    vector_3 = functools.reduce(jnp.add, [piece[:span] for piece in pieces])
    return sigma_update(terms, fetch(terms, "row", 1), span), canonical(vector_3) * (1.0 / MODULUS)


def solution(mesh):
    placed = (
        P("row", "col", None, None, None),
        P("row", "col", None),
        P("row", "col", None),
        P("row", "col"),
        P(None, ("row", "col")),
        P(None, ("row", "col")),
    )
    return jax.shard_map(
        local, mesh=mesh, in_specs=placed, out_specs=(P(), P(None, ("row", "col"))), check_vma=False
    )
```

```python
import functools

import jax
import jax.numpy as jnp
from jax import lax
from jax.experimental import pallas as pl
from jax.experimental.pallas import tpu as pltpu
from jax.sharding import PartitionSpec as P

STEP_COUNT = 3

MODULUS = 65521.0
HALF_MODULUS = 32760.0
BASE = 256.0
EXACT_DEPTH = 1024
DENSE_CELLS = 4
VMEM_LIMIT = 16 * 1024 * 1024
SMALL_LIMIT = 4 * 1024 * 1024


def reduce_centered(values):
    return values - MODULUS * jnp.floor(values * (1.0 / MODULUS) + 0.5)


def canonical(values):
    reduced = reduce_centered(values)
    return jnp.where(reduced < 0, reduced + MODULUS, reduced)


def balanced_digits(values):
    high = jnp.floor(values * (1.0 / BASE) + 0.5)
    return high, values - BASE * high


def stacked_digits(values):
    high, low = balanced_digits(values)
    return jnp.concatenate([high, low], 0).astype(jnp.bfloat16)


def centred_digits(residues):
    return stacked_digits(jnp.where(residues > HALF_MODULUS, residues - MODULUS, residues))


def partner(index, shift, size):
    return index ^ shift if size & (size - 1) == 0 else (index + shift) % size


def shift_of(index, other, size):
    return index ^ other if size & (size - 1) == 0 else (other - index) % size


def fetch(piece, axis, shift):
    size = lax.axis_size(axis)
    return lax.ppermute(piece, axis, [(partner(i, shift, size), i) for i in range(size)])


def scatter_pieces(pieces, axis):
    size = lax.axis_size(axis)
    came = [
        lax.ppermute(pieces[shift], axis, [(i, partner(i, shift, size)) for i in range(size)])
        for shift in reversed(range(1, size))
    ]
    return [pieces[0]] + came


def call(kernel, operands, outs, before=(), scratch=(), limit=SMALL_LIMIT, flops=0):
    def body(*refs):
        kernel(*refs[: len(operands)], *refs[len(operands) + len(before) :])

    vmem = pl.BlockSpec(memory_space=pltpu.VMEM)
    return pl.pallas_call(
        body,
        in_specs=[vmem] * len(operands) + [pl.BlockSpec(memory_space=pl.ANY)] * len(before),
        out_specs=[vmem] * len(outs),
        out_shape=outs,
        scratch_shapes=list(scratch),
        compiler_params=pltpu.CompilerParams(vmem_limit_bytes=limit),
        cost_estimate=pl.CostEstimate(flops=flops, bytes_accessed=0, transcendentals=0),
    )(*(pltpu.with_memory_space_constraint(part, pltpu.VMEM) for part in operands), *before)


def held(*shape):
    return pltpu.VMEM(shape, jnp.float32)


def stack_after(pieces, before=()):
    def kernel(*refs):
        for index, ref in enumerate(refs[:-1]):
            refs[-1][index] = ref[...]

    return call(kernel, pieces, [held(len(pieces), *pieces[0].shape)], before)[0]


def sum_after(pieces, before=()):
    def kernel(*refs):
        refs[-1][...] = functools.reduce(jnp.add, [ref[...] for ref in refs[:-1]])

    return call(kernel, pieces, [held(*pieces[0].shape)], before)[0]


def fetch_evens(piece, axis):
    return [fetch(piece, axis, shift) for shift in range(2, lax.axis_size(axis), 2)]


def gather_evens(piece, axis, before=()):
    return stack_after([piece] + fetch_evens(piece, axis), before)


def gather_odds(evens, axis):
    size = lax.axis_size(axis)
    assert size > 1 and size & (size - 1) == 0
    return fetch(evens, axis, 1)


def dot_pairs(left, right):
    return lax.dot_general(left, right, (((1,), (1,)), ((), ())), preferred_element_type=jnp.float32)


def combine(high, middle, low):
    return reduce_centered(15.0 * high + 256.0 * reduce_centered(middle) + low)


def pack_square(square, width):
    span = square.shape[0]
    rows = span * span // width
    return jnp.concatenate([square[j * rows : (j + 1) * rows] for j in range(width // span)], 1)


def unpack_square(packed, span):
    count = packed.shape[1] // span
    return jnp.concatenate([packed[:, j * span : (j + 1) * span] for j in range(count)], 0)


def build_kernel(sizes, *refs):
    entries_ref, x_ref, y_ref, dense_ref, x_out, y_out, token_ref = refs[3:10]
    rows_ref, cols_ref, count_ref, tiles, sems = refs[10:]
    n_row, n_col, piece_blocks, group = sizes
    _, _, slot_count, tile_len, _ = entries_ref.shape
    me_row, me_col = lax.axis_index("row"), lax.axis_index("col")
    chunk_count = slot_count // group

    def chunk(index):
        source = entries_ref.at[0, 0, pl.ds(index * group, group)]
        return pltpu.make_async_copy(source, tiles.at[pl.ds(index * group, group)], sems.at[index])

    small = [*zip(refs[:3], refs[10:13]), (y_ref, y_out), (x_ref, x_out)]
    small = [
        pltpu.make_async_copy(source, target, sems.at[chunk_count + index])
        for index, (source, target) in enumerate(small)
    ]
    for copy in small[:3]:
        copy.start()
    sure_count = min(2, chunk_count)
    for index in range(sure_count):
        chunk(index).start()

    def clear(block, carry):
        dense_ref[block] = jnp.zeros(dense_ref.shape[1:], dense_ref.dtype)
        return carry

    half = dense_ref.shape[0] // 2
    lax.fori_loop(0, half, clear, 0)
    for copy in small[:3]:
        copy.wait()
    used_count = jnp.maximum((count_ref[0, 0] + group - 1) // group, sure_count)
    for index in range(sure_count, chunk_count):

        @pl.when(index < used_count)
        def _():
            chunk(index).start()

    for copy in small[3:]:
        copy.start()
    lax.fori_loop(half, dense_ref.shape[0], clear, 0)

    def place(slot):
        row, col = rows_ref[0, 0, slot], cols_ref[0, 0, slot]
        row_shift = shift_of(me_col, row // piece_blocks, n_col)
        col_shift = shift_of(me_row, col // piece_blocks, n_row)
        col_place = col_shift % 2 * (n_row // 2) + col_shift // 2
        block = row_shift * piece_blocks + row % piece_blocks
        start = (col_place * piece_blocks + col % piece_blocks) * tile_len
        values = jnp.where(slot < count_ref[0, 0], tiles[slot], 0.0)
        values = jnp.where(values > HALF_MODULUS, values - MODULUS, values).T
        both = jnp.concatenate(balanced_digits(values), 1).astype(jnp.bfloat16)
        dense_ref[block, pl.ds(pl.multiple_of(start, tile_len), tile_len), :] = both

    def step(index, carry):
        chunk(index).wait()
        for offset in range(group):
            place(index * group + offset)
        return carry

    lax.fori_loop(0, used_count, step, 0)
    for copy in small[3:]:
        copy.wait()
    token_ref[...] = jnp.zeros_like(token_ref)


def build_dense(tiles, block_x, block_y, sizes):
    tile_rows, tile_cols, tile_count, tile_entries = tiles
    n_row, n_col, piece_blocks = sizes
    _, _, slot_count, tile_len, _ = tile_entries.shape
    group = next(size for size in (8, 4, 2, 1) if slot_count % size == 0)
    shape = (n_col * piece_blocks, n_row * piece_blocks * tile_len, 2 * tile_len)
    hbm = pl.BlockSpec(memory_space=pltpu.HBM)
    rows, cols, entries, x_piece, y_piece = (
        pltpu.with_memory_space_constraint(part, pltpu.HBM)
        for part in (tile_rows, tile_cols, tile_entries, block_x, block_y)
    )
    return pl.pallas_call(
        functools.partial(build_kernel, (*sizes, group)),
        in_specs=[hbm, hbm, pl.BlockSpec(memory_space=pl.ANY), hbm, hbm, hbm],
        out_specs=[pl.BlockSpec(memory_space=pltpu.VMEM)] * 4,
        out_shape=[
            pltpu.VMEM(shape, jnp.bfloat16),
            held(*block_x.shape),
            held(*block_y.shape),
            held(8, 128),
        ],
        scratch_shapes=[
            *(pltpu.SMEM(part.shape, part.dtype) for part in (tile_rows, tile_cols, tile_count)),
            pltpu.VMEM((slot_count, tile_len, tile_len), jnp.float32),
            pltpu.SemaphoreType.DMA((slot_count // group + 5,)),
        ],
        compiler_params=pltpu.CompilerParams(vmem_limit_bytes=VMEM_LIMIT),
        cost_estimate=pl.CostEstimate(
            flops=8 * tile_entries.size, bytes_accessed=8 * tile_entries.size, transcendentals=0
        ),
    )(rows, cols, tile_count, entries, x_piece, y_piece)


def half_products(half, span, pieces_ref, dense_ref, digits, block):
    _, depth, width = dense_ref.shape
    tile_len, half_depth = width // 2, depth // 2
    high = middle = low = 0.0
    for start in range(0, half_depth, EXACT_DEPTH):
        stop = min(start + EXACT_DEPTH, half_depth)
        products = jnp.dot(
            digits[:, start:stop],
            dense_ref[block, half * half_depth + start : half * half_depth + stop, :],
            preferred_element_type=jnp.float32,
        )
        products = reduce_centered(products)
        high = high + products[:span, :tile_len]
        middle = middle + products[:span, tile_len:] + products[span:, :tile_len]
        low = low + products[span:, tile_len:]
    return high, middle, low


def fill_digits(span, pieces_ref, digits):
    piece_len = pieces_ref.shape[2]
    for d in range(pieces_ref.shape[0]):
        vector = reduce_centered(pieces_ref[d, :span, :])
        digits[:, d * piece_len : (d + 1) * piece_len] = stacked_digits(vector)


def first_half_kernel(span, pieces_ref, dense_ref, sums_ref, digits):
    fill_digits(span, pieces_ref, digits)
    tile_len = dense_ref.shape[2] // 2
    for block in range(dense_ref.shape[0]):
        parts = half_products(0, span, pieces_ref, dense_ref, digits, block)
        for index, part in enumerate(parts):
            sums_ref[index, :, block * tile_len : (block + 1) * tile_len] = part


def half_of_core(packed):
    rows = packed.shape[0] // 2
    return jnp.where(lax.axis_index("row") % 2 == 0, packed[:rows], packed[rows:])


def second_half_kernel(span, pieces_ref, evens_ref, sums_ref, dense_ref, *refs):
    outs, digits = refs[:-1], refs[-1]
    n_col = len(outs)
    fill_digits(span, pieces_ref, digits)
    row_blocks, _, width = dense_ref.shape
    tile_len = width // 2
    piece_blocks = row_blocks // n_col
    for e in reversed(range(n_col)):
        for sub in range(piece_blocks):
            block = e * piece_blocks + sub
            parts = half_products(1, span, pieces_ref, dense_ref, digits, block)
            parts = (
                part + sums_ref[index, :, block * tile_len : (block + 1) * tile_len]
                for index, part in enumerate(parts)
            )
            outs[e][:span, sub * tile_len : (sub + 1) * tile_len] = combine(*parts)
    if outs[0].shape[0] > span:
        packed = jnp.sum(pieces_ref[:, span:, :], 0) + jnp.sum(evens_ref[:, span:, :], 0)
        packed = half_of_core(packed)
        for out in outs:
            out[span:, :] = packed


def dense_first(evens, span, dense):
    row_blocks, depth, width = dense.shape
    return call(
        functools.partial(first_half_kernel, span),
        [evens, dense],
        [held(3, span, row_blocks * width // 2)],
        scratch=[pltpu.VMEM((2 * span, depth // 2), jnp.bfloat16)],
        limit=VMEM_LIMIT,
        flops=2 * span * dense.size,
    )[0]


def dense_second(odds, evens, sums, span, n_col, dense, before):
    _, depth, _ = dense.shape
    _, rows, piece_len = odds.shape
    return list(
        call(
            functools.partial(second_half_kernel, span),
            [odds, evens, sums, dense],
            [held(span + (rows - span) // 2, piece_len)] * n_col,
            before,
            scratch=[pltpu.VMEM((2 * span, depth // 2), jnp.bfloat16)],
            limit=VMEM_LIMIT,
            flops=2 * span * dense.size,
        )
    )


def left_kernel(n_row, x_evens, x_odds, dense_ref, evens_ref, odds_ref):
    row_blocks, _, width = dense_ref.shape
    tile_len = width // 2
    _, span, piece_len = x_evens.shape
    piece_blocks = piece_len // tile_len
    x_digits = [
        centred_digits((x_odds if e % 2 else x_evens)[e // 2])
        for e in range(row_blocks // piece_blocks)
    ]
    for place in range(n_row):
        by_high = by_low = high_part = low_part = 0.0
        for block in range(row_blocks):
            sub = block % piece_blocks
            left = x_digits[block // piece_blocks][:, sub * tile_len : (sub + 1) * tile_len]
            right = dense_ref[block, place * piece_len : (place + 1) * piece_len, :]
            high_part = high_part + dot_pairs(left, right[:, :tile_len])
            low_part = low_part + dot_pairs(left, right[:, tile_len:])
            if (block + 1) * tile_len % EXACT_DEPTH == 0 or block == row_blocks - 1:
                by_high = by_high + reduce_centered(high_part)
                by_low = by_low + reduce_centered(low_part)
                high_part = low_part = 0.0
        piece = combine(by_high[:span], by_low[:span] + by_high[span:], by_low[span:])
        if place < n_row // 2:
            evens_ref[place] = piece
        else:
            odds_ref[place - n_row // 2] = piece


def dense_left(x_pairs, n_row, dense, before):
    _, span, piece_len = x_pairs[0].shape
    return call(
        functools.partial(left_kernel, n_row),
        [*x_pairs, dense],
        [held(n_row // 2, span, piece_len)] * 2,
        before,
        limit=VMEM_LIMIT,
        flops=4 * span * dense.size,
    )


def sparse_tiles(tiles, sizes):
    tile_rows, tile_cols, tile_count, tile_entries = tiles
    n_row, n_col, piece_blocks = sizes
    entries, rows, cols = tile_entries[0, 0], tile_rows[0, 0], tile_cols[0, 0]
    row_shift = shift_of(lax.axis_index("col"), rows // piece_blocks, n_col)
    col_shift = shift_of(lax.axis_index("row"), cols // piece_blocks, n_row)
    col_place = col_shift % 2 * (n_row // 2) + col_shift // 2
    positions = (
        row_shift * piece_blocks + rows % piece_blocks,
        col_place * piece_blocks + cols % piece_blocks,
        tile_count[0, 0],
    )
    entries = jnp.where(entries > HALF_MODULUS, entries - MODULUS, entries)
    return positions, jnp.stack(balanced_digits(entries), 1).astype(jnp.bfloat16)


def sparse_product(vector, spec, places, targets, count, blocks, a_digits):
    span, tile_len = vector.shape[0], a_digits.shape[-1]
    v_digits = stacked_digits(vector).reshape(2 * span, -1, tile_len)
    picked = jnp.take(v_digits, places, axis=1)
    products = jnp.einsum(spec, picked, a_digits, preferred_element_type=jnp.float32)
    products = reduce_centered(products)
    residues = combine(
        products[:, 0, :span],
        products[:, 0, span:] + products[:, 1, :span],
        products[:, 1, span:],
    )
    live = jnp.arange(targets.shape[0], dtype=jnp.int32) < count
    onehot = targets[None, :] == jnp.arange(blocks, dtype=jnp.int32)[:, None]
    onehot = (onehot & live[None, :]).astype(jnp.float32)
    summed = jnp.einsum("bt,twi->wbi", onehot, residues, precision=lax.Precision.HIGHEST)
    return reduce_centered(summed).reshape(span, blocks * tile_len)


def sparse_second(odds, evens, span, n_col, positions, a_digits):
    rows, cols, count = positions
    pieces = [*evens, *odds]
    piece_len = pieces[0].shape[1]
    blocks = n_col * piece_len // a_digits.shape[-1]
    vector = reduce_centered(jnp.concatenate([piece[:span] for piece in pieces], 1))
    product = sparse_product(vector, "ntk,tdik->tdni", cols, rows, count, blocks, a_digits)
    packed = half_of_core(functools.reduce(jnp.add, [piece[span:] for piece in pieces]))
    outs = [product[:, e * piece_len : (e + 1) * piece_len] for e in range(n_col)]
    return [jnp.concatenate([out, packed], 0) for out in outs]


def sparse_left(x_pairs, n_row, positions, a_digits):
    rows, cols, count = positions
    n_col = 2 * x_pairs[0].shape[0]
    x_pieces = [x_pairs[e % 2][e // 2] for e in range(n_col)]
    piece_len = x_pieces[0].shape[1]
    values = jnp.concatenate(x_pieces, 1)
    values = jnp.where(values > HALF_MODULUS, values - MODULUS, values)
    blocks = n_row * piece_len // a_digits.shape[-1]
    product = sparse_product(values, "nti,tdik->tdnk", rows, cols, count, blocks, a_digits)
    pieces = [product[:, d * piece_len : (d + 1) * piece_len] for d in range(n_row)]
    return jnp.stack(pieces[: n_row // 2]), jnp.stack(pieces[n_row // 2 :])


def add_and_part(kept, came, before=()):
    def kernel(kept_ref, came_ref, evens_ref, odds_ref):
        for index in range(kept.shape[0]):
            (odds_ref if index % 2 else evens_ref)[index // 2] = kept_ref[index] + came_ref[index]

    return call(kernel, [kept, came], [held(kept.shape[0] // 2, *kept.shape[1:])] * 2, before)


def append_projections(w_parts, pieces, earlier):
    span, piece_len = pieces[0].shape
    rows = span * span // piece_len

    def kernel(*refs):
        piece_refs, refs = refs[: len(pieces)], refs[len(pieces) :]
        earlier_refs, refs = refs[: len(earlier)], refs[len(earlier) :]
        w_refs, out_ref = refs[:-1], refs[-1]
        summed = functools.reduce(jnp.add, [ref[...] for ref in piece_refs])
        out_ref[:span, :] = summed
        w_piece = functools.reduce(jnp.add, [ref[...] for ref in w_refs])
        w_digits = stacked_digits(reduce_centered(w_piece))
        for index, vector in enumerate([summed] + [ref[...] for ref in earlier_refs]):
            products = dot_pairs(w_digits, stacked_digits(reduce_centered(vector)))
            square = combine(
                reduce_centered(products[:span, :span]),
                reduce_centered(products[:span, span:]) + reduce_centered(products[span:, :span]),
                reduce_centered(products[span:, span:]),
            )
            start = span + index * rows
            out_ref[start : start + rows, :] = pack_square(square, piece_len)

    outs = [held(span + (len(earlier) + 1) * rows, piece_len)]
    return call(kernel, [*pieces, *earlier, *w_parts], outs)[0]


def multiply_mod(left, right):
    span = left.shape[0]
    left = stacked_digits(left)
    high, low = (part.astype(jnp.bfloat16) for part in balanced_digits(right))
    by_high = jnp.dot(left, high, preferred_element_type=jnp.float32)
    by_low = jnp.dot(left, low, preferred_element_type=jnp.float32)
    return combine(
        reduce_centered(by_high[:span]), by_low[:span] + by_high[span:], by_low[span:]
    )


def sigma_update(mine, other, span):
    rows = span * span // mine.shape[1]

    def kernel(mine_ref, other_ref, out_ref):
        first = lax.axis_index("row") % 2 == 0
        mine, other = reduce_centered(mine_ref[...]), reduce_centered(other_ref[...])
        packed = jnp.concatenate([jnp.where(first, mine, other), jnp.where(first, other, mine)], 0)
        c_3, c_1, c_2 = (
            unpack_square(packed[index * rows : (index + 1) * rows], span) for index in range(3)
        )
        e_2 = reduce_centered(c_1 - multiply_mod(c_1, c_2))
        both = reduce_centered(c_1 + e_2)
        start = multiply_mod(e_2, c_1)
        rest = c_1 - multiply_mod(both, c_2)
        e_3 = reduce_centered(multiply_mod(start, c_3) + rest)
        out_ref[0] = canonical(-multiply_mod(e_3, start)) * (1.0 / MODULUS)
        out_ref[1] = canonical(start + multiply_mod(e_3, both)) * (1.0 / MODULUS)
        out_ref[2] = canonical(-both - e_3) * (1.0 / MODULUS)

    outs = [jax.ShapeDtypeStruct((STEP_COUNT, span, span), jnp.float32)]
    return call(kernel, [mine, other], outs)[0]


def local(tile_entries, tile_rows, tile_cols, tile_count, block_x, block_y):
    _, _, slot_count, tile_len, _ = tile_entries.shape
    span, piece_len = block_y.shape
    piece_blocks = piece_len // tile_len
    n_row, n_col = lax.axis_size("row"), lax.axis_size("col")
    packed_rows = span * span // piece_len
    tiles = (tile_rows, tile_cols, tile_count, tile_entries)
    sizes = (n_row, n_col, piece_blocks)
    is_dense = n_col * piece_blocks * n_row * piece_blocks <= DENSE_CELLS * slot_count
    if is_dense:
        dense, x_own, y_own, token = build_dense(tiles, block_x, block_y, sizes)
        before = [token]
    else:
        positions, a_digits = sparse_tiles(tiles, sizes)
        x_own, y_own, before = block_x, block_y, []

    def multiply_evens(evens):
        return dense_first(evens, span, dense) if is_dense else evens

    def multiply_odds(odds, evens, sums, before):
        if is_dense:
            return dense_second(odds, evens, sums, span, n_col, dense, before)
        return sparse_second(odds, evens, span, n_col, positions, a_digits)

    def multiply(evens, before):
        return multiply_odds(gather_odds(evens, "row"), evens, multiply_evens(evens), before)

    y_came = fetch_evens(block_y, "row")
    x_came = fetch_evens(block_x, "col")
    evens = stack_after([y_own] + y_came, [*before, *x_came])
    x_evens = stack_after([x_own] + x_came)
    outs = multiply(evens, [x_evens])
    x_pairs = [x_evens, gather_odds(x_evens, "col")]
    if is_dense:
        w_evens, w_odds = dense_left(x_pairs, n_row, dense, [outs[0]])
    else:
        w_evens, w_odds = sparse_left(x_pairs, n_row, positions, a_digits)
    vector_1 = sum_after(scatter_pieces(outs, "col"), [w_odds])
    w_came = fetch(w_odds, "row", 1)
    outs = multiply(gather_evens(vector_1, "row"), [w_came])
    pieces = scatter_pieces(outs, "col")
    w_kept, shift, before = w_evens, 2, []
    while shift < n_row:
        w_kept, w_sent = add_and_part(w_kept, w_came, before)
        w_came = fetch(w_sent, "row", shift)
        shift, before = 2 * shift, [outs[0]]
    vector_2 = append_projections([w_kept[0], w_came[0]], pieces, [y_own, vector_1])
    outs = multiply(gather_evens(vector_2, "row"), [])
    pieces = scatter_pieces(outs, "col")
    terms = functools.reduce(jnp.add, [piece[span:] for piece in pieces])
    vector_3 = functools.reduce(jnp.add, [piece[:span] for piece in pieces])
    return sigma_update(terms, fetch(terms, "row", 1), span), canonical(vector_3) * (1.0 / MODULUS)


def solution(mesh):
    placed = (
        P("row", "col", None, None, None),
        P("row", "col", None),
        P("row", "col", None),
        P("row", "col"),
        P(None, ("row", "col")),
        P(None, ("row", "col")),
    )
    return jax.shard_map(
        local, mesh=mesh, in_specs=placed, out_specs=(P(), P(None, ("row", "col"))), check_vma=False
    )
```

```python
import functools

import jax
import jax.numpy as jnp
from jax import lax
from jax.experimental import pallas as pl
from jax.experimental.pallas import tpu as pltpu
from jax.sharding import PartitionSpec as P

STEP_COUNT = 3

MODULUS = 65521.0
HALF_MODULUS = 32760.0
BASE = 256.0
EXACT_DEPTH = 1024
DENSE_CELLS = 4
VMEM_LIMIT = 16 * 1024 * 1024
SMALL_LIMIT = 4 * 1024 * 1024


def reduce_centered(values):
    return values - MODULUS * jnp.floor(values * (1.0 / MODULUS) + 0.5)


def canonical(values):
    reduced = reduce_centered(values)
    return jnp.where(reduced < 0, reduced + MODULUS, reduced)


def balanced_digits(values):
    high = jnp.floor(values * (1.0 / BASE) + 0.5)
    return high, values - BASE * high


def stacked_digits(values):
    high, low = balanced_digits(values)
    return jnp.concatenate([high, low], 0).astype(jnp.bfloat16)


def centred_digits(residues):
    return stacked_digits(jnp.where(residues > HALF_MODULUS, residues - MODULUS, residues))


def partner(index, shift, size):
    return index ^ shift if size & (size - 1) == 0 else (index + shift) % size


def shift_of(index, other, size):
    return index ^ other if size & (size - 1) == 0 else (other - index) % size


def fetch(piece, axis, shift):
    size = lax.axis_size(axis)
    return lax.ppermute(piece, axis, [(partner(i, shift, size), i) for i in range(size)])


def scatter_pieces(pieces, axis):
    size = lax.axis_size(axis)
    came = [
        lax.ppermute(pieces[shift], axis, [(i, partner(i, shift, size)) for i in range(size)])
        for shift in reversed(range(1, size))
    ]
    return [pieces[0]] + came


def call(kernel, operands, outs, before=(), scratch=(), limit=SMALL_LIMIT, flops=0):
    def body(*refs):
        kernel(*refs[: len(operands)], *refs[len(operands) + len(before) :])

    vmem = pl.BlockSpec(memory_space=pltpu.VMEM)
    return pl.pallas_call(
        body,
        in_specs=[vmem] * len(operands) + [pl.BlockSpec(memory_space=pl.ANY)] * len(before),
        out_specs=[vmem] * len(outs),
        out_shape=outs,
        scratch_shapes=list(scratch),
        compiler_params=pltpu.CompilerParams(vmem_limit_bytes=limit),
        cost_estimate=pl.CostEstimate(flops=flops, bytes_accessed=0, transcendentals=0),
    )(*(pltpu.with_memory_space_constraint(part, pltpu.VMEM) for part in operands), *before)


def held(*shape):
    return pltpu.VMEM(shape, jnp.float32)


def stack_after(pieces, before=()):
    def kernel(*refs):
        for index, ref in enumerate(refs[:-1]):
            refs[-1][index] = ref[...]

    return call(kernel, pieces, [held(len(pieces), *pieces[0].shape)], before)[0]


def sum_after(pieces, before=()):
    def kernel(*refs):
        refs[-1][...] = functools.reduce(jnp.add, [ref[...] for ref in refs[:-1]])

    return call(kernel, pieces, [held(*pieces[0].shape)], before)[0]


def fetch_evens(piece, axis):
    return [fetch(piece, axis, shift) for shift in range(2, lax.axis_size(axis), 2)]


def fetch_odds(evens, axis):
    size = lax.axis_size(axis)
    assert size > 2 and size & (size - 1) == 0
    return fetch(evens, axis, 1)


def dot_pairs(left, right):
    return lax.dot_general(left, right, (((1,), (1,)), ((), ())), preferred_element_type=jnp.float32)


def combine(high, middle, low):
    return reduce_centered(15.0 * high + 256.0 * reduce_centered(middle) + low)


def pack_square(square, width):
    span = square.shape[0]
    rows = span * span // width
    return jnp.concatenate([square[j * rows : (j + 1) * rows] for j in range(width // span)], 1)


def unpack_square(packed, span):
    count = packed.shape[1] // span
    return jnp.concatenate([packed[:, j * span : (j + 1) * span] for j in range(count)], 0)


def build_kernel(sizes, *refs):
    entries_ref, x_ref, y_ref, dense_ref, x_out, y_out, token_ref = refs[3:10]
    rows_ref, cols_ref, count_ref, tiles, sems = refs[10:]
    n_row, n_col, piece_blocks, group = sizes
    _, _, slot_count, tile_len, _ = entries_ref.shape
    me_row, me_col = lax.axis_index("row"), lax.axis_index("col")
    chunk_count = slot_count // group

    def chunk(index):
        source = entries_ref.at[0, 0, pl.ds(index * group, group)]
        return pltpu.make_async_copy(source, tiles.at[pl.ds(index * group, group)], sems.at[index])

    small = [*zip(refs[:3], refs[10:13]), (y_ref, y_out), (x_ref, x_out)]
    small = [
        pltpu.make_async_copy(source, target, sems.at[chunk_count + index])
        for index, (source, target) in enumerate(small)
    ]
    for copy in small[:3]:
        copy.start()
    sure_count = min(2, chunk_count)
    for index in range(sure_count):
        chunk(index).start()

    def clear(block, carry):
        dense_ref[block] = jnp.zeros(dense_ref.shape[1:], dense_ref.dtype)
        return carry

    half = dense_ref.shape[0] // 2
    lax.fori_loop(0, half, clear, 0)
    for copy in small[:3]:
        copy.wait()
    used_count = jnp.maximum((count_ref[0, 0] + group - 1) // group, sure_count)
    for index in range(sure_count, chunk_count):

        @pl.when(index < used_count)
        def _():
            chunk(index).start()

    for copy in small[3:]:
        copy.start()
    lax.fori_loop(half, dense_ref.shape[0], clear, 0)

    def place(slot):
        row, col = rows_ref[0, 0, slot], cols_ref[0, 0, slot]
        row_shift = shift_of(me_col, row // piece_blocks, n_col)
        col_shift = shift_of(me_row, col // piece_blocks, n_row)
        col_place = col_shift % 2 * (n_row // 2) + col_shift // 2
        block = row_shift * piece_blocks + row % piece_blocks
        start = (col_place * piece_blocks + col % piece_blocks) * tile_len
        values = jnp.where(slot < count_ref[0, 0], tiles[slot], 0.0)
        values = jnp.where(values > HALF_MODULUS, values - MODULUS, values).T
        both = jnp.concatenate(balanced_digits(values), 1).astype(jnp.bfloat16)
        dense_ref[block, pl.ds(pl.multiple_of(start, tile_len), tile_len), :] = both

    def step(index, carry):
        chunk(index).wait()
        for offset in range(group):
            place(index * group + offset)
        return carry

    lax.fori_loop(0, used_count, step, 0)
    for copy in small[3:]:
        copy.wait()
    token_ref[...] = jnp.zeros_like(token_ref)


def build_dense(tiles, block_x, block_y, sizes):
    tile_rows, tile_cols, tile_count, tile_entries = tiles
    n_row, n_col, piece_blocks = sizes
    _, _, slot_count, tile_len, _ = tile_entries.shape
    group = next(size for size in (8, 4, 2, 1) if slot_count % size == 0)
    shape = (n_col * piece_blocks, n_row * piece_blocks * tile_len, 2 * tile_len)
    hbm = pl.BlockSpec(memory_space=pltpu.HBM)
    rows, cols, entries, x_piece, y_piece = (
        pltpu.with_memory_space_constraint(part, pltpu.HBM)
        for part in (tile_rows, tile_cols, tile_entries, block_x, block_y)
    )
    return pl.pallas_call(
        functools.partial(build_kernel, (*sizes, group)),
        in_specs=[hbm, hbm, pl.BlockSpec(memory_space=pl.ANY), hbm, hbm, hbm],
        out_specs=[pl.BlockSpec(memory_space=pltpu.VMEM)] * 4,
        out_shape=[
            pltpu.VMEM(shape, jnp.bfloat16),
            held(*block_x.shape),
            held(*block_y.shape),
            held(8, 128),
        ],
        scratch_shapes=[
            *(pltpu.SMEM(part.shape, part.dtype) for part in (tile_rows, tile_cols, tile_count)),
            pltpu.VMEM((slot_count, tile_len, tile_len), jnp.float32),
            pltpu.SemaphoreType.DMA((slot_count // group + 5,)),
        ],
        compiler_params=pltpu.CompilerParams(vmem_limit_bytes=VMEM_LIMIT),
        cost_estimate=pl.CostEstimate(
            flops=8 * tile_entries.size, bytes_accessed=8 * tile_entries.size, transcendentals=0
        ),
    )(rows, cols, tile_count, entries, x_piece, y_piece)


def part_products(start, span, dense_ref, digits, block):
    tile_len = dense_ref.shape[2] // 2
    high = middle = low = 0.0
    for begin in range(0, digits.shape[1], EXACT_DEPTH):
        end = min(begin + EXACT_DEPTH, digits.shape[1])
        products = jnp.dot(
            digits[:, begin:end],
            dense_ref[block, start + begin : start + end, :],
            preferred_element_type=jnp.float32,
        )
        products = reduce_centered(products)
        high = high + products[:span, :tile_len]
        middle = middle + products[:span, tile_len:] + products[span:, :tile_len]
        low = low + products[span:, tile_len:]
    return high, middle, low


def fill_digits(span, pieces, digits):
    for d, piece in enumerate(pieces):
        piece_len = piece.shape[1]
        vector = reduce_centered(piece[:span])
        digits[:, d * piece_len : (d + 1) * piece_len] = stacked_digits(vector)


def first_part_kernel(span, own_ref, evens_ref, odd_ref, dense_ref, sums_ref, digits):
    evens = [evens_ref[index] for index in range(evens_ref.shape[0])]
    fill_digits(span, [own_ref[...], *evens, odd_ref[...]], digits)
    tile_len = dense_ref.shape[2] // 2
    for block in range(dense_ref.shape[0]):
        parts = part_products(0, span, dense_ref, digits, block)
        for index, part in enumerate(parts):
            sums_ref[index, :, block * tile_len : (block + 1) * tile_len] = part


def half_of_core(packed):
    rows = packed.shape[0] // 2
    return jnp.where(lax.axis_index("row") % 2 == 0, packed[:rows], packed[rows:])


def second_part_kernel(span, odds_ref, own_ref, evens_ref, odd_ref, sums_ref, dense_ref, *refs):
    outs, digits = refs[:-1], refs[-1]
    n_col = len(outs)
    fill_digits(span, [odds_ref[index] for index in range(odds_ref.shape[0])], digits)
    row_blocks, depth, width = dense_ref.shape
    tile_len = width // 2
    piece_blocks = row_blocks // n_col
    for e in reversed(range(n_col)):
        for sub in range(piece_blocks):
            block = e * piece_blocks + sub
            parts = part_products(depth - digits.shape[1], span, dense_ref, digits, block)
            parts = (
                part + sums_ref[index, :, block * tile_len : (block + 1) * tile_len]
                for index, part in enumerate(parts)
            )
            outs[e][:span, sub * tile_len : (sub + 1) * tile_len] = combine(*parts)
    if outs[0].shape[0] > span:
        packed = own_ref[span:, :] + odd_ref[span:, :]
        packed = packed + jnp.sum(evens_ref[:, span:, :], 0) + jnp.sum(odds_ref[:, span:, :], 0)
        packed = half_of_core(packed)
        for out in outs:
            out[span:, :] = packed


def dense_first(known, span, dense):
    row_blocks, _, width = dense.shape
    columns = (known[1].shape[0] + 2) * known[0].shape[1]
    return call(
        functools.partial(first_part_kernel, span),
        [*known, dense],
        [held(3, span, row_blocks * width // 2)],
        scratch=[pltpu.VMEM((2 * span, columns), jnp.bfloat16)],
        limit=VMEM_LIMIT,
        flops=2 * span * dense.size,
    )[0]


def dense_second(odds, known, sums, span, n_col, dense, before):
    _, rows, piece_len = odds.shape
    return list(
        call(
            functools.partial(second_part_kernel, span),
            [odds, *known, sums, dense],
            [held(span + (rows - span) // 2, piece_len)] * n_col,
            before,
            scratch=[pltpu.VMEM((2 * span, odds.shape[0] * piece_len), jnp.bfloat16)],
            limit=VMEM_LIMIT,
            flops=2 * span * dense.size,
        )
    )


def left_kernel(n_row, x_evens, x_odds, dense_ref, evens_ref, odds_ref):
    row_blocks, _, width = dense_ref.shape
    tile_len = width // 2
    _, span, piece_len = x_evens.shape
    piece_blocks = piece_len // tile_len
    x_digits = [
        centred_digits((x_odds if e % 2 else x_evens)[e // 2])
        for e in range(row_blocks // piece_blocks)
    ]
    for place in range(n_row):
        by_high = by_low = high_part = low_part = 0.0
        for block in range(row_blocks):
            sub = block % piece_blocks
            left = x_digits[block // piece_blocks][:, sub * tile_len : (sub + 1) * tile_len]
            right = dense_ref[block, place * piece_len : (place + 1) * piece_len, :]
            high_part = high_part + dot_pairs(left, right[:, :tile_len])
            low_part = low_part + dot_pairs(left, right[:, tile_len:])
            if (block + 1) * tile_len % EXACT_DEPTH == 0 or block == row_blocks - 1:
                by_high = by_high + reduce_centered(high_part)
                by_low = by_low + reduce_centered(low_part)
                high_part = low_part = 0.0
        piece = combine(by_high[:span], by_low[:span] + by_high[span:], by_low[span:])
        if place < n_row // 2:
            evens_ref[place] = piece
        else:
            odds_ref[place - n_row // 2] = piece


def dense_left(x_pairs, n_row, dense, before):
    _, span, piece_len = x_pairs[0].shape
    return call(
        functools.partial(left_kernel, n_row),
        [*x_pairs, dense],
        [held(n_row // 2, span, piece_len)] * 2,
        before,
        limit=VMEM_LIMIT,
        flops=4 * span * dense.size,
    )


def sparse_tiles(tiles, sizes):
    tile_rows, tile_cols, tile_count, tile_entries = tiles
    n_row, n_col, piece_blocks = sizes
    entries, rows, cols = tile_entries[0, 0], tile_rows[0, 0], tile_cols[0, 0]
    row_shift = shift_of(lax.axis_index("col"), rows // piece_blocks, n_col)
    col_shift = shift_of(lax.axis_index("row"), cols // piece_blocks, n_row)
    col_place = col_shift % 2 * (n_row // 2) + col_shift // 2
    positions = (
        row_shift * piece_blocks + rows % piece_blocks,
        col_place * piece_blocks + cols % piece_blocks,
        tile_count[0, 0],
    )
    entries = jnp.where(entries > HALF_MODULUS, entries - MODULUS, entries)
    return positions, jnp.stack(balanced_digits(entries), 1).astype(jnp.bfloat16)


def sparse_product(vector, spec, places, targets, count, blocks, a_digits):
    span, tile_len = vector.shape[0], a_digits.shape[-1]
    v_digits = stacked_digits(vector).reshape(2 * span, -1, tile_len)
    picked = jnp.take(v_digits, places, axis=1)
    products = jnp.einsum(spec, picked, a_digits, preferred_element_type=jnp.float32)
    products = reduce_centered(products)
    residues = combine(
        products[:, 0, :span],
        products[:, 0, span:] + products[:, 1, :span],
        products[:, 1, span:],
    )
    live = jnp.arange(targets.shape[0], dtype=jnp.int32) < count
    onehot = targets[None, :] == jnp.arange(blocks, dtype=jnp.int32)[:, None]
    onehot = (onehot & live[None, :]).astype(jnp.float32)
    summed = jnp.einsum("bt,twi->wbi", onehot, residues, precision=lax.Precision.HIGHEST)
    return reduce_centered(summed).reshape(span, blocks * tile_len)


def sparse_second(odds, known, span, n_col, positions, a_digits):
    rows, cols, count = positions
    own, evens, odd = known
    pieces = [own, *evens, odd, *odds]
    piece_len = pieces[0].shape[1]
    blocks = n_col * piece_len // a_digits.shape[-1]
    vector = reduce_centered(jnp.concatenate([piece[:span] for piece in pieces], 1))
    product = sparse_product(vector, "ntk,tdik->tdni", cols, rows, count, blocks, a_digits)
    packed = half_of_core(functools.reduce(jnp.add, [piece[span:] for piece in pieces]))
    outs = [product[:, e * piece_len : (e + 1) * piece_len] for e in range(n_col)]
    return [jnp.concatenate([out, packed], 0) for out in outs]


def sparse_left(x_pairs, n_row, positions, a_digits):
    rows, cols, count = positions
    n_col = 2 * x_pairs[0].shape[0]
    x_pieces = [x_pairs[e % 2][e // 2] for e in range(n_col)]
    piece_len = x_pieces[0].shape[1]
    values = jnp.concatenate(x_pieces, 1)
    values = jnp.where(values > HALF_MODULUS, values - MODULUS, values)
    blocks = n_row * piece_len // a_digits.shape[-1]
    product = sparse_product(values, "nti,tdik->tdnk", rows, cols, count, blocks, a_digits)
    pieces = [product[:, d * piece_len : (d + 1) * piece_len] for d in range(n_row)]
    return jnp.stack(pieces[: n_row // 2]), jnp.stack(pieces[n_row // 2 :])


def add_and_part(kept, came, before=()):
    def kernel(kept_ref, came_ref, evens_ref, odds_ref):
        for index in range(kept.shape[0]):
            (odds_ref if index % 2 else evens_ref)[index // 2] = kept_ref[index] + came_ref[index]

    return call(kernel, [kept, came], [held(kept.shape[0] // 2, *kept.shape[1:])] * 2, before)


def append_projections(w_parts, pieces, earlier):
    span, piece_len = pieces[0].shape
    rows = span * span // piece_len

    def kernel(*refs):
        piece_refs, refs = refs[: len(pieces)], refs[len(pieces) :]
        earlier_refs, refs = refs[: len(earlier)], refs[len(earlier) :]
        w_refs, out_ref = refs[:-1], refs[-1]
        summed = functools.reduce(jnp.add, [ref[...] for ref in piece_refs])
        out_ref[:span, :] = summed
        w_piece = functools.reduce(jnp.add, [ref[...] for ref in w_refs])
        w_digits = stacked_digits(reduce_centered(w_piece))
        for index, vector in enumerate([summed] + [ref[...] for ref in earlier_refs]):
            products = dot_pairs(w_digits, stacked_digits(reduce_centered(vector)))
            square = combine(
                reduce_centered(products[:span, :span]),
                reduce_centered(products[:span, span:]) + reduce_centered(products[span:, :span]),
                reduce_centered(products[span:, span:]),
            )
            start = span + index * rows
            out_ref[start : start + rows, :] = pack_square(square, piece_len)

    outs = [held(span + (len(earlier) + 1) * rows, piece_len)]
    return call(kernel, [*pieces, *earlier, *w_parts], outs)[0]


def multiply_mod(left, right):
    span = left.shape[0]
    left = stacked_digits(left)
    high, low = (part.astype(jnp.bfloat16) for part in balanced_digits(right))
    by_high = jnp.dot(left, high, preferred_element_type=jnp.float32)
    by_low = jnp.dot(left, low, preferred_element_type=jnp.float32)
    return combine(
        reduce_centered(by_high[:span]), by_low[:span] + by_high[span:], by_low[span:]
    )


def sigma_update(mine, other, span):
    rows = span * span // mine.shape[1]

    def kernel(mine_ref, other_ref, out_ref):
        first = lax.axis_index("row") % 2 == 0
        mine, other = reduce_centered(mine_ref[...]), reduce_centered(other_ref[...])
        packed = jnp.concatenate([jnp.where(first, mine, other), jnp.where(first, other, mine)], 0)
        c_3, c_1, c_2 = (
            unpack_square(packed[index * rows : (index + 1) * rows], span) for index in range(3)
        )
        e_2 = reduce_centered(c_1 - multiply_mod(c_1, c_2))
        both = reduce_centered(c_1 + e_2)
        start = multiply_mod(e_2, c_1)
        rest = c_1 - multiply_mod(both, c_2)
        e_3 = reduce_centered(multiply_mod(start, c_3) + rest)
        out_ref[0] = canonical(-multiply_mod(e_3, start)) * (1.0 / MODULUS)
        out_ref[1] = canonical(start + multiply_mod(e_3, both)) * (1.0 / MODULUS)
        out_ref[2] = canonical(-both - e_3) * (1.0 / MODULUS)

    outs = [jax.ShapeDtypeStruct((STEP_COUNT, span, span), jnp.float32)]
    return call(kernel, [mine, other], outs)[0]


def local(tile_entries, tile_rows, tile_cols, tile_count, block_x, block_y):
    _, _, slot_count, tile_len, _ = tile_entries.shape
    span, piece_len = block_y.shape
    piece_blocks = piece_len // tile_len
    n_row, n_col = lax.axis_size("row"), lax.axis_size("col")
    packed_rows = span * span // piece_len
    tiles = (tile_rows, tile_cols, tile_count, tile_entries)
    sizes = (n_row, n_col, piece_blocks)
    is_dense = n_col * piece_blocks * n_row * piece_blocks <= DENSE_CELLS * slot_count
    if is_dense:
        dense, x_own, y_own, token = build_dense(tiles, block_x, block_y, sizes)
        before = [token]
    else:
        positions, a_digits = sparse_tiles(tiles, sizes)
        x_own, y_own, before = block_x, block_y, []

    def multiply(own, piece, before=(), stack_before=()):
        evens = fetch_evens(piece, "row")
        odd = fetch(piece, "row", 1)
        evens = stack_after(evens, [odd, *stack_before])
        odds = fetch_odds(evens, "row")
        known = [own, evens, odd]
        if is_dense:
            sums = dense_first(known, span, dense)
            return dense_second(odds, known, sums, span, n_col, dense, before)
        return sparse_second(odds, known, span, n_col, positions, a_digits)

    x_came = fetch_evens(block_x, "col")
    x_evens = stack_after([x_own] + x_came)
    outs = multiply(y_own, block_y, [x_evens], [*before, *x_came])
    x_pairs = [x_evens, fetch_odds(x_evens, "col")]
    if is_dense:
        w_evens, w_odds = dense_left(x_pairs, n_row, dense, [outs[0]])
    else:
        w_evens, w_odds = sparse_left(x_pairs, n_row, positions, a_digits)
    vector_1 = sum_after(scatter_pieces(outs, "col"), [w_odds])
    w_came = fetch(sum_after([w_odds], [vector_1]), "row", 1)
    outs = multiply(vector_1, vector_1, [w_came])
    pieces = scatter_pieces(outs, "col")
    w_kept, shift, before = w_evens, 2, []
    while shift < n_row:
        w_kept, w_sent = add_and_part(w_kept, w_came, before)
        w_came = fetch(w_sent, "row", shift)
        shift, before = 2 * shift, [outs[0]]
    vector_2 = append_projections([w_kept[0], w_came[0]], pieces, [y_own, vector_1])
    outs = multiply(vector_2, vector_2)
    pieces = scatter_pieces(outs, "col")
    terms = functools.reduce(jnp.add, [piece[span:] for piece in pieces])
    vector_3 = functools.reduce(jnp.add, [piece[:span] for piece in pieces])
    return sigma_update(terms, fetch(terms, "row", 1), span), canonical(vector_3) * (1.0 / MODULUS)


def solution(mesh):
    placed = (
        P("row", "col", None, None, None),
        P("row", "col", None),
        P("row", "col", None),
        P("row", "col"),
        P(None, ("row", "col")),
        P(None, ("row", "col")),
    )
    return jax.shard_map(
        local, mesh=mesh, in_specs=placed, out_specs=(P(), P(None, ("row", "col"))), check_vma=False
    )
```

```python
import functools

import jax
import jax.numpy as jnp
from jax import lax
from jax.experimental import pallas as pl
from jax.experimental.pallas import tpu as pltpu
from jax.sharding import PartitionSpec as P

STEP_COUNT = 3

MODULUS = 65521.0
HALF_MODULUS = 32760.0
BASE = 256.0
EXACT_DEPTH = 1024
DENSE_CELLS = 4
VMEM_LIMIT = 16 * 1024 * 1024
SMALL_LIMIT = 4 * 1024 * 1024


def reduce_centered(values):
    return values - MODULUS * jnp.floor(values * (1.0 / MODULUS) + 0.5)


def canonical(values):
    reduced = reduce_centered(values)
    return jnp.where(reduced < 0, reduced + MODULUS, reduced)


def balanced_digits(values):
    high = jnp.floor(values * (1.0 / BASE) + 0.5)
    return high, values - BASE * high


def stacked_digits(values):
    high, low = balanced_digits(values)
    return jnp.concatenate([high, low], 0).astype(jnp.bfloat16)


def centred_digits(residues):
    return stacked_digits(jnp.where(residues > HALF_MODULUS, residues - MODULUS, residues))


def partner(index, shift, size):
    return index ^ shift if size & (size - 1) == 0 else (index + shift) % size


def shift_of(index, other, size):
    return index ^ other if size & (size - 1) == 0 else (other - index) % size


def fetch(piece, axis, shift):
    size = lax.axis_size(axis)
    return lax.ppermute(piece, axis, [(partner(i, shift, size), i) for i in range(size)])


def scatter_pieces(pieces, axis):
    size = lax.axis_size(axis)
    came = [
        lax.ppermute(pieces[shift], axis, [(i, partner(i, shift, size)) for i in range(size)])
        for shift in reversed(range(1, size))
    ]
    return [pieces[0]] + came


def call(kernel, operands, outs, before=(), scratch=(), limit=SMALL_LIMIT, flops=0):
    def body(*refs):
        kernel(*refs[: len(operands)], *refs[len(operands) + len(before) :])

    vmem = pl.BlockSpec(memory_space=pltpu.VMEM)
    return pl.pallas_call(
        body,
        in_specs=[vmem] * len(operands) + [pl.BlockSpec(memory_space=pl.ANY)] * len(before),
        out_specs=[vmem] * len(outs),
        out_shape=outs,
        scratch_shapes=list(scratch),
        compiler_params=pltpu.CompilerParams(vmem_limit_bytes=limit),
        cost_estimate=pl.CostEstimate(flops=flops, bytes_accessed=0, transcendentals=0),
    )(*(pltpu.with_memory_space_constraint(part, pltpu.VMEM) for part in operands), *before)


def held(*shape):
    return pltpu.VMEM(shape, jnp.float32)


def stack_after(pieces, before=()):
    def kernel(*refs):
        for index, ref in enumerate(refs[:-1]):
            refs[-1][index] = ref[...]

    return call(kernel, pieces, [held(len(pieces), *pieces[0].shape)], before)[0]


def sum_after(pieces, before=()):
    def kernel(*refs):
        refs[-1][...] = functools.reduce(jnp.add, [ref[...] for ref in refs[:-1]])

    return call(kernel, pieces, [held(*pieces[0].shape)], before)[0]


def fetch_evens(piece, axis):
    return [fetch(piece, axis, shift) for shift in range(2, lax.axis_size(axis), 2)]


def gather_evens(piece, axis, before=()):
    return stack_after([piece] + fetch_evens(piece, axis), before)


def gather_odds(evens, axis):
    size = lax.axis_size(axis)
    assert size > 1 and size & (size - 1) == 0
    return fetch(evens, axis, 1)


def dot_pairs(left, right):
    return lax.dot_general(left, right, (((1,), (1,)), ((), ())), preferred_element_type=jnp.float32)


def combine(high, middle, low):
    return reduce_centered(15.0 * high + 256.0 * reduce_centered(middle) + low)


def pack_square(square, width):
    span = square.shape[0]
    rows = span * span // width
    return jnp.concatenate([square[j * rows : (j + 1) * rows] for j in range(width // span)], 1)


def unpack_square(packed, span):
    count = packed.shape[1] // span
    return jnp.concatenate([packed[:, j * span : (j + 1) * span] for j in range(count)], 0)


def build_kernel(sizes, *refs):
    entries_ref, x_ref, y_ref, dense_ref, x_out, y_out, token_ref = refs[3:10]
    rows_ref, cols_ref, count_ref, tiles, sems = refs[10:]
    n_row, n_col, piece_blocks, group = sizes
    _, _, slot_count, tile_len, _ = entries_ref.shape
    me_row, me_col = lax.axis_index("row"), lax.axis_index("col")
    chunk_count = slot_count // group

    def chunk(index):
        source = entries_ref.at[0, 0, pl.ds(index * group, group)]
        return pltpu.make_async_copy(source, tiles.at[pl.ds(index * group, group)], sems.at[index])

    small = [*zip(refs[:3], refs[10:13]), (y_ref, y_out), (x_ref, x_out)]
    small = [
        pltpu.make_async_copy(source, target, sems.at[chunk_count + index])
        for index, (source, target) in enumerate(small)
    ]
    for copy in small[:3]:
        copy.start()
    sure_count = min(2, chunk_count)
    for index in range(sure_count):
        chunk(index).start()

    def clear(block, carry):
        dense_ref[block] = jnp.zeros(dense_ref.shape[1:], dense_ref.dtype)
        return carry

    half = dense_ref.shape[0] // 2
    lax.fori_loop(0, half, clear, 0)
    for copy in small[:3]:
        copy.wait()
    used_count = jnp.maximum((count_ref[0, 0] + group - 1) // group, sure_count)
    for index in range(sure_count, chunk_count):

        @pl.when(index < used_count)
        def _():
            chunk(index).start()

    for copy in small[3:]:
        copy.start()
    lax.fori_loop(half, dense_ref.shape[0], clear, 0)

    def place(slot):
        row, col = rows_ref[0, 0, slot], cols_ref[0, 0, slot]
        row_shift = shift_of(me_col, row // piece_blocks, n_col)
        col_shift = shift_of(me_row, col // piece_blocks, n_row)
        col_place = col_shift % 2 * (n_row // 2) + col_shift // 2
        block = row_shift * piece_blocks + row % piece_blocks
        start = (col_place * piece_blocks + col % piece_blocks) * tile_len
        values = jnp.where(slot < count_ref[0, 0], tiles[slot], 0.0)
        values = jnp.where(values > HALF_MODULUS, values - MODULUS, values).T
        both = jnp.concatenate(balanced_digits(values), 1).astype(jnp.bfloat16)
        dense_ref[block, pl.ds(pl.multiple_of(start, tile_len), tile_len), :] = both

    def step(index, carry):
        chunk(index).wait()
        for offset in range(group):
            place(index * group + offset)
        return carry

    lax.fori_loop(0, used_count, step, 0)
    for copy in small[3:]:
        copy.wait()
    token_ref[...] = jnp.zeros_like(token_ref)


def build_dense(tiles, block_x, block_y, sizes):
    tile_rows, tile_cols, tile_count, tile_entries = tiles
    n_row, n_col, piece_blocks = sizes
    _, _, slot_count, tile_len, _ = tile_entries.shape
    group = next(size for size in (8, 4, 2, 1) if slot_count % size == 0)
    shape = (n_col * piece_blocks, n_row * piece_blocks * tile_len, 2 * tile_len)
    hbm = pl.BlockSpec(memory_space=pltpu.HBM)
    rows, cols, entries, x_piece, y_piece = (
        pltpu.with_memory_space_constraint(part, pltpu.HBM)
        for part in (tile_rows, tile_cols, tile_entries, block_x, block_y)
    )
    return pl.pallas_call(
        functools.partial(build_kernel, (*sizes, group)),
        in_specs=[hbm, hbm, pl.BlockSpec(memory_space=pl.ANY), hbm, hbm, hbm],
        out_specs=[pl.BlockSpec(memory_space=pltpu.VMEM)] * 4,
        out_shape=[
            pltpu.VMEM(shape, jnp.bfloat16),
            held(*block_x.shape),
            held(*block_y.shape),
            held(8, 128),
        ],
        scratch_shapes=[
            *(pltpu.SMEM(part.shape, part.dtype) for part in (tile_rows, tile_cols, tile_count)),
            pltpu.VMEM((slot_count, tile_len, tile_len), jnp.float32),
            pltpu.SemaphoreType.DMA((slot_count // group + 5,)),
        ],
        compiler_params=pltpu.CompilerParams(vmem_limit_bytes=VMEM_LIMIT),
        cost_estimate=pl.CostEstimate(
            flops=8 * tile_entries.size, bytes_accessed=8 * tile_entries.size, transcendentals=0
        ),
    )(rows, cols, tile_count, entries, x_piece, y_piece)


def half_products(half, span, pieces_ref, dense_ref, digits, block):
    _, depth, width = dense_ref.shape
    tile_len, half_depth = width // 2, depth // 2
    high = middle = low = 0.0
    for start in range(0, half_depth, EXACT_DEPTH):
        stop = min(start + EXACT_DEPTH, half_depth)
        products = jnp.dot(
            digits[:, start:stop],
            dense_ref[block, half * half_depth + start : half * half_depth + stop, :],
            preferred_element_type=jnp.float32,
        )
        products = reduce_centered(products)
        high = high + products[:span, :tile_len]
        middle = middle + products[:span, tile_len:] + products[span:, :tile_len]
        low = low + products[span:, tile_len:]
    return high, middle, low


def fill_digits(span, pieces_ref, digits):
    piece_len = pieces_ref.shape[2]
    for d in range(pieces_ref.shape[0]):
        vector = reduce_centered(pieces_ref[d, :span, :])
        digits[:, d * piece_len : (d + 1) * piece_len] = stacked_digits(vector)


def first_half_kernel(span, pieces_ref, dense_ref, sums_ref, digits):
    fill_digits(span, pieces_ref, digits)
    tile_len = dense_ref.shape[2] // 2
    for block in range(dense_ref.shape[0]):
        parts = half_products(0, span, pieces_ref, dense_ref, digits, block)
        for index, part in enumerate(parts):
            sums_ref[index, :, block * tile_len : (block + 1) * tile_len] = part


def half_of_core(packed):
    rows = packed.shape[0] // 2
    return jnp.where(lax.axis_index("row") % 2 == 0, packed[:rows], packed[rows:])


def second_half_kernel(span, n_col, pieces_ref, evens_ref, sums_ref, dense_ref, *refs):
    tails, outs, digits = refs[: -n_col - 1], refs[-n_col - 1 : -1], refs[-1]
    fill_digits(span, pieces_ref, digits)
    row_blocks, _, width = dense_ref.shape
    tile_len = width // 2
    piece_blocks = row_blocks // n_col
    for e in reversed(range(n_col)):
        for sub in range(piece_blocks):
            block = e * piece_blocks + sub
            parts = half_products(1, span, pieces_ref, dense_ref, digits, block)
            parts = (
                part + sums_ref[index, :, block * tile_len : (block + 1) * tile_len]
                for index, part in enumerate(parts)
            )
            outs[e][:span, sub * tile_len : (sub + 1) * tile_len] = combine(*parts)
    if outs[0].shape[0] > span:
        packed = jnp.sum(pieces_ref[:, span:, :], 0) + jnp.sum(evens_ref[:, span:, :], 0)
        packed = half_of_core(jnp.concatenate([packed, *(tail[...] for tail in tails)], 0))
        for out in outs:
            out[span:, :] = packed


def dense_first(evens, span, dense):
    row_blocks, depth, width = dense.shape
    return call(
        functools.partial(first_half_kernel, span),
        [evens, dense],
        [held(3, span, row_blocks * width // 2)],
        scratch=[pltpu.VMEM((2 * span, depth // 2), jnp.bfloat16)],
        limit=VMEM_LIMIT,
        flops=2 * span * dense.size,
    )[0]


def dense_second(odds, evens, sums, span, n_col, tails, dense, before):
    _, depth, _ = dense.shape
    _, rows, piece_len = odds.shape
    rows = rows + sum(tail.shape[0] for tail in tails)
    return list(
        call(
            functools.partial(second_half_kernel, span, n_col),
            [odds, evens, sums, dense, *tails],
            [held(span + (rows - span) // 2, piece_len)] * n_col,
            before,
            scratch=[pltpu.VMEM((2 * span, depth // 2), jnp.bfloat16)],
            limit=VMEM_LIMIT,
            flops=2 * span * dense.size,
        )
    )


def project(terms):
    products = functools.reduce(jnp.add, [dot_pairs(left, right) for left, right in terms])
    span = products.shape[0] // 2
    square = combine(
        reduce_centered(products[:span, :span]),
        reduce_centered(products[:span, span:]) + reduce_centered(products[span:, :span]),
        reduce_centered(products[span:, span:]),
    )
    return pack_square(square, terms[0][0].shape[1])


def left_kernel(n_row, x_evens, x_odds, dense_ref, *refs):
    rows_refs, (evens_ref, odds_ref, term_ref) = refs[:-3], refs[-3:]
    row_blocks, _, width = dense_ref.shape
    tile_len = width // 2
    _, span, piece_len = x_evens.shape
    piece_blocks = piece_len // tile_len
    x_digits = [
        centred_digits((x_odds if e % 2 else x_evens)[e // 2])
        for e in range(row_blocks // piece_blocks)
    ]
    term = project([(x, stacked_digits(ref[...])) for x, ref in zip(x_digits, rows_refs)])
    term_ref[...] = term
    part_rows = term.shape[0] // odds_ref.shape[0]
    for place in range(n_row):
        by_high = by_low = high_part = low_part = 0.0
        for block in range(row_blocks):
            sub = block % piece_blocks
            left = x_digits[block // piece_blocks][:, sub * tile_len : (sub + 1) * tile_len]
            right = dense_ref[block, place * piece_len : (place + 1) * piece_len, :]
            high_part = high_part + dot_pairs(left, right[:, :tile_len])
            low_part = low_part + dot_pairs(left, right[:, tile_len:])
            if (block + 1) * tile_len % EXACT_DEPTH == 0 or block == row_blocks - 1:
                by_high = by_high + reduce_centered(high_part)
                by_low = by_low + reduce_centered(low_part)
                high_part = low_part = 0.0
        piece = combine(by_high[:span], by_low[:span] + by_high[span:], by_low[span:])
        if place < n_row // 2:
            evens_ref[place] = piece
        else:
            index = place - n_row // 2
            odds_ref[index, :span, :] = piece
            odds_ref[index, span:, :] = term[index * part_rows : (index + 1) * part_rows]


def dense_left(x_pairs, outs, n_row, dense):
    _, span, piece_len = x_pairs[0].shape
    count, rows = n_row // 2, span * span // piece_len
    return call(
        functools.partial(left_kernel, n_row),
        [*x_pairs, dense, *outs],
        [
            held(count, span, piece_len),
            held(count, span + rows // count, piece_len),
            held(rows, piece_len),
        ],
        limit=VMEM_LIMIT,
        flops=4 * span * dense.size,
    )


def sparse_tiles(tiles, sizes):
    tile_rows, tile_cols, tile_count, tile_entries = tiles
    n_row, n_col, piece_blocks = sizes
    entries, rows, cols = tile_entries[0, 0], tile_rows[0, 0], tile_cols[0, 0]
    row_shift = shift_of(lax.axis_index("col"), rows // piece_blocks, n_col)
    col_shift = shift_of(lax.axis_index("row"), cols // piece_blocks, n_row)
    col_place = col_shift % 2 * (n_row // 2) + col_shift // 2
    positions = (
        row_shift * piece_blocks + rows % piece_blocks,
        col_place * piece_blocks + cols % piece_blocks,
        tile_count[0, 0],
    )
    entries = jnp.where(entries > HALF_MODULUS, entries - MODULUS, entries)
    return positions, jnp.stack(balanced_digits(entries), 1).astype(jnp.bfloat16)


def sparse_product(vector, spec, places, targets, count, blocks, a_digits):
    span, tile_len = vector.shape[0], a_digits.shape[-1]
    v_digits = stacked_digits(vector).reshape(2 * span, -1, tile_len)
    picked = jnp.take(v_digits, places, axis=1)
    products = jnp.einsum(spec, picked, a_digits, preferred_element_type=jnp.float32)
    products = reduce_centered(products)
    residues = combine(
        products[:, 0, :span],
        products[:, 0, span:] + products[:, 1, :span],
        products[:, 1, span:],
    )
    live = jnp.arange(targets.shape[0], dtype=jnp.int32) < count
    onehot = targets[None, :] == jnp.arange(blocks, dtype=jnp.int32)[:, None]
    onehot = (onehot & live[None, :]).astype(jnp.float32)
    summed = jnp.einsum("bt,twi->wbi", onehot, residues, precision=lax.Precision.HIGHEST)
    return reduce_centered(summed).reshape(span, blocks * tile_len)


def sparse_second(odds, evens, span, n_col, tails, positions, a_digits):
    rows, cols, count = positions
    pieces = [*evens, *odds]
    piece_len = pieces[0].shape[1]
    blocks = n_col * piece_len // a_digits.shape[-1]
    vector = reduce_centered(jnp.concatenate([piece[:span] for piece in pieces], 1))
    product = sparse_product(vector, "ntk,tdik->tdni", cols, rows, count, blocks, a_digits)
    packed = functools.reduce(jnp.add, [piece[span:] for piece in pieces])
    packed = half_of_core(jnp.concatenate([packed, *tails], 0))
    outs = [product[:, e * piece_len : (e + 1) * piece_len] for e in range(n_col)]
    return [jnp.concatenate([out, packed], 0) for out in outs]


def sparse_left(x_pairs, outs, n_row, positions, a_digits):
    rows, cols, count = positions
    n_col = 2 * x_pairs[0].shape[0]
    x_pieces = [x_pairs[e % 2][e // 2] for e in range(n_col)]
    piece_len = x_pieces[0].shape[1]
    values = jnp.concatenate(x_pieces, 1)
    values = jnp.where(values > HALF_MODULUS, values - MODULUS, values)
    blocks = n_row * piece_len // a_digits.shape[-1]
    product = sparse_product(values, "nti,tdik->tdnk", rows, cols, count, blocks, a_digits)
    pieces = [product[:, d * piece_len : (d + 1) * piece_len] for d in range(n_row)]
    term = 0.0
    for x_piece, rows_piece in zip(x_pieces, outs):
        term = term + project([(centred_digits(x_piece), stacked_digits(rows_piece))])
    odds = jnp.stack(pieces[n_row // 2 :])
    below = term.reshape(odds.shape[0], -1, piece_len)
    return jnp.stack(pieces[: n_row // 2]), jnp.concatenate([odds, below], 1), term


def add_and_part(kept, came, term, before=()):
    count, span, piece_len = kept.shape
    half, rows = count // 2, term.shape[0]
    part = rows // half if half > 1 else 0

    def kernel(kept_ref, came_ref, term_ref, evens_ref, odds_ref, out_ref):
        below = [came_ref[index, span:, :] for index in range(count)]
        total = term_ref[...] + jnp.concatenate(below, 0)
        out_ref[...] = total
        for index in range(count):
            piece = kept_ref[index] + came_ref[index, :span, :]
            if index % 2 == 0:
                evens_ref[index // 2] = piece
            else:
                odds_ref[index // 2, :span, :] = piece
        if part:
            for index in range(half):
                odds_ref[index, span:, :] = total[index * part : (index + 1) * part]

    outs = [
        held(half, span, piece_len),
        held(half, span + part, piece_len),
        held(rows, piece_len),
    ]
    return call(kernel, [kept, came, term], outs, before)


def append_projections(kept, came, term, term_came, pieces, vector_1):
    span, piece_len = pieces[0].shape
    rows = term.shape[0]

    def kernel(*refs):
        piece_refs, refs = refs[: len(pieces)], refs[len(pieces) :]
        vector_ref, kept_ref, came_ref, term_ref, term_came_ref, out_ref, first_ref = refs
        summed = functools.reduce(jnp.add, [ref[...] for ref in piece_refs])
        out_ref[:span, :] = summed
        w_digits = stacked_digits(reduce_centered(kept_ref[0] + came_ref[0]))
        first_ref[...] = term_ref[...] + term_came_ref[...]
        for index, vector in enumerate([summed, vector_ref[...]]):
            start = span + index * rows
            digits = stacked_digits(reduce_centered(vector))
            out_ref[start : start + rows, :] = project([(w_digits, digits)])

    outs = [held(span + 2 * rows, piece_len), held(rows, piece_len)]
    return call(kernel, [*pieces, vector_1, kept, came, term, term_came], outs)


def multiply_mod(left, right):
    span = left.shape[0]
    left = stacked_digits(left)
    high, low = (part.astype(jnp.bfloat16) for part in balanced_digits(right))
    by_high = jnp.dot(left, high, preferred_element_type=jnp.float32)
    by_low = jnp.dot(left, low, preferred_element_type=jnp.float32)
    return combine(
        reduce_centered(by_high[:span]), by_low[:span] + by_high[span:], by_low[span:]
    )


def sigma_update(mine, other, span):
    rows = span * span // mine.shape[1]

    def kernel(mine_ref, other_ref, out_ref):
        first = lax.axis_index("row") % 2 == 0
        mine, other = reduce_centered(mine_ref[...]), reduce_centered(other_ref[...])
        packed = jnp.concatenate([jnp.where(first, mine, other), jnp.where(first, other, mine)], 0)
        c_3, c_2, c_1 = (
            unpack_square(packed[index * rows : (index + 1) * rows], span) for index in range(3)
        )
        e_2 = reduce_centered(c_1 - multiply_mod(c_1, c_2))
        both = reduce_centered(c_1 + e_2)
        start = multiply_mod(e_2, c_1)
        rest = c_1 - multiply_mod(both, c_2)
        e_3 = reduce_centered(multiply_mod(start, c_3) + rest)
        out_ref[0] = canonical(-multiply_mod(e_3, start)) * (1.0 / MODULUS)
        out_ref[1] = canonical(start + multiply_mod(e_3, both)) * (1.0 / MODULUS)
        out_ref[2] = canonical(-both - e_3) * (1.0 / MODULUS)

    outs = [jax.ShapeDtypeStruct((STEP_COUNT, span, span), jnp.float32)]
    return call(kernel, [mine, other], outs)[0]


def local(tile_entries, tile_rows, tile_cols, tile_count, block_x, block_y):
    _, _, slot_count, tile_len, _ = tile_entries.shape
    span, piece_len = block_y.shape
    piece_blocks = piece_len // tile_len
    n_row, n_col = lax.axis_size("row"), lax.axis_size("col")
    packed_rows = span * span // piece_len
    tiles = (tile_rows, tile_cols, tile_count, tile_entries)
    sizes = (n_row, n_col, piece_blocks)
    is_dense = n_col * piece_blocks * n_row * piece_blocks <= DENSE_CELLS * slot_count
    if is_dense:
        dense, x_own, y_own, token = build_dense(tiles, block_x, block_y, sizes)
        before = [token]
    else:
        positions, a_digits = sparse_tiles(tiles, sizes)
        x_own, y_own, before = block_x, block_y, []

    def multiply_evens(evens):
        return dense_first(evens, span, dense) if is_dense else evens

    def multiply(evens, before=(), tails=()):
        odds, sums = gather_odds(evens, "row"), multiply_evens(evens)
        if is_dense:
            return dense_second(odds, evens, sums, span, n_col, tails, dense, before)
        return sparse_second(odds, evens, span, n_col, tails, positions, a_digits)

    y_came = fetch_evens(block_y, "row")
    x_came = fetch_evens(block_x, "col")
    evens = stack_after([y_own] + y_came, [*before, *x_came])
    x_evens = stack_after([x_own] + x_came)
    outs = multiply(evens, [x_evens])
    x_pairs = [x_evens, gather_odds(x_evens, "col")]
    if is_dense:
        w_kept, w_odds, term = dense_left(x_pairs, outs, n_row, dense)
    else:
        w_kept, w_odds, term = sparse_left(x_pairs, outs, n_row, positions, a_digits)
    vector_1 = sum_after(scatter_pieces(outs, "col"), [w_odds])
    w_came = fetch(w_odds, "row", 1)
    outs = multiply(gather_evens(vector_1, "row"), [w_came])
    pieces = scatter_pieces(outs, "col")
    shift, before = 2, []
    while shift < n_row:
        w_kept, w_sent, term = add_and_part(w_kept, w_came, term, before)
        w_came = fetch(w_sent, "row", shift)
        shift, before = 2 * shift, [outs[0]]
    term_came = fetch(term, "row", n_row // 2)
    vector_2, first = append_projections(w_kept, w_came, term, term_came, pieces, vector_1)
    outs = multiply(gather_evens(vector_2, "row"), tails=[first])
    pieces = scatter_pieces(outs, "col")
    terms = functools.reduce(jnp.add, [piece[span:] for piece in pieces])
    vector_3 = functools.reduce(jnp.add, [piece[:span] for piece in pieces])
    return sigma_update(terms, fetch(terms, "row", 1), span), canonical(vector_3) * (1.0 / MODULUS)


def solution(mesh):
    placed = (
        P("row", "col", None, None, None),
        P("row", "col", None),
        P("row", "col", None),
        P("row", "col"),
        P(None, ("row", "col")),
        P(None, ("row", "col")),
    )
    return jax.shard_map(
        local, mesh=mesh, in_specs=placed, out_specs=(P(), P(None, ("row", "col"))), check_vma=False
    )
```

```python
import functools

import jax
import jax.numpy as jnp
from jax import lax
from jax.experimental import pallas as pl
from jax.experimental.pallas import tpu as pltpu
from jax.sharding import PartitionSpec as P

STEP_COUNT = 3

MODULUS = 65521.0
HALF_MODULUS = 32760.0
BASE = 256.0
EXACT_DEPTH = 1024
DENSE_CELLS = 4
VMEM_LIMIT = 16 * 1024 * 1024
SMALL_LIMIT = 4 * 1024 * 1024


def reduce_centered(values):
    return values - MODULUS * jnp.floor(values * (1.0 / MODULUS) + 0.5)


def canonical(values):
    reduced = reduce_centered(values)
    return jnp.where(reduced < 0, reduced + MODULUS, reduced)


def balanced_digits(values):
    high = jnp.floor(values * (1.0 / BASE) + 0.5)
    return high, values - BASE * high


def stacked_digits(values):
    high, low = balanced_digits(values)
    return jnp.concatenate([high, low], 0).astype(jnp.bfloat16)


def centred_digits(residues):
    return stacked_digits(jnp.where(residues > HALF_MODULUS, residues - MODULUS, residues))


def partner(index, shift, size):
    return index ^ shift if size & (size - 1) == 0 else (index + shift) % size


def shift_of(index, other, size):
    return index ^ other if size & (size - 1) == 0 else (other - index) % size


def fetch(piece, axis, shift):
    size = lax.axis_size(axis)
    return lax.ppermute(piece, axis, [(partner(i, shift, size), i) for i in range(size)])


def scatter_pieces(pieces, axis):
    size = lax.axis_size(axis)
    came = [
        lax.ppermute(pieces[shift], axis, [(i, partner(i, shift, size)) for i in range(size)])
        for shift in reversed(range(1, size))
    ]
    return [pieces[0]] + came


def call(kernel, operands, outs, before=(), scratch=(), limit=SMALL_LIMIT, flops=0):
    def body(*refs):
        kernel(*refs[: len(operands)], *refs[len(operands) + len(before) :])

    vmem = pl.BlockSpec(memory_space=pltpu.VMEM)
    return pl.pallas_call(
        body,
        in_specs=[vmem] * len(operands) + [pl.BlockSpec(memory_space=pl.ANY)] * len(before),
        out_specs=[vmem] * len(outs),
        out_shape=outs,
        scratch_shapes=list(scratch),
        compiler_params=pltpu.CompilerParams(vmem_limit_bytes=limit),
        cost_estimate=pl.CostEstimate(flops=flops, bytes_accessed=0, transcendentals=0),
    )(*(pltpu.with_memory_space_constraint(part, pltpu.VMEM) for part in operands), *before)


def held(*shape):
    return pltpu.VMEM(shape, jnp.float32)


def stack_after(pieces, before=()):
    def kernel(*refs):
        for index, ref in enumerate(refs[:-1]):
            refs[-1][index] = ref[...]

    return call(kernel, pieces, [held(len(pieces), *pieces[0].shape)], before)[0]


def sum_after(pieces, before=()):
    def kernel(*refs):
        refs[-1][...] = functools.reduce(jnp.add, [ref[...] for ref in refs[:-1]])

    return call(kernel, pieces, [held(*pieces[0].shape)], before)[0]


def fetch_evens(piece, axis):
    return [fetch(piece, axis, shift) for shift in range(2, lax.axis_size(axis), 2)]


def gather_evens(piece, axis, before=()):
    return stack_after([piece] + fetch_evens(piece, axis), before)


def gather_odds(evens, axis):
    size = lax.axis_size(axis)
    assert size > 1 and size & (size - 1) == 0
    return fetch(evens, axis, 1)


def dot_pairs(left, right):
    return lax.dot_general(left, right, (((1,), (1,)), ((), ())), preferred_element_type=jnp.float32)


def combine(high, middle, low):
    return reduce_centered(15.0 * high + 256.0 * reduce_centered(middle) + low)


def pack_square(square, width):
    span = square.shape[0]
    rows = span * span // width
    return jnp.concatenate([square[j * rows : (j + 1) * rows] for j in range(width // span)], 1)


def unpack_square(packed, span):
    count = packed.shape[1] // span
    return jnp.concatenate([packed[:, j * span : (j + 1) * span] for j in range(count)], 0)


def build_kernel(sizes, *refs):
    entries_ref, dense_ref, token_ref, rows_ref, cols_ref, count_ref, tiles, sems = refs[3:]
    n_row, n_col, piece_blocks, group = sizes
    _, _, slot_count, tile_len, _ = entries_ref.shape
    me_row, me_col = lax.axis_index("row"), lax.axis_index("col")
    chunk_count = slot_count // group

    def chunk(index):
        source = entries_ref.at[0, 0, pl.ds(index * group, group)]
        return pltpu.make_async_copy(source, tiles.at[pl.ds(index * group, group)], sems.at[index])

    small = zip(refs[:3], (rows_ref, cols_ref, count_ref))
    small = [
        pltpu.make_async_copy(source, target, sems.at[chunk_count + index])
        for index, (source, target) in enumerate(small)
    ]
    for copy in small:
        copy.start()
    sure_count = min(2, chunk_count)
    for index in range(sure_count):
        chunk(index).start()

    def clear(block, carry):
        dense_ref[block] = jnp.zeros(dense_ref.shape[1:], dense_ref.dtype)
        return carry

    half = dense_ref.shape[0] // 2
    lax.fori_loop(0, half, clear, 0)
    for copy in small:
        copy.wait()
    used_count = jnp.maximum((count_ref[0, 0] + group - 1) // group, sure_count)
    for index in range(sure_count, chunk_count):

        @pl.when(index < used_count)
        def _():
            chunk(index).start()

    lax.fori_loop(half, dense_ref.shape[0], clear, 0)

    def place(slot):
        row, col = rows_ref[0, 0, slot], cols_ref[0, 0, slot]
        row_shift = shift_of(me_col, row // piece_blocks, n_col)
        col_shift = shift_of(me_row, col // piece_blocks, n_row)
        col_place = col_shift % 2 * (n_row // 2) + col_shift // 2
        block = row_shift * piece_blocks + row % piece_blocks
        start = (col_place * piece_blocks + col % piece_blocks) * tile_len
        values = jnp.where(slot < count_ref[0, 0], tiles[slot], 0.0)
        values = jnp.where(values > HALF_MODULUS, values - MODULUS, values).T
        both = jnp.concatenate(balanced_digits(values), 1).astype(jnp.bfloat16)
        dense_ref[block, pl.ds(pl.multiple_of(start, tile_len), tile_len), :] = both

    def step(index, carry):
        chunk(index).wait()
        for offset in range(group):
            place(index * group + offset)
        return carry

    lax.fori_loop(0, used_count, step, 0)
    token_ref[...] = jnp.zeros_like(token_ref)


def load_pieces(*pieces):
    def kernel(*refs):
        count, sems = len(pieces), refs[-1]
        copies = [
            pltpu.make_async_copy(refs[index], refs[count + index], sems.at[index])
            for index in range(count)
        ]
        for copy in copies:
            copy.start()
        for copy in copies:
            copy.wait()

    return pl.pallas_call(
        kernel,
        in_specs=[pl.BlockSpec(memory_space=pltpu.HBM)] * len(pieces),
        out_specs=[pl.BlockSpec(memory_space=pltpu.VMEM)] * len(pieces),
        out_shape=[held(*piece.shape) for piece in pieces],
        scratch_shapes=[pltpu.SemaphoreType.DMA((len(pieces),))],
        compiler_params=pltpu.CompilerParams(vmem_limit_bytes=SMALL_LIMIT),
    )(*(pltpu.with_memory_space_constraint(piece, pltpu.HBM) for piece in pieces))


def build_dense(tiles, sizes):
    tile_rows, tile_cols, tile_count, tile_entries = tiles
    n_row, n_col, piece_blocks = sizes
    _, _, slot_count, tile_len, _ = tile_entries.shape
    group = next(size for size in (8, 4, 2, 1) if slot_count % size == 0)
    shape = (n_col * piece_blocks, n_row * piece_blocks * tile_len, 2 * tile_len)
    hbm = pl.BlockSpec(memory_space=pltpu.HBM)
    rows, cols, entries = (
        pltpu.with_memory_space_constraint(part, pltpu.HBM)
        for part in (tile_rows, tile_cols, tile_entries)
    )
    return pl.pallas_call(
        functools.partial(build_kernel, (*sizes, group)),
        in_specs=[hbm, hbm, pl.BlockSpec(memory_space=pl.ANY), hbm],
        out_specs=[pl.BlockSpec(memory_space=pltpu.VMEM)] * 2,
        out_shape=[pltpu.VMEM(shape, jnp.bfloat16), held(8, 128)],
        scratch_shapes=[
            *(pltpu.SMEM(part.shape, part.dtype) for part in (tile_rows, tile_cols, tile_count)),
            pltpu.VMEM((slot_count, tile_len, tile_len), jnp.float32),
            pltpu.SemaphoreType.DMA((slot_count // group + 3,)),
        ],
        compiler_params=pltpu.CompilerParams(vmem_limit_bytes=VMEM_LIMIT),
        cost_estimate=pl.CostEstimate(
            flops=8 * tile_entries.size, bytes_accessed=8 * tile_entries.size, transcendentals=0
        ),
    )(rows, cols, tile_count, entries)


def half_products(half, span, pieces_ref, dense_ref, digits, block):
    _, depth, width = dense_ref.shape
    tile_len, half_depth = width // 2, depth // 2
    high = middle = low = 0.0
    for start in range(0, half_depth, EXACT_DEPTH):
        stop = min(start + EXACT_DEPTH, half_depth)
        products = jnp.dot(
            digits[:, start:stop],
            dense_ref[block, half * half_depth + start : half * half_depth + stop, :],
            preferred_element_type=jnp.float32,
        )
        products = reduce_centered(products)
        high = high + products[:span, :tile_len]
        middle = middle + products[:span, tile_len:] + products[span:, :tile_len]
        low = low + products[span:, tile_len:]
    return high, middle, low


def fill_digits(span, pieces_ref, digits):
    piece_len = pieces_ref.shape[2]
    for d in range(pieces_ref.shape[0]):
        vector = reduce_centered(pieces_ref[d, :span, :])
        digits[:, d * piece_len : (d + 1) * piece_len] = stacked_digits(vector)


def first_half_kernel(span, pieces_ref, dense_ref, sums_ref, digits):
    fill_digits(span, pieces_ref, digits)
    tile_len = dense_ref.shape[2] // 2
    for block in range(dense_ref.shape[0]):
        parts = half_products(0, span, pieces_ref, dense_ref, digits, block)
        for index, part in enumerate(parts):
            sums_ref[index, :, block * tile_len : (block + 1) * tile_len] = part


def half_of_core(packed):
    rows = packed.shape[0] // 2
    return jnp.where(lax.axis_index("row") % 2 == 0, packed[:rows], packed[rows:])


def second_half_kernel(span, n_col, pieces_ref, evens_ref, sums_ref, dense_ref, *refs):
    tails, outs, digits = refs[: -n_col - 1], refs[-n_col - 1 : -1], refs[-1]
    fill_digits(span, pieces_ref, digits)
    row_blocks, _, width = dense_ref.shape
    tile_len = width // 2
    piece_blocks = row_blocks // n_col
    for e in reversed(range(n_col)):
        for sub in range(piece_blocks):
            block = e * piece_blocks + sub
            parts = half_products(1, span, pieces_ref, dense_ref, digits, block)
            parts = (
                part + sums_ref[index, :, block * tile_len : (block + 1) * tile_len]
                for index, part in enumerate(parts)
            )
            outs[e][:span, sub * tile_len : (sub + 1) * tile_len] = combine(*parts)
    if outs[0].shape[0] > span:
        packed = jnp.sum(pieces_ref[:, span:, :], 0) + jnp.sum(evens_ref[:, span:, :], 0)
        packed = half_of_core(jnp.concatenate([packed, *(tail[...] for tail in tails)], 0))
        for out in outs:
            out[span:, :] = packed


def dense_first(evens, span, dense):
    row_blocks, depth, width = dense.shape
    return call(
        functools.partial(first_half_kernel, span),
        [evens, dense],
        [held(3, span, row_blocks * width // 2)],
        scratch=[pltpu.VMEM((2 * span, depth // 2), jnp.bfloat16)],
        limit=VMEM_LIMIT,
        flops=2 * span * dense.size,
    )[0]


def dense_second(odds, evens, sums, span, n_col, tails, dense, before):
    _, depth, _ = dense.shape
    _, rows, piece_len = odds.shape
    rows = rows + sum(tail.shape[0] for tail in tails)
    return list(
        call(
            functools.partial(second_half_kernel, span, n_col),
            [odds, evens, sums, dense, *tails],
            [held(span + (rows - span) // 2, piece_len)] * n_col,
            before,
            scratch=[pltpu.VMEM((2 * span, depth // 2), jnp.bfloat16)],
            limit=VMEM_LIMIT,
            flops=2 * span * dense.size,
        )
    )


def project(terms):
    products = functools.reduce(jnp.add, [dot_pairs(left, right) for left, right in terms])
    span = products.shape[0] // 2
    square = combine(
        reduce_centered(products[:span, :span]),
        reduce_centered(products[:span, span:]) + reduce_centered(products[span:, :span]),
        reduce_centered(products[span:, span:]),
    )
    return pack_square(square, terms[0][0].shape[1])


def left_kernel(n_row, x_evens, x_odds, dense_ref, *refs):
    rows_refs, (evens_ref, odds_ref, term_ref) = refs[:-3], refs[-3:]
    row_blocks, _, width = dense_ref.shape
    tile_len = width // 2
    _, span, piece_len = x_evens.shape
    piece_blocks = piece_len // tile_len
    x_digits = [
        centred_digits((x_odds if e % 2 else x_evens)[e // 2])
        for e in range(row_blocks // piece_blocks)
    ]
    term = project([(x, stacked_digits(ref[...])) for x, ref in zip(x_digits, rows_refs)])
    term_ref[...] = term
    part_rows = term.shape[0] // odds_ref.shape[0]
    for place in range(n_row):
        by_high = by_low = high_part = low_part = 0.0
        for block in range(row_blocks):
            sub = block % piece_blocks
            left = x_digits[block // piece_blocks][:, sub * tile_len : (sub + 1) * tile_len]
            right = dense_ref[block, place * piece_len : (place + 1) * piece_len, :]
            high_part = high_part + dot_pairs(left, right[:, :tile_len])
            low_part = low_part + dot_pairs(left, right[:, tile_len:])
            if (block + 1) * tile_len % EXACT_DEPTH == 0 or block == row_blocks - 1:
                by_high = by_high + reduce_centered(high_part)
                by_low = by_low + reduce_centered(low_part)
                high_part = low_part = 0.0
        piece = combine(by_high[:span], by_low[:span] + by_high[span:], by_low[span:])
        if place < n_row // 2:
            evens_ref[place] = piece
        else:
            index = place - n_row // 2
            odds_ref[index, :span, :] = piece
            odds_ref[index, span:, :] = term[index * part_rows : (index + 1) * part_rows]


def dense_left(x_pairs, outs, n_row, dense):
    _, span, piece_len = x_pairs[0].shape
    count, rows = n_row // 2, span * span // piece_len
    return call(
        functools.partial(left_kernel, n_row),
        [*x_pairs, dense, *outs],
        [
            held(count, span, piece_len),
            held(count, span + rows // count, piece_len),
            held(rows, piece_len),
        ],
        limit=VMEM_LIMIT,
        flops=4 * span * dense.size,
    )


def sparse_tiles(tiles, sizes):
    tile_rows, tile_cols, tile_count, tile_entries = tiles
    n_row, n_col, piece_blocks = sizes
    entries, rows, cols = tile_entries[0, 0], tile_rows[0, 0], tile_cols[0, 0]
    row_shift = shift_of(lax.axis_index("col"), rows // piece_blocks, n_col)
    col_shift = shift_of(lax.axis_index("row"), cols // piece_blocks, n_row)
    col_place = col_shift % 2 * (n_row // 2) + col_shift // 2
    positions = (
        row_shift * piece_blocks + rows % piece_blocks,
        col_place * piece_blocks + cols % piece_blocks,
        tile_count[0, 0],
    )
    entries = jnp.where(entries > HALF_MODULUS, entries - MODULUS, entries)
    return positions, jnp.stack(balanced_digits(entries), 1).astype(jnp.bfloat16)


def sparse_product(vector, spec, places, targets, count, blocks, a_digits):
    span, tile_len = vector.shape[0], a_digits.shape[-1]
    v_digits = stacked_digits(vector).reshape(2 * span, -1, tile_len)
    picked = jnp.take(v_digits, places, axis=1)
    products = jnp.einsum(spec, picked, a_digits, preferred_element_type=jnp.float32)
    products = reduce_centered(products)
    residues = combine(
        products[:, 0, :span],
        products[:, 0, span:] + products[:, 1, :span],
        products[:, 1, span:],
    )
    live = jnp.arange(targets.shape[0], dtype=jnp.int32) < count
    onehot = targets[None, :] == jnp.arange(blocks, dtype=jnp.int32)[:, None]
    onehot = (onehot & live[None, :]).astype(jnp.float32)
    summed = jnp.einsum("bt,twi->wbi", onehot, residues, precision=lax.Precision.HIGHEST)
    return reduce_centered(summed).reshape(span, blocks * tile_len)


def sparse_second(odds, evens, span, n_col, tails, positions, a_digits):
    rows, cols, count = positions
    pieces = [*evens, *odds]
    piece_len = pieces[0].shape[1]
    blocks = n_col * piece_len // a_digits.shape[-1]
    vector = reduce_centered(jnp.concatenate([piece[:span] for piece in pieces], 1))
    product = sparse_product(vector, "ntk,tdik->tdni", cols, rows, count, blocks, a_digits)
    packed = functools.reduce(jnp.add, [piece[span:] for piece in pieces])
    packed = half_of_core(jnp.concatenate([packed, *tails], 0))
    outs = [product[:, e * piece_len : (e + 1) * piece_len] for e in range(n_col)]
    return [jnp.concatenate([out, packed], 0) for out in outs]


def sparse_left(x_pairs, outs, n_row, positions, a_digits):
    rows, cols, count = positions
    n_col = 2 * x_pairs[0].shape[0]
    x_pieces = [x_pairs[e % 2][e // 2] for e in range(n_col)]
    piece_len = x_pieces[0].shape[1]
    values = jnp.concatenate(x_pieces, 1)
    values = jnp.where(values > HALF_MODULUS, values - MODULUS, values)
    blocks = n_row * piece_len // a_digits.shape[-1]
    product = sparse_product(values, "nti,tdik->tdnk", rows, cols, count, blocks, a_digits)
    pieces = [product[:, d * piece_len : (d + 1) * piece_len] for d in range(n_row)]
    term = 0.0
    for x_piece, rows_piece in zip(x_pieces, outs):
        term = term + project([(centred_digits(x_piece), stacked_digits(rows_piece))])
    odds = jnp.stack(pieces[n_row // 2 :])
    below = term.reshape(odds.shape[0], -1, piece_len)
    return jnp.stack(pieces[: n_row // 2]), jnp.concatenate([odds, below], 1), term


def add_and_part(kept, came, term, before=()):
    count, span, piece_len = kept.shape
    half, rows = count // 2, term.shape[0]
    part = rows // half if half > 1 else 0

    def kernel(kept_ref, came_ref, term_ref, evens_ref, odds_ref, out_ref):
        below = [came_ref[index, span:, :] for index in range(count)]
        total = term_ref[...] + jnp.concatenate(below, 0)
        out_ref[...] = total
        for index in range(count):
            piece = kept_ref[index] + came_ref[index, :span, :]
            if index % 2 == 0:
                evens_ref[index // 2] = piece
            else:
                odds_ref[index // 2, :span, :] = piece
        if part:
            for index in range(half):
                odds_ref[index, span:, :] = total[index * part : (index + 1) * part]

    outs = [
        held(half, span, piece_len),
        held(half, span + part, piece_len),
        held(rows, piece_len),
    ]
    return call(kernel, [kept, came, term], outs, before)


def append_projections(kept, came, term, term_came, pieces, vector_1):
    span, piece_len = pieces[0].shape
    rows = term.shape[0]

    def kernel(*refs):
        piece_refs, refs = refs[: len(pieces)], refs[len(pieces) :]
        vector_ref, kept_ref, came_ref, term_ref, term_came_ref, out_ref, first_ref = refs
        summed = functools.reduce(jnp.add, [ref[...] for ref in piece_refs])
        out_ref[:span, :] = summed
        w_digits = stacked_digits(reduce_centered(kept_ref[0] + came_ref[0]))
        first_ref[...] = term_ref[...] + term_came_ref[...]
        for index, vector in enumerate([summed, vector_ref[...]]):
            start = span + index * rows
            digits = stacked_digits(reduce_centered(vector))
            out_ref[start : start + rows, :] = project([(w_digits, digits)])

    outs = [held(span + 2 * rows, piece_len), held(rows, piece_len)]
    return call(kernel, [*pieces, vector_1, kept, came, term, term_came], outs)


def multiply_mod(left, right):
    span = left.shape[0]
    left = stacked_digits(left)
    high, low = (part.astype(jnp.bfloat16) for part in balanced_digits(right))
    by_high = jnp.dot(left, high, preferred_element_type=jnp.float32)
    by_low = jnp.dot(left, low, preferred_element_type=jnp.float32)
    return combine(
        reduce_centered(by_high[:span]), by_low[:span] + by_high[span:], by_low[span:]
    )


def sigma_update(mine, other, span):
    rows = span * span // mine.shape[1]

    def kernel(mine_ref, other_ref, out_ref):
        first = lax.axis_index("row") % 2 == 0
        mine, other = reduce_centered(mine_ref[...]), reduce_centered(other_ref[...])
        packed = jnp.concatenate([jnp.where(first, mine, other), jnp.where(first, other, mine)], 0)
        c_3, c_2, c_1 = (
            unpack_square(packed[index * rows : (index + 1) * rows], span) for index in range(3)
        )
        e_2 = reduce_centered(c_1 - multiply_mod(c_1, c_2))
        both = reduce_centered(c_1 + e_2)
        start = multiply_mod(e_2, c_1)
        rest = c_1 - multiply_mod(both, c_2)
        e_3 = reduce_centered(multiply_mod(start, c_3) + rest)
        out_ref[0] = canonical(-multiply_mod(e_3, start)) * (1.0 / MODULUS)
        out_ref[1] = canonical(start + multiply_mod(e_3, both)) * (1.0 / MODULUS)
        out_ref[2] = canonical(-both - e_3) * (1.0 / MODULUS)

    outs = [jax.ShapeDtypeStruct((STEP_COUNT, span, span), jnp.float32)]
    return call(kernel, [mine, other], outs)[0]


def local(tile_entries, tile_rows, tile_cols, tile_count, block_x, block_y):
    _, _, slot_count, tile_len, _ = tile_entries.shape
    span, piece_len = block_y.shape
    piece_blocks = piece_len // tile_len
    n_row, n_col = lax.axis_size("row"), lax.axis_size("col")
    packed_rows = span * span // piece_len
    tiles = (tile_rows, tile_cols, tile_count, tile_entries)
    sizes = (n_row, n_col, piece_blocks)
    is_dense = n_col * piece_blocks * n_row * piece_blocks <= DENSE_CELLS * slot_count
    if is_dense:
        dense, token = build_dense(tiles, sizes)
        before = [token]
    else:
        positions, a_digits = sparse_tiles(tiles, sizes)
        before = []

    def multiply_evens(evens):
        return dense_first(evens, span, dense) if is_dense else evens

    def multiply(evens, before=(), tails=()):
        odds, sums = gather_odds(evens, "row"), multiply_evens(evens)
        if is_dense:
            return dense_second(odds, evens, sums, span, n_col, tails, dense, before)
        return sparse_second(odds, evens, span, n_col, tails, positions, a_digits)

    x_own, y_own = load_pieces(block_x, block_y)
    y_came = fetch_evens(y_own, "row")
    x_came = fetch_evens(x_own, "col")
    evens = stack_after([y_own] + y_came, [*before, *x_came])
    x_evens = stack_after([x_own] + x_came)
    outs = multiply(evens, [x_evens])
    x_pairs = [x_evens, gather_odds(x_evens, "col")]
    if is_dense:
        w_kept, w_odds, term = dense_left(x_pairs, outs, n_row, dense)
    else:
        w_kept, w_odds, term = sparse_left(x_pairs, outs, n_row, positions, a_digits)
    vector_1 = sum_after(scatter_pieces(outs, "col"), [w_odds])
    w_came = fetch(w_odds, "row", 1)
    outs = multiply(gather_evens(vector_1, "row"), [w_came])
    pieces = scatter_pieces(outs, "col")
    shift, before = 2, []
    while shift < n_row:
        w_kept, w_sent, term = add_and_part(w_kept, w_came, term, before)
        w_came = fetch(w_sent, "row", shift)
        shift, before = 2 * shift, [outs[0]]
    term_came = fetch(term, "row", n_row // 2)
    vector_2, first = append_projections(w_kept, w_came, term, term_came, pieces, vector_1)
    outs = multiply(gather_evens(vector_2, "row"), tails=[first])
    pieces = scatter_pieces(outs, "col")
    terms = functools.reduce(jnp.add, [piece[span:] for piece in pieces])
    vector_3 = functools.reduce(jnp.add, [piece[:span] for piece in pieces])
    return sigma_update(terms, fetch(terms, "row", 1), span), canonical(vector_3) * (1.0 / MODULUS)


def solution(mesh):
    placed = (
        P("row", "col", None, None, None),
        P("row", "col", None),
        P("row", "col", None),
        P("row", "col"),
        P(None, ("row", "col")),
        P(None, ("row", "col")),
    )
    return jax.shard_map(
        local, mesh=mesh, in_specs=placed, out_specs=(P(), P(None, ("row", "col"))), check_vma=False
    )
```

```python
import functools

import jax
import jax.numpy as jnp
from jax import lax
from jax.experimental import pallas as pl
from jax.experimental.pallas import tpu as pltpu
from jax.sharding import PartitionSpec as P

STEP_COUNT = 3

MODULUS = 65521.0
HALF_MODULUS = 32760.0
BASE = 256.0
EXACT_DEPTH = 1024
DENSE_CELLS = 4
VMEM_LIMIT = 16 * 1024 * 1024
SMALL_LIMIT = 4 * 1024 * 1024


def reduce_centered(values):
    return values - MODULUS * jnp.floor(values * (1.0 / MODULUS) + 0.5)


def canonical(values):
    reduced = reduce_centered(values)
    return jnp.where(reduced < 0, reduced + MODULUS, reduced)


def balanced_digits(values):
    high = jnp.floor(values * (1.0 / BASE) + 0.5)
    return high, values - BASE * high


def stacked_digits(values):
    high, low = balanced_digits(values)
    return jnp.concatenate([high, low], 0).astype(jnp.bfloat16)


def centred_digits(residues):
    return stacked_digits(jnp.where(residues > HALF_MODULUS, residues - MODULUS, residues))


def partner(index, shift, size):
    return index ^ shift if size & (size - 1) == 0 else (index + shift) % size


def shift_of(index, other, size):
    return index ^ other if size & (size - 1) == 0 else (other - index) % size


def fetch(piece, axis, shift):
    size = lax.axis_size(axis)
    return lax.ppermute(piece, axis, [(partner(i, shift, size), i) for i in range(size)])


def scatter_pieces(pieces, axis):
    size = lax.axis_size(axis)
    came = [
        lax.ppermute(pieces[shift], axis, [(i, partner(i, shift, size)) for i in range(size)])
        for shift in reversed(range(1, size))
    ]
    return [pieces[0]] + came


def call(kernel, operands, outs, before=(), scratch=(), limit=SMALL_LIMIT, flops=0):
    def body(*refs):
        kernel(*refs[: len(operands)], *refs[len(operands) + len(before) :])

    vmem = pl.BlockSpec(memory_space=pltpu.VMEM)
    return pl.pallas_call(
        body,
        in_specs=[vmem] * len(operands) + [pl.BlockSpec(memory_space=pl.ANY)] * len(before),
        out_specs=[vmem] * len(outs),
        out_shape=outs,
        scratch_shapes=list(scratch),
        compiler_params=pltpu.CompilerParams(vmem_limit_bytes=limit),
        cost_estimate=pl.CostEstimate(flops=flops, bytes_accessed=0, transcendentals=0),
    )(*(pltpu.with_memory_space_constraint(part, pltpu.VMEM) for part in operands), *before)


def held(*shape):
    return pltpu.VMEM(shape, jnp.float32)


def stack_after(pieces, before=()):
    def kernel(*refs):
        for index, ref in enumerate(refs[:-1]):
            refs[-1][index] = ref[...]

    return call(kernel, pieces, [held(len(pieces), *pieces[0].shape)], before)[0]


def sum_after(pieces, before=()):
    def kernel(*refs):
        refs[-1][...] = functools.reduce(jnp.add, [ref[...] for ref in refs[:-1]])

    return call(kernel, pieces, [held(*pieces[0].shape)], before)[0]


def fetch_evens(piece, axis):
    return [fetch(piece, axis, shift) for shift in range(2, lax.axis_size(axis), 2)]


def gather_evens(piece, axis, before=()):
    return stack_after([piece] + fetch_evens(piece, axis), before)


def gather_odds(evens, axis):
    size = lax.axis_size(axis)
    assert size > 1 and size & (size - 1) == 0
    return fetch(evens, axis, 1)


def dot_pairs(left, right):
    return lax.dot_general(left, right, (((1,), (1,)), ((), ())), preferred_element_type=jnp.float32)


def combine(high, middle, low):
    return reduce_centered(15.0 * high + 256.0 * reduce_centered(middle) + low)


def pack_square(square, width):
    span = square.shape[0]
    rows = span * span // width
    return jnp.concatenate([square[j * rows : (j + 1) * rows] for j in range(width // span)], 1)


def unpack_square(packed, span):
    count = packed.shape[1] // span
    return jnp.concatenate([packed[:, j * span : (j + 1) * span] for j in range(count)], 0)


def build_kernel(sizes, *refs):
    entries_ref, x_ref, y_ref, dense_ref, x_out, y_out, token_ref = refs[3:10]
    rows_ref, cols_ref, count_ref, tiles, sems = refs[10:]
    n_row, n_col, piece_blocks, group = sizes
    _, _, slot_count, tile_len, _ = entries_ref.shape
    me_row, me_col = lax.axis_index("row"), lax.axis_index("col")
    chunk_count = slot_count // group

    def chunk(index):
        source = entries_ref.at[0, 0, pl.ds(index * group, group)]
        return pltpu.make_async_copy(source, tiles.at[pl.ds(index * group, group)], sems.at[index])

    small = [*zip(refs[:3], refs[10:13]), (y_ref, y_out), (x_ref, x_out)]
    small = [
        pltpu.make_async_copy(source, target, sems.at[chunk_count + index])
        for index, (source, target) in enumerate(small)
    ]
    for copy in small[:3]:
        copy.start()
    sure_count = min(2, chunk_count)
    for index in range(sure_count):
        chunk(index).start()

    def clear(block, carry):
        dense_ref[block] = jnp.zeros(dense_ref.shape[1:], dense_ref.dtype)
        return carry

    half = dense_ref.shape[0] // 2
    lax.fori_loop(0, half, clear, 0)
    for copy in small[:3]:
        copy.wait()
    used_count = jnp.maximum((count_ref[0, 0] + group - 1) // group, sure_count)
    for index in range(sure_count, chunk_count):

        @pl.when(index < used_count)
        def _():
            chunk(index).start()

    for copy in small[3:]:
        copy.start()
    lax.fori_loop(half, dense_ref.shape[0], clear, 0)

    def place(slot):
        row, col = rows_ref[0, 0, slot], cols_ref[0, 0, slot]
        row_shift = shift_of(me_col, row // piece_blocks, n_col)
        col_shift = shift_of(me_row, col // piece_blocks, n_row)
        col_place = col_shift % 2 * (n_row // 2) + col_shift // 2
        block = row_shift * piece_blocks + row % piece_blocks
        start = (col_place * piece_blocks + col % piece_blocks) * tile_len
        values = jnp.where(slot < count_ref[0, 0], tiles[slot], 0.0)
        values = jnp.where(values > HALF_MODULUS, values - MODULUS, values).T
        both = jnp.concatenate(balanced_digits(values), 1).astype(jnp.bfloat16)
        dense_ref[block, pl.ds(pl.multiple_of(start, tile_len), tile_len), :] = both

    def step(index, carry):
        chunk(index).wait()
        for offset in range(group):
            place(index * group + offset)
        return carry

    lax.fori_loop(0, used_count, step, 0)
    for copy in small[3:]:
        copy.wait()
    token_ref[...] = jnp.zeros_like(token_ref)


def build_dense(tiles, block_x, block_y, sizes):
    tile_rows, tile_cols, tile_count, tile_entries = tiles
    n_row, n_col, piece_blocks = sizes
    _, _, slot_count, tile_len, _ = tile_entries.shape
    group = next(size for size in (8, 4, 2, 1) if slot_count % size == 0)
    shape = (n_col * piece_blocks, n_row * piece_blocks * tile_len, 2 * tile_len)
    hbm = pl.BlockSpec(memory_space=pltpu.HBM)
    rows, cols, entries, x_piece, y_piece = (
        pltpu.with_memory_space_constraint(part, pltpu.HBM)
        for part in (tile_rows, tile_cols, tile_entries, block_x, block_y)
    )
    return pl.pallas_call(
        functools.partial(build_kernel, (*sizes, group)),
        in_specs=[hbm, hbm, pl.BlockSpec(memory_space=pl.ANY), hbm, hbm, hbm],
        out_specs=[pl.BlockSpec(memory_space=pltpu.VMEM)] * 4,
        out_shape=[
            pltpu.VMEM(shape, jnp.bfloat16),
            held(*block_x.shape),
            held(*block_y.shape),
            held(8, 128),
        ],
        scratch_shapes=[
            *(pltpu.SMEM(part.shape, part.dtype) for part in (tile_rows, tile_cols, tile_count)),
            pltpu.VMEM((slot_count, tile_len, tile_len), jnp.float32),
            pltpu.SemaphoreType.DMA((slot_count // group + 5,)),
        ],
        compiler_params=pltpu.CompilerParams(vmem_limit_bytes=VMEM_LIMIT),
        cost_estimate=pl.CostEstimate(
            flops=8 * tile_entries.size, bytes_accessed=8 * tile_entries.size, transcendentals=0
        ),
    )(rows, cols, tile_count, entries, x_piece, y_piece)


def half_products(half, span, pieces_ref, dense_ref, digits, block):
    _, depth, width = dense_ref.shape
    tile_len, half_depth = width // 2, depth // 2
    high = middle = low = 0.0
    for start in range(0, half_depth, EXACT_DEPTH):
        stop = min(start + EXACT_DEPTH, half_depth)
        products = jnp.dot(
            digits[:, start:stop],
            dense_ref[block, half * half_depth + start : half * half_depth + stop, :],
            preferred_element_type=jnp.float32,
        )
        products = reduce_centered(products)
        high = high + products[:span, :tile_len]
        middle = middle + products[:span, tile_len:] + products[span:, :tile_len]
        low = low + products[span:, tile_len:]
    return high, middle, low


def fill_digits(span, pieces_ref, digits):
    piece_len = pieces_ref.shape[2]
    for d in range(pieces_ref.shape[0]):
        vector = reduce_centered(pieces_ref[d, :span, :])
        digits[:, d * piece_len : (d + 1) * piece_len] = stacked_digits(vector)


def first_half_kernel(span, pieces_ref, dense_ref, sums_ref, digits):
    fill_digits(span, pieces_ref, digits)
    tile_len = dense_ref.shape[2] // 2
    for block in range(dense_ref.shape[0]):
        parts = half_products(0, span, pieces_ref, dense_ref, digits, block)
        for index, part in enumerate(parts):
            sums_ref[index, :, block * tile_len : (block + 1) * tile_len] = part


def half_of_core(packed):
    rows = packed.shape[0] // 2
    return jnp.where(lax.axis_index("row") % 2 == 0, packed[:rows], packed[rows:])


def second_half_kernel(span, n_col, pieces_ref, evens_ref, sums_ref, dense_ref, *refs):
    tails, outs, digits = refs[: -n_col - 1], refs[-n_col - 1 : -1], refs[-1]
    fill_digits(span, pieces_ref, digits)
    row_blocks, _, width = dense_ref.shape
    tile_len = width // 2
    piece_blocks = row_blocks // n_col
    for e in reversed(range(n_col)):
        for sub in range(piece_blocks):
            block = e * piece_blocks + sub
            parts = half_products(1, span, pieces_ref, dense_ref, digits, block)
            parts = (
                part + sums_ref[index, :, block * tile_len : (block + 1) * tile_len]
                for index, part in enumerate(parts)
            )
            outs[e][:span, sub * tile_len : (sub + 1) * tile_len] = combine(*parts)
    if outs[0].shape[0] > span:
        packed = jnp.sum(pieces_ref[:, span:, :], 0) + jnp.sum(evens_ref[:, span:, :], 0)
        packed = half_of_core(jnp.concatenate([packed, *(tail[...] for tail in tails)], 0))
        for out in outs:
            out[span:, :] = packed


def dense_first(evens, span, dense):
    row_blocks, depth, width = dense.shape
    return call(
        functools.partial(first_half_kernel, span),
        [evens, dense],
        [held(3, span, row_blocks * width // 2)],
        scratch=[pltpu.VMEM((2 * span, depth // 2), jnp.bfloat16)],
        limit=VMEM_LIMIT,
        flops=2 * span * dense.size,
    )[0]


def dense_second(odds, evens, sums, span, n_col, tails, dense, before):
    _, depth, _ = dense.shape
    _, rows, piece_len = odds.shape
    rows = rows + sum(tail.shape[0] for tail in tails)
    return list(
        call(
            functools.partial(second_half_kernel, span, n_col),
            [odds, evens, sums, dense, *tails],
            [held(span + (rows - span) // 2, piece_len)] * n_col,
            before,
            scratch=[pltpu.VMEM((2 * span, depth // 2), jnp.bfloat16)],
            limit=VMEM_LIMIT,
            flops=2 * span * dense.size,
        )
    )


def project(terms):
    products = functools.reduce(jnp.add, [dot_pairs(left, right) for left, right in terms])
    span = products.shape[0] // 2
    square = combine(
        reduce_centered(products[:span, :span]),
        reduce_centered(products[:span, span:]) + reduce_centered(products[span:, :span]),
        reduce_centered(products[span:, span:]),
    )
    return pack_square(square, terms[0][0].shape[1])


def left_kernel(n_row, x_evens, x_odds, dense_ref, *refs):
    rows_refs, (evens_ref, odds_ref, term_ref) = refs[:-3], refs[-3:]
    row_blocks, _, width = dense_ref.shape
    tile_len = width // 2
    _, span, piece_len = x_evens.shape
    piece_blocks = piece_len // tile_len
    x_digits = [
        centred_digits((x_odds if e % 2 else x_evens)[e // 2])
        for e in range(row_blocks // piece_blocks)
    ]
    term = project([(x, stacked_digits(ref[...])) for x, ref in zip(x_digits, rows_refs)])
    term_ref[...] = term
    part_rows = term.shape[0] // odds_ref.shape[0]
    for place in range(n_row):
        by_high = by_low = high_part = low_part = 0.0
        for block in range(row_blocks):
            sub = block % piece_blocks
            left = x_digits[block // piece_blocks][:, sub * tile_len : (sub + 1) * tile_len]
            right = dense_ref[block, place * piece_len : (place + 1) * piece_len, :]
            high_part = high_part + dot_pairs(left, right[:, :tile_len])
            low_part = low_part + dot_pairs(left, right[:, tile_len:])
            if (block + 1) * tile_len % EXACT_DEPTH == 0 or block == row_blocks - 1:
                by_high = by_high + reduce_centered(high_part)
                by_low = by_low + reduce_centered(low_part)
                high_part = low_part = 0.0
        piece = combine(by_high[:span], by_low[:span] + by_high[span:], by_low[span:])
        if place < n_row // 2:
            evens_ref[place] = piece
        else:
            index = place - n_row // 2
            odds_ref[index, :span, :] = piece
            odds_ref[index, span:, :] = term[index * part_rows : (index + 1) * part_rows]


def dense_left(x_pairs, outs, n_row, dense):
    _, span, piece_len = x_pairs[0].shape
    count, rows = n_row // 2, span * span // piece_len
    return call(
        functools.partial(left_kernel, n_row),
        [*x_pairs, dense, *outs],
        [
            held(count, span, piece_len),
            held(count, span + rows // count, piece_len),
            held(rows, piece_len),
        ],
        limit=VMEM_LIMIT,
        flops=4 * span * dense.size,
    )


def sparse_tiles(tiles, sizes):
    tile_rows, tile_cols, tile_count, tile_entries = tiles
    n_row, n_col, piece_blocks = sizes
    entries, rows, cols = tile_entries[0, 0], tile_rows[0, 0], tile_cols[0, 0]
    row_shift = shift_of(lax.axis_index("col"), rows // piece_blocks, n_col)
    col_shift = shift_of(lax.axis_index("row"), cols // piece_blocks, n_row)
    col_place = col_shift % 2 * (n_row // 2) + col_shift // 2
    positions = (
        row_shift * piece_blocks + rows % piece_blocks,
        col_place * piece_blocks + cols % piece_blocks,
        tile_count[0, 0],
    )
    entries = jnp.where(entries > HALF_MODULUS, entries - MODULUS, entries)
    return positions, jnp.stack(balanced_digits(entries), 1).astype(jnp.bfloat16)


def sparse_product(vector, spec, places, targets, count, blocks, a_digits):
    span, tile_len = vector.shape[0], a_digits.shape[-1]
    v_digits = stacked_digits(vector).reshape(2 * span, -1, tile_len)
    picked = jnp.take(v_digits, places, axis=1)
    products = jnp.einsum(spec, picked, a_digits, preferred_element_type=jnp.float32)
    products = reduce_centered(products)
    residues = combine(
        products[:, 0, :span],
        products[:, 0, span:] + products[:, 1, :span],
        products[:, 1, span:],
    )
    live = jnp.arange(targets.shape[0], dtype=jnp.int32) < count
    onehot = targets[None, :] == jnp.arange(blocks, dtype=jnp.int32)[:, None]
    onehot = (onehot & live[None, :]).astype(jnp.float32)
    summed = jnp.einsum("bt,twi->wbi", onehot, residues, precision=lax.Precision.HIGHEST)
    return reduce_centered(summed).reshape(span, blocks * tile_len)


def sparse_second(odds, evens, span, n_col, tails, positions, a_digits):
    rows, cols, count = positions
    pieces = [*evens, *odds]
    piece_len = pieces[0].shape[1]
    blocks = n_col * piece_len // a_digits.shape[-1]
    vector = reduce_centered(jnp.concatenate([piece[:span] for piece in pieces], 1))
    product = sparse_product(vector, "ntk,tdik->tdni", cols, rows, count, blocks, a_digits)
    packed = functools.reduce(jnp.add, [piece[span:] for piece in pieces])
    packed = half_of_core(jnp.concatenate([packed, *tails], 0))
    outs = [product[:, e * piece_len : (e + 1) * piece_len] for e in range(n_col)]
    return [jnp.concatenate([out, packed], 0) for out in outs]


def sparse_left(x_pairs, outs, n_row, positions, a_digits):
    rows, cols, count = positions
    n_col = 2 * x_pairs[0].shape[0]
    x_pieces = [x_pairs[e % 2][e // 2] for e in range(n_col)]
    piece_len = x_pieces[0].shape[1]
    values = jnp.concatenate(x_pieces, 1)
    values = jnp.where(values > HALF_MODULUS, values - MODULUS, values)
    blocks = n_row * piece_len // a_digits.shape[-1]
    product = sparse_product(values, "nti,tdik->tdnk", rows, cols, count, blocks, a_digits)
    pieces = [product[:, d * piece_len : (d + 1) * piece_len] for d in range(n_row)]
    term = 0.0
    for x_piece, rows_piece in zip(x_pieces, outs):
        term = term + project([(centred_digits(x_piece), stacked_digits(rows_piece))])
    odds = jnp.stack(pieces[n_row // 2 :])
    below = term.reshape(odds.shape[0], -1, piece_len)
    return jnp.stack(pieces[: n_row // 2]), jnp.concatenate([odds, below], 1), term


def add_and_part(kept, came, term, before=()):
    count, span, piece_len = kept.shape
    half, rows = count // 2, term.shape[0]
    part = rows // half if half > 1 else 0

    def kernel(kept_ref, came_ref, term_ref, evens_ref, odds_ref, out_ref):
        below = [came_ref[index, span:, :] for index in range(count)]
        total = term_ref[...] + jnp.concatenate(below, 0)
        out_ref[...] = total
        for index in range(count):
            piece = kept_ref[index] + came_ref[index, :span, :]
            if index % 2 == 0:
                evens_ref[index // 2] = piece
            else:
                odds_ref[index // 2, :span, :] = piece
        if part:
            for index in range(half):
                odds_ref[index, span:, :] = total[index * part : (index + 1) * part]

    outs = [
        held(half, span, piece_len),
        held(half, span + part, piece_len),
        held(rows, piece_len),
    ]
    return call(kernel, [kept, came, term], outs, before)


def append_projections(kept, came, term, term_came, pieces, vector_1):
    span, piece_len = pieces[0].shape
    rows = term.shape[0]

    def kernel(*refs):
        piece_refs, refs = refs[: len(pieces)], refs[len(pieces) :]
        vector_ref, kept_ref, came_ref, term_ref, term_came_ref, out_ref, first_ref = refs
        summed = functools.reduce(jnp.add, [ref[...] for ref in piece_refs])
        out_ref[:span, :] = summed
        w_digits = stacked_digits(reduce_centered(kept_ref[0] + came_ref[0]))
        first_ref[...] = term_ref[...] + term_came_ref[...]
        for index, vector in enumerate([summed, vector_ref[...]]):
            start = span + index * rows
            digits = stacked_digits(reduce_centered(vector))
            out_ref[start : start + rows, :] = project([(w_digits, digits)])

    outs = [held(span + 2 * rows, piece_len), held(rows, piece_len)]
    return call(kernel, [*pieces, vector_1, kept, came, term, term_came], outs)


def multiply_mod(left, right):
    span = left.shape[0]
    left = stacked_digits(left)
    high, low = (part.astype(jnp.bfloat16) for part in balanced_digits(right))
    by_high = jnp.dot(left, high, preferred_element_type=jnp.float32)
    by_low = jnp.dot(left, low, preferred_element_type=jnp.float32)
    return combine(
        reduce_centered(by_high[:span]), by_low[:span] + by_high[span:], by_low[span:]
    )


def sigma_update(mine, other, span):
    rows = span * span // mine.shape[1]

    def kernel(mine_ref, other_ref, out_ref):
        first = lax.axis_index("row") % 2 == 0
        mine, other = reduce_centered(mine_ref[...]), reduce_centered(other_ref[...])
        packed = jnp.concatenate([jnp.where(first, mine, other), jnp.where(first, other, mine)], 0)
        c_3, c_2, c_1 = (
            unpack_square(packed[index * rows : (index + 1) * rows], span) for index in range(3)
        )
        e_2 = reduce_centered(c_1 - multiply_mod(c_1, c_2))
        both = reduce_centered(c_1 + e_2)
        start = multiply_mod(e_2, c_1)
        rest = c_1 - multiply_mod(both, c_2)
        e_3 = reduce_centered(multiply_mod(start, c_3) + rest)
        out_ref[0] = canonical(-multiply_mod(e_3, start)) * (1.0 / MODULUS)
        out_ref[1] = canonical(start + multiply_mod(e_3, both)) * (1.0 / MODULUS)
        out_ref[2] = canonical(-both - e_3) * (1.0 / MODULUS)

    outs = [jax.ShapeDtypeStruct((STEP_COUNT, span, span), jnp.float32)]
    return call(kernel, [mine, other], outs)[0]


def local(tile_entries, tile_rows, tile_cols, tile_count, block_x, block_y):
    _, _, slot_count, tile_len, _ = tile_entries.shape
    span, piece_len = block_y.shape
    piece_blocks = piece_len // tile_len
    n_row, n_col = lax.axis_size("row"), lax.axis_size("col")
    packed_rows = span * span // piece_len
    tiles = (tile_rows, tile_cols, tile_count, tile_entries)
    sizes = (n_row, n_col, piece_blocks)
    is_dense = n_col * piece_blocks * n_row * piece_blocks <= DENSE_CELLS * slot_count
    if is_dense:
        dense, x_own, y_own, token = build_dense(tiles, block_x, block_y, sizes)
        before = [token]
    else:
        positions, a_digits = sparse_tiles(tiles, sizes)
        x_own, y_own, before = block_x, block_y, []

    def multiply_evens(evens):
        return dense_first(evens, span, dense) if is_dense else evens

    def multiply(evens, before=(), tails=()):
        odds, sums = gather_odds(evens, "row"), multiply_evens(evens)
        if is_dense:
            return dense_second(odds, evens, sums, span, n_col, tails, dense, before)
        return sparse_second(odds, evens, span, n_col, tails, positions, a_digits)

    y_came = fetch_evens(block_y, "row")
    x_came = fetch_evens(block_x, "col")
    evens = stack_after([y_own] + y_came, [*before, *x_came])
    outs = multiply(evens)
    x_evens = stack_after([x_own] + x_came, [outs[0]])
    x_pairs = [x_evens, gather_odds(x_evens, "col")]
    if is_dense:
        w_kept, w_odds, term = dense_left(x_pairs, outs, n_row, dense)
    else:
        w_kept, w_odds, term = sparse_left(x_pairs, outs, n_row, positions, a_digits)
    vector_1 = sum_after(scatter_pieces(outs, "col"), [w_odds])
    w_came = fetch(w_odds, "row", 1)
    outs = multiply(gather_evens(vector_1, "row"), [w_came])
    pieces = scatter_pieces(outs, "col")
    shift, before = 2, []
    while shift < n_row:
        w_kept, w_sent, term = add_and_part(w_kept, w_came, term, before)
        w_came = fetch(w_sent, "row", shift)
        shift, before = 2 * shift, [outs[0]]
    term_came = fetch(term, "row", n_row // 2)
    vector_2, first = append_projections(w_kept, w_came, term, term_came, pieces, vector_1)
    outs = multiply(gather_evens(vector_2, "row"), tails=[first])
    pieces = scatter_pieces(outs, "col")
    terms = functools.reduce(jnp.add, [piece[span:] for piece in pieces])
    vector_3 = functools.reduce(jnp.add, [piece[:span] for piece in pieces])
    return sigma_update(terms, fetch(terms, "row", 1), span), canonical(vector_3) * (1.0 / MODULUS)


def solution(mesh):
    placed = (
        P("row", "col", None, None, None),
        P("row", "col", None),
        P("row", "col", None),
        P("row", "col"),
        P(None, ("row", "col")),
        P(None, ("row", "col")),
    )
    return jax.shard_map(
        local, mesh=mesh, in_specs=placed, out_specs=(P(), P(None, ("row", "col"))), check_vma=False
    )
```

```python
import functools

import jax
import jax.numpy as jnp
from jax import lax
from jax.experimental import pallas as pl
from jax.experimental.pallas import tpu as pltpu
from jax.sharding import PartitionSpec as P

STEP_COUNT = 3

MODULUS = 65521.0
HALF_MODULUS = 32760.0
BASE = 256.0
ROUND_TO_BASE = 1.5 * 2.0**31
EXACT_DEPTH = 1024
DENSE_CELLS = 4
VMEM_LIMIT = 16 * 1024 * 1024
SMALL_LIMIT = 4 * 1024 * 1024


def reduce_centered(values):
    return values - MODULUS * jnp.floor(values * (1.0 / MODULUS) + 0.5)


def canonical(values):
    reduced = reduce_centered(values)
    return jnp.where(reduced < 0, reduced + MODULUS, reduced)


def balanced_digits(values):
    high = jnp.floor(values * (1.0 / BASE) + 0.5)
    return high, values - BASE * high


def stacked_digits(values):
    high, low = balanced_digits(values)
    return jnp.concatenate([high, low], 0).astype(jnp.bfloat16)


def centred_digits(residues):
    return stacked_digits(jnp.where(residues > HALF_MODULUS, residues - MODULUS, residues))


def partner(index, shift, size):
    return index ^ shift if size & (size - 1) == 0 else (index + shift) % size


def shift_of(index, other, size):
    return index ^ other if size & (size - 1) == 0 else (other - index) % size


def fetch(piece, axis, shift):
    size = lax.axis_size(axis)
    return lax.ppermute(piece, axis, [(partner(i, shift, size), i) for i in range(size)])


def scatter_pieces(pieces, axis):
    size = lax.axis_size(axis)
    came = [
        lax.ppermute(pieces[shift], axis, [(i, partner(i, shift, size)) for i in range(size)])
        for shift in reversed(range(1, size))
    ]
    return [pieces[0]] + came


def call(kernel, operands, outs, before=(), scratch=(), limit=SMALL_LIMIT, flops=0):
    def body(*refs):
        kernel(*refs[: len(operands)], *refs[len(operands) + len(before) :])

    vmem = pl.BlockSpec(memory_space=pltpu.VMEM)
    return pl.pallas_call(
        body,
        in_specs=[vmem] * len(operands) + [pl.BlockSpec(memory_space=pl.ANY)] * len(before),
        out_specs=[vmem] * len(outs),
        out_shape=outs,
        scratch_shapes=list(scratch),
        compiler_params=pltpu.CompilerParams(vmem_limit_bytes=limit),
        cost_estimate=pl.CostEstimate(flops=flops, bytes_accessed=0, transcendentals=0),
    )(*(pltpu.with_memory_space_constraint(part, pltpu.VMEM) for part in operands), *before)


def held(*shape):
    return pltpu.VMEM(shape, jnp.float32)


def stack_after(pieces, before=()):
    def kernel(*refs):
        for index, ref in enumerate(refs[:-1]):
            refs[-1][index] = ref[...]

    return call(kernel, pieces, [held(len(pieces), *pieces[0].shape)], before)[0]


def sum_after(pieces, before=()):
    def kernel(*refs):
        refs[-1][...] = functools.reduce(jnp.add, [ref[...] for ref in refs[:-1]])

    return call(kernel, pieces, [held(*pieces[0].shape)], before)[0]


def fetch_evens(piece, axis):
    return [fetch(piece, axis, shift) for shift in range(2, lax.axis_size(axis), 2)]


def gather_evens(piece, axis, before=()):
    return stack_after([piece] + fetch_evens(piece, axis), before)


def gather_odds(evens, axis):
    size = lax.axis_size(axis)
    assert size > 1 and size & (size - 1) == 0
    return fetch(evens, axis, 1)


def dot_pairs(left, right):
    return lax.dot_general(left, right, (((1,), (1,)), ((), ())), preferred_element_type=jnp.float32)


def combine(high, middle, low):
    return reduce_centered(15.0 * high + 256.0 * reduce_centered(middle) + low)


def pack_square(square, width):
    span = square.shape[0]
    rows = span * span // width
    return jnp.concatenate([square[j * rows : (j + 1) * rows] for j in range(width // span)], 1)


def unpack_square(packed, span):
    count = packed.shape[1] // span
    return jnp.concatenate([packed[:, j * span : (j + 1) * span] for j in range(count)], 0)


def build_kernel(sizes, *refs):
    entries_ref, x_ref, y_ref, dense_ref, x_out, y_out, token_ref = refs[3:10]
    rows_ref, cols_ref, count_ref, tiles, sems = refs[10:]
    n_row, n_col, piece_blocks, group = sizes
    _, _, slot_count, tile_len, _ = entries_ref.shape
    me_row, me_col = lax.axis_index("row"), lax.axis_index("col")
    chunk_count = slot_count // group

    def chunk(index):
        source = entries_ref.at[0, 0, pl.ds(index * group, group)]
        return pltpu.make_async_copy(source, tiles.at[pl.ds(index * group, group)], sems.at[index])

    small = [*zip(refs[:3], refs[10:13]), (y_ref, y_out), (x_ref, x_out)]
    small = [
        pltpu.make_async_copy(source, target, sems.at[chunk_count + index])
        for index, (source, target) in enumerate(small)
    ]
    for copy in small[:3]:
        copy.start()
    sure_count = min(2, chunk_count)
    for index in range(sure_count):
        chunk(index).start()

    def clear(block, carry):
        dense_ref[block] = jnp.zeros(dense_ref.shape[1:], dense_ref.dtype)
        return carry

    half = dense_ref.shape[0] // 2
    lax.fori_loop(0, half, clear, 0)
    for copy in small[:3]:
        copy.wait()
    used_count = jnp.maximum((count_ref[0, 0] + group - 1) // group, sure_count)
    for index in range(sure_count, chunk_count):

        @pl.when(index < used_count)
        def _():
            chunk(index).start()

    for copy in small[3:]:
        copy.start()
    lax.fori_loop(half, dense_ref.shape[0], clear, 0)

    def cell(slot):
        row, col = rows_ref[0, 0, slot], cols_ref[0, 0, slot]
        row_shift = shift_of(me_col, row // piece_blocks, n_col)
        col_shift = shift_of(me_row, col // piece_blocks, n_row)
        col_place = col_shift % 2 * (n_row // 2) + col_shift // 2
        block = row_shift * piece_blocks + row % piece_blocks
        start = (col_place * piece_blocks + col % piece_blocks) * tile_len
        return block, pl.ds(pl.multiple_of(start, tile_len), tile_len)

    def place(slot):
        values = tiles[slot]
        values = jnp.where(values > HALF_MODULUS, values - MODULUS, values).T
        rounded = (values + ROUND_TO_BASE) - ROUND_TO_BASE
        both = jnp.concatenate([rounded * (1.0 / BASE), values - rounded], 1)
        block, columns = cell(slot)
        dense_ref[block, columns, :] = both.astype(jnp.bfloat16)

    def step(index, carry):
        chunk(index).wait()
        for offset in range(group):
            place(index * group + offset)
        return carry

    lax.fori_loop(0, used_count, step, 0)

    def erase(slot, carry):
        block, columns = cell(slot)
        dense_ref[block, columns, :] = jnp.zeros((tile_len, 2 * tile_len), dense_ref.dtype)
        return carry

    lax.fori_loop(count_ref[0, 0], used_count * group, erase, 0)
    for copy in small[3:]:
        copy.wait()
    token_ref[...] = jnp.zeros_like(token_ref)


def build_dense(tiles, block_x, block_y, sizes):
    tile_rows, tile_cols, tile_count, tile_entries = tiles
    n_row, n_col, piece_blocks = sizes
    _, _, slot_count, tile_len, _ = tile_entries.shape
    group = next(size for size in (8, 4, 2, 1) if slot_count % size == 0)
    shape = (n_col * piece_blocks, n_row * piece_blocks * tile_len, 2 * tile_len)
    hbm = pl.BlockSpec(memory_space=pltpu.HBM)
    rows, cols, entries, x_piece, y_piece = (
        pltpu.with_memory_space_constraint(part, pltpu.HBM)
        for part in (tile_rows, tile_cols, tile_entries, block_x, block_y)
    )
    return pl.pallas_call(
        functools.partial(build_kernel, (*sizes, group)),
        in_specs=[hbm, hbm, pl.BlockSpec(memory_space=pl.ANY), hbm, hbm, hbm],
        out_specs=[pl.BlockSpec(memory_space=pltpu.VMEM)] * 4,
        out_shape=[
            pltpu.VMEM(shape, jnp.bfloat16),
            held(*block_x.shape),
            held(*block_y.shape),
            held(8, 128),
        ],
        scratch_shapes=[
            *(pltpu.SMEM(part.shape, part.dtype) for part in (tile_rows, tile_cols, tile_count)),
            pltpu.VMEM((slot_count, tile_len, tile_len), jnp.float32),
            pltpu.SemaphoreType.DMA((slot_count // group + 5,)),
        ],
        compiler_params=pltpu.CompilerParams(vmem_limit_bytes=VMEM_LIMIT),
        cost_estimate=pl.CostEstimate(
            flops=8 * tile_entries.size, bytes_accessed=8 * tile_entries.size, transcendentals=0
        ),
    )(rows, cols, tile_count, entries, x_piece, y_piece)


def half_products(half, span, pieces_ref, dense_ref, digits, block):
    _, depth, width = dense_ref.shape
    tile_len, half_depth = width // 2, depth // 2
    high = middle = low = 0.0
    for start in range(0, half_depth, EXACT_DEPTH):
        stop = min(start + EXACT_DEPTH, half_depth)
        products = jnp.dot(
            digits[:, start:stop],
            dense_ref[block, half * half_depth + start : half * half_depth + stop, :],
            preferred_element_type=jnp.float32,
        )
        products = reduce_centered(products)
        high = high + products[:span, :tile_len]
        middle = middle + products[:span, tile_len:] + products[span:, :tile_len]
        low = low + products[span:, tile_len:]
    return high, middle, low


def fill_digits(span, pieces_ref, digits):
    piece_len = pieces_ref.shape[2]
    for d in range(pieces_ref.shape[0]):
        vector = reduce_centered(pieces_ref[d, :span, :])
        digits[:, d * piece_len : (d + 1) * piece_len] = stacked_digits(vector)


def first_half_kernel(span, pieces_ref, dense_ref, sums_ref, digits):
    fill_digits(span, pieces_ref, digits)
    tile_len = dense_ref.shape[2] // 2
    for block in range(dense_ref.shape[0]):
        parts = half_products(0, span, pieces_ref, dense_ref, digits, block)
        for index, part in enumerate(parts):
            sums_ref[index, :, block * tile_len : (block + 1) * tile_len] = part


def half_of_core(packed):
    rows = packed.shape[0] // 2
    return jnp.where(lax.axis_index("row") % 2 == 0, packed[:rows], packed[rows:])


def second_half_kernel(span, n_col, pieces_ref, evens_ref, sums_ref, dense_ref, *refs):
    tails, outs, digits = refs[: -n_col - 1], refs[-n_col - 1 : -1], refs[-1]
    fill_digits(span, pieces_ref, digits)
    row_blocks, _, width = dense_ref.shape
    tile_len = width // 2
    piece_blocks = row_blocks // n_col
    for e in reversed(range(n_col)):
        for sub in range(piece_blocks):
            block = e * piece_blocks + sub
            parts = half_products(1, span, pieces_ref, dense_ref, digits, block)
            parts = (
                part + sums_ref[index, :, block * tile_len : (block + 1) * tile_len]
                for index, part in enumerate(parts)
            )
            outs[e][:span, sub * tile_len : (sub + 1) * tile_len] = combine(*parts)
    if outs[0].shape[0] > span:
        packed = jnp.sum(pieces_ref[:, span:, :], 0) + jnp.sum(evens_ref[:, span:, :], 0)
        packed = half_of_core(jnp.concatenate([packed, *(tail[...] for tail in tails)], 0))
        for out in outs:
            out[span:, :] = packed


def dense_first(evens, span, dense):
    row_blocks, depth, width = dense.shape
    return call(
        functools.partial(first_half_kernel, span),
        [evens, dense],
        [held(3, span, row_blocks * width // 2)],
        scratch=[pltpu.VMEM((2 * span, depth // 2), jnp.bfloat16)],
        limit=VMEM_LIMIT,
        flops=2 * span * dense.size,
    )[0]


def dense_second(odds, evens, sums, span, n_col, tails, dense, before):
    _, depth, _ = dense.shape
    _, rows, piece_len = odds.shape
    rows = rows + sum(tail.shape[0] for tail in tails)
    return list(
        call(
            functools.partial(second_half_kernel, span, n_col),
            [odds, evens, sums, dense, *tails],
            [held(span + (rows - span) // 2, piece_len)] * n_col,
            before,
            scratch=[pltpu.VMEM((2 * span, depth // 2), jnp.bfloat16)],
            limit=VMEM_LIMIT,
            flops=2 * span * dense.size,
        )
    )


def project(terms):
    products = functools.reduce(jnp.add, [dot_pairs(left, right) for left, right in terms])
    span = products.shape[0] // 2
    square = combine(
        reduce_centered(products[:span, :span]),
        reduce_centered(products[:span, span:]) + reduce_centered(products[span:, :span]),
        reduce_centered(products[span:, span:]),
    )
    return pack_square(square, terms[0][0].shape[1])


def left_kernel(n_row, x_evens, x_odds, dense_ref, *refs):
    rows_refs, (evens_ref, odds_ref, term_ref) = refs[:-3], refs[-3:]
    row_blocks, _, width = dense_ref.shape
    tile_len = width // 2
    _, span, piece_len = x_evens.shape
    piece_blocks = piece_len // tile_len
    x_digits = [
        centred_digits((x_odds if e % 2 else x_evens)[e // 2])
        for e in range(row_blocks // piece_blocks)
    ]
    term = project([(x, stacked_digits(ref[...])) for x, ref in zip(x_digits, rows_refs)])
    term_ref[...] = term
    part_rows = term.shape[0] // odds_ref.shape[0]
    for place in range(n_row):
        by_high = by_low = high_part = low_part = 0.0
        for block in range(row_blocks):
            sub = block % piece_blocks
            left = x_digits[block // piece_blocks][:, sub * tile_len : (sub + 1) * tile_len]
            right = dense_ref[block, place * piece_len : (place + 1) * piece_len, :]
            high_part = high_part + dot_pairs(left, right[:, :tile_len])
            low_part = low_part + dot_pairs(left, right[:, tile_len:])
            if (block + 1) * tile_len % EXACT_DEPTH == 0 or block == row_blocks - 1:
                by_high = by_high + reduce_centered(high_part)
                by_low = by_low + reduce_centered(low_part)
                high_part = low_part = 0.0
        piece = combine(by_high[:span], by_low[:span] + by_high[span:], by_low[span:])
        if place < n_row // 2:
            evens_ref[place] = piece
        else:
            index = place - n_row // 2
            odds_ref[index, :span, :] = piece
            odds_ref[index, span:, :] = term[index * part_rows : (index + 1) * part_rows]


def dense_left(x_pairs, outs, n_row, dense):
    _, span, piece_len = x_pairs[0].shape
    count, rows = n_row // 2, span * span // piece_len
    return call(
        functools.partial(left_kernel, n_row),
        [*x_pairs, dense, *outs],
        [
            held(count, span, piece_len),
            held(count, span + rows // count, piece_len),
            held(rows, piece_len),
        ],
        limit=VMEM_LIMIT,
        flops=4 * span * dense.size,
    )


def sparse_tiles(tiles, sizes):
    tile_rows, tile_cols, tile_count, tile_entries = tiles
    n_row, n_col, piece_blocks = sizes
    entries, rows, cols = tile_entries[0, 0], tile_rows[0, 0], tile_cols[0, 0]
    row_shift = shift_of(lax.axis_index("col"), rows // piece_blocks, n_col)
    col_shift = shift_of(lax.axis_index("row"), cols // piece_blocks, n_row)
    col_place = col_shift % 2 * (n_row // 2) + col_shift // 2
    positions = (
        row_shift * piece_blocks + rows % piece_blocks,
        col_place * piece_blocks + cols % piece_blocks,
        tile_count[0, 0],
    )
    entries = jnp.where(entries > HALF_MODULUS, entries - MODULUS, entries)
    return positions, jnp.stack(balanced_digits(entries), 1).astype(jnp.bfloat16)


def sparse_product(vector, spec, places, targets, count, blocks, a_digits):
    span, tile_len = vector.shape[0], a_digits.shape[-1]
    v_digits = stacked_digits(vector).reshape(2 * span, -1, tile_len)
    picked = jnp.take(v_digits, places, axis=1)
    products = jnp.einsum(spec, picked, a_digits, preferred_element_type=jnp.float32)
    products = reduce_centered(products)
    residues = combine(
        products[:, 0, :span],
        products[:, 0, span:] + products[:, 1, :span],
        products[:, 1, span:],
    )
    live = jnp.arange(targets.shape[0], dtype=jnp.int32) < count
    onehot = targets[None, :] == jnp.arange(blocks, dtype=jnp.int32)[:, None]
    onehot = (onehot & live[None, :]).astype(jnp.float32)
    summed = jnp.einsum("bt,twi->wbi", onehot, residues, precision=lax.Precision.HIGHEST)
    return reduce_centered(summed).reshape(span, blocks * tile_len)


def sparse_second(odds, evens, span, n_col, tails, positions, a_digits):
    rows, cols, count = positions
    pieces = [*evens, *odds]
    piece_len = pieces[0].shape[1]
    blocks = n_col * piece_len // a_digits.shape[-1]
    vector = reduce_centered(jnp.concatenate([piece[:span] for piece in pieces], 1))
    product = sparse_product(vector, "ntk,tdik->tdni", cols, rows, count, blocks, a_digits)
    packed = functools.reduce(jnp.add, [piece[span:] for piece in pieces])
    packed = half_of_core(jnp.concatenate([packed, *tails], 0))
    outs = [product[:, e * piece_len : (e + 1) * piece_len] for e in range(n_col)]
    return [jnp.concatenate([out, packed], 0) for out in outs]


def sparse_left(x_pairs, outs, n_row, positions, a_digits):
    rows, cols, count = positions
    n_col = 2 * x_pairs[0].shape[0]
    x_pieces = [x_pairs[e % 2][e // 2] for e in range(n_col)]
    piece_len = x_pieces[0].shape[1]
    values = jnp.concatenate(x_pieces, 1)
    values = jnp.where(values > HALF_MODULUS, values - MODULUS, values)
    blocks = n_row * piece_len // a_digits.shape[-1]
    product = sparse_product(values, "nti,tdik->tdnk", rows, cols, count, blocks, a_digits)
    pieces = [product[:, d * piece_len : (d + 1) * piece_len] for d in range(n_row)]
    term = 0.0
    for x_piece, rows_piece in zip(x_pieces, outs):
        term = term + project([(centred_digits(x_piece), stacked_digits(rows_piece))])
    odds = jnp.stack(pieces[n_row // 2 :])
    below = term.reshape(odds.shape[0], -1, piece_len)
    return jnp.stack(pieces[: n_row // 2]), jnp.concatenate([odds, below], 1), term


def add_and_part(kept, came, term, before=()):
    count, span, piece_len = kept.shape
    half, rows = count // 2, term.shape[0]
    part = rows // half if half > 1 else 0

    def kernel(kept_ref, came_ref, term_ref, evens_ref, odds_ref, out_ref):
        below = [came_ref[index, span:, :] for index in range(count)]
        total = term_ref[...] + jnp.concatenate(below, 0)
        out_ref[...] = total
        for index in range(count):
            piece = kept_ref[index] + came_ref[index, :span, :]
            if index % 2 == 0:
                evens_ref[index // 2] = piece
            else:
                odds_ref[index // 2, :span, :] = piece
        if part:
            for index in range(half):
                odds_ref[index, span:, :] = total[index * part : (index + 1) * part]

    outs = [
        held(half, span, piece_len),
        held(half, span + part, piece_len),
        held(rows, piece_len),
    ]
    return call(kernel, [kept, came, term], outs, before)


def append_projections(kept, came, term, term_came, pieces, vector_1):
    span, piece_len = pieces[0].shape
    rows = term.shape[0]

    def kernel(*refs):
        piece_refs, refs = refs[: len(pieces)], refs[len(pieces) :]
        vector_ref, kept_ref, came_ref, term_ref, term_came_ref, out_ref, first_ref = refs
        summed = functools.reduce(jnp.add, [ref[...] for ref in piece_refs])
        out_ref[:span, :] = summed
        w_digits = stacked_digits(reduce_centered(kept_ref[0] + came_ref[0]))
        first_ref[...] = term_ref[...] + term_came_ref[...]
        for index, vector in enumerate([summed, vector_ref[...]]):
            start = span + index * rows
            digits = stacked_digits(reduce_centered(vector))
            out_ref[start : start + rows, :] = project([(w_digits, digits)])

    outs = [held(span + 2 * rows, piece_len), held(rows, piece_len)]
    return call(kernel, [*pieces, vector_1, kept, came, term, term_came], outs)


def multiply_mod(left, right):
    span = left.shape[0]
    left = stacked_digits(left)
    high, low = (part.astype(jnp.bfloat16) for part in balanced_digits(right))
    by_high = jnp.dot(left, high, preferred_element_type=jnp.float32)
    by_low = jnp.dot(left, low, preferred_element_type=jnp.float32)
    return combine(
        reduce_centered(by_high[:span]), by_low[:span] + by_high[span:], by_low[span:]
    )


def sigma_update(mine, other, span):
    rows = span * span // mine.shape[1]

    def kernel(mine_ref, other_ref, out_ref):
        first = lax.axis_index("row") % 2 == 0
        mine, other = reduce_centered(mine_ref[...]), reduce_centered(other_ref[...])
        packed = jnp.concatenate([jnp.where(first, mine, other), jnp.where(first, other, mine)], 0)
        c_3, c_2, c_1 = (
            unpack_square(packed[index * rows : (index + 1) * rows], span) for index in range(3)
        )
        e_2 = reduce_centered(c_1 - multiply_mod(c_1, c_2))
        both = reduce_centered(c_1 + e_2)
        start = multiply_mod(e_2, c_1)
        rest = c_1 - multiply_mod(both, c_2)
        e_3 = reduce_centered(multiply_mod(start, c_3) + rest)
        out_ref[0] = canonical(-multiply_mod(e_3, start)) * (1.0 / MODULUS)
        out_ref[1] = canonical(start + multiply_mod(e_3, both)) * (1.0 / MODULUS)
        out_ref[2] = canonical(-both - e_3) * (1.0 / MODULUS)

    outs = [jax.ShapeDtypeStruct((STEP_COUNT, span, span), jnp.float32)]
    return call(kernel, [mine, other], outs)[0]


def local(tile_entries, tile_rows, tile_cols, tile_count, block_x, block_y):
    _, _, slot_count, tile_len, _ = tile_entries.shape
    span, piece_len = block_y.shape
    piece_blocks = piece_len // tile_len
    n_row, n_col = lax.axis_size("row"), lax.axis_size("col")
    packed_rows = span * span // piece_len
    tiles = (tile_rows, tile_cols, tile_count, tile_entries)
    sizes = (n_row, n_col, piece_blocks)
    is_dense = n_col * piece_blocks * n_row * piece_blocks <= DENSE_CELLS * slot_count
    if is_dense:
        dense, x_own, y_own, token = build_dense(tiles, block_x, block_y, sizes)
        before = [token]
    else:
        positions, a_digits = sparse_tiles(tiles, sizes)
        x_own, y_own, before = block_x, block_y, []

    def multiply_evens(evens):
        return dense_first(evens, span, dense) if is_dense else evens

    def multiply(evens, before=(), tails=()):
        odds, sums = gather_odds(evens, "row"), multiply_evens(evens)
        if is_dense:
            return dense_second(odds, evens, sums, span, n_col, tails, dense, before)
        return sparse_second(odds, evens, span, n_col, tails, positions, a_digits)

    y_came = fetch_evens(block_y, "row")
    x_came = fetch_evens(block_x, "col")
    evens = stack_after([y_own] + y_came, [*before, *x_came])
    x_evens = stack_after([x_own] + x_came)
    outs = multiply(evens, [x_evens])
    x_pairs = [x_evens, gather_odds(x_evens, "col")]
    if is_dense:
        w_kept, w_odds, term = dense_left(x_pairs, outs, n_row, dense)
    else:
        w_kept, w_odds, term = sparse_left(x_pairs, outs, n_row, positions, a_digits)
    vector_1 = sum_after(scatter_pieces(outs, "col"), [w_odds])
    w_came = fetch(w_odds, "row", 1)
    outs = multiply(gather_evens(vector_1, "row"), [w_came])
    pieces = scatter_pieces(outs, "col")
    shift, before = 2, []
    while shift < n_row:
        w_kept, w_sent, term = add_and_part(w_kept, w_came, term, before)
        w_came = fetch(w_sent, "row", shift)
        shift, before = 2 * shift, [outs[0]]
    term_came = fetch(term, "row", n_row // 2)
    vector_2, first = append_projections(w_kept, w_came, term, term_came, pieces, vector_1)
    outs = multiply(gather_evens(vector_2, "row"), tails=[first])
    pieces = scatter_pieces(outs, "col")
    terms = functools.reduce(jnp.add, [piece[span:] for piece in pieces])
    vector_3 = functools.reduce(jnp.add, [piece[:span] for piece in pieces])
    return sigma_update(terms, fetch(terms, "row", 1), span), canonical(vector_3) * (1.0 / MODULUS)


def solution(mesh):
    placed = (
        P("row", "col", None, None, None),
        P("row", "col", None),
        P("row", "col", None),
        P("row", "col"),
        P(None, ("row", "col")),
        P(None, ("row", "col")),
    )
    return jax.shard_map(
        local, mesh=mesh, in_specs=placed, out_specs=(P(), P(None, ("row", "col"))), check_vma=False
    )
```

```python
import functools

import jax
import jax.numpy as jnp
from jax import lax
from jax.experimental import pallas as pl
from jax.experimental.pallas import tpu as pltpu
from jax.sharding import PartitionSpec as P

STEP_COUNT = 3

MODULUS = 65521.0
HALF_MODULUS = 32760.0
BASE = 256.0
ROUND_TO_BASE = 1.5 * 2.0**31
EXACT_DEPTH = 1024
DENSE_CELLS = 4
VMEM_LIMIT = 16 * 1024 * 1024
SMALL_LIMIT = 4 * 1024 * 1024


def reduce_centered(values):
    return values - MODULUS * jnp.floor(values * (1.0 / MODULUS) + 0.5)


def canonical(values):
    reduced = reduce_centered(values)
    return jnp.where(reduced < 0, reduced + MODULUS, reduced)


def balanced_digits(values):
    high = jnp.floor(values * (1.0 / BASE) + 0.5)
    return high, values - BASE * high


def stacked_digits(values):
    high, low = balanced_digits(values)
    return jnp.concatenate([high, low], 0).astype(jnp.bfloat16)


def centred_digits(residues):
    return stacked_digits(jnp.where(residues > HALF_MODULUS, residues - MODULUS, residues))


def partner(index, shift, size):
    return index ^ shift if size & (size - 1) == 0 else (index + shift) % size


def shift_of(index, other, size):
    return index ^ other if size & (size - 1) == 0 else (other - index) % size


def fetch(piece, axis, shift):
    size = lax.axis_size(axis)
    return lax.ppermute(piece, axis, [(partner(i, shift, size), i) for i in range(size)])


def scatter_pieces(pieces, axis):
    size = lax.axis_size(axis)
    came = [
        lax.ppermute(pieces[shift], axis, [(i, partner(i, shift, size)) for i in range(size)])
        for shift in reversed(range(1, size))
    ]
    return [pieces[0]] + came


def call(kernel, operands, outs, before=(), scratch=(), limit=SMALL_LIMIT, flops=0):
    def body(*refs):
        kernel(*refs[: len(operands)], *refs[len(operands) + len(before) :])

    vmem = pl.BlockSpec(memory_space=pltpu.VMEM)
    return pl.pallas_call(
        body,
        in_specs=[vmem] * len(operands) + [pl.BlockSpec(memory_space=pl.ANY)] * len(before),
        out_specs=[vmem] * len(outs),
        out_shape=outs,
        scratch_shapes=list(scratch),
        compiler_params=pltpu.CompilerParams(vmem_limit_bytes=limit),
        cost_estimate=pl.CostEstimate(flops=flops, bytes_accessed=0, transcendentals=0),
    )(*(pltpu.with_memory_space_constraint(part, pltpu.VMEM) for part in operands), *before)


def held(*shape):
    return pltpu.VMEM(shape, jnp.float32)


def stack_after(pieces, before=()):
    def kernel(*refs):
        for index, ref in enumerate(refs[:-1]):
            refs[-1][index] = ref[...]

    return call(kernel, pieces, [held(len(pieces), *pieces[0].shape)], before)[0]


def sum_after(pieces, before=()):
    def kernel(*refs):
        refs[-1][...] = functools.reduce(jnp.add, [ref[...] for ref in refs[:-1]])

    return call(kernel, pieces, [held(*pieces[0].shape)], before)[0]


def fetch_evens(piece, axis):
    return [fetch(piece, axis, shift) for shift in range(2, lax.axis_size(axis), 2)]


def gather_evens(piece, axis, before=()):
    return stack_after([piece] + fetch_evens(piece, axis), before)


def gather_odds(evens, axis):
    size = lax.axis_size(axis)
    assert size > 1 and size & (size - 1) == 0
    return fetch(evens, axis, 1)


def dot_pairs(left, right):
    return lax.dot_general(left, right, (((1,), (1,)), ((), ())), preferred_element_type=jnp.float32)


def combine(high, middle, low):
    return reduce_centered(15.0 * high + 256.0 * reduce_centered(middle) + low)


def pack_square(square, width):
    span = square.shape[0]
    rows = span * span // width
    return jnp.concatenate([square[j * rows : (j + 1) * rows] for j in range(width // span)], 1)


def unpack_square(packed, span):
    count = packed.shape[1] // span
    return jnp.concatenate([packed[:, j * span : (j + 1) * span] for j in range(count)], 0)


def build_kernel(sizes, *refs):
    entries_ref, x_ref, y_ref, dense_ref, x_out, y_out, token_ref = refs[3:10]
    rows_ref, cols_ref, count_ref, tiles, sems = refs[10:]
    n_row, n_col, piece_blocks, group = sizes
    _, _, slot_count, tile_len, _ = entries_ref.shape
    me_row, me_col = lax.axis_index("row"), lax.axis_index("col")
    chunk_count = slot_count // group

    def chunk(index):
        source = entries_ref.at[0, 0, pl.ds(index * group, group)]
        return pltpu.make_async_copy(source, tiles.at[pl.ds(index * group, group)], sems.at[index])

    small = [*zip(refs[:3], refs[10:13]), (y_ref, y_out), (x_ref, x_out)]
    small = [
        pltpu.make_async_copy(source, target, sems.at[chunk_count + index])
        for index, (source, target) in enumerate(small)
    ]
    for copy in small[:3]:
        copy.start()
    sure_count = min(2, chunk_count)
    for index in range(sure_count):
        chunk(index).start()

    def clear(block, carry):
        dense_ref[block] = jnp.zeros(dense_ref.shape[1:], dense_ref.dtype)
        return carry

    half = dense_ref.shape[0] // 2
    lax.fori_loop(0, half, clear, 0)
    for copy in small[:3]:
        copy.wait()
    used_count = jnp.maximum((count_ref[0, 0] + group - 1) // group, sure_count)
    for index in range(sure_count, chunk_count):

        @pl.when(index < used_count)
        def _():
            chunk(index).start()

    for copy in small[3:]:
        copy.start()
    lax.fori_loop(half, dense_ref.shape[0], clear, 0)

    def cell(slot):
        row, col = rows_ref[0, 0, slot], cols_ref[0, 0, slot]
        row_shift = shift_of(me_col, row // piece_blocks, n_col)
        col_shift = shift_of(me_row, col // piece_blocks, n_row)
        col_place = col_shift % 2 * (n_row // 2) + col_shift // 2
        block = row_shift * piece_blocks + row % piece_blocks
        start = (col_place * piece_blocks + col % piece_blocks) * tile_len
        return block, pl.ds(pl.multiple_of(start, tile_len), tile_len)

    def place(slot):
        values = tiles[slot]
        values = jnp.where(values > HALF_MODULUS, values - MODULUS, values).T
        rounded = (values + ROUND_TO_BASE) - ROUND_TO_BASE
        both = jnp.concatenate([rounded * (1.0 / BASE), values - rounded], 1)
        block, columns = cell(slot)
        dense_ref[block, columns, :] = both.astype(jnp.bfloat16)

    def step(index, carry):
        chunk(index).wait()
        for offset in range(group):
            place(index * group + offset)
        return carry

    lax.fori_loop(0, used_count, step, 0)

    def erase(slot, carry):
        block, columns = cell(slot)
        dense_ref[block, columns, :] = jnp.zeros((tile_len, 2 * tile_len), dense_ref.dtype)
        return carry

    lax.fori_loop(count_ref[0, 0], used_count * group, erase, 0)
    for copy in small[3:]:
        copy.wait()
    token_ref[...] = jnp.zeros_like(token_ref)


def build_dense(tiles, block_x, block_y, sizes):
    tile_rows, tile_cols, tile_count, tile_entries = tiles
    n_row, n_col, piece_blocks = sizes
    _, _, slot_count, tile_len, _ = tile_entries.shape
    group = next(size for size in (8, 4, 2, 1) if slot_count % size == 0)
    shape = (n_col * piece_blocks, n_row * piece_blocks * tile_len, 2 * tile_len)
    hbm = pl.BlockSpec(memory_space=pltpu.HBM)
    rows, cols, entries, x_piece, y_piece = (
        pltpu.with_memory_space_constraint(part, pltpu.HBM)
        for part in (tile_rows, tile_cols, tile_entries, block_x, block_y)
    )
    return pl.pallas_call(
        functools.partial(build_kernel, (*sizes, group)),
        in_specs=[hbm, hbm, pl.BlockSpec(memory_space=pl.ANY), hbm, hbm, hbm],
        out_specs=[pl.BlockSpec(memory_space=pltpu.VMEM)] * 4,
        out_shape=[
            pltpu.VMEM(shape, jnp.bfloat16),
            held(*block_x.shape),
            held(*block_y.shape),
            held(8, 128),
        ],
        scratch_shapes=[
            *(pltpu.SMEM(part.shape, part.dtype) for part in (tile_rows, tile_cols, tile_count)),
            pltpu.VMEM((slot_count, tile_len, tile_len), jnp.float32),
            pltpu.SemaphoreType.DMA((slot_count // group + 5,)),
        ],
        compiler_params=pltpu.CompilerParams(vmem_limit_bytes=VMEM_LIMIT),
        cost_estimate=pl.CostEstimate(
            flops=8 * tile_entries.size, bytes_accessed=8 * tile_entries.size, transcendentals=0
        ),
    )(rows, cols, tile_count, entries, x_piece, y_piece)


def half_products(half, span, pieces_ref, dense_ref, digits, block):
    _, depth, width = dense_ref.shape
    tile_len, half_depth = width // 2, depth // 2
    high = middle = low = 0.0
    for start in range(0, half_depth, EXACT_DEPTH):
        stop = min(start + EXACT_DEPTH, half_depth)
        products = jnp.dot(
            digits[:, start:stop],
            dense_ref[block, half * half_depth + start : half * half_depth + stop, :],
            preferred_element_type=jnp.float32,
        )
        products = reduce_centered(products)
        high = high + products[:span, :tile_len]
        middle = middle + products[:span, tile_len:] + products[span:, :tile_len]
        low = low + products[span:, tile_len:]
    return high, middle, low


def fill_digits(span, pieces_ref, digits):
    piece_len = pieces_ref.shape[2]
    for d in range(pieces_ref.shape[0]):
        vector = reduce_centered(pieces_ref[d, :span, :])
        digits[:, d * piece_len : (d + 1) * piece_len] = stacked_digits(vector)


def first_half_kernel(span, pieces_ref, dense_ref, sums_ref, digits):
    fill_digits(span, pieces_ref, digits)
    tile_len = dense_ref.shape[2] // 2
    for block in range(dense_ref.shape[0]):
        parts = half_products(0, span, pieces_ref, dense_ref, digits, block)
        for index, part in enumerate(parts):
            sums_ref[index, :, block * tile_len : (block + 1) * tile_len] = part


def half_of_core(packed):
    rows = packed.shape[0] // 2
    return jnp.where(lax.axis_index("row") % 2 == 0, packed[:rows], packed[rows:])


def second_half_kernel(span, n_col, pieces_ref, evens_ref, sums_ref, dense_ref, *refs):
    tails, outs, digits = refs[: -n_col - 1], refs[-n_col - 1 : -1], refs[-1]
    fill_digits(span, pieces_ref, digits)
    row_blocks, _, width = dense_ref.shape
    tile_len = width // 2
    piece_blocks = row_blocks // n_col
    for e in reversed(range(n_col)):
        for sub in range(piece_blocks):
            block = e * piece_blocks + sub
            parts = half_products(1, span, pieces_ref, dense_ref, digits, block)
            parts = (
                part + sums_ref[index, :, block * tile_len : (block + 1) * tile_len]
                for index, part in enumerate(parts)
            )
            outs[e][:span, sub * tile_len : (sub + 1) * tile_len] = combine(*parts)
    if outs[0].shape[0] > span:
        packed = jnp.sum(pieces_ref[:, span:, :], 0) + jnp.sum(evens_ref[:, span:, :], 0)
        packed = half_of_core(jnp.concatenate([packed, *(tail[...] for tail in tails)], 0))
        for out in outs:
            out[span:, :] = packed


def whole_kernel(span, odds_ref, evens_ref, dense_ref, *refs):
    outs, even_digits, odd_digits = refs[:-2], refs[-2], refs[-1]
    fill_digits(span, evens_ref, even_digits)
    fill_digits(span, odds_ref, odd_digits)
    tile_len = dense_ref.shape[2] // 2
    piece_blocks = dense_ref.shape[0] // len(outs)
    for e in reversed(range(len(outs))):
        for sub in range(piece_blocks):
            block = e * piece_blocks + sub
            first = half_products(0, span, evens_ref, dense_ref, even_digits, block)
            second = half_products(1, span, odds_ref, dense_ref, odd_digits, block)
            parts = (left + right for left, right in zip(first, second))
            outs[e][:, sub * tile_len : (sub + 1) * tile_len] = combine(*parts)


def dense_whole(odds, evens, span, n_col, dense, before):
    _, depth, _ = dense.shape
    _, _, piece_len = odds.shape
    return list(
        call(
            functools.partial(whole_kernel, span),
            [odds, evens, dense],
            [held(span, piece_len)] * n_col,
            before,
            scratch=[pltpu.VMEM((2 * span, depth // 2), jnp.bfloat16)] * 2,
            limit=VMEM_LIMIT,
            flops=4 * span * dense.size,
        )
    )


def dense_first(evens, span, dense):
    row_blocks, depth, width = dense.shape
    return call(
        functools.partial(first_half_kernel, span),
        [evens, dense],
        [held(3, span, row_blocks * width // 2)],
        scratch=[pltpu.VMEM((2 * span, depth // 2), jnp.bfloat16)],
        limit=VMEM_LIMIT,
        flops=2 * span * dense.size,
    )[0]


def dense_second(odds, evens, sums, span, n_col, tails, dense, before):
    _, depth, _ = dense.shape
    _, rows, piece_len = odds.shape
    rows = rows + sum(tail.shape[0] for tail in tails)
    return list(
        call(
            functools.partial(second_half_kernel, span, n_col),
            [odds, evens, sums, dense, *tails],
            [held(span + (rows - span) // 2, piece_len)] * n_col,
            before,
            scratch=[pltpu.VMEM((2 * span, depth // 2), jnp.bfloat16)],
            limit=VMEM_LIMIT,
            flops=2 * span * dense.size,
        )
    )


def project(terms):
    products = functools.reduce(jnp.add, [dot_pairs(left, right) for left, right in terms])
    span = products.shape[0] // 2
    square = combine(
        reduce_centered(products[:span, :span]),
        reduce_centered(products[:span, span:]) + reduce_centered(products[span:, :span]),
        reduce_centered(products[span:, span:]),
    )
    return pack_square(square, terms[0][0].shape[1])


def left_kernel(n_row, x_evens, x_odds, dense_ref, *refs):
    rows_refs, (evens_ref, odds_ref, term_ref) = refs[:-3], refs[-3:]
    row_blocks, _, width = dense_ref.shape
    tile_len = width // 2
    _, span, piece_len = x_evens.shape
    piece_blocks = piece_len // tile_len
    x_digits = [
        centred_digits((x_odds if e % 2 else x_evens)[e // 2])
        for e in range(row_blocks // piece_blocks)
    ]
    term = project([(x, stacked_digits(ref[...])) for x, ref in zip(x_digits, rows_refs)])
    term_ref[...] = term
    part_rows = term.shape[0] // odds_ref.shape[0]
    for place in range(n_row):
        by_high = by_low = high_part = low_part = 0.0
        for block in range(row_blocks):
            sub = block % piece_blocks
            left = x_digits[block // piece_blocks][:, sub * tile_len : (sub + 1) * tile_len]
            right = dense_ref[block, place * piece_len : (place + 1) * piece_len, :]
            high_part = high_part + dot_pairs(left, right[:, :tile_len])
            low_part = low_part + dot_pairs(left, right[:, tile_len:])
            if (block + 1) * tile_len % EXACT_DEPTH == 0 or block == row_blocks - 1:
                by_high = by_high + reduce_centered(high_part)
                by_low = by_low + reduce_centered(low_part)
                high_part = low_part = 0.0
        piece = combine(by_high[:span], by_low[:span] + by_high[span:], by_low[span:])
        if place < n_row // 2:
            evens_ref[place] = piece
        else:
            index = place - n_row // 2
            odds_ref[index, :span, :] = piece
            odds_ref[index, span:, :] = term[index * part_rows : (index + 1) * part_rows]


def dense_left(x_pairs, outs, n_row, dense):
    _, span, piece_len = x_pairs[0].shape
    count, rows = n_row // 2, span * span // piece_len
    return call(
        functools.partial(left_kernel, n_row),
        [*x_pairs, dense, *outs],
        [
            held(count, span, piece_len),
            held(count, span + rows // count, piece_len),
            held(rows, piece_len),
        ],
        limit=VMEM_LIMIT,
        flops=4 * span * dense.size,
    )


def sparse_tiles(tiles, sizes):
    tile_rows, tile_cols, tile_count, tile_entries = tiles
    n_row, n_col, piece_blocks = sizes
    entries, rows, cols = tile_entries[0, 0], tile_rows[0, 0], tile_cols[0, 0]
    row_shift = shift_of(lax.axis_index("col"), rows // piece_blocks, n_col)
    col_shift = shift_of(lax.axis_index("row"), cols // piece_blocks, n_row)
    col_place = col_shift % 2 * (n_row // 2) + col_shift // 2
    positions = (
        row_shift * piece_blocks + rows % piece_blocks,
        col_place * piece_blocks + cols % piece_blocks,
        tile_count[0, 0],
    )
    entries = jnp.where(entries > HALF_MODULUS, entries - MODULUS, entries)
    return positions, jnp.stack(balanced_digits(entries), 1).astype(jnp.bfloat16)


def sparse_product(vector, spec, places, targets, count, blocks, a_digits):
    span, tile_len = vector.shape[0], a_digits.shape[-1]
    v_digits = stacked_digits(vector).reshape(2 * span, -1, tile_len)
    picked = jnp.take(v_digits, places, axis=1)
    products = jnp.einsum(spec, picked, a_digits, preferred_element_type=jnp.float32)
    products = reduce_centered(products)
    residues = combine(
        products[:, 0, :span],
        products[:, 0, span:] + products[:, 1, :span],
        products[:, 1, span:],
    )
    live = jnp.arange(targets.shape[0], dtype=jnp.int32) < count
    onehot = targets[None, :] == jnp.arange(blocks, dtype=jnp.int32)[:, None]
    onehot = (onehot & live[None, :]).astype(jnp.float32)
    summed = jnp.einsum("bt,twi->wbi", onehot, residues, precision=lax.Precision.HIGHEST)
    return reduce_centered(summed).reshape(span, blocks * tile_len)


def sparse_second(odds, evens, span, n_col, tails, positions, a_digits):
    rows, cols, count = positions
    pieces = [*evens, *odds]
    piece_len = pieces[0].shape[1]
    blocks = n_col * piece_len // a_digits.shape[-1]
    vector = reduce_centered(jnp.concatenate([piece[:span] for piece in pieces], 1))
    product = sparse_product(vector, "ntk,tdik->tdni", cols, rows, count, blocks, a_digits)
    packed = functools.reduce(jnp.add, [piece[span:] for piece in pieces])
    packed = half_of_core(jnp.concatenate([packed, *tails], 0))
    outs = [product[:, e * piece_len : (e + 1) * piece_len] for e in range(n_col)]
    return [jnp.concatenate([out, packed], 0) for out in outs]


def sparse_left(x_pairs, outs, n_row, positions, a_digits):
    rows, cols, count = positions
    n_col = 2 * x_pairs[0].shape[0]
    x_pieces = [x_pairs[e % 2][e // 2] for e in range(n_col)]
    piece_len = x_pieces[0].shape[1]
    values = jnp.concatenate(x_pieces, 1)
    values = jnp.where(values > HALF_MODULUS, values - MODULUS, values)
    blocks = n_row * piece_len // a_digits.shape[-1]
    product = sparse_product(values, "nti,tdik->tdnk", rows, cols, count, blocks, a_digits)
    pieces = [product[:, d * piece_len : (d + 1) * piece_len] for d in range(n_row)]
    term = 0.0
    for x_piece, rows_piece in zip(x_pieces, outs):
        term = term + project([(centred_digits(x_piece), stacked_digits(rows_piece))])
    odds = jnp.stack(pieces[n_row // 2 :])
    below = term.reshape(odds.shape[0], -1, piece_len)
    return jnp.stack(pieces[: n_row // 2]), jnp.concatenate([odds, below], 1), term


def add_and_part(kept, came, term, before=()):
    count, span, piece_len = kept.shape
    half, rows = count // 2, term.shape[0]
    part = rows // half if half > 1 else 0

    def kernel(kept_ref, came_ref, term_ref, evens_ref, odds_ref, out_ref):
        below = [came_ref[index, span:, :] for index in range(count)]
        total = term_ref[...] + jnp.concatenate(below, 0)
        out_ref[...] = total
        for index in range(count):
            piece = kept_ref[index] + came_ref[index, :span, :]
            if index % 2 == 0:
                evens_ref[index // 2] = piece
            else:
                odds_ref[index // 2, :span, :] = piece
        if part:
            for index in range(half):
                odds_ref[index, span:, :] = total[index * part : (index + 1) * part]

    outs = [
        held(half, span, piece_len),
        held(half, span + part, piece_len),
        held(rows, piece_len),
    ]
    return call(kernel, [kept, came, term], outs, before)


def append_projections(kept, came, term, term_came, pieces, vector_1):
    span, piece_len = pieces[0].shape
    rows = term.shape[0]

    def kernel(*refs):
        piece_refs, refs = refs[: len(pieces)], refs[len(pieces) :]
        vector_ref, kept_ref, came_ref, term_ref, term_came_ref, out_ref, first_ref = refs
        summed = functools.reduce(jnp.add, [ref[...] for ref in piece_refs])
        out_ref[:span, :] = summed
        w_digits = stacked_digits(reduce_centered(kept_ref[0] + came_ref[0]))
        first_ref[...] = term_ref[...] + term_came_ref[...]
        for index, vector in enumerate([summed, vector_ref[...]]):
            start = span + index * rows
            digits = stacked_digits(reduce_centered(vector))
            out_ref[start : start + rows, :] = project([(w_digits, digits)])

    outs = [held(span + 2 * rows, piece_len), held(rows, piece_len)]
    return call(kernel, [*pieces, vector_1, kept, came, term, term_came], outs)


def multiply_mod(left, right):
    span = left.shape[0]
    left = stacked_digits(left)
    high, low = (part.astype(jnp.bfloat16) for part in balanced_digits(right))
    by_high = jnp.dot(left, high, preferred_element_type=jnp.float32)
    by_low = jnp.dot(left, low, preferred_element_type=jnp.float32)
    return combine(
        reduce_centered(by_high[:span]), by_low[:span] + by_high[span:], by_low[span:]
    )


def sigma_update(mine, other, span):
    rows = span * span // mine.shape[1]

    def kernel(mine_ref, other_ref, out_ref):
        first = lax.axis_index("row") % 2 == 0
        mine, other = reduce_centered(mine_ref[...]), reduce_centered(other_ref[...])
        packed = jnp.concatenate([jnp.where(first, mine, other), jnp.where(first, other, mine)], 0)
        c_3, c_2, c_1 = (
            unpack_square(packed[index * rows : (index + 1) * rows], span) for index in range(3)
        )
        e_2 = reduce_centered(c_1 - multiply_mod(c_1, c_2))
        both = reduce_centered(c_1 + e_2)
        start = multiply_mod(e_2, c_1)
        rest = c_1 - multiply_mod(both, c_2)
        e_3 = reduce_centered(multiply_mod(start, c_3) + rest)
        out_ref[0] = canonical(-multiply_mod(e_3, start)) * (1.0 / MODULUS)
        out_ref[1] = canonical(start + multiply_mod(e_3, both)) * (1.0 / MODULUS)
        out_ref[2] = canonical(-both - e_3) * (1.0 / MODULUS)

    outs = [jax.ShapeDtypeStruct((STEP_COUNT, span, span), jnp.float32)]
    return call(kernel, [mine, other], outs)[0]


def local(tile_entries, tile_rows, tile_cols, tile_count, block_x, block_y):
    _, _, slot_count, tile_len, _ = tile_entries.shape
    span, piece_len = block_y.shape
    piece_blocks = piece_len // tile_len
    n_row, n_col = lax.axis_size("row"), lax.axis_size("col")
    packed_rows = span * span // piece_len
    tiles = (tile_rows, tile_cols, tile_count, tile_entries)
    sizes = (n_row, n_col, piece_blocks)
    is_dense = n_col * piece_blocks * n_row * piece_blocks <= DENSE_CELLS * slot_count
    if is_dense:
        dense, x_own, y_own, token = build_dense(tiles, block_x, block_y, sizes)
        before = [token]
    else:
        positions, a_digits = sparse_tiles(tiles, sizes)
        x_own, y_own, before = block_x, block_y, []

    def multiply_evens(evens):
        return dense_first(evens, span, dense) if is_dense else evens

    def multiply(evens, before=(), tails=()):
        odds, sums = gather_odds(evens, "row"), multiply_evens(evens)
        if is_dense:
            return dense_second(odds, evens, sums, span, n_col, tails, dense, before)
        return sparse_second(odds, evens, span, n_col, tails, positions, a_digits)

    y_came = fetch_evens(block_y, "row")
    x_came = fetch_evens(block_x, "col")
    evens = stack_after([y_own] + y_came, [*before, *x_came])
    x_evens = stack_after([x_own] + x_came)
    outs = multiply(evens, [x_evens])
    x_pairs = [x_evens, gather_odds(x_evens, "col")]
    if is_dense:
        w_kept, w_odds, term = dense_left(x_pairs, outs, n_row, dense)
    else:
        w_kept, w_odds, term = sparse_left(x_pairs, outs, n_row, positions, a_digits)
    vector_1 = sum_after(scatter_pieces(outs, "col"), [w_odds])
    w_came = fetch(w_odds, "row", 1)
    evens = gather_evens(vector_1, "row")
    if is_dense:
        outs = dense_whole(gather_odds(evens, "row"), evens, span, n_col, dense, [w_came])
    else:
        outs = multiply(evens)
    pieces = scatter_pieces(outs, "col")
    shift, before = 2, []
    while shift < n_row:
        w_kept, w_sent, term = add_and_part(w_kept, w_came, term, before)
        w_came = fetch(w_sent, "row", shift)
        shift, before = 2 * shift, [outs[0]]
    term_came = fetch(term, "row", n_row // 2)
    vector_2, first = append_projections(w_kept, w_came, term, term_came, pieces, vector_1)
    outs = multiply(gather_evens(vector_2, "row"), tails=[first])
    pieces = scatter_pieces(outs, "col")
    terms = functools.reduce(jnp.add, [piece[span:] for piece in pieces])
    vector_3 = functools.reduce(jnp.add, [piece[:span] for piece in pieces])
    return sigma_update(terms, fetch(terms, "row", 1), span), canonical(vector_3) * (1.0 / MODULUS)


def solution(mesh):
    placed = (
        P("row", "col", None, None, None),
        P("row", "col", None),
        P("row", "col", None),
        P("row", "col"),
        P(None, ("row", "col")),
        P(None, ("row", "col")),
    )
    return jax.shard_map(
        local, mesh=mesh, in_specs=placed, out_specs=(P(), P(None, ("row", "col"))), check_vma=False
    )
```

```python
import functools

import jax
import jax.numpy as jnp
from jax import lax
from jax.experimental import pallas as pl
from jax.experimental.pallas import tpu as pltpu
from jax.sharding import PartitionSpec as P

STEP_COUNT = 3

MODULUS = 65521.0
HALF_MODULUS = 32760.0
BASE = 256.0
ROUND_TO_BASE = 1.5 * 2.0**31
EXACT_DEPTH = 1024
DENSE_CELLS = 4
VMEM_LIMIT = 16 * 1024 * 1024
SMALL_LIMIT = 4 * 1024 * 1024


def reduce_centered(values):
    return values - MODULUS * jnp.floor(values * (1.0 / MODULUS) + 0.5)


def canonical(values):
    reduced = reduce_centered(values)
    return jnp.where(reduced < 0, reduced + MODULUS, reduced)


def balanced_digits(values):
    high = jnp.floor(values * (1.0 / BASE) + 0.5)
    return high, values - BASE * high


def stacked_digits(values):
    high, low = balanced_digits(values)
    return jnp.concatenate([high, low], 0).astype(jnp.bfloat16)


def centred_digits(residues):
    return stacked_digits(jnp.where(residues > HALF_MODULUS, residues - MODULUS, residues))


def partner(index, shift, size):
    return index ^ shift if size & (size - 1) == 0 else (index + shift) % size


def shift_of(index, other, size):
    return index ^ other if size & (size - 1) == 0 else (other - index) % size


def fetch(piece, axis, shift):
    size = lax.axis_size(axis)
    return lax.ppermute(piece, axis, [(partner(i, shift, size), i) for i in range(size)])


def scatter_pieces(pieces, axis):
    size = lax.axis_size(axis)
    came = [
        lax.ppermute(pieces[shift], axis, [(i, partner(i, shift, size)) for i in range(size)])
        for shift in reversed(range(1, size))
    ]
    return [pieces[0]] + came


def call(kernel, operands, outs, before=(), scratch=(), limit=SMALL_LIMIT, flops=0):
    def body(*refs):
        kernel(*refs[: len(operands)], *refs[len(operands) + len(before) :])

    vmem = pl.BlockSpec(memory_space=pltpu.VMEM)
    return pl.pallas_call(
        body,
        in_specs=[vmem] * len(operands) + [pl.BlockSpec(memory_space=pl.ANY)] * len(before),
        out_specs=[vmem] * len(outs),
        out_shape=outs,
        scratch_shapes=list(scratch),
        compiler_params=pltpu.CompilerParams(vmem_limit_bytes=limit),
        cost_estimate=pl.CostEstimate(flops=flops, bytes_accessed=0, transcendentals=0),
    )(*(pltpu.with_memory_space_constraint(part, pltpu.VMEM) for part in operands), *before)


def held(*shape):
    return pltpu.VMEM(shape, jnp.float32)


def stack_after(pieces, before=()):
    def kernel(*refs):
        for index, ref in enumerate(refs[:-1]):
            refs[-1][index] = ref[...]

    return call(kernel, pieces, [held(len(pieces), *pieces[0].shape)], before)[0]


def sum_after(pieces, before=()):
    def kernel(*refs):
        refs[-1][...] = functools.reduce(jnp.add, [ref[...] for ref in refs[:-1]])

    return call(kernel, pieces, [held(*pieces[0].shape)], before)[0]


def fetch_evens(piece, axis):
    return [fetch(piece, axis, shift) for shift in range(2, lax.axis_size(axis), 2)]


def gather_evens(piece, axis, before=()):
    return stack_after([piece] + fetch_evens(piece, axis), before)


def gather_odds(evens, axis):
    size = lax.axis_size(axis)
    assert size > 1 and size & (size - 1) == 0
    return fetch(evens, axis, 1)


def dot_pairs(left, right):
    return lax.dot_general(left, right, (((1,), (1,)), ((), ())), preferred_element_type=jnp.float32)


def combine(high, middle, low):
    return reduce_centered(15.0 * high + 256.0 * reduce_centered(middle) + low)


def pack_square(square, width):
    span = square.shape[0]
    rows = span * span // width
    return jnp.concatenate([square[j * rows : (j + 1) * rows] for j in range(width // span)], 1)


def unpack_square(packed, span):
    count = packed.shape[1] // span
    return jnp.concatenate([packed[:, j * span : (j + 1) * span] for j in range(count)], 0)


def build_kernel(sizes, *refs):
    entries_ref, x_ref, y_ref, dense_ref, x_out, y_out, token_ref = refs[3:10]
    rows_ref, cols_ref, count_ref, tiles, sems = refs[10:]
    n_row, n_col, piece_blocks, group = sizes
    _, _, slot_count, tile_len, _ = entries_ref.shape
    me_row, me_col = lax.axis_index("row"), lax.axis_index("col")
    chunk_count = slot_count // group

    def chunk(index):
        source = entries_ref.at[0, 0, pl.ds(index * group, group)]
        return pltpu.make_async_copy(source, tiles.at[pl.ds(index * group, group)], sems.at[index])

    small = [*zip(refs[:3], refs[10:13]), (y_ref, y_out), (x_ref, x_out)]
    small = [
        pltpu.make_async_copy(source, target, sems.at[chunk_count + index])
        for index, (source, target) in enumerate(small)
    ]
    for copy in small[:3]:
        copy.start()
    sure_count = min(2, chunk_count)
    for index in range(sure_count):
        chunk(index).start()

    def clear(block, carry):
        dense_ref[block] = jnp.zeros(dense_ref.shape[1:], dense_ref.dtype)
        return carry

    half = dense_ref.shape[0] // 2
    lax.fori_loop(0, half, clear, 0)
    for copy in small[:3]:
        copy.wait()
    used_count = jnp.maximum((count_ref[0, 0] + group - 1) // group, sure_count)
    for index in range(sure_count, chunk_count):

        @pl.when(index < used_count)
        def _():
            chunk(index).start()

    for copy in small[3:]:
        copy.start()
    lax.fori_loop(half, dense_ref.shape[0], clear, 0)

    def cell(slot):
        row, col = rows_ref[0, 0, slot], cols_ref[0, 0, slot]
        row_shift = shift_of(me_col, row // piece_blocks, n_col)
        col_shift = shift_of(me_row, col // piece_blocks, n_row)
        col_place = col_shift % 2 * (n_row // 2) + col_shift // 2
        block = row_shift * piece_blocks + row % piece_blocks
        start = (col_place * piece_blocks + col % piece_blocks) * tile_len
        return block, pl.ds(pl.multiple_of(start, tile_len), tile_len)

    def place(slot):
        values = tiles[slot]
        values = jnp.where(values > HALF_MODULUS, values - MODULUS, values).T
        rounded = (values + ROUND_TO_BASE) - ROUND_TO_BASE
        both = jnp.concatenate([rounded * (1.0 / BASE), values - rounded], 1)
        block, columns = cell(slot)
        dense_ref[block, columns, :] = both.astype(jnp.bfloat16)

    def step(index, carry):
        chunk(index).wait()
        for offset in range(group):
            place(index * group + offset)
        return carry

    lax.fori_loop(0, used_count, step, 0)

    def erase(slot, carry):
        block, columns = cell(slot)
        dense_ref[block, columns, :] = jnp.zeros((tile_len, 2 * tile_len), dense_ref.dtype)
        return carry

    lax.fori_loop(count_ref[0, 0], used_count * group, erase, 0)
    for copy in small[3:]:
        copy.wait()
    token_ref[...] = jnp.zeros_like(token_ref)


def build_dense(tiles, block_x, block_y, sizes):
    tile_rows, tile_cols, tile_count, tile_entries = tiles
    n_row, n_col, piece_blocks = sizes
    _, _, slot_count, tile_len, _ = tile_entries.shape
    group = next(size for size in (8, 4, 2, 1) if slot_count % size == 0)
    shape = (n_col * piece_blocks, n_row * piece_blocks * tile_len, 2 * tile_len)
    hbm = pl.BlockSpec(memory_space=pltpu.HBM)
    rows, cols, entries, x_piece, y_piece = (
        pltpu.with_memory_space_constraint(part, pltpu.HBM)
        for part in (tile_rows, tile_cols, tile_entries, block_x, block_y)
    )
    return pl.pallas_call(
        functools.partial(build_kernel, (*sizes, group)),
        in_specs=[hbm, hbm, pl.BlockSpec(memory_space=pl.ANY), hbm, hbm, hbm],
        out_specs=[pl.BlockSpec(memory_space=pltpu.VMEM)] * 4,
        out_shape=[
            pltpu.VMEM(shape, jnp.bfloat16),
            held(*block_x.shape),
            held(*block_y.shape),
            held(8, 128),
        ],
        scratch_shapes=[
            *(pltpu.SMEM(part.shape, part.dtype) for part in (tile_rows, tile_cols, tile_count)),
            pltpu.VMEM((slot_count, tile_len, tile_len), jnp.float32),
            pltpu.SemaphoreType.DMA((slot_count // group + 5,)),
        ],
        compiler_params=pltpu.CompilerParams(vmem_limit_bytes=VMEM_LIMIT),
        cost_estimate=pl.CostEstimate(
            flops=8 * tile_entries.size, bytes_accessed=8 * tile_entries.size, transcendentals=0
        ),
    )(rows, cols, tile_count, entries, x_piece, y_piece)


def half_products(half, span, pieces_ref, dense_ref, digits, block):
    _, depth, width = dense_ref.shape
    tile_len, half_depth = width // 2, depth // 2
    high = middle = low = 0.0
    for start in range(0, half_depth, EXACT_DEPTH):
        stop = min(start + EXACT_DEPTH, half_depth)
        products = jnp.dot(
            digits[:, start:stop],
            dense_ref[block, half * half_depth + start : half * half_depth + stop, :],
            preferred_element_type=jnp.float32,
        )
        products = reduce_centered(products)
        high = high + products[:span, :tile_len]
        middle = middle + products[:span, tile_len:] + products[span:, :tile_len]
        low = low + products[span:, tile_len:]
    return high, middle, low


def fill_digits(span, pieces_ref, digits):
    piece_len = pieces_ref.shape[2]
    for d in range(pieces_ref.shape[0]):
        vector = reduce_centered(pieces_ref[d, :span, :])
        digits[:, d * piece_len : (d + 1) * piece_len] = stacked_digits(vector)


def first_half_kernel(span, pieces_ref, dense_ref, sums_ref, digits):
    fill_digits(span, pieces_ref, digits)
    tile_len = dense_ref.shape[2] // 2
    for block in range(dense_ref.shape[0]):
        parts = half_products(0, span, pieces_ref, dense_ref, digits, block)
        sums_ref[:, block * tile_len : (block + 1) * tile_len] = combine(*parts)


def half_of_core(packed):
    rows = packed.shape[0] // 2
    return jnp.where(lax.axis_index("row") % 2 == 0, packed[:rows], packed[rows:])


def second_half_kernel(span, n_col, pieces_ref, evens_ref, sums_ref, dense_ref, *refs):
    tails, outs, digits = refs[: -n_col - 1], refs[-n_col - 1 : -1], refs[-1]
    fill_digits(span, pieces_ref, digits)
    row_blocks, _, width = dense_ref.shape
    tile_len = width // 2
    piece_blocks = row_blocks // n_col
    for e in reversed(range(n_col)):
        for sub in range(piece_blocks):
            block = e * piece_blocks + sub
            parts = half_products(1, span, pieces_ref, dense_ref, digits, block)
            first = sums_ref[:, block * tile_len : (block + 1) * tile_len]
            outs[e][:span, sub * tile_len : (sub + 1) * tile_len] = combine(*parts) + first
    if outs[0].shape[0] > span:
        packed = jnp.sum(pieces_ref[:, span:, :], 0) + jnp.sum(evens_ref[:, span:, :], 0)
        packed = half_of_core(jnp.concatenate([packed, *(tail[...] for tail in tails)], 0))
        for out in outs:
            out[span:, :] = packed


def whole_kernel(span, odds_ref, evens_ref, dense_ref, *refs):
    outs, even_digits, odd_digits = refs[:-2], refs[-2], refs[-1]
    fill_digits(span, evens_ref, even_digits)
    fill_digits(span, odds_ref, odd_digits)
    tile_len = dense_ref.shape[2] // 2
    piece_blocks = dense_ref.shape[0] // len(outs)
    for e in reversed(range(len(outs))):
        for sub in range(piece_blocks):
            block = e * piece_blocks + sub
            first = half_products(0, span, evens_ref, dense_ref, even_digits, block)
            second = half_products(1, span, odds_ref, dense_ref, odd_digits, block)
            parts = (left + right for left, right in zip(first, second))
            outs[e][:, sub * tile_len : (sub + 1) * tile_len] = combine(*parts)


def dense_whole(odds, evens, span, n_col, dense, before):
    _, depth, _ = dense.shape
    _, _, piece_len = odds.shape
    return list(
        call(
            functools.partial(whole_kernel, span),
            [odds, evens, dense],
            [held(span, piece_len)] * n_col,
            before,
            scratch=[pltpu.VMEM((2 * span, depth // 2), jnp.bfloat16)] * 2,
            limit=VMEM_LIMIT,
            flops=4 * span * dense.size,
        )
    )


def dense_first(evens, span, dense):
    row_blocks, depth, width = dense.shape
    return call(
        functools.partial(first_half_kernel, span),
        [evens, dense],
        [held(span, row_blocks * width // 2)],
        scratch=[pltpu.VMEM((2 * span, depth // 2), jnp.bfloat16)],
        limit=VMEM_LIMIT,
        flops=2 * span * dense.size,
    )[0]


def dense_second(odds, evens, sums, span, n_col, tails, dense, before):
    _, depth, _ = dense.shape
    _, rows, piece_len = odds.shape
    rows = rows + sum(tail.shape[0] for tail in tails)
    return list(
        call(
            functools.partial(second_half_kernel, span, n_col),
            [odds, evens, sums, dense, *tails],
            [held(span + (rows - span) // 2, piece_len)] * n_col,
            before,
            scratch=[pltpu.VMEM((2 * span, depth // 2), jnp.bfloat16)],
            limit=VMEM_LIMIT,
            flops=2 * span * dense.size,
        )
    )


def project(terms):
    products = functools.reduce(jnp.add, [dot_pairs(left, right) for left, right in terms])
    span = products.shape[0] // 2
    square = combine(
        reduce_centered(products[:span, :span]),
        reduce_centered(products[:span, span:]) + reduce_centered(products[span:, :span]),
        reduce_centered(products[span:, span:]),
    )
    return pack_square(square, terms[0][0].shape[1])


def left_kernel(n_row, x_evens, x_odds, dense_ref, *refs):
    rows_refs, (evens_ref, odds_ref, term_ref) = refs[:-3], refs[-3:]
    row_blocks, _, width = dense_ref.shape
    tile_len = width // 2
    _, span, piece_len = x_evens.shape
    piece_blocks = piece_len // tile_len
    x_digits = [
        centred_digits((x_odds if e % 2 else x_evens)[e // 2])
        for e in range(row_blocks // piece_blocks)
    ]
    rows = [stacked_digits(reduce_centered(ref[...])) for ref in rows_refs]
    term = project([*zip(x_digits, rows)])
    term_ref[...] = term
    part_rows = term.shape[0] // odds_ref.shape[0]
    for place in range(n_row):
        by_high = by_low = high_part = low_part = 0.0
        for block in range(row_blocks):
            sub = block % piece_blocks
            left = x_digits[block // piece_blocks][:, sub * tile_len : (sub + 1) * tile_len]
            right = dense_ref[block, place * piece_len : (place + 1) * piece_len, :]
            high_part = high_part + dot_pairs(left, right[:, :tile_len])
            low_part = low_part + dot_pairs(left, right[:, tile_len:])
            if (block + 1) * tile_len % EXACT_DEPTH == 0 or block == row_blocks - 1:
                by_high = by_high + reduce_centered(high_part)
                by_low = by_low + reduce_centered(low_part)
                high_part = low_part = 0.0
        piece = combine(by_high[:span], by_low[:span] + by_high[span:], by_low[span:])
        if place < n_row // 2:
            evens_ref[place] = piece
        else:
            index = place - n_row // 2
            odds_ref[index, :span, :] = piece
            odds_ref[index, span:, :] = term[index * part_rows : (index + 1) * part_rows]


def dense_left(x_pairs, outs, n_row, dense):
    _, span, piece_len = x_pairs[0].shape
    count, rows = n_row // 2, span * span // piece_len
    return call(
        functools.partial(left_kernel, n_row),
        [*x_pairs, dense, *outs],
        [
            held(count, span, piece_len),
            held(count, span + rows // count, piece_len),
            held(rows, piece_len),
        ],
        limit=VMEM_LIMIT,
        flops=4 * span * dense.size,
    )


def sparse_tiles(tiles, sizes):
    tile_rows, tile_cols, tile_count, tile_entries = tiles
    n_row, n_col, piece_blocks = sizes
    entries, rows, cols = tile_entries[0, 0], tile_rows[0, 0], tile_cols[0, 0]
    row_shift = shift_of(lax.axis_index("col"), rows // piece_blocks, n_col)
    col_shift = shift_of(lax.axis_index("row"), cols // piece_blocks, n_row)
    col_place = col_shift % 2 * (n_row // 2) + col_shift // 2
    positions = (
        row_shift * piece_blocks + rows % piece_blocks,
        col_place * piece_blocks + cols % piece_blocks,
        tile_count[0, 0],
    )
    entries = jnp.where(entries > HALF_MODULUS, entries - MODULUS, entries)
    return positions, jnp.stack(balanced_digits(entries), 1).astype(jnp.bfloat16)


def sparse_product(vector, spec, places, targets, count, blocks, a_digits):
    span, tile_len = vector.shape[0], a_digits.shape[-1]
    v_digits = stacked_digits(vector).reshape(2 * span, -1, tile_len)
    picked = jnp.take(v_digits, places, axis=1)
    products = jnp.einsum(spec, picked, a_digits, preferred_element_type=jnp.float32)
    products = reduce_centered(products)
    residues = combine(
        products[:, 0, :span],
        products[:, 0, span:] + products[:, 1, :span],
        products[:, 1, span:],
    )
    live = jnp.arange(targets.shape[0], dtype=jnp.int32) < count
    onehot = targets[None, :] == jnp.arange(blocks, dtype=jnp.int32)[:, None]
    onehot = (onehot & live[None, :]).astype(jnp.float32)
    summed = jnp.einsum("bt,twi->wbi", onehot, residues, precision=lax.Precision.HIGHEST)
    return reduce_centered(summed).reshape(span, blocks * tile_len)


def sparse_second(odds, evens, span, n_col, tails, positions, a_digits):
    rows, cols, count = positions
    pieces = [*evens, *odds]
    piece_len = pieces[0].shape[1]
    blocks = n_col * piece_len // a_digits.shape[-1]
    vector = reduce_centered(jnp.concatenate([piece[:span] for piece in pieces], 1))
    product = sparse_product(vector, "ntk,tdik->tdni", cols, rows, count, blocks, a_digits)
    packed = functools.reduce(jnp.add, [piece[span:] for piece in pieces])
    packed = half_of_core(jnp.concatenate([packed, *tails], 0))
    outs = [product[:, e * piece_len : (e + 1) * piece_len] for e in range(n_col)]
    return [jnp.concatenate([out, packed], 0) for out in outs]


def sparse_left(x_pairs, outs, n_row, positions, a_digits):
    rows, cols, count = positions
    n_col = 2 * x_pairs[0].shape[0]
    x_pieces = [x_pairs[e % 2][e // 2] for e in range(n_col)]
    piece_len = x_pieces[0].shape[1]
    values = jnp.concatenate(x_pieces, 1)
    values = jnp.where(values > HALF_MODULUS, values - MODULUS, values)
    blocks = n_row * piece_len // a_digits.shape[-1]
    product = sparse_product(values, "nti,tdik->tdnk", rows, cols, count, blocks, a_digits)
    pieces = [product[:, d * piece_len : (d + 1) * piece_len] for d in range(n_row)]
    term = 0.0
    for x_piece, rows_piece in zip(x_pieces, outs):
        term = term + project([(centred_digits(x_piece), stacked_digits(rows_piece))])
    odds = jnp.stack(pieces[n_row // 2 :])
    below = term.reshape(odds.shape[0], -1, piece_len)
    return jnp.stack(pieces[: n_row // 2]), jnp.concatenate([odds, below], 1), term


def add_and_part(kept, came, term, before=()):
    count, span, piece_len = kept.shape
    half, rows = count // 2, term.shape[0]
    part = rows // half if half > 1 else 0

    def kernel(kept_ref, came_ref, term_ref, evens_ref, odds_ref, out_ref):
        below = [came_ref[index, span:, :] for index in range(count)]
        total = term_ref[...] + jnp.concatenate(below, 0)
        out_ref[...] = total
        for index in range(count):
            piece = kept_ref[index] + came_ref[index, :span, :]
            if index % 2 == 0:
                evens_ref[index // 2] = piece
            else:
                odds_ref[index // 2, :span, :] = piece
        if part:
            for index in range(half):
                odds_ref[index, span:, :] = total[index * part : (index + 1) * part]

    outs = [
        held(half, span, piece_len),
        held(half, span + part, piece_len),
        held(rows, piece_len),
    ]
    return call(kernel, [kept, came, term], outs, before)


def append_projections(kept, came, term, term_came, pieces, vector_1):
    span, piece_len = pieces[0].shape
    rows = term.shape[0]

    def kernel(*refs):
        piece_refs, refs = refs[: len(pieces)], refs[len(pieces) :]
        vector_ref, kept_ref, came_ref, term_ref, term_came_ref, out_ref, first_ref = refs
        summed = functools.reduce(jnp.add, [ref[...] for ref in piece_refs])
        out_ref[:span, :] = summed
        w_digits = stacked_digits(reduce_centered(kept_ref[0] + came_ref[0]))
        first_ref[...] = term_ref[...] + term_came_ref[...]
        for index, vector in enumerate([summed, vector_ref[...]]):
            start = span + index * rows
            digits = stacked_digits(reduce_centered(vector))
            out_ref[start : start + rows, :] = project([(w_digits, digits)])

    outs = [held(span + 2 * rows, piece_len), held(rows, piece_len)]
    return call(kernel, [*pieces, vector_1, kept, came, term, term_came], outs)


def multiply_mod(left, right):
    span = left.shape[0]
    left = stacked_digits(left)
    high, low = (part.astype(jnp.bfloat16) for part in balanced_digits(right))
    by_high = jnp.dot(left, high, preferred_element_type=jnp.float32)
    by_low = jnp.dot(left, low, preferred_element_type=jnp.float32)
    return combine(
        reduce_centered(by_high[:span]), by_low[:span] + by_high[span:], by_low[span:]
    )


def sigma_update(mine, other, span):
    rows = span * span // mine.shape[1]

    def kernel(mine_ref, other_ref, out_ref):
        first = lax.axis_index("row") % 2 == 0
        mine, other = reduce_centered(mine_ref[...]), reduce_centered(other_ref[...])
        packed = jnp.concatenate([jnp.where(first, mine, other), jnp.where(first, other, mine)], 0)
        c_3, c_2, c_1 = (
            unpack_square(packed[index * rows : (index + 1) * rows], span) for index in range(3)
        )
        e_2 = reduce_centered(c_1 - multiply_mod(c_1, c_2))
        both = reduce_centered(c_1 + e_2)
        start = multiply_mod(e_2, c_1)
        rest = c_1 - multiply_mod(both, c_2)
        e_3 = reduce_centered(multiply_mod(start, c_3) + rest)
        out_ref[0] = canonical(-multiply_mod(e_3, start)) * (1.0 / MODULUS)
        out_ref[1] = canonical(start + multiply_mod(e_3, both)) * (1.0 / MODULUS)
        out_ref[2] = canonical(-both - e_3) * (1.0 / MODULUS)

    outs = [jax.ShapeDtypeStruct((STEP_COUNT, span, span), jnp.float32)]
    return call(kernel, [mine, other], outs)[0]


def local(tile_entries, tile_rows, tile_cols, tile_count, block_x, block_y):
    _, _, slot_count, tile_len, _ = tile_entries.shape
    span, piece_len = block_y.shape
    piece_blocks = piece_len // tile_len
    n_row, n_col = lax.axis_size("row"), lax.axis_size("col")
    packed_rows = span * span // piece_len
    tiles = (tile_rows, tile_cols, tile_count, tile_entries)
    sizes = (n_row, n_col, piece_blocks)
    is_dense = n_col * piece_blocks * n_row * piece_blocks <= DENSE_CELLS * slot_count
    if is_dense:
        dense, x_own, y_own, token = build_dense(tiles, block_x, block_y, sizes)
        before = [token]
    else:
        positions, a_digits = sparse_tiles(tiles, sizes)
        x_own, y_own, before = block_x, block_y, []

    def multiply_evens(evens):
        return dense_first(evens, span, dense) if is_dense else evens

    def multiply(evens, before=(), tails=()):
        odds, sums = gather_odds(evens, "row"), multiply_evens(evens)
        if is_dense:
            return dense_second(odds, evens, sums, span, n_col, tails, dense, before)
        return sparse_second(odds, evens, span, n_col, tails, positions, a_digits)

    y_came = fetch_evens(block_y, "row")
    x_came = fetch_evens(block_x, "col")
    evens = stack_after([y_own] + y_came, [*before, *x_came])
    x_evens = stack_after([x_own] + x_came)
    outs = multiply(evens, [x_evens])
    x_pairs = [x_evens, gather_odds(x_evens, "col")]
    if is_dense:
        w_kept, w_odds, term = dense_left(x_pairs, outs, n_row, dense)
    else:
        w_kept, w_odds, term = sparse_left(x_pairs, outs, n_row, positions, a_digits)
    vector_1 = sum_after(scatter_pieces(outs, "col"), [w_odds])
    w_came = fetch(w_odds, "row", 1)
    evens = gather_evens(vector_1, "row")
    if is_dense:
        outs = dense_whole(gather_odds(evens, "row"), evens, span, n_col, dense, [w_came])
    else:
        outs = multiply(evens)
    pieces = scatter_pieces(outs, "col")
    shift, before = 2, []
    while shift < n_row:
        w_kept, w_sent, term = add_and_part(w_kept, w_came, term, before)
        w_came = fetch(w_sent, "row", shift)
        shift, before = 2 * shift, [outs[0]]
    term_came = fetch(term, "row", n_row // 2)
    vector_2, first = append_projections(w_kept, w_came, term, term_came, pieces, vector_1)
    outs = multiply(gather_evens(vector_2, "row"), tails=[first])
    pieces = scatter_pieces(outs, "col")
    terms = functools.reduce(jnp.add, [piece[span:] for piece in pieces])
    vector_3 = functools.reduce(jnp.add, [piece[:span] for piece in pieces])
    return sigma_update(terms, fetch(terms, "row", 1), span), canonical(vector_3) * (1.0 / MODULUS)


def solution(mesh):
    placed = (
        P("row", "col", None, None, None),
        P("row", "col", None),
        P("row", "col", None),
        P("row", "col"),
        P(None, ("row", "col")),
        P(None, ("row", "col")),
    )
    return jax.shard_map(
        local, mesh=mesh, in_specs=placed, out_specs=(P(), P(None, ("row", "col"))), check_vma=False
    )
```
